32 devices in a mesh: groups: 2 (over x), space: 8 (over z, y), member: 2 (over core).
Axes of the slice: x: 2, y: 2, z: 4, core: 2. Of those that a mesh axis runs over, the one named last changes fastest.
Arguments:
- latents: bfloat16 [8, 256, 1024], P(('groups', 'member'), 'space'), parts along dimension 0, may hold values from -6 to 6
- grid_embed: bfloat16 [4096, 1024], P(('groups', 'space')), parts along dimension 0, may hold values from -40 to 40
- norm_gain: float32 [1024], replicated, may hold values from 0.5 to 1.5
- w_msg: bfloat16 [1024, 1024], replicated, may hold values from -0.1875 to 0.1875
- w_hidden: bfloat16 [1024, 1024], replicated, may hold values from -0.1875 to 0.1875
- variable_projection: bfloat16 [1024, 100], replicated, may hold values from -0.1875 to 0.1875
- present_condition: float32 [8, 100, 2048], P(('groups', 'member'), None, 'space'), parts along dimension 0, may hold values from -6 to 6
- verifying_field: float32 [100, 4096], P(None, ('groups', 'space')), parts along dimension 1, may hold values from -6 to 6
- cell_surface: float32 [4096], P(('groups', 'space')), parts along dimension 0, may hold values from 0.6 to 12.6
- send_rows: int32 [8, 8, 8], P('space'), may hold values from 0 to 31, as said below
- edge_slot: int32 [12288], P('space'), may hold values from 0 to 63, as said below
- edge_dst: int32 [12288], P('space'), may hold values from 0 to 256, as said below
- edge_weight: float32 [12288], P('space'), may hold values from 0.25 to 4
Outputs:
- latent_grad: bfloat16 [8, 256, 1024], P(('groups', 'member'), 'space'), parts along dimension 0
- loss: float32 [2], P('groups'), parts along dimension 0
- msg_weight_grad: float32 [2048, 1024], P(('groups', 'space', 'member')), parts along dimension 0
- hidden_weight_grad: float32 [2048, 1024], P(('groups', 'space', 'member')), parts along dimension 0
- out_weight_grad: float32 [2048, 100], P(('groups', 'space', 'member')), parts along dimension 0
The draws below stay inside these ranges and needn't reach their ends.
There are 2 independent parts, one for each index of `groups`. The reference program is written for one: setup_inputs(seed, part) draws one part's arguments, and reference() takes and returns one part's arrays. A program takes and returns all parts, laid end to end along the dimension named above; an argument that names none is the same for every part. Nothing has to cross between parts.
Inputs may be any that keep to these rules, and one draw needn't show every extreme that they name: Each list send_rows[s, r] holds 8 different local rows of shard s. `edge_slot`: every value 0 to 63 is named by some live edge of every shard; padded entries hold 0. `edge_dst`: within each shard's block the values never fall; every grid point receives 2 to 6 live edges; padded entries, all at the end of a shard's block, hold 256; in every draw one shard has no padded entry.
All inputs are finite; a program needn't handle non-finite values.
Results may differ from the reference program's by a relative error of at most 0.017.
Values may be sent and summed in bfloat16 or wider, within the bound.
No kernel may reach another device: no remote copies, remote signals or barrier semaphores. Data moves between devices by JAX's collectives and lax.ppermute only.
A program may use at most 128 MiB of HBM per device.

```python
import math
import jax
import jax.numpy as jnp
from jax import lax

D = 1024
VARS = 100
POINT_DEV = 256
NODE_DEV = 32
CAP = 8
KMOST = 6
MEMBERS = 4
POINTS = 2048
NODES = 256
EDGE_DEV = 1536
N_SPACE = 8


def edge_plan(key):
    order_rank = jax.random.permutation(jax.random.fold_in(key, 101), N_SPACE).astype(jnp.int32)
    ceiling = 2 + (KMOST - 2) * order_rank // max(N_SPACE - 1, 1)
    chosen = jax.random.randint(jax.random.fold_in(key, 102), (N_SPACE, POINT_DEV), 2, KMOST + 1)
    counts = jnp.minimum(chosen, ceiling[:, None])
    counts = jnp.where(order_rank[:, None] == N_SPACE - 1, KMOST, counts).astype(jnp.int32)
    bounds = jnp.cumsum(counts, axis=1).astype(jnp.int32)
    totals = bounds[:, -1]
    edge_index = jnp.arange(EDGE_DEV).astype(jnp.int32)
    targets = jax.vmap(lambda row: jnp.searchsorted(row, edge_index, side='right'))(bounds).astype(jnp.int32)
    is_live = edge_index[None, :] < totals[:, None]
    targets = jnp.where(is_live, targets, POINT_DEV).astype(jnp.int32)
    spread = N_SPACE * CAP
    shard_keys = jax.random.split(jax.random.fold_in(key, 103), N_SPACE)
    orders = jax.vmap(lambda k: jax.random.permutation(k, spread))(shard_keys).astype(jnp.int32)
    others = jax.random.randint(jax.random.fold_in(key, 104), (N_SPACE, EDGE_DEV), 0, spread).astype(jnp.int32)
    leading = jnp.pad(orders, ((0, 0), (0, EDGE_DEV - spread)))
    slots = jnp.where(edge_index[None, :] < spread, leading, others)
    slots = jnp.where(is_live, slots, 0).astype(jnp.int32)
    return (slots.reshape(-1), targets.reshape(-1))


def draw_edge_slot(key, part):
    plan = edge_plan(key)
    return plan[0]


def draw_edge_dst(key, part):
    plan = edge_plan(key)
    return plan[1]


def draw_send_rows(key, part):
    key = jax.random.fold_in(key, 7)
    pair_keys = jax.random.split(key, N_SPACE * N_SPACE)
    chosen = jax.vmap(lambda k: jax.random.permutation(k, NODE_DEV)[:CAP])(pair_keys)
    return chosen.reshape(N_SPACE, N_SPACE, CAP).astype(jnp.int32)


def draw_cell_surface(key, part):
    key = jax.random.fold_in(key, 9)
    fraction = jnp.arange(POINTS).astype(jnp.float32) / max(POINTS - 1, 1)
    roughness = jnp.exp(jax.random.uniform(key, (POINTS,), minval=math.log(0.7), maxval=math.log(1.4)))
    return ((1.0 + 2.0 * fraction) * roughness).astype(jnp.float32)


def draw_grid_embed(key, part):
    key = jax.random.fold_in(key, 5)
    first_key, second_key, third_key = jax.random.split(key, 3)
    columns = jnp.exp(jax.random.uniform(second_key, (D,), minval=0.0, maxval=math.log(10.0))) / 3.0
    row_scale = jnp.exp(jax.random.uniform(third_key, (POINTS, 1), minval=0.0, maxval=math.log(10.0))) / 3.0
    base = jax.random.normal(first_key, (POINTS, D))
    base = jnp.clip(base, -4.0, 4.0)
    return jnp.clip(base * columns * row_scale, -40.0, 40.0).astype(jnp.bfloat16)


def level_of(stream_key, dims, cuts, low, high):
    def one(axis_at, parts):
        steps = jax.random.uniform(jax.random.fold_in(jax.random.fold_in(stream_key, 6), axis_at), (parts,), jnp.float32, low / len(cuts), high / len(cuts))
        return jnp.repeat(jnp.exp(steps), dims[axis_at] // parts).reshape((-1,) + (1,) * (len(dims) - axis_at - 1))

    factor_of = one(*cuts[0])
    for cut in cuts[1:]:
        factor_of = factor_of * one(*cut)
    return factor_of


def centred(rng, dims, scale, bound, cuts=(), kind=jnp.bfloat16):
    array = scale * jax.random.normal(rng, dims, jnp.float32)
    if cuts:
        array = array * level_of(rng, dims, cuts, -0.22, 0.18)
    return jnp.clip(array, -bound, bound).astype(kind)


def setup_inputs(seed: int = 0, part: int = 0) -> dict:
    keys = jax.random.split(jax.random.key(seed), 14)
    own_keys = jax.random.split(jax.random.fold_in(keys[13], part), 14)
    latents = centred(own_keys[0], (MEMBERS, NODES, D), 1.0, 6.0, ((0, 2), (1, 8)))
    grid_embed = draw_grid_embed(jax.random.fold_in(jax.random.fold_in(keys[13], part), 71), part)
    norm_gain = jnp.clip(1.0 + 0.1 * jax.random.normal(keys[2], (D,), jnp.float32), 0.5, 1.5)
    w_msg = centred(keys[3], (D, D), D ** -0.5, 0.1875)
    w_hidden = centred(keys[4], (D, D), D ** -0.5, 0.1875)
    variable_projection = centred(keys[5], (D, VARS), D ** -0.5, 0.1875)
    present_condition = centred(own_keys[6], (MEMBERS, VARS, POINTS), 1.0, 6.0, ((0, 2), (2, 8)), jnp.float32)
    verifying_field = centred(own_keys[7], (VARS, POINTS), 1.0, 6.0, ((1, 8),), jnp.float32)
    cell_surface = draw_cell_surface(jax.random.fold_in(jax.random.fold_in(keys[13], part), 71), part)
    send_rows = draw_send_rows(jax.random.fold_in(keys[13], 71), part)
    edge_slot = draw_edge_slot(jax.random.fold_in(keys[13], 71), part)
    edge_dst = draw_edge_dst(jax.random.fold_in(keys[13], 71), part)
    edge_weight = jnp.clip(jnp.exp(math.log(4.0) - 2.7725887 * jax.random.uniform(keys[12], (N_SPACE * EDGE_DEV,), jnp.float32) ** level_of(keys[12], (N_SPACE * EDGE_DEV,), ((0, 8),), -0.2, 0.2)), 0.25, 4.0)
    return {"latents": latents, "grid_embed": grid_embed, "norm_gain": norm_gain, "w_msg": w_msg, "w_hidden": w_hidden, "variable_projection": variable_projection, "present_condition": present_condition, "verifying_field": verifying_field, "cell_surface": cell_surface, "send_rows": send_rows, "edge_slot": edge_slot, "edge_dst": edge_dst, "edge_weight": edge_weight}


smoothing = 0.1
epsilon = 1e-06

def matmul(left, right):
    return jnp.dot(left.astype(jnp.float32), right.astype(jnp.float32), precision=lax.Precision.HIGHEST, preferred_element_type=jnp.float32)

def eased_magnitude(delta):
    return jnp.sqrt(delta * delta + smoothing * smoothing)

def eased_sign(delta):
    return delta / jnp.sqrt(delta * delta + smoothing * smoothing)

def loss_pieces(realization_field, reference_analysis, location_factors):
    realization_total = realization_field.shape[0]
    leading_realization = eased_magnitude(realization_field - reference_analysis[None])
    couple_dispersion = realization_field[:, None] - realization_field[None, :]
    above_diagonal = (lax.broadcasted_iota(jnp.int32, (realization_total, realization_total), 0) < lax.broadcasted_iota(jnp.int32, (realization_total, realization_total), 1)).astype(realization_field.dtype)
    spread_term = lax.optimization_barrier(jnp.sum(eased_magnitude(couple_dispersion) * above_diagonal[:, :, None, None], axis=(0, 1)))
    score = lax.optimization_barrier(jnp.mean(leading_realization, axis=0)) - spread_term / (realization_total * (realization_total - 1))
    accumulated_pieces = jnp.sum(score * location_factors[None, :])
    eased_derivative = eased_sign(realization_field - reference_analysis[None]) / realization_total - lax.optimization_barrier(jnp.sum(eased_sign(couple_dispersion), axis=1)) / (realization_total * (realization_total - 1))
    return (accumulated_pieces, (eased_derivative * location_factors[None, None, :]).astype(jnp.bfloat16))

def reference(latents, grid_embed, norm_gain, w_msg, w_hidden, variable_projection, present_condition, verifying_field, cell_surface, send_rows, edge_slot, edge_dst, edge_weight):
    shard_ids = (jnp.arange(N_SPACE * EDGE_DEV) // EDGE_DEV).astype(jnp.int32)
    sender = (edge_slot // CAP).astype(jnp.int32)
    position = (edge_slot % CAP).astype(jnp.int32)
    source_node = (sender * NODE_DEV + send_rows[sender, shard_ids, position]).astype(jnp.int32)
    is_live = edge_dst < POINT_DEV
    grid_point = jnp.where(is_live, shard_ids * POINT_DEV + edge_dst, POINTS).astype(jnp.int32)
    clipped = jnp.minimum(grid_point, POINTS - 1)
    factors = jnp.where(is_live, edge_weight, jnp.zeros_like(edge_weight))
    weight_sum = jax.ops.segment_sum(factors, grid_point, num_segments=POINTS + 1)[:POINTS]
    embed = grid_embed.astype(jnp.float32)
    saved = []
    realization_fields = []
    for realization_number in range(MEMBERS):
        messages = matmul(latents[realization_number], w_msg).astype(jnp.bfloat16)
        picked = messages[source_node].astype(jnp.float32) * factors[:, None]
        weighted = jax.ops.segment_sum(picked, grid_point, num_segments=POINTS + 1)[:POINTS]
        hidden = embed + weighted / weight_sum[:, None]
        root_mean = jnp.sqrt(lax.optimization_barrier(jnp.mean(hidden * hidden, axis=-1, keepdims=True)) + epsilon)
        unit_rows = hidden / root_mean
        normed = (unit_rows * norm_gain).astype(jnp.bfloat16)
        inner = matmul(normed, w_hidden)
        live_realizations = jax.nn.gelu(inner).astype(jnp.bfloat16)
        realization_fields.append(present_condition[realization_number] + matmul(live_realizations, variable_projection).T)
        saved.append((unit_rows, root_mean, normed, inner, live_realizations))
    realization_field = jnp.stack(realization_fields)
    accumulated_pieces, field_sensitivity = loss_pieces(realization_field, verifying_field, cell_surface)
    loss = (accumulated_pieces / (POINTS * VARS)).reshape(1)
    hidden_weight_grad = jnp.zeros((D, D), jnp.float32)
    out_weight_grad = jnp.zeros((D, VARS), jnp.float32)
    msg_weight_grad = jnp.zeros((D, D), jnp.float32)
    latent_list = []
    for realization_number in range(MEMBERS):
        unit_rows, root_mean, normed, inner, live_realizations = saved[realization_number]
        member_grad = field_sensitivity[realization_number].T
        grad_act = matmul(member_grad, variable_projection.T)
        out_weight_grad = out_weight_grad + matmul(live_realizations.T, member_grad)
        unused, pullback = jax.vjp(jax.nn.gelu, inner)
        grad_inner = pullback(grad_act)[0].astype(jnp.bfloat16)
        hidden_weight_grad = hidden_weight_grad + matmul(normed.T, grad_inner)
        grad_normed = matmul(grad_inner, w_hidden.T)
        scaled = grad_normed * norm_gain
        grad_hidden = (scaled - unit_rows * lax.optimization_barrier(jnp.mean(scaled * unit_rows, axis=-1, keepdims=True))) / root_mean
        grad_weighted = grad_hidden / weight_sum[:, None]
        edge_rows = grad_weighted[clipped] * factors[:, None]

        def add_shard(carry, pieces):
            shard_rows, shard_nodes = pieces
            shard_part = jax.ops.segment_sum(shard_rows, shard_nodes, num_segments=NODES)
            return (carry + lax.optimization_barrier(shard_part.astype(jnp.bfloat16)).astype(carry.dtype), None)
        grad_sum, unused_out = lax.scan(add_shard, jnp.zeros((NODES, D), edge_rows.dtype), (edge_rows.reshape(N_SPACE, EDGE_DEV, D), source_node.reshape(N_SPACE, EDGE_DEV)))
        grad_rows = grad_sum.astype(jnp.bfloat16)
        latent_list.append(matmul(grad_rows, w_msg.T).astype(jnp.bfloat16))
        msg_weight_grad = msg_weight_grad + matmul(latents[realization_number].T, grad_rows)
    latent_grad = jnp.stack(latent_list)
    return (latent_grad, loss, msg_weight_grad, hidden_weight_grad, out_weight_grad)
```

```python
import functools

import jax
import jax.numpy as jnp
from jax import lax
from jax.experimental import pallas as pl
from jax.experimental.pallas import tpu as pltpu
from jax.sharding import PartitionSpec as P

smoothing = 0.1
epsilon = 1e-06
tile = 256
lanes = 128
f32 = jnp.float32
bf16 = jnp.bfloat16


def mm(left, right, left_dim, right_dim):
    return lax.dot_general(
        left, right, (((left_dim,), (right_dim,)), ((), ())), preferred_element_type=f32
    )


def call(body, outs, args, scratch=(), limit=30, scalars=()):
    whole = pl.BlockSpec(memory_space=pltpu.VMEM)
    small = pl.BlockSpec(memory_space=pltpu.SMEM)
    return pl.pallas_call(
        body,
        out_shape=outs,
        in_specs=[small if i in scalars else whole for i in range(len(args))],
        out_specs=[whole] * len(outs),
        scratch_shapes=scratch,
        compiler_params=pltpu.CompilerParams(vmem_limit_bytes=limit * 2**20),
    )(*args)


def shape(dims, kind):
    return jax.ShapeDtypeStruct(dims, kind)


def select_kernel(lists_ref, latents_ref, send_ref, pick_ref):
    peers, cap = lists_ref.shape
    members, nodes, width = latents_ref.shape
    at = lax.broadcasted_iota(jnp.int32, (cap, members * nodes), 0)
    column = lax.broadcasted_iota(jnp.int32, (cap, members * nodes), 1)
    rows = []
    for peer in range(peers):
        wanted = jnp.zeros((cap, members * nodes), jnp.int32)
        for j in range(cap):
            wanted = jnp.where(at == j, lists_ref[peer, j], wanted)
        for member in range(members):
            rows.append((column == wanted + member * nodes).astype(f32))
    pick = jnp.concatenate(rows, axis=0).astype(bf16)
    pick_ref[...] = pick
    table = latents_ref[...].reshape(members * nodes, width)
    send_ref[...] = mm(pick, table, 1, 0).astype(bf16).reshape(send_ref.shape)


def edge_kernel(cap, members, slot_ref, dst_ref, weight_ref, share_ref):
    slot, dst, weight = slot_ref[...], dst_ref[...], weight_ref[...]
    rows = share_ref.shape[0] // 2
    points = share_ref.shape[1] // members
    edges = slot.shape[1]
    sender = lax.div(slot, cap)
    place = sender * (members * cap) + (slot - sender * cap)
    hit = lax.broadcasted_iota(jnp.int32, (rows, edges), 0) == place
    into = (lax.broadcasted_iota(jnp.int32, (points, edges), 0) == dst).astype(f32).astype(bf16)
    high = weight.astype(bf16).astype(f32)
    table = mm(jnp.where(hit, high, 0.0).astype(bf16), into, 1, 1) + mm(
        jnp.where(hit, weight - high, 0.0).astype(bf16), into, 1, 1
    )
    table = table / jnp.sum(table, axis=0, keepdims=True)
    for member in range(members):
        high = table.astype(bf16)
        columns = slice(member * points, (member + 1) * points)
        share_ref[0:rows, columns] = high
        share_ref[rows : 2 * rows, columns] = (table - high.astype(f32)).astype(bf16)
        table = jnp.concatenate([table[rows - cap :], table[: rows - cap]], axis=0)


def forward_kernel(
    received_ref, w_msg_ref, share_ref, embed_ref, gain_ref, w_hidden_ref, project_ref, present_ref,
    field_ref, sent_ref, normed_ref, active_ref, slope_ref, unit_ref, inverse_ref,
):
    points, width = embed_ref.shape
    members, variables, _ = present_ref.shape
    messages = mm(received_ref[...], w_msg_ref[...], 1, 0).astype(bf16)
    messages = jnp.concatenate([messages, messages], axis=0)
    gain = gain_ref[...]
    for begin in range(0, members * points, lanes):
        rows = slice(begin, begin + lanes)
        source = slice(begin % points, begin % points + lanes)
        hidden = embed_ref[source, :].astype(f32) + mm(share_ref[:, rows], messages, 0, 0)
        inverse = lax.rsqrt(jnp.mean(hidden * hidden, axis=-1, keepdims=True) + epsilon)
        unit = hidden * inverse
        unit_ref[rows, :] = unit
        inverse_ref[rows, :] = inverse
        normed_ref[rows, :] = (unit * gain).astype(bf16)
    root = 0.7978845608028654
    cubic = 0.044715
    for member in range(members):
        rows = slice(member * points, (member + 1) * points)
        for begin in range(0, width, tile):
            columns = slice(begin, begin + tile)
            inner = mm(normed_ref[rows, :], w_hidden_ref[:, columns], 1, 0)
            square = inner * inner
            bend = jnp.tanh(inner * (root + root * cubic * square))
            half = 0.5 + 0.5 * bend
            active_ref[rows, columns] = (inner * half).astype(bf16)
            slope_ref[rows, columns] = half + (0.5 * inner) * (1.0 - bend * bend) * (
                root + 3.0 * root * cubic * square
            )
        out = mm(project_ref[...], active_ref[rows, :], 1, 1)
        field = present_ref[member] + out[:variables]
        field_ref[member] = field
        sent_ref[member] = field.astype(bf16)


def turn_kernel(core_ref, normed_ref, active_ref, received_ref, normed_t_ref, active_t_ref, received_t_ref, *, block):
    core = core_ref[0]
    width = normed_ref.shape[1]
    for source, target in (
        (normed_ref, normed_t_ref), (active_ref, active_t_ref), (received_ref, received_t_ref)
    ):
        for begin in range(0, width, tile):
            turned = source[:, begin : begin + tile].T
            for piece in range(0, tile, block):
                index = (begin + piece) // block
                at = index // 2 * block
                target[(index % 2) ^ core, at : at + block, :] = turned[piece : piece + block]


def score_kernel(
    own_ref, other_ref, truth_ref, cell_ref, project_ref, slope_ref, normed_t_ref, active_t_ref,
    inner_ref, hidden_ref, out_ref, pred_ref,
):
    members, variables, points = own_ref.shape
    width = slope_ref.shape[1]
    total = 2 * members
    pairs = total * (total - 1)

    def eased(delta):
        square = delta * delta + smoothing * smoothing
        inverse = lax.rsqrt(square)
        return square * inverse, delta * inverse

    truth, cell = truth_ref[...], cell_ref[...]
    own = [own_ref[m] for m in range(members)]
    other = [other_ref[m].astype(f32) for m in range(members)]
    score = jnp.zeros_like(truth)
    pulls = [jnp.zeros_like(truth) for _ in own]
    grads = []
    for m in range(members):
        size, sign = eased(own[m] - truth)
        score = score + size * (1.0 / total)
        grads.append(sign * (1.0 / total))
    for m in range(members):
        for n in range(m + 1, members):
            size, sign = eased(own[m] - own[n])
            score = score - size * (1.0 / pairs)
            pulls[m] = pulls[m] + sign
            pulls[n] = pulls[n] - sign
        for n in range(members):
            size, sign = eased(own[m] - other[n])
            score = score - size * (0.5 / pairs)
            pulls[m] = pulls[m] + sign
    loss = jnp.sum(score * cell)
    pred_ref[...] = jnp.zeros_like(pred_ref)
    for m in range(members):
        grad = (grads[m] - pulls[m] * (1.0 / pairs)) * cell
        pred_ref[0:variables, m * points : (m + 1) * points] = grad
    pred = pred_ref[...].astype(bf16)
    for m in range(members):
        rows = slice(m * points, (m + 1) * points)
        part = pred[:, rows]
        for begin in range(0, width, tile):
            columns = slice(begin, begin + tile)
            grad = mm(part, project_ref[:, columns], 0, 0)
            inner_ref[rows, columns] = (grad * slope_ref[rows, columns]).astype(bf16)
    for begin in range(0, width, tile):
        columns = slice(begin, begin + tile)
        hidden_ref[:, columns] = mm(normed_t_ref[1], inner_ref[:, columns], 1, 0).astype(bf16)
    for side in range(2):
        part = mm(active_t_ref[side], pred, 1, 1)
        spot = lax.broadcasted_iota(jnp.int32, part.shape, 1) == variables
        out_ref[side] = jnp.where(spot, loss, part)


def back_kernel(
    inner_ref, w_hidden_ref, gain_ref, unit_ref, inverse_ref, share_ref, normed_t_ref, received_t_ref,
    slots_ref, hidden_ref, message_ref, scaled_ref, grad_ref,
):
    width = gain_ref.shape[1]
    rows_all = inner_ref.shape[0]
    rows_slot = share_ref.shape[0] // 2
    for begin_row in range(0, rows_all, tile):
        rows = slice(begin_row, begin_row + tile)
        dots = jnp.zeros((tile, 1), f32)
        for begin in range(0, width, tile):
            columns = slice(begin, begin + tile)
            scaled = mm(inner_ref[rows, :], w_hidden_ref[columns, :], 1, 1) * gain_ref[:, columns]
            dots = dots + jnp.sum(scaled * unit_ref[rows, columns], axis=-1, keepdims=True)
            scaled_ref[rows, columns] = scaled
        dots = dots * (1.0 / width)
        inverse = inverse_ref[rows, :]
        for begin in range(0, width, tile):
            columns = slice(begin, begin + tile)
            grad_ref[rows, columns] = (
                (scaled_ref[rows, columns] - unit_ref[rows, columns] * dots) * inverse
            ).astype(bf16)
    for begin in range(0, width, tile):
        columns = slice(begin, begin + tile)
        both = mm(share_ref[...], grad_ref[:, columns], 1, 0)
        slots = (both[:rows_slot] + both[rows_slot:]).astype(bf16)
        slots_ref[:, columns] = slots
        for side in range(2):
            message_ref[side, :, columns] = mm(received_t_ref[side], slots, 1, 0).astype(bf16)
    for begin in range(0, width, tile):
        columns = slice(begin, begin + tile)
        hidden_ref[:, columns] = mm(normed_t_ref[0], inner_ref[:, columns], 1, 0)


def latent_kernel(pick_ref, back_ref, w_msg_ref, grad_ref):
    rows = mm(pick_ref[...], back_ref[...], 0, 0).astype(bf16)
    grad_ref[...] = mm(rows, w_msg_ref[...], 1, 1).astype(bf16).reshape(grad_ref.shape)


def on_device(
    latents, grid_embed, norm_gain, w_msg, w_hidden, variable_projection, present_condition, verifying_field,
    cell_surface, send_rows, edge_slot, edge_dst, edge_weight,
):
    members, nodes, width = latents.shape
    points = grid_embed.shape[0]
    variables = variable_projection.shape[1]
    peers = lax.axis_size("space")
    cores = lax.axis_size("member")
    cap = send_rows.shape[2]
    slot_rows = peers * members * cap
    rows_all = members * points
    half = width // cores
    block = half // peers
    core = lax.axis_index("member").astype(jnp.int32).reshape(1)
    swap = [(0, 1), (1, 0)]

    send, pick = call(
        select_kernel,
        [shape((peers, members * cap, width), bf16), shape((slot_rows, members * nodes), bf16)],
        [send_rows[0], latents],
        scalars=(0,),
    )
    received = lax.all_to_all(send, "space", split_axis=0, concat_axis=0, tiled=True)
    received = received.reshape(slot_rows, width)
    (share,) = call(
        functools.partial(edge_kernel, cap, members),
        [shape((2 * slot_rows, rows_all), bf16)],
        [edge_slot[None], edge_dst[None], edge_weight[None]],
    )
    project = jnp.pad(variable_projection.T, ((0, lanes - variables), (0, 0)))
    gain = norm_gain[None]
    field, sent, normed, active, slope, unit, inverse = call(
        forward_kernel,
        [
            shape((members, variables, points), f32),
            shape((members, variables, points), bf16),
            shape((rows_all, width), bf16),
            shape((rows_all, width), bf16),
            shape((rows_all, width), f32),
            shape((rows_all, width), f32),
            shape((rows_all, 1), f32),
        ],
        [received, w_msg, share, grid_embed, gain, w_hidden, project, present_condition],
    )
    other = lax.ppermute(sent, "member", swap)
    normed_t, active_t, received_t = call(
        functools.partial(turn_kernel, block=block),
        [
            shape((cores, half, rows_all), bf16),
            shape((cores, half, rows_all), bf16),
            shape((cores, half, slot_rows), bf16),
        ],
        [core, normed, active, received],
        scalars=(0,),
    )
    grad_inner, hidden_send, out_parts = call(
        score_kernel,
        [
            shape((rows_all, width), bf16),
            shape((half, width), bf16),
            shape((cores, half, lanes), f32),
        ],
        [field, other, verifying_field, cell_surface[None], project, slope, normed_t, active_t],
        scratch=[pltpu.VMEM((lanes, rows_all), f32)],
    )
    hidden_other = lax.ppermute(hidden_send, "member", swap)
    out_other = lax.ppermute(out_parts[1], "member", swap)
    slots, hidden_keep, message_parts = call(
        back_kernel,
        [
            shape((slot_rows, width), bf16),
            shape((half, width), f32),
            shape((cores, half, width), bf16),
        ],
        [grad_inner, w_hidden, gain, unit, inverse, share, normed_t, received_t],
        scratch=[pltpu.VMEM((rows_all, width), f32), pltpu.VMEM((rows_all, width), bf16)],
    )
    message_other = lax.ppermute(message_parts[1], "member", swap)

    def scatter(values):
        pieces = values.reshape(peers, block, values.shape[-1])
        arrived = lax.all_to_all(pieces, "space", split_axis=0, concat_axis=0, tiled=True)
        return jnp.sum(arrived.astype(f32), axis=0)

    back = lax.all_to_all(
        slots.reshape(peers, members * cap, width), "space", split_axis=0, concat_axis=0, tiled=True
    )
    hidden_weight_grad = scatter((hidden_keep + hidden_other.astype(f32)).astype(bf16))
    out_sum = scatter(out_parts[0] + out_other)
    msg_weight_grad = scatter((message_parts[0].astype(f32) + message_other.astype(f32)).astype(bf16))
    (latent_grad,) = call(
        latent_kernel, [shape(latents.shape, bf16)], [pick, back.reshape(slot_rows, width), w_msg]
    )
    loss = (out_sum[0, variables] / (points * peers * variables)).reshape(1)
    return (latent_grad, loss, msg_weight_grad, hidden_weight_grad, out_sum[:, :variables])


def solution(mesh):
    placed = (
        P(("groups", "member"), "space", None),
        P(("groups", "space"), None),
        P(),
        P(),
        P(),
        P(),
        P(("groups", "member"), None, "space"),
        P(None, ("groups", "space")),
        P(("groups", "space")),
        P("space", None, None),
        P("space"),
        P("space"),
        P("space"),
    )
    return jax.shard_map(
        on_device,
        mesh=mesh,
        in_specs=placed,
        out_specs=(
            P(("groups", "member"), "space", None),
            P("groups"),
            P(("groups", "space", "member"), None),
            P(("groups", "space", "member"), None),
            P(("groups", "space", "member"), None),
        ),
        check_vma=False,
    )
```

```python
import functools

import jax
import jax.numpy as jnp
from jax import lax
from jax.experimental import pallas as pl
from jax.experimental.pallas import tpu as pltpu
from jax.sharding import PartitionSpec as P

smoothing = 0.1
epsilon = 1e-06
tile = 256
lanes = 128
f32 = jnp.float32
bf16 = jnp.bfloat16


def mm(left, right, left_dim, right_dim):
    return lax.dot_general(
        left, right, (((left_dim,), (right_dim,)), ((), ())), preferred_element_type=f32
    )


def call(body, outs, args, scratch=(), limit=16, scalars=(), scalar_outs=()):
    whole = pl.BlockSpec(memory_space=pltpu.VMEM)
    small = pl.BlockSpec(memory_space=pltpu.SMEM)
    return pl.pallas_call(
        body,
        out_shape=[jax.ShapeDtypeStruct(dims, kind) for dims, kind in outs],
        in_specs=[small if i in scalars else whole for i in range(len(args))],
        out_specs=[small if i in scalar_outs else whole for i in range(len(outs))],
        scratch_shapes=scratch,
        compiler_params=pltpu.CompilerParams(vmem_limit_bytes=limit * 2**20),
    )(*args)


def place():
    space = lax.axis_index("space")
    return lax.div(space, 2), lax.rem(space, 2), lax.axis_index("member")


def swap(value, axis, size, step):
    return lax.ppermute(value, axis, [(i, i ^ step) for i in range(size)])


def select_kernel(lists_ref, latents_ref, pick_ref, *send_refs):
    peers, cap = lists_ref.shape
    members, nodes, width = latents_ref.shape
    me = lax.axis_index("space")
    at = lax.broadcasted_iota(jnp.int32, (cap, members * nodes), 0)
    column = lax.broadcasted_iota(jnp.int32, (cap, members * nodes), 1)
    rows = []
    for step in range(peers):
        peer = me ^ step
        wanted = jnp.zeros((cap, members * nodes), jnp.int32)
        for j in range(cap):
            wanted = jnp.where(at == j, lists_ref[peer, j], wanted)
        for member in range(members):
            rows.append((column == wanted + member * nodes).astype(f32))
    pick = jnp.concatenate(rows, axis=0).astype(bf16)
    pick_ref[...] = pick
    table = latents_ref[...].reshape(members * nodes, width)
    sent = mm(pick, table, 1, 0).astype(bf16)
    for step in range(peers):
        send_refs[step][...] = sent[step * members * cap : (step + 1) * members * cap]


def columns_kernel(block, latents_ref, own_ref, *rest):
    send_refs, held_ref = rest[:-1], rest[-1]
    members, nodes, width = latents_ref.shape
    _, line, core = place()
    table = latents_ref[...].reshape(members * nodes, width).astype(f32)
    for kind in range(4):
        parts = [table[:, at : at + block] for at in range(kind * block, width, 4 * block)]
        held_ref[kind] = jnp.concatenate(parts, axis=1).astype(bf16)
    mine = line * 2 + core
    own_ref[...] = held_ref[mine]
    for step in range(1, 4):
        send_refs[step - 1][...] = held_ref[mine ^ step]


def edge_kernel(cap, members, slot_ref, dst_ref, weight_ref, share_ref):
    edges = slot_ref.shape[0]
    slot = slot_ref[...].reshape(1, edges)
    dst = dst_ref[...].reshape(1, edges)
    weight = weight_ref[...].reshape(1, edges)
    rows = share_ref.shape[0] // 2
    points = share_ref.shape[1] // members
    sender = lax.div(slot, cap)
    spot = (sender ^ lax.axis_index("space")) * (members * cap) + (slot - sender * cap)
    hit = lax.broadcasted_iota(jnp.int32, (rows, edges), 0) == spot
    into = (lax.broadcasted_iota(jnp.int32, (points, edges), 0) == dst).astype(f32).astype(bf16)
    high = weight.astype(bf16).astype(f32)
    table = mm(jnp.where(hit, high, 0.0).astype(bf16), into, 1, 1) + mm(
        jnp.where(hit, weight - high, 0.0).astype(bf16), into, 1, 1
    )
    table = table / jnp.sum(table, axis=0, keepdims=True)
    for member in range(members):
        high = table.astype(bf16)
        columns = slice(member * points, (member + 1) * points)
        share_ref[0:rows, columns] = high
        share_ref[rows : 2 * rows, columns] = (table - high.astype(f32)).astype(bf16)
        table = jnp.concatenate([table[rows - cap :], table[: rows - cap]], axis=0)


def forward_kernel(
    peers, w_msg_ref, share_ref, embed_ref, gain_ref, w_hidden_ref, project_ref, present_ref, *rest
):
    received = rest[:peers]
    field_ref, sent_ref, normed_ref, active_ref, slope_ref, unit_ref, inverse_ref = rest[peers:]
    points, width = embed_ref.shape
    variables, members, _ = present_ref.shape
    arrived = jnp.concatenate([r[...] for r in received], axis=0)
    messages = mm(arrived, w_msg_ref[...], 1, 0).astype(bf16)
    messages = jnp.concatenate([messages, messages], axis=0)
    gain = gain_ref[...].reshape(1, width)
    for begin in range(0, members * points, lanes):
        rows = slice(begin, begin + lanes)
        source = slice(begin % points, begin % points + lanes)
        hidden = embed_ref[source, :].astype(f32) + mm(share_ref[:, rows], messages, 0, 0)
        inverse = lax.rsqrt(jnp.mean(hidden * hidden, axis=-1, keepdims=True) + epsilon)
        unit = hidden * inverse
        unit_ref[rows, :] = unit
        inverse_ref[rows, :] = inverse
        normed_ref[rows, :] = (unit * gain).astype(bf16)
    root = 0.7978845608028654
    cubic = 0.044715
    for member in range(members):
        rows = slice(member * points, (member + 1) * points)
        for begin in range(0, width, tile):
            columns = slice(begin, begin + tile)
            inner = mm(normed_ref[rows, :], w_hidden_ref[:, columns], 1, 0)
            square = inner * inner
            bend = jnp.tanh(inner * (root + root * cubic * square))
            half = 0.5 + 0.5 * bend
            active_ref[rows, columns] = (inner * half).astype(bf16)
            slope_ref[rows, columns] = half + (0.5 * inner) * (1.0 - bend * bend) * (
                root + 3.0 * root * cubic * square
            )
        field = present_ref[:, member, :] + mm(project_ref[...], active_ref[rows, :], 1, 1)
        field_ref[member] = field
        sent_ref[member] = field.astype(bf16)


def turn_kernel(normed_ref, active_ref, normed_t_ref, active_t_ref):
    _, _, levels, block, _ = normed_t_ref.shape
    width = normed_ref.shape[1]
    level, line, core = place()
    for source, target in ((normed_ref, normed_t_ref), (active_ref, active_t_ref)):
        for begin in range(0, width, tile):
            turned = source[:, begin : begin + tile].T
            for piece in range(0, tile, block):
                index = (begin + piece) // block
                far = (index // 2 % 2) ^ line
                step = (index // 4) ^ level
                target[(index % 2) ^ core, 1 - far, levels - 1 - step] = turned[piece : piece + block]


def split_loss(part, variables):
    column = lax.broadcasted_iota(jnp.int32, part.shape, 1)
    spots = (column == variables) | (column == variables + 1)
    total = jnp.sum(jnp.where(spots, part, 0.0), axis=1, keepdims=True)
    high = total.astype(bf16).astype(f32)
    return jnp.where(column == variables, high, jnp.where(column == variables + 1, total - high, part))


def score_kernel(
    own_ref, other_ref, truth_ref, cell_ref, project_ref, slope_ref, normed_t_ref, active_t_ref,
    inner_ref, pred_ref, loss_ref, far_ref, near_ref, hold_ref,
):
    members, variables, points = own_ref.shape
    width = slope_ref.shape[1]
    total = 2 * members
    pairs = total * (total - 1)

    def eased(delta):
        square = delta * delta + smoothing * smoothing
        inverse = lax.rsqrt(square)
        return square * inverse, delta * inverse

    truth, cell = truth_ref[...], cell_ref[...].reshape(1, points)
    own = [own_ref[m] for m in range(members)]
    other = [other_ref[m].astype(f32) for m in range(members)]
    score = jnp.zeros_like(truth)
    pulls = [jnp.zeros_like(truth) for _ in own]
    grads = []
    for m in range(members):
        size, sign = eased(own[m] - truth)
        score = score + size * (1.0 / total)
        grads.append(sign * (1.0 / total))
    for m in range(members):
        for n in range(m + 1, members):
            size, sign = eased(own[m] - own[n])
            score = score - size * (1.0 / pairs)
            pulls[m] = pulls[m] + sign
            pulls[n] = pulls[n] - sign
        for n in range(members):
            size, sign = eased(own[m] - other[n])
            score = score - size * (0.5 / pairs)
            pulls[m] = pulls[m] + sign
    loss = jnp.sum(score * cell)
    loss_ref[0] = loss
    hold_ref[...] = jnp.zeros_like(hold_ref)
    for m in range(members):
        grad = (grads[m] - pulls[m] * (1.0 / pairs)) * cell
        hold_ref[0:variables, m * points : (m + 1) * points] = grad
    pred = hold_ref[...].astype(bf16)
    pred_ref[...] = pred
    for m in range(members):
        rows = slice(m * points, (m + 1) * points)
        part = pred[:variables, rows]
        for begin in range(0, width, tile):
            columns = slice(begin, begin + tile)
            grad = mm(part, project_ref[:, columns], 0, 0)
            inner_ref[rows, columns] = (grad * slope_ref[rows, columns]).astype(bf16)
    weight_parts(normed_t_ref, active_t_ref, inner_ref, pred, loss, variables, 1, 0, far_ref)
    weight_parts(normed_t_ref, active_t_ref, inner_ref, pred, loss, variables, 1, 1, near_ref)


def weight_parts(normed_t_ref, active_t_ref, inner_ref, pred, loss, variables, side, half, out_ref):
    width = inner_ref.shape[1]
    depth = normed_t_ref.shape[-1]
    normed = normed_t_ref[side, half].reshape(-1, depth)
    for begin in range(0, width, tile):
        columns = slice(begin, begin + tile)
        out_ref[:, columns] = mm(normed, inner_ref[:, columns], 1, 0).astype(out_ref.dtype)
    part = mm(active_t_ref[side, half].reshape(-1, depth), pred, 1, 1)
    part = jnp.where(lax.broadcasted_iota(jnp.int32, part.shape, 1) == variables, loss, part)
    out_ref[:, width:] = split_loss(part, variables).astype(out_ref.dtype)


def pair_kernel(
    variables, half, loss_ref, normed_t_ref, active_t_ref, inner_ref, pred_ref, arrived_ref, *out_refs
):
    hold_ref = out_refs[-1]
    width = inner_ref.shape[1]
    weight_parts(
        normed_t_ref, active_t_ref, inner_ref, pred_ref[...], loss_ref[0], variables, 0, half, hold_ref
    )
    count = hold_ref.shape[0] // (len(out_refs) - 1)
    for i, out_ref in enumerate(out_refs[:-1]):
        rows = slice(i * count, (i + 1) * count)
        total = hold_ref[rows, :] + arrived_ref[rows, :].astype(f32)
        out_ref[:, :width] = total[:, :width].astype(out_ref.dtype)
        out_ref[:, width:] = split_loss(total[:, width:], variables).astype(out_ref.dtype)


def line_kernel(variables, begin, width, kept_ref, arrived_ref, *out_refs):
    block = out_refs[0].shape[0]
    for i, out_ref in enumerate(out_refs):
        rows = slice(i * block, (i + 1) * block)
        total = kept_ref[begin + i * block : begin + (i + 1) * block, :] + arrived_ref[rows, :].astype(f32)
        out_ref[:, :width] = total[:, :width].astype(out_ref.dtype)
        out_ref[:, width:] = split_loss(total[:, width:], variables).astype(out_ref.dtype)


def back_kernel(inner_ref, w_hidden_ref, gain_ref, unit_ref, inverse_ref, share_ref, *rest):
    slot_refs, (scaled_ref, grad_ref) = rest[:-2], rest[-2:]
    rows_all, width = inner_ref.shape
    rows_slot = share_ref.shape[0] // 2
    gain = gain_ref[...].reshape(1, width)
    for begin_row in range(0, rows_all, tile):
        rows = slice(begin_row, begin_row + tile)
        dots = jnp.zeros((tile, 1), f32)
        for begin in range(0, width, tile):
            columns = slice(begin, begin + tile)
            scaled = mm(inner_ref[rows, :], w_hidden_ref[columns, :], 1, 1) * gain[:, columns]
            dots = dots + jnp.sum(scaled * unit_ref[rows, columns], axis=-1, keepdims=True)
            scaled_ref[rows, columns] = scaled
        dots = dots * (1.0 / width)
        inverse = inverse_ref[rows, :]
        for begin in range(0, width, tile):
            columns = slice(begin, begin + tile)
            grad_ref[rows, columns] = (
                (scaled_ref[rows, columns] - unit_ref[rows, columns] * dots) * inverse
            ).astype(bf16)
    count = rows_slot // len(slot_refs)
    for begin in range(0, width, tile):
        columns = slice(begin, begin + tile)
        both = mm(share_ref[...], grad_ref[:, columns], 1, 0)
        slots = (both[:rows_slot] + both[rows_slot:]).astype(bf16)
        for i, slot_ref in enumerate(slot_refs):
            slot_ref[:, columns] = slots[i * count : (i + 1) * count]


def owner_kernel(pick_ref, *rest):
    arrived = jnp.concatenate([r[...] for r in rest[:-1]], axis=0)
    rest[-1][...] = mm(pick_ref[...], arrived, 0, 0).astype(bf16)


def latent_kernel(rows_ref, w_msg_ref, grad_ref):
    grad_ref[...] = mm(rows_ref[...], w_msg_ref[...], 1, 1).astype(bf16).reshape(grad_ref.shape)


def message_kernel(levels, *refs):
    latent_refs, row_refs, own_ref = refs[:4], refs[4:8], refs[8]
    send_refs, held_ref = refs[9:-1], refs[-1]
    level, _, _ = place()
    left = jnp.concatenate([r[...] for r in latent_refs], axis=0)
    right = jnp.concatenate([r[...] for r in row_refs], axis=0)
    block = own_ref.shape[0]
    for begin in range(0, right.shape[1], tile):
        columns = slice(begin, begin + tile)
        held_ref[:, :, columns] = mm(left, right[:, columns], 0, 0).reshape(levels, block, tile)
    own_ref[...] = held_ref[level]
    for step in range(1, levels):
        send_refs[step - 1][...] = held_ref[level ^ step].astype(bf16)


def hidden_sum_kernel(variables, scale, own_ref, *rest):
    hidden_ref, out_ref, loss_ref = rest[-3:]
    total = own_ref[...]
    for r in rest[:-3]:
        total = total + r[...].astype(f32)
    width = hidden_ref.shape[1]
    hidden_ref[...] = total[:, :width]
    part = total[:, width:]
    out_ref[...] = part[:, :variables]
    column = lax.broadcasted_iota(jnp.int32, (8, part.shape[1]), 1)
    spots = (column == variables) | (column == variables + 1)
    first = lax.broadcasted_iota(jnp.int32, (8, part.shape[1]), 0) == 0
    loss_ref[0] = jnp.sum(jnp.where(spots & first, part[:8], 0.0)) * scale


def sum_kernel(own_ref, *rest):
    total = own_ref[...]
    for r in rest[:-1]:
        total = total + r[...].astype(f32)
    rest[-1][...] = total


def on_device(
    latents, grid_embed, norm_gain, w_msg, w_hidden, variable_projection, present_condition, verifying_field,
    cell_surface, send_rows, edge_slot, edge_dst, edge_weight,
):
    members, nodes, width = latents.shape
    points = grid_embed.shape[0]
    variables = variable_projection.shape[1]
    peers = lax.axis_size("space")
    cores = lax.axis_size("member")
    cap = send_rows.shape[2]
    rows_peer = members * cap
    rows_slot = peers * rows_peer
    rows_all = members * points
    levels = peers // 2
    block = width // (peers * cores)
    half = levels * block
    wide = width + -(-(variables + 2) // lanes) * lanes
    both = ("space", "member")
    project = variable_projection.T

    pick, *send = call(
        select_kernel,
        [((rows_slot, members * nodes), bf16)] + [((rows_peer, width), bf16)] * peers,
        [send_rows[0], latents],
        limit=4,
        scalars=(0,),
    )
    received = [send[0]] + [swap(send[k], "space", peers, k) for k in range(1, peers)]
    (share,) = call(
        functools.partial(edge_kernel, cap, members),
        [((2 * rows_slot, rows_all), bf16)],
        [edge_slot, edge_dst, edge_weight],
        limit=8,
    )
    own_columns, *send_columns = call(
        functools.partial(columns_kernel, block),
        [((members * nodes, half), bf16)] * 4,
        [latents],
        scratch=[pltpu.VMEM((4, members * nodes, half), bf16)],
        limit=4,
    )
    columns = [own_columns] + [
        swap(send_columns[k - 1], both, peers * cores, k) for k in range(1, 4)
    ]
    field, sent, normed, active, slope, unit, inverse = call(
        functools.partial(forward_kernel, peers),
        [
            ((members, variables, points), f32),
            ((members, variables, points), bf16),
            ((rows_all, width), bf16),
            ((rows_all, width), bf16),
            ((rows_all, width), f32),
            ((rows_all, width), f32),
            ((rows_all, 1), f32),
        ],
        [w_msg, share, grid_embed, norm_gain, w_hidden, project, present_condition.transpose(1, 0, 2)]
        + received,
        limit=20,
    )
    other = swap(sent, "member", cores, 1)
    normed_t, active_t = call(
        turn_kernel,
        [((cores, 2, levels, block, rows_all), bf16)] * 2,
        [normed, active],
        limit=8,
    )
    grad_inner, pred, loss_part, far, near = call(
        score_kernel,
        [
            ((rows_all, width), bf16),
            ((lanes, rows_all), bf16),
            ((1,), f32),
            ((half, wide), bf16),
            ((half, wide), bf16),
        ],
        [field, other, verifying_field, cell_surface, project, slope, normed_t, active_t],
        scratch=[pltpu.VMEM((lanes, rows_all), f32)],
        limit=16,
        scalar_outs=(2,),
    )
    far_other = swap(far, "member", cores, 1)
    near_other = swap(near, "member", cores, 1)
    slots = call(
        back_kernel,
        [((rows_peer, width), bf16)] * peers,
        [grad_inner, w_hidden, norm_gain, unit, inverse, share],
        scratch=[pltpu.VMEM((rows_all, width), f32), pltpu.VMEM((rows_all, width), bf16)],
        limit=16,
    )
    parts = [loss_part, normed_t, active_t, grad_inner, pred]
    first, second = call(
        functools.partial(pair_kernel, variables, 0),
        [((half // 2, wide), bf16)] * 2,
        parts + [far_other],
        scratch=[pltpu.VMEM((half, wide), f32)],
        limit=12,
        scalars=(0,),
    )
    first_other = swap(first, "space", peers, 1)
    second_other = swap(second, "space", peers, 1)
    back = [slots[0]] + [swap(slots[k], "space", peers, k) for k in range(1, peers)]
    (kept,) = call(
        functools.partial(pair_kernel, variables, 1),
        [((half, wide), f32)],
        parts + [near_other],
        scratch=[pltpu.VMEM((half, wide), f32)],
        limit=12,
        scalars=(0,),
    )
    early = call(
        functools.partial(line_kernel, variables, 0, width),
        [((block, wide), bf16)] * (levels // 2),
        [kept, first_other],
        limit=6,
    )
    arrived = [swap(early[i], "space", peers, 2 * (levels - 1 - i)) for i in range(levels // 2)]
    late = call(
        functools.partial(line_kernel, variables, half // 2, width),
        [((block, wide), bf16)] * (levels // 2 - 1) + [((block, wide), f32)],
        [kept, second_other],
        limit=6,
    )
    arrived += [swap(late[i], "space", peers, 2 * (levels // 2 - 1 - i)) for i in range(levels // 2 - 1)]
    (rows,) = call(owner_kernel, [((members * nodes, width), bf16)], [pick] + back, limit=4)
    other_rows = [swap(rows, both, peers * cores, k) for k in range(1, 4)]
    (latent_grad,) = call(latent_kernel, [(latents.shape, bf16)], [rows, w_msg], limit=8)
    own_message, *send_message = call(
        functools.partial(message_kernel, levels),
        [((block, width), f32)] + [((block, width), bf16)] * (levels - 1),
        columns + [rows] + other_rows,
        scratch=[pltpu.VMEM((levels, block, width), f32)],
        limit=8,
    )
    arrived_message = [swap(send_message[k - 1], "space", peers, 2 * k) for k in range(1, levels)]
    hidden_weight_grad, out_weight_grad, loss = call(
        functools.partial(hidden_sum_kernel, variables, 1.0 / (points * peers * variables)),
        [((block, width), f32), ((block, variables), f32), ((1,), f32)],
        [late[-1]] + arrived,
        limit=6,
        scalar_outs=(2,),
    )
    (msg_weight_grad,) = call(
        sum_kernel, [((block, width), f32)], [own_message] + arrived_message, limit=6
    )
    return (latent_grad, loss, msg_weight_grad, hidden_weight_grad, out_weight_grad)


def solution(mesh):
    placed = (
        P(("groups", "member"), "space", None),
        P(("groups", "space"), None),
        P(),
        P(),
        P(),
        P(),
        P(("groups", "member"), None, "space"),
        P(None, ("groups", "space")),
        P(("groups", "space")),
        P("space", None, None),
        P("space"),
        P("space"),
        P("space"),
    )
    return jax.shard_map(
        on_device,
        mesh=mesh,
        in_specs=placed,
        out_specs=(
            P(("groups", "member"), "space", None),
            P("groups"),
            P(("groups", "space", "member"), None),
            P(("groups", "space", "member"), None),
            P(("groups", "space", "member"), None),
        ),
        check_vma=False,
    )
```

```python
import functools

import jax
import jax.numpy as jnp
from jax import lax
from jax.experimental import pallas as pl
from jax.experimental.pallas import tpu as pltpu
from jax.sharding import PartitionSpec as P

smoothing = 0.1
epsilon = 1e-06
tile = 256
lanes = 128
f32 = jnp.float32
bf16 = jnp.bfloat16


def mm(left, right, left_dim, right_dim):
    return lax.dot_general(
        left, right, (((left_dim,), (right_dim,)), ((), ())), preferred_element_type=f32
    )


def call(body, outs, args, scratch=(), limit=16, scalars=(), scalar_outs=(), places=(), after=()):
    whole = pl.BlockSpec(memory_space=pltpu.VMEM)
    small = pl.BlockSpec(memory_space=pltpu.SMEM)
    far_place = pl.BlockSpec(memory_space=pltpu.HBM)
    any_place = pl.BlockSpec(memory_space=pl.ANY)
    count = len(after)
    args = [pltpu.with_memory_space_constraint(x, pltpu.HBM) if i in places else x for i, x in enumerate(args)]

    def inner(*refs):
        body(*refs[count:])

    specs = [small if i in scalars else far_place if i in places else whole for i in range(len(args))]
    return pl.pallas_call(
        inner if count else body,
        out_shape=[jax.ShapeDtypeStruct(dims, kind) for dims, kind in outs],
        in_specs=[any_place] * count + specs,
        out_specs=[small if i in scalar_outs else whole for i in range(len(outs))],
        scratch_shapes=scratch,
        compiler_params=pltpu.CompilerParams(vmem_limit_bytes=limit * 2**20),
        cost_estimate=pl.CostEstimate(flops=0, bytes_accessed=0, transcendentals=0),
    )(*after, *args)


def place():
    space = lax.axis_index("space")
    return lax.div(space, 2), lax.rem(space, 2), lax.axis_index("member")


def swap(value, axis, size, step):
    return lax.ppermute(value, axis, [(i, i ^ step) for i in range(size)])


def select_kernel(lists_ref, latents_ref, send_ref, pick_ref, small_ref, table_ref, sems):
    _, peers, cap = lists_ref.shape
    members, nodes, width = latents_ref.shape
    lists = pltpu.make_async_copy(lists_ref, small_ref, sems.at[0])
    table = pltpu.make_async_copy(latents_ref, table_ref, sems.at[1])
    lists.start()
    table.start()
    lists.wait()
    at = lax.broadcasted_iota(jnp.int32, (cap, members * nodes), 0)
    column = lax.broadcasted_iota(jnp.int32, (cap, members * nodes), 1)
    rows = []
    for peer in range(peers):
        wanted = jnp.zeros((cap, members * nodes), jnp.int32)
        for j in range(cap):
            wanted = jnp.where(at == j, small_ref[0, peer, j], wanted)
        for member in range(members):
            rows.append((column == wanted + member * nodes).astype(f32))
    pick = jnp.concatenate(rows, axis=0).astype(bf16)
    pick_ref[...] = pick
    table.wait()
    sent = mm(pick, table_ref[...].reshape(members * nodes, width), 1, 0)
    send_ref[...] = sent.astype(bf16).reshape(send_ref.shape)


def stage_kernel(
    cap, block, slot_ref, dst_ref, weight_ref, latents_ref, w_msg_ref, w_hidden_ref, embed_ref, gain_ref,
    project_ref, present_ref, share_ref, columns_ref, *rest,
):
    staged_refs, sems = rest[:-1], rest[-1]
    sources = (w_msg_ref, w_hidden_ref, embed_ref, gain_ref, project_ref, present_ref)
    copies = [
        pltpu.make_async_copy(source, target, sems.at[i])
        for i, (source, target) in enumerate(zip(sources, staged_refs, strict=True))
    ]
    for copy in copies:
        copy.start()
    columns_part(block, latents_ref, columns_ref)
    edge_part(cap, latents_ref.shape[0], slot_ref, dst_ref, weight_ref, share_ref)
    for copy in copies:
        copy.wait()


def columns_part(block, latents_ref, columns_ref):
    members, nodes, width = latents_ref.shape
    kinds = columns_ref.shape[0]
    table = latents_ref[...].reshape(members * nodes, width).astype(f32)
    for kind in range(kinds):
        parts = [table[:, at : at + block] for at in range(kind * block, width, kinds * block)]
        columns_ref[kind] = jnp.concatenate(parts, axis=1).astype(bf16)


def edge_part(cap, members, slot_ref, dst_ref, weight_ref, share_ref):
    edges = slot_ref.shape[0]
    slot = slot_ref[...].reshape(1, edges)
    dst = dst_ref[...].reshape(1, edges)
    weight = weight_ref[...].reshape(1, edges)
    rows = share_ref.shape[0] // 2
    points = share_ref.shape[1] // members
    sender = lax.div(slot, cap)
    spot = sender * (members * cap) + (slot - sender * cap)
    hit = lax.broadcasted_iota(jnp.int32, (rows, edges), 0) == spot
    into = (lax.broadcasted_iota(jnp.int32, (points, edges), 0) == dst).astype(f32).astype(bf16)
    high = weight.astype(bf16).astype(f32)
    table = mm(jnp.where(hit, high, 0.0).astype(bf16), into, 1, 1) + mm(
        jnp.where(hit, weight - high, 0.0).astype(bf16), into, 1, 1
    )
    table = table / jnp.sum(table, axis=0, keepdims=True)
    for member in range(members):
        high = table.astype(bf16)
        columns = slice(member * points, (member + 1) * points)
        share_ref[0:rows, columns] = high
        share_ref[rows : 2 * rows, columns] = (table - high.astype(f32)).astype(bf16)
        table = jnp.concatenate([table[rows - cap :], table[: rows - cap]], axis=0)


def forward_kernel(
    received_ref, w_msg_ref, share_ref, embed_ref, gain_ref, w_hidden_ref, project_ref, present_ref,
    field_ref, sent_ref, normed_ref, active_ref, slope_ref, unit_ref, inverse_ref,
):
    points, width = embed_ref.shape
    variables, members, _ = present_ref.shape
    messages = mm(received_ref[...], w_msg_ref[...], 1, 0).astype(bf16)
    messages = jnp.concatenate([messages, messages], axis=0)
    gain = gain_ref[...].reshape(1, width)
    for begin in range(0, members * points, lanes):
        rows = slice(begin, begin + lanes)
        source = slice(begin % points, begin % points + lanes)
        hidden = embed_ref[source, :].astype(f32) + mm(share_ref[:, rows], messages, 0, 0)
        inverse = lax.rsqrt(jnp.mean(hidden * hidden, axis=-1, keepdims=True) + epsilon)
        unit = hidden * inverse
        unit_ref[rows, :] = unit
        inverse_ref[rows, :] = inverse
        normed_ref[rows, :] = (unit * gain).astype(bf16)
    root = 0.7978845608028654
    cubic = 0.044715
    for member in range(members):
        rows = slice(member * points, (member + 1) * points)
        for begin in range(0, width, tile):
            columns = slice(begin, begin + tile)
            inner = mm(normed_ref[rows, :], w_hidden_ref[:, columns], 1, 0)
            square = inner * inner
            bend = jnp.tanh(inner * (root + root * cubic * square))
            half = 0.5 + 0.5 * bend
            active_ref[rows, columns] = (inner * half).astype(bf16)
            slope_ref[rows, columns] = half + (0.5 * inner) * (1.0 - bend * bend) * (
                root + 3.0 * root * cubic * square
            )
        field = present_ref[:, member, :] + mm(project_ref[...], active_ref[rows, :], 1, 1)
        field_ref[member] = field
        sent_ref[member] = field.astype(bf16)


def turn_kernel(normed_ref, active_ref, normed_t_ref, active_t_ref):
    _, _, levels, block, _ = normed_t_ref.shape
    width = normed_ref.shape[1]
    level, line, core = place()
    for source, target in ((normed_ref, normed_t_ref), (active_ref, active_t_ref)):
        for begin in range(0, width, tile):
            turned = source[:, begin : begin + tile].T
            for piece in range(0, tile, block):
                index = (begin + piece) // block
                far = (index // 2 % 2) ^ line
                step = (index // 4) ^ level
                target[(index % 2) ^ core, 1 - far, levels - 1 - step] = turned[piece : piece + block]


def split_loss(part, variables):
    column = lax.broadcasted_iota(jnp.int32, part.shape, 1)
    spots = (column == variables) | (column == variables + 1)
    total = jnp.sum(jnp.where(spots, part, 0.0), axis=1, keepdims=True)
    high = total.astype(bf16).astype(f32)
    return jnp.where(column == variables, high, jnp.where(column == variables + 1, total - high, part))


def score_kernel(
    own_ref, other_ref, truth_ref, cell_ref, project_ref, slope_ref, normed_t_ref, active_t_ref,
    inner_ref, pred_ref, loss_ref, far_ref, near_ref, hold_ref,
):
    members, variables, points = own_ref.shape
    width = slope_ref.shape[1]
    total = 2 * members
    pairs = total * (total - 1)

    def eased(delta):
        square = delta * delta + smoothing * smoothing
        inverse = lax.rsqrt(square)
        return square * inverse, delta * inverse

    truth, cell = truth_ref[...], cell_ref[...].reshape(1, points)
    own = [own_ref[m] for m in range(members)]
    other = [other_ref[m].astype(f32) for m in range(members)]
    score = jnp.zeros_like(truth)
    pulls = [jnp.zeros_like(truth) for _ in own]
    grads = []
    for m in range(members):
        size, sign = eased(own[m] - truth)
        score = score + size * (1.0 / total)
        grads.append(sign * (1.0 / total))
    for m in range(members):
        for n in range(m + 1, members):
            size, sign = eased(own[m] - own[n])
            score = score - size * (1.0 / pairs)
            pulls[m] = pulls[m] + sign
            pulls[n] = pulls[n] - sign
        for n in range(members):
            size, sign = eased(own[m] - other[n])
            score = score - size * (0.5 / pairs)
            pulls[m] = pulls[m] + sign
    loss = jnp.sum(score * cell)
    loss_ref[0] = loss
    hold_ref[...] = jnp.zeros_like(hold_ref)
    for m in range(members):
        grad = (grads[m] - pulls[m] * (1.0 / pairs)) * cell
        hold_ref[0:variables, m * points : (m + 1) * points] = grad
    pred = hold_ref[...].astype(bf16)
    pred_ref[...] = pred
    for m in range(members):
        rows = slice(m * points, (m + 1) * points)
        part = pred[:variables, rows]
        for begin in range(0, width, tile):
            columns = slice(begin, begin + tile)
            grad = mm(part, project_ref[:, columns], 0, 0)
            inner_ref[rows, columns] = (grad * slope_ref[rows, columns]).astype(bf16)
    weight_parts(normed_t_ref, active_t_ref, inner_ref, pred, loss, variables, 1, 0, far_ref)
    weight_parts(normed_t_ref, active_t_ref, inner_ref, pred, loss, variables, 1, 1, near_ref)


def weight_parts(normed_t_ref, active_t_ref, inner_ref, pred, loss, variables, side, half, out_ref):
    width = inner_ref.shape[1]
    depth = normed_t_ref.shape[-1]
    normed = normed_t_ref[side, half].reshape(-1, depth)
    for begin in range(0, width, tile):
        columns = slice(begin, begin + tile)
        out_ref[:, columns] = mm(normed, inner_ref[:, columns], 1, 0).astype(out_ref.dtype)
    part = mm(active_t_ref[side, half].reshape(-1, depth), pred, 1, 1)
    part = jnp.where(lax.broadcasted_iota(jnp.int32, part.shape, 1) == variables, loss, part)
    out_ref[:, width:] = split_loss(part, variables).astype(out_ref.dtype)


def pair_kernel(
    variables, half, loss_ref, normed_t_ref, active_t_ref, inner_ref, pred_ref, arrived_ref, *out_refs
):
    hold_ref = out_refs[-1]
    width = inner_ref.shape[1]
    weight_parts(
        normed_t_ref, active_t_ref, inner_ref, pred_ref[...], loss_ref[0], variables, 0, half, hold_ref
    )
    count = hold_ref.shape[0] // (len(out_refs) - 1)
    for i, out_ref in enumerate(out_refs[:-1]):
        rows = slice(i * count, (i + 1) * count)
        total = hold_ref[rows, :] + arrived_ref[rows, :].astype(f32)
        out_ref[:, :width] = total[:, :width].astype(out_ref.dtype)
        out_ref[:, width:] = split_loss(total[:, width:], variables).astype(out_ref.dtype)


def line_kernel(variables, begin, width, kept_ref, arrived_ref, *out_refs):
    block = out_refs[0].shape[0]
    for i, out_ref in enumerate(out_refs):
        rows = slice(i * block, (i + 1) * block)
        total = kept_ref[begin + i * block : begin + (i + 1) * block, :] + arrived_ref[rows, :].astype(f32)
        out_ref[:, :width] = total[:, :width].astype(out_ref.dtype)
        out_ref[:, width:] = split_loss(total[:, width:], variables).astype(out_ref.dtype)


def back_kernel(inner_ref, w_hidden_ref, gain_ref, unit_ref, inverse_ref, grad_ref, scaled_ref):
    rows_all, width = inner_ref.shape
    gain = gain_ref[...].reshape(1, width)
    for begin_row in range(0, rows_all, tile):
        rows = slice(begin_row, begin_row + tile)
        dots = jnp.zeros((tile, 1), f32)
        for begin in range(0, width, tile):
            columns = slice(begin, begin + tile)
            scaled = mm(inner_ref[rows, :], w_hidden_ref[columns, :], 1, 1) * gain[:, columns]
            dots = dots + jnp.sum(scaled * unit_ref[rows, columns], axis=-1, keepdims=True)
            scaled_ref[rows, columns] = scaled
        dots = dots * (1.0 / width)
        inverse = inverse_ref[rows, :]
        for begin in range(0, width, tile):
            columns = slice(begin, begin + tile)
            grad_ref[rows, columns] = (
                (scaled_ref[rows, columns] - unit_ref[rows, columns] * dots) * inverse
            ).astype(bf16)


def slot_kernel(share_ref, grad_ref, slots_ref):
    rows = share_ref.shape[0] // 2
    for begin in range(0, grad_ref.shape[1], tile):
        columns = slice(begin, begin + tile)
        both = mm(share_ref[...], grad_ref[:, columns], 1, 0)
        slots_ref[:, columns] = (both[:rows] + both[rows:]).astype(bf16)


def owner_kernel(pick_ref, arrived_ref, rows_ref, copies_ref):
    rows = mm(pick_ref[...], arrived_ref[...], 0, 0).astype(bf16)
    rows_ref[...] = rows
    for kind in range(copies_ref.shape[0]):
        copies_ref[kind] = rows


def latent_kernel(rows_ref, w_msg_ref, grad_ref):
    grad_ref[...] = mm(rows_ref[...], w_msg_ref[...], 1, 1).astype(bf16).reshape(grad_ref.shape)


def message_kernel(levels, columns_ref, rows_ref, own_ref, *rest):
    send_refs, held_ref = rest[:-1], rest[-1]
    level, _, _ = place()
    block = own_ref.shape[0]
    for begin in range(0, rows_ref.shape[1], tile):
        columns = slice(begin, begin + tile)
        held_ref[:, :, columns] = mm(columns_ref[...], rows_ref[:, columns], 0, 0).reshape(levels, block, tile)
    own_ref[...] = held_ref[level]
    for step in range(1, levels):
        send_refs[step - 1][...] = held_ref[level ^ step].astype(bf16)


def hidden_sum_kernel(variables, scale, own_ref, *rest):
    hidden_ref, out_ref, loss_ref = rest[-3:]
    total = own_ref[...]
    for r in rest[:-3]:
        total = total + r[...].astype(f32)
    width = hidden_ref.shape[1]
    hidden_ref[...] = total[:, :width]
    part = total[:, width:]
    out_ref[...] = part[:, :variables]
    column = lax.broadcasted_iota(jnp.int32, (8, part.shape[1]), 1)
    spots = (column == variables) | (column == variables + 1)
    first = lax.broadcasted_iota(jnp.int32, (8, part.shape[1]), 0) == 0
    loss_ref[0] = jnp.sum(jnp.where(spots & first, part[:8], 0.0)) * scale


def sum_kernel(own_ref, *rest):
    total = own_ref[...]
    for r in rest[:-1]:
        total = total + r[...].astype(f32)
    rest[-1][...] = total


def on_device(
    latents, grid_embed, norm_gain, w_msg, w_hidden, variable_projection, present_condition, verifying_field,
    cell_surface, send_rows, edge_slot, edge_dst, edge_weight,
):
    members, nodes, width = latents.shape
    points = grid_embed.shape[0]
    variables = variable_projection.shape[1]
    peers = lax.axis_size("space")
    cores = lax.axis_size("member")
    cap = send_rows.shape[2]
    rows_peer = members * cap
    rows_slot = peers * rows_peer
    rows_all = members * points
    levels = peers // 2
    block = width // (peers * cores)
    half = levels * block
    wide = width + -(-(variables + 2) // lanes) * lanes
    kinds = 2 * cores
    quads = [list(range(at, at + kinds)) for at in range(0, peers * cores, kinds)]
    exchange_quad = functools.partial(
        lax.all_to_all, axis_name=("space", "member"), split_axis=0, concat_axis=0, tiled=True,
        axis_index_groups=quads,
    )
    project = variable_projection.T

    exchange = functools.partial(
        lax.all_to_all, axis_name="space", split_axis=0, concat_axis=0, tiled=True
    )
    send, pick = call(
        select_kernel,
        [((peers, rows_peer, width), bf16), ((rows_slot, members * nodes), bf16)],
        [send_rows, latents],
        scratch=[
            pltpu.SMEM(send_rows.shape, jnp.int32),
            pltpu.VMEM(latents.shape, bf16),
            pltpu.SemaphoreType.DMA((2,)),
        ],
        limit=4,
        places=(0, 1),
    )
    received = exchange(send).reshape(rows_slot, width)
    present = present_condition.transpose(1, 0, 2)
    fixed = [w_msg, w_hidden, grid_embed, norm_gain, project, present]
    share, own_columns, *rest = call(
        functools.partial(stage_kernel, cap, block),
        [((2 * rows_slot, rows_all), bf16), ((kinds, members * nodes, half), bf16)]
        + [(x.shape, x.dtype) for x in fixed],
        [edge_slot, edge_dst, edge_weight, latents] + fixed,
        scratch=[pltpu.SemaphoreType.DMA((len(fixed),))],
        limit=16,
        places=tuple(range(4, 4 + len(fixed))),
        after=[pick],
    )
    columns = exchange_quad(own_columns).reshape(kinds * members * nodes, half)
    w_msg_near, w_hidden_near, embed, gain, project_near, present = rest
    field, sent, normed, active, slope, unit, inverse = call(
        forward_kernel,
        [
            ((members, variables, points), f32),
            ((members, variables, points), bf16),
            ((rows_all, width), bf16),
            ((rows_all, width), bf16),
            ((rows_all, width), f32),
            ((rows_all, width), f32),
            ((rows_all, 1), f32),
        ],
        [received, w_msg_near, share, embed, gain, w_hidden_near, project_near, present],
        limit=20,
        after=[columns],
    )
    other = swap(sent, "member", cores, 1)
    normed_t, active_t = call(
        turn_kernel,
        [((cores, 2, levels, block, rows_all), bf16)] * 2,
        [normed, active],
        limit=8,
    )
    grad_inner, pred, loss_part, far, near = call(
        score_kernel,
        [
            ((rows_all, width), bf16),
            ((lanes, rows_all), bf16),
            ((1,), f32),
            ((half, wide), bf16),
            ((half, wide), bf16),
        ],
        [field, other, verifying_field, cell_surface, project_near, slope, normed_t, active_t],
        scratch=[pltpu.VMEM((lanes, rows_all), f32)],
        limit=16,
        scalar_outs=(2,),
    )
    far_other = swap(far, "member", cores, 1)
    near_other = swap(near, "member", cores, 1)
    (grad_hidden,) = call(
        back_kernel,
        [((rows_all, width), bf16)],
        [grad_inner, w_hidden_near, gain, unit, inverse],
        scratch=[pltpu.VMEM((rows_all, width), f32)],
        limit=14,
    )
    parts = [loss_part, normed_t, active_t, grad_inner, pred]
    first, second = call(
        functools.partial(pair_kernel, variables, 0),
        [((half // 2, wide), bf16)] * 2,
        parts + [far_other],
        scratch=[pltpu.VMEM((half, wide), f32)],
        limit=12,
        scalars=(0,),
        after=[grad_hidden],
    )
    first_other = swap(first, "space", peers, 1)
    second_other = swap(second, "space", peers, 1)
    (slots,) = call(
        slot_kernel, [((rows_slot, width), bf16)], [share, grad_hidden], limit=6, after=[first]
    )
    back = exchange(slots.reshape(peers, rows_peer, width)).reshape(rows_slot, width)
    (kept,) = call(
        functools.partial(pair_kernel, variables, 1),
        [((half, wide), f32)],
        parts + [near_other],
        scratch=[pltpu.VMEM((half, wide), f32)],
        limit=12,
        scalars=(0,),
        after=[slots],
    )
    early = call(
        functools.partial(line_kernel, variables, 0, width),
        [((block, wide), bf16)] * (levels // 2),
        [kept, first_other],
        limit=6,
    )
    arrived = [swap(early[i], "space", peers, 2 * (levels - 1 - i)) for i in range(levels // 2)]
    rows, copies = call(
        owner_kernel,
        [((members * nodes, width), bf16), ((kinds, members * nodes, width), bf16)],
        [pick, back],
        limit=4,
        after=early[:1],
    )
    all_rows = exchange_quad(copies).reshape(kinds * members * nodes, width)
    late = call(
        functools.partial(line_kernel, variables, half // 2, width),
        [((block, wide), bf16)] * (levels // 2 - 1) + [((block, wide), f32)],
        [kept, second_other],
        limit=6,
        after=[rows],
    )
    arrived += [swap(late[i], "space", peers, 2 * (levels // 2 - 1 - i)) for i in range(levels // 2 - 1)]
    own_message, *send_message = call(
        functools.partial(message_kernel, levels),
        [((block, width), f32)] + [((block, width), bf16)] * (levels - 1),
        [columns, all_rows],
        scratch=[pltpu.VMEM((levels, block, width), f32)],
        limit=8,
        after=late[:1],
    )
    arrived_message = [swap(send_message[k - 1], "space", peers, 2 * k) for k in range(1, levels)]
    (latent_grad,) = call(
        latent_kernel, [(latents.shape, bf16)], [rows, w_msg], limit=8, after=[own_message]
    )
    hidden_weight_grad, out_weight_grad, loss = call(
        functools.partial(hidden_sum_kernel, variables, 1.0 / (points * peers * variables)),
        [((block, width), f32), ((block, variables), f32), ((1,), f32)],
        [late[-1]] + arrived,
        limit=6,
        scalar_outs=(2,),
        after=[own_message],
    )
    (msg_weight_grad,) = call(
        sum_kernel,
        [((block, width), f32)],
        [own_message] + arrived_message,
        limit=6,
        after=[hidden_weight_grad],
    )
    return (latent_grad, loss, msg_weight_grad, hidden_weight_grad, out_weight_grad)


def solution(mesh):
    placed = (
        P(("groups", "member"), "space", None),
        P(("groups", "space"), None),
        P(),
        P(),
        P(),
        P(),
        P(("groups", "member"), None, "space"),
        P(None, ("groups", "space")),
        P(("groups", "space")),
        P("space", None, None),
        P("space"),
        P("space"),
        P("space"),
    )
    return jax.shard_map(
        on_device,
        mesh=mesh,
        in_specs=placed,
        out_specs=(
            P(("groups", "member"), "space", None),
            P("groups"),
            P(("groups", "space", "member"), None),
            P(("groups", "space", "member"), None),
            P(("groups", "space", "member"), None),
        ),
        check_vma=False,
    )
```

```python
import functools

import jax
import jax.numpy as jnp
from jax import lax
from jax.experimental import pallas as pl
from jax.experimental.pallas import tpu as pltpu
from jax.sharding import PartitionSpec as P

smoothing = 0.1
epsilon = 1e-06
tile = 256
lanes = 128
f32 = jnp.float32
bf16 = jnp.bfloat16


def mm(left, right, left_dim, right_dim):
    return lax.dot_general(
        left, right, (((left_dim,), (right_dim,)), ((), ())), preferred_element_type=f32
    )


def call(body, outs, args, scratch=(), limit=16, scalars=(), scalar_outs=(), places=(), after=()):
    whole = pl.BlockSpec(memory_space=pltpu.VMEM)
    small = pl.BlockSpec(memory_space=pltpu.SMEM)
    far_place = pl.BlockSpec(memory_space=pltpu.HBM)
    any_place = pl.BlockSpec(memory_space=pl.ANY)
    count = len(after)
    args = [pltpu.with_memory_space_constraint(x, pltpu.HBM) if i in places else x for i, x in enumerate(args)]

    def inner(*refs):
        body(*refs[count:])

    specs = [small if i in scalars else far_place if i in places else whole for i in range(len(args))]
    return pl.pallas_call(
        inner if count else body,
        out_shape=[jax.ShapeDtypeStruct(dims, kind) for dims, kind in outs],
        in_specs=[any_place] * count + specs,
        out_specs=[small if i in scalar_outs else whole for i in range(len(outs))],
        scratch_shapes=scratch,
        compiler_params=pltpu.CompilerParams(vmem_limit_bytes=limit * 2**20),
        cost_estimate=pl.CostEstimate(flops=0, bytes_accessed=0, transcendentals=0),
    )(*after, *args)


def place():
    space = lax.axis_index("space")
    return lax.div(space, 2), lax.rem(space, 2), lax.axis_index("member")


def swap(value, axis, size, step):
    return lax.ppermute(value, axis, [(i, i ^ step) for i in range(size)])


def select_kernel(lists_ref, latents_ref, send_ref, pick_ref, small_ref, table_ref, sems):
    _, peers, cap = lists_ref.shape
    members, nodes, width = latents_ref.shape
    lists = pltpu.make_async_copy(lists_ref, small_ref, sems.at[0])
    table = pltpu.make_async_copy(latents_ref, table_ref, sems.at[1])
    lists.start()
    table.start()
    lists.wait()
    at = lax.broadcasted_iota(jnp.int32, (cap, members * nodes), 0)
    column = lax.broadcasted_iota(jnp.int32, (cap, members * nodes), 1)
    rows = []
    for peer in range(peers):
        wanted = jnp.zeros((cap, members * nodes), jnp.int32)
        for j in range(cap):
            wanted = jnp.where(at == j, small_ref[0, peer, j], wanted)
        for member in range(members):
            rows.append((column == wanted + member * nodes).astype(f32))
    pick = jnp.concatenate(rows, axis=0).astype(bf16)
    pick_ref[...] = pick
    table.wait()
    sent = mm(pick, table_ref[...].reshape(members * nodes, width), 1, 0)
    send_ref[...] = sent.astype(bf16).reshape(send_ref.shape)


def stage_kernel(
    cap, members, slot_ref, dst_ref, weight_ref, w_msg_ref, w_hidden_ref, embed_ref, gain_ref,
    project_ref, present_ref, share_ref, *rest,
):
    staged_refs, sems = rest[:-1], rest[-1]
    sources = (w_msg_ref, w_hidden_ref, embed_ref, gain_ref, project_ref, present_ref)
    copies = [
        pltpu.make_async_copy(source, target, sems.at[i])
        for i, (source, target) in enumerate(zip(sources, staged_refs, strict=True))
    ]
    for copy in copies:
        copy.start()
    edge_part(cap, members, slot_ref, dst_ref, weight_ref, share_ref)
    for copy in copies:
        copy.wait()


def edge_part(cap, members, slot_ref, dst_ref, weight_ref, share_ref):
    edges = slot_ref.shape[0]
    slot = slot_ref[...].reshape(1, edges)
    dst = dst_ref[...].reshape(1, edges)
    weight = weight_ref[...].reshape(1, edges)
    rows = share_ref.shape[0] // 2
    points = share_ref.shape[1] // members
    sender = lax.div(slot, cap)
    spot = sender * (members * cap) + (slot - sender * cap)
    hit = lax.broadcasted_iota(jnp.int32, (rows, edges), 0) == spot
    into = (lax.broadcasted_iota(jnp.int32, (points, edges), 0) == dst).astype(f32).astype(bf16)
    high = weight.astype(bf16).astype(f32)
    table = mm(jnp.where(hit, high, 0.0).astype(bf16), into, 1, 1) + mm(
        jnp.where(hit, weight - high, 0.0).astype(bf16), into, 1, 1
    )
    table = table / jnp.sum(table, axis=0, keepdims=True)
    for member in range(members):
        high = table.astype(bf16)
        columns = slice(member * points, (member + 1) * points)
        share_ref[0:rows, columns] = high
        share_ref[rows : 2 * rows, columns] = (table - high.astype(f32)).astype(bf16)
        table = jnp.concatenate([table[rows - cap :], table[: rows - cap]], axis=0)


def forward_kernel(
    received_ref, w_msg_ref, share_ref, embed_ref, gain_ref, w_hidden_ref, project_ref, present_ref,
    field_ref, sent_ref, normed_ref, active_ref, slope_ref, unit_ref, inverse_ref,
):
    points, width = embed_ref.shape
    variables, members, _ = present_ref.shape
    messages = mm(received_ref[...], w_msg_ref[...], 1, 0).astype(bf16)
    messages = jnp.concatenate([messages, messages], axis=0)
    gain = gain_ref[...].reshape(1, width)
    for begin in range(0, members * points, lanes):
        rows = slice(begin, begin + lanes)
        source = slice(begin % points, begin % points + lanes)
        hidden = embed_ref[source, :].astype(f32) + mm(share_ref[:, rows], messages, 0, 0)
        inverse = lax.rsqrt(jnp.mean(hidden * hidden, axis=-1, keepdims=True) + epsilon)
        unit = hidden * inverse
        unit_ref[rows, :] = unit
        inverse_ref[rows, :] = inverse
        normed_ref[rows, :] = (unit * gain).astype(bf16)
    root = 0.7978845608028654
    cubic = 0.044715
    for member in range(members):
        rows = slice(member * points, (member + 1) * points)
        for begin in range(0, width, tile):
            columns = slice(begin, begin + tile)
            inner = mm(normed_ref[rows, :], w_hidden_ref[:, columns], 1, 0)
            square = inner * inner
            bend = jnp.tanh(inner * (root + root * cubic * square))
            half = 0.5 + 0.5 * bend
            active_ref[rows, columns] = (inner * half).astype(bf16)
            slope_ref[rows, columns] = half + (0.5 * inner) * (1.0 - bend * bend) * (
                root + 3.0 * root * cubic * square
            )
        field = present_ref[:, member, :] + mm(project_ref[...], active_ref[rows, :], 1, 1)
        field_ref[member] = field
        sent_ref[member] = field.astype(bf16)


def turn_kernel(normed_ref, active_ref, received_ref, normed_t_ref, active_t_ref, keep_ref, give_ref):
    _, _, levels, block, _ = normed_t_ref.shape
    width = normed_ref.shape[1]
    level, line, core = place()
    for source, targets in (
        (received_ref, (keep_ref, give_ref)), (normed_ref, normed_t_ref), (active_ref, active_t_ref)
    ):
        for begin in range(0, width, tile):
            turned = source[:, begin : begin + tile].T
            for piece in range(0, tile, block):
                index = (begin + piece) // block
                far = (index // 2 % 2) ^ line
                step = (index // 4) ^ level
                side = (index % 2) ^ core
                value = turned[piece : piece + block]
                if source is received_ref:
                    for which in range(2):
                        @pl.when(side == which)
                        def _(target=targets[which]):
                            target[1 - far, levels - 1 - step] = value
                else:
                    targets[side, 1 - far, levels - 1 - step] = value


def split_loss(part, variables):
    column = lax.broadcasted_iota(jnp.int32, part.shape, 1)
    spots = (column == variables) | (column == variables + 1)
    total = jnp.sum(jnp.where(spots, part, 0.0), axis=1, keepdims=True)
    high = total.astype(bf16).astype(f32)
    return jnp.where(column == variables, high, jnp.where(column == variables + 1, total - high, part))


def score_kernel(
    own_ref, other_ref, truth_ref, cell_ref, project_ref, slope_ref, normed_t_ref, active_t_ref,
    inner_ref, pred_ref, loss_ref, far_ref, near_ref, hold_ref,
):
    members, variables, points = own_ref.shape
    width = slope_ref.shape[1]
    total = 2 * members
    pairs = total * (total - 1)

    def eased(delta):
        square = delta * delta + smoothing * smoothing
        inverse = lax.rsqrt(square)
        return square * inverse, delta * inverse

    truth, cell = truth_ref[...], cell_ref[...].reshape(1, points)
    own = [own_ref[m] for m in range(members)]
    other = [other_ref[m].astype(f32) for m in range(members)]
    score = jnp.zeros_like(truth)
    pulls = [jnp.zeros_like(truth) for _ in own]
    grads = []
    for m in range(members):
        size, sign = eased(own[m] - truth)
        score = score + size * (1.0 / total)
        grads.append(sign * (1.0 / total))
    for m in range(members):
        for n in range(m + 1, members):
            size, sign = eased(own[m] - own[n])
            score = score - size * (1.0 / pairs)
            pulls[m] = pulls[m] + sign
            pulls[n] = pulls[n] - sign
        for n in range(members):
            size, sign = eased(own[m] - other[n])
            score = score - size * (0.5 / pairs)
            pulls[m] = pulls[m] + sign
    loss = jnp.sum(score * cell)
    loss_ref[0] = loss
    hold_ref[...] = jnp.zeros_like(hold_ref)
    for m in range(members):
        grad = (grads[m] - pulls[m] * (1.0 / pairs)) * cell
        hold_ref[0:variables, m * points : (m + 1) * points] = grad
    pred = hold_ref[...].astype(bf16)
    pred_ref[...] = pred
    for m in range(members):
        rows = slice(m * points, (m + 1) * points)
        part = pred[:variables, rows]
        for begin in range(0, width, tile):
            columns = slice(begin, begin + tile)
            grad = mm(part, project_ref[:, columns], 0, 0)
            inner_ref[rows, columns] = (grad * slope_ref[rows, columns]).astype(bf16)
    weight_parts(normed_t_ref, active_t_ref, inner_ref, pred, loss, variables, 1, 0, far_ref)
    weight_parts(normed_t_ref, active_t_ref, inner_ref, pred, loss, variables, 1, 1, near_ref)


def weight_parts(normed_t_ref, active_t_ref, inner_ref, pred, loss, variables, side, half, out_ref):
    width = inner_ref.shape[1]
    depth = normed_t_ref.shape[-1]
    normed = normed_t_ref[side, half].reshape(-1, depth)
    for begin in range(0, width, tile):
        columns = slice(begin, begin + tile)
        out_ref[:, columns] = mm(normed, inner_ref[:, columns], 1, 0).astype(out_ref.dtype)
    part = mm(active_t_ref[side, half].reshape(-1, depth), pred, 1, 1)
    part = jnp.where(lax.broadcasted_iota(jnp.int32, part.shape, 1) == variables, loss, part)
    out_ref[:, width:] = split_loss(part, variables).astype(out_ref.dtype)


def pair_kernel(
    variables, half, loss_ref, normed_t_ref, active_t_ref, inner_ref, pred_ref, arrived_ref, *out_refs
):
    hold_ref = out_refs[-1]
    width = inner_ref.shape[1]
    weight_parts(
        normed_t_ref, active_t_ref, inner_ref, pred_ref[...], loss_ref[0], variables, 0, half, hold_ref
    )
    count = hold_ref.shape[0] // (len(out_refs) - 1)
    for i, out_ref in enumerate(out_refs[:-1]):
        rows = slice(i * count, (i + 1) * count)
        total = hold_ref[rows, :] + arrived_ref[rows, :].astype(f32)
        out_ref[:, :width] = total[:, :width].astype(out_ref.dtype)
        out_ref[:, width:] = split_loss(total[:, width:], variables).astype(out_ref.dtype)


def line_kernel(variables, width, kept_ref, arrived_ref, *out_refs):
    block = out_refs[0].shape[0]
    for i, out_ref in enumerate(out_refs):
        rows = slice(i * block, (i + 1) * block)
        total = kept_ref[rows, :] + arrived_ref[rows, :].astype(f32)
        out_ref[:, :width] = total[:, :width].astype(out_ref.dtype)
        if out_ref.shape[1] > width:
            out_ref[:, width:] = split_loss(total[:, width:], variables).astype(out_ref.dtype)


def back_kernel(inner_ref, w_hidden_ref, gain_ref, unit_ref, inverse_ref, grad_ref, scaled_ref):
    rows_all, width = inner_ref.shape
    gain = gain_ref[...].reshape(1, width)
    for begin_row in range(0, rows_all, tile):
        rows = slice(begin_row, begin_row + tile)
        dots = jnp.zeros((tile, 1), f32)
        for begin in range(0, width, tile):
            columns = slice(begin, begin + tile)
            scaled = mm(inner_ref[rows, :], w_hidden_ref[columns, :], 1, 1) * gain[:, columns]
            dots = dots + jnp.sum(scaled * unit_ref[rows, columns], axis=-1, keepdims=True)
            scaled_ref[rows, columns] = scaled
        dots = dots * (1.0 / width)
        inverse = inverse_ref[rows, :]
        for begin in range(0, width, tile):
            columns = slice(begin, begin + tile)
            grad_ref[rows, columns] = (
                (scaled_ref[rows, columns] - unit_ref[rows, columns] * dots) * inverse
            ).astype(bf16)


def slot_kernel(share_ref, grad_ref, slots_ref):
    rows = share_ref.shape[0] // 2
    for begin in range(0, grad_ref.shape[1], tile):
        columns = slice(begin, begin + tile)
        both = mm(share_ref[...], grad_ref[:, columns], 1, 0)
        slots_ref[:, columns] = (both[:rows] + both[rows:]).astype(bf16)


def owner_kernel(pick_ref, arrived_ref, w_msg_ref, grad_ref):
    rows = mm(pick_ref[...], arrived_ref[...], 0, 0).astype(bf16)
    grad_ref[...] = mm(rows, w_msg_ref[...], 1, 1).astype(bf16).reshape(grad_ref.shape)


def message_kernel(keep_ref, give_ref, slots_ref, other_ref, far_ref, near_ref, copy_ref):
    copy_ref[...] = slots_ref[...].reshape(copy_ref.shape)
    depth = keep_ref.shape[-1]
    for half, out_ref in ((0, far_ref), (1, near_ref)):
        own = keep_ref[half].reshape(-1, depth)
        other = give_ref[half].reshape(-1, depth)
        for begin in range(0, out_ref.shape[1], tile):
            columns = slice(begin, begin + tile)
            total = mm(own, slots_ref[:, columns], 1, 0) + mm(other, other_ref[:, columns], 1, 0)
            out_ref[:, columns] = total.astype(out_ref.dtype)


def hidden_sum_kernel(variables, scale, own_ref, *rest):
    hidden_ref, out_ref, loss_ref = rest[-3:]
    total = own_ref[...]
    for r in rest[:-3]:
        total = total + r[...].astype(f32)
    width = hidden_ref.shape[1]
    hidden_ref[...] = total[:, :width]
    part = total[:, width:]
    out_ref[...] = part[:, :variables]
    column = lax.broadcasted_iota(jnp.int32, (8, part.shape[1]), 1)
    spots = (column == variables) | (column == variables + 1)
    first = lax.broadcasted_iota(jnp.int32, (8, part.shape[1]), 0) == 0
    loss_ref[0] = jnp.sum(jnp.where(spots & first, part[:8], 0.0)) * scale


def sum_kernel(own_ref, *rest):
    total = own_ref[...]
    for r in rest[:-1]:
        total = total + r[...].astype(f32)
    rest[-1][...] = total


def on_device(
    latents, grid_embed, norm_gain, w_msg, w_hidden, variable_projection, present_condition, verifying_field,
    cell_surface, send_rows, edge_slot, edge_dst, edge_weight,
):
    members, nodes, width = latents.shape
    points = grid_embed.shape[0]
    variables = variable_projection.shape[1]
    peers = lax.axis_size("space")
    cores = lax.axis_size("member")
    cap = send_rows.shape[2]
    rows_peer = members * cap
    rows_slot = peers * rows_peer
    rows_all = members * points
    levels = peers // 2
    block = width // (peers * cores)
    half = levels * block
    wide = width + -(-(variables + 2) // lanes) * lanes
    project = variable_projection.T

    exchange = functools.partial(
        lax.all_to_all, axis_name="space", split_axis=0, concat_axis=0, tiled=True
    )
    send, pick = call(
        select_kernel,
        [((peers, rows_peer, width), bf16), ((rows_slot, members * nodes), bf16)],
        [send_rows, latents],
        scratch=[
            pltpu.SMEM(send_rows.shape, jnp.int32),
            pltpu.VMEM(latents.shape, bf16),
            pltpu.SemaphoreType.DMA((2,)),
        ],
        limit=4,
        places=(0, 1),
    )
    received = exchange(send).reshape(rows_slot, width)
    present = present_condition.transpose(1, 0, 2)
    fixed = [w_msg, w_hidden, grid_embed, norm_gain, project, present]
    share, *staged = call(
        functools.partial(stage_kernel, cap, members),
        [((2 * rows_slot, rows_all), bf16)] + [(x.shape, x.dtype) for x in fixed],
        [edge_slot, edge_dst, edge_weight] + fixed,
        scratch=[pltpu.SemaphoreType.DMA((len(fixed),))],
        limit=16,
        places=tuple(range(3, 3 + len(fixed))),
        after=[pick],
    )
    w_msg_near, w_hidden_near, embed, gain, project_near, present = staged
    field, sent, normed, active, slope, unit, inverse = call(
        forward_kernel,
        [
            ((members, variables, points), f32),
            ((members, variables, points), bf16),
            ((rows_all, width), bf16),
            ((rows_all, width), bf16),
            ((rows_all, width), f32),
            ((rows_all, width), f32),
            ((rows_all, 1), f32),
        ],
        [received, w_msg_near, share, embed, gain, w_hidden_near, project_near, present],
        limit=20,
    )
    other = swap(sent, "member", cores, 1)
    normed_t, active_t, received_keep, received_give = call(
        turn_kernel,
        [((cores, 2, levels, block, rows_all), bf16)] * 2 + [((2, levels, block, rows_slot), bf16)] * 2,
        [normed, active, received],
        limit=8,
    )
    received_other = swap(received_give, "member", cores, 1)
    grad_inner, pred, loss_part, far, near = call(
        score_kernel,
        [
            ((rows_all, width), bf16),
            ((lanes, rows_all), bf16),
            ((1,), f32),
            ((half, wide), bf16),
            ((half, wide), bf16),
        ],
        [field, other, verifying_field, cell_surface, project_near, slope, normed_t, active_t],
        scratch=[pltpu.VMEM((lanes, rows_all), f32)],
        limit=16,
        scalar_outs=(2,),
    )
    far_other = swap(far, "member", cores, 1)
    near_other = swap(near, "member", cores, 1)
    (grad_hidden,) = call(
        back_kernel,
        [((rows_all, width), bf16)],
        [grad_inner, w_hidden_near, gain, unit, inverse],
        scratch=[pltpu.VMEM((rows_all, width), f32)],
        limit=14,
    )
    parts = [loss_part, normed_t, active_t, grad_inner, pred]
    (hidden_far,) = call(
        functools.partial(pair_kernel, variables, 0),
        [((half, wide), bf16)],
        parts + [far_other],
        scratch=[pltpu.VMEM((half, wide), f32)],
        limit=12,
        scalars=(0,),
        after=[grad_hidden],
    )
    hidden_arrived = swap(hidden_far, "space", peers, 1)
    (slots,) = call(
        slot_kernel, [((rows_slot, width), bf16)], [share, grad_hidden], limit=6, after=[hidden_far]
    )
    slots_other = swap(slots, "member", cores, 1)
    message_far, message_near, slots_out = call(
        message_kernel,
        [((half, width), bf16), ((half, width), f32), ((peers, rows_peer, width), bf16)],
        [received_keep, received_other, slots, slots_other],
        limit=8,
    )
    message_arrived = swap(message_far, "space", peers, 1)
    back = exchange(slots_out).reshape(rows_slot, width)
    (hidden_near,) = call(
        functools.partial(pair_kernel, variables, 1),
        [((half, wide), f32)],
        parts + [near_other],
        scratch=[pltpu.VMEM((half, wide), f32)],
        limit=12,
        scalars=(0,),
        after=[message_far],
    )

    def spread(near, arrived):
        *sent, own = call(
            functools.partial(line_kernel, variables, width),
            [((block, near.shape[1]), bf16)] * (levels - 1) + [((block, near.shape[1]), f32)],
            [near, arrived],
            limit=6,
        )
        return own, [swap(x, "space", peers, 2 * (levels - 1 - i)) for i, x in enumerate(sent)]

    hidden_own, hidden_parts = spread(hidden_near, hidden_arrived)
    message_own, message_parts = spread(message_near, message_arrived)
    (latent_grad,) = call(
        owner_kernel, [(latents.shape, bf16)], [pick, back, w_msg], limit=8, after=[hidden_own]
    )
    hidden_weight_grad, out_weight_grad, loss = call(
        functools.partial(hidden_sum_kernel, variables, 1.0 / (points * peers * variables)),
        [((block, width), f32), ((block, variables), f32), ((1,), f32)],
        [hidden_own] + hidden_parts,
        limit=6,
        scalar_outs=(2,),
        after=[message_own],
    )
    (msg_weight_grad,) = call(
        sum_kernel,
        [((block, width), f32)],
        [message_own] + message_parts,
        limit=6,
        after=[hidden_weight_grad],
    )
    return (latent_grad, loss, msg_weight_grad, hidden_weight_grad, out_weight_grad)


def solution(mesh):
    placed = (
        P(("groups", "member"), "space", None),
        P(("groups", "space"), None),
        P(),
        P(),
        P(),
        P(),
        P(("groups", "member"), None, "space"),
        P(None, ("groups", "space")),
        P(("groups", "space")),
        P("space", None, None),
        P("space"),
        P("space"),
        P("space"),
    )
    return jax.shard_map(
        on_device,
        mesh=mesh,
        in_specs=placed,
        out_specs=(
            P(("groups", "member"), "space", None),
            P("groups"),
            P(("groups", "space", "member"), None),
            P(("groups", "space", "member"), None),
            P(("groups", "space", "member"), None),
        ),
        check_vma=False,
    )
```

```python
import functools

import jax
import jax.numpy as jnp
from jax import lax
from jax.experimental import pallas as pl
from jax.experimental.pallas import tpu as pltpu
from jax.sharding import PartitionSpec as P

smoothing = 0.1
epsilon = 1e-06
tile = 256
lanes = 128
packed = 16
f32 = jnp.float32
bf16 = jnp.bfloat16


def mm(left, right, left_dim, right_dim):
    return lax.dot_general(
        left, right, (((left_dim,), (right_dim,)), ((), ())), preferred_element_type=f32
    )


def call(body, outs, args, scratch=(), limit=16, scalars=(), scalar_outs=(), places=(), after=(), cost=0):
    whole = pl.BlockSpec(memory_space=pltpu.VMEM)
    small = pl.BlockSpec(memory_space=pltpu.SMEM)
    far_place = pl.BlockSpec(memory_space=pltpu.HBM)
    any_place = pl.BlockSpec(memory_space=pl.ANY)
    count = len(after)
    args = [pltpu.with_memory_space_constraint(x, pltpu.HBM) if i in places else x for i, x in enumerate(args)]

    def inner(*refs):
        body(*refs[count:])

    specs = [small if i in scalars else far_place if i in places else whole for i in range(len(args))]
    return pl.pallas_call(
        inner if count else body,
        out_shape=[jax.ShapeDtypeStruct(dims, kind) for dims, kind in outs],
        in_specs=[any_place] * count + specs,
        out_specs=[small if i in scalar_outs else whole for i in range(len(outs))],
        scratch_shapes=scratch,
        compiler_params=pltpu.CompilerParams(vmem_limit_bytes=limit * 2**20),
        cost_estimate=pl.CostEstimate(flops=cost, bytes_accessed=0, transcendentals=0),
    )(*after, *args)


def place():
    space = lax.axis_index("space")
    return lax.div(space, 2), lax.rem(space, 2), lax.axis_index("member")


def swap(value, axis, size, step):
    return lax.ppermute(value, axis, [(i, i ^ step) for i in range(size)])


def select_kernel(lists_ref, latents_ref, send_ref, pick_ref, small_ref, table_ref, sems):
    _, peers, cap = lists_ref.shape
    members, nodes, width = latents_ref.shape
    lists = pltpu.make_async_copy(lists_ref, small_ref, sems.at[0])
    table = pltpu.make_async_copy(latents_ref, table_ref, sems.at[1])
    lists.start()
    table.start()
    lists.wait()
    at = lax.broadcasted_iota(jnp.int32, (cap, members * nodes), 0)
    column = lax.broadcasted_iota(jnp.int32, (cap, members * nodes), 1)
    rows = []
    for peer in range(peers):
        wanted = jnp.zeros((cap, members * nodes), jnp.int32)
        for j in range(cap):
            wanted = jnp.where(at == j, small_ref[0, peer, j], wanted)
        for member in range(members):
            rows.append((column == wanted + member * nodes).astype(f32))
    pick = jnp.concatenate(rows, axis=0).astype(bf16)
    pick_ref[...] = pick
    table.wait()
    sent = mm(pick, table_ref[...].reshape(members * nodes, width), 1, 0)
    send_ref[...] = sent.astype(bf16).reshape(send_ref.shape)


def stage_kernel(cap, members, count, *refs):
    edge_refs, source_refs, share_ref = refs[:3], refs[3 : 3 + count], refs[3 + count]
    staged_refs, held_refs, sems = refs[4 + count : 4 + 2 * count], refs[4 + 2 * count : -1], refs[-1]
    copies = [
        pltpu.make_async_copy(source, target, sems.at[i])
        for i, (source, target) in enumerate(
            zip(edge_refs + source_refs, held_refs + staged_refs, strict=True)
        )
    ]
    for copy in copies:
        copy.start()
    for copy in copies[:3]:
        copy.wait()
    edge_part(cap, members, *held_refs, share_ref)
    for copy in copies[3:]:
        copy.wait()


def edge_part(cap, members, slot_ref, dst_ref, weight_ref, share_ref):
    edges = slot_ref.shape[0]
    slot = slot_ref[...].reshape(1, edges)
    dst = dst_ref[...].reshape(1, edges)
    weight = weight_ref[...].reshape(1, edges)
    rows = share_ref.shape[0] // 2
    points = share_ref.shape[1] // members
    sender = lax.div(slot, cap)
    spot = sender * (members * cap) + (slot - sender * cap)
    hit = lax.broadcasted_iota(jnp.int32, (rows, edges), 0) == spot
    into = (lax.broadcasted_iota(jnp.int32, (points, edges), 0) == dst).astype(f32).astype(bf16)
    high = weight.astype(bf16).astype(f32)
    table = mm(jnp.where(hit, high, 0.0).astype(bf16), into, 1, 1) + mm(
        jnp.where(hit, weight - high, 0.0).astype(bf16), into, 1, 1
    )
    table = table / jnp.sum(table, axis=0, keepdims=True)
    for member in range(members):
        high = table.astype(bf16)
        columns = slice(member * points, (member + 1) * points)
        share_ref[0:rows, columns] = high
        share_ref[rows : 2 * rows, columns] = (table - high.astype(f32)).astype(bf16)
        table = jnp.concatenate([table[rows - cap :], table[: rows - cap]], axis=0)


def forward_kernel(
    received_ref, w_msg_ref, share_ref, embed_ref, gain_ref, w_hidden_ref, project_ref, present_ref,
    field_ref, sent_ref, normed_ref, active_ref, slope_ref, unit_ref, inverse_ref, weights_ref, sem,
):
    points, width = embed_ref.shape
    weights = pltpu.make_async_copy(w_hidden_ref, weights_ref, sem)
    weights.start()
    variables, members, _ = present_ref.shape
    messages = mm(received_ref[...], w_msg_ref[...], 1, 0).astype(bf16)
    messages = jnp.concatenate([messages, messages], axis=0)
    gain = gain_ref[...].reshape(1, width)
    for begin in range(0, members * points, lanes):
        rows = slice(begin, begin + lanes)
        source = slice(begin % points, begin % points + lanes)
        hidden = embed_ref[source, :].astype(f32) + mm(share_ref[:, rows], messages, 0, 0)
        inverse = lax.rsqrt(jnp.mean(hidden * hidden, axis=-1, keepdims=True) + epsilon)
        unit = hidden * inverse
        unit_ref[rows, :] = unit
        inverse_ref[rows, :] = inverse
        normed_ref[rows, :] = (unit * gain).astype(bf16)
    weights.wait()
    root = 0.7978845608028654
    cubic = 0.044715
    for member in range(members):
        rows = slice(member * points, (member + 1) * points)
        for begin in range(0, width, tile):
            columns = slice(begin, begin + tile)
            inner = mm(normed_ref[rows, :], weights_ref[:, columns], 1, 0)
            square = inner * inner
            bend = jnp.tanh(inner * (root + root * cubic * square))
            half = 0.5 + 0.5 * bend
            active_ref[rows, columns] = (inner * half).astype(bf16)
            slope_ref[rows, columns] = half + (0.5 * inner) * (1.0 - bend * bend) * (
                root + 3.0 * root * cubic * square
            )
        field = present_ref[:, member, :] + mm(project_ref[...], active_ref[rows, :], 1, 1)
        field_ref[member] = field
        sent_ref[member] = field.astype(bf16)


def turn_kernel(normed_ref, active_ref, received_ref, normed_t_ref, active_t_ref, keep_ref, give_ref):
    _, _, levels, block, _ = normed_t_ref.shape
    width = normed_ref.shape[1]
    level, line, core = place()
    for source, targets in (
        (received_ref, (keep_ref, give_ref)), (normed_ref, normed_t_ref), (active_ref, active_t_ref)
    ):
        for begin in range(0, width, tile):
            turned = source[:, begin : begin + tile].T
            for piece in range(0, tile, block):
                index = (begin + piece) // block
                far = (index // 2 % 2) ^ line
                step = (index // 4) ^ level
                side = (index % 2) ^ core
                value = turned[piece : piece + block]
                if source is received_ref:
                    for which in range(2):
                        @pl.when(side == which)
                        def _(target=targets[which]):
                            target[1 - far, levels - 1 - step] = value
                else:
                    targets[side, 1 - far, levels - 1 - step] = value


def split_loss(part, variables):
    column = lax.broadcasted_iota(jnp.int32, part.shape, 1)
    spots = (column == variables) | (column == variables + 1)
    total = jnp.sum(jnp.where(spots, part, 0.0), axis=1, keepdims=True)
    high = total.astype(bf16).astype(f32)
    return jnp.where(column == variables, high, jnp.where(column == variables + 1, total - high, part))


def score_kernel(
    own_ref, other_ref, truth_ref, cell_ref, project_ref, slope_ref, normed_t_ref, active_t_ref,
    inner_ref, pred_ref, loss_ref, far_ref, near_ref, hold_ref,
):
    members, variables, points = own_ref.shape
    width = slope_ref.shape[1]
    total = 2 * members
    pairs = total * (total - 1)

    def eased(delta):
        square = delta * delta + smoothing * smoothing
        inverse = lax.rsqrt(square)
        return square * inverse, delta * inverse

    truth, cell = truth_ref[...], cell_ref[...].reshape(1, points)
    own = [own_ref[m] for m in range(members)]
    other = [other_ref[m].astype(f32) for m in range(members)]
    score = jnp.zeros_like(truth)
    pulls = [jnp.zeros_like(truth) for _ in own]
    grads = []
    for m in range(members):
        size, sign = eased(own[m] - truth)
        score = score + size * (1.0 / total)
        grads.append(sign * (1.0 / total))
    for m in range(members):
        for n in range(m + 1, members):
            size, sign = eased(own[m] - own[n])
            score = score - size * (1.0 / pairs)
            pulls[m] = pulls[m] + sign
            pulls[n] = pulls[n] - sign
        for n in range(members):
            size, sign = eased(own[m] - other[n])
            score = score - size * (0.5 / pairs)
            pulls[m] = pulls[m] + sign
    loss = jnp.sum(score * cell)
    loss_ref[0] = loss
    hold_ref[...] = jnp.zeros_like(hold_ref)
    for m in range(members):
        grad = (grads[m] - pulls[m] * (1.0 / pairs)) * cell
        hold_ref[0:variables, m * points : (m + 1) * points] = grad
    pred = hold_ref[...].astype(bf16)
    pred_ref[...] = pred
    for m in range(members):
        rows = slice(m * points, (m + 1) * points)
        part = pred[:variables, rows]
        for begin in range(0, width, tile):
            columns = slice(begin, begin + tile)
            grad = mm(part, project_ref[:, columns], 0, 0)
            inner_ref[rows, columns] = (grad * slope_ref[rows, columns]).astype(bf16)
    weight_parts(normed_t_ref, active_t_ref, inner_ref, pred, loss, variables, 1, 0, far_ref)
    weight_parts(normed_t_ref, active_t_ref, inner_ref, pred, loss, variables, 1, 1, near_ref)


def weight_parts(normed_t_ref, active_t_ref, inner_ref, pred, loss, variables, side, half, out_ref):
    width = inner_ref.shape[1]
    depth = normed_t_ref.shape[-1]
    normed = normed_t_ref[side, half].reshape(-1, depth)
    for begin in range(0, width, tile):
        columns = slice(begin, begin + tile)
        out_ref[:, columns] = mm(normed, inner_ref[:, columns], 1, 0).astype(out_ref.dtype)
    part = mm(active_t_ref[side, half].reshape(-1, depth), pred, 1, 1)
    part = jnp.where(lax.broadcasted_iota(jnp.int32, part.shape, 1) == variables, loss, part)
    out_ref[:, width:] = split_loss(part, variables).astype(out_ref.dtype)


def pack(out_ref, begin, part):
    pad = part.shape[1]
    for i in range(part.shape[0] // packed):
        out_ref[begin : begin + packed, i * pad : (i + 1) * pad] = part[i * packed : (i + 1) * packed]


def unpack(in_ref, begin, count, pad):
    parts = [in_ref[begin : begin + packed, i * pad : (i + 1) * pad] for i in range(count // packed)]
    return jnp.concatenate(parts, axis=0).astype(f32)


def far_kernel(
    variables, loss_ref, normed_t_ref, active_t_ref, inner_ref, pred_ref, arrived_ref, slots_ref,
    first_ref, second_ref, hold_ref,
):
    width = inner_ref.shape[1]
    weight_parts(normed_t_ref, active_t_ref, inner_ref, pred_ref[...], loss_ref[0], variables, 0, 0, hold_ref)
    count = second_ref.shape[0] - packed
    for begin in (0, count):
        rows = slice(begin, begin + count)
        total = hold_ref[rows, :width] + arrived_ref[rows, :width].astype(f32)
        part = hold_ref[rows, width:] + arrived_ref[rows, width:].astype(f32)
        part = split_loss(part, variables).astype(bf16)
        if begin == 0:
            first_ref[rows, :width] = total.astype(bf16)
            first_ref[rows, width:] = part
        else:
            second_ref[0:count, :] = total.astype(bf16)
            pack(second_ref, count, part)
    peers, rows, _ = slots_ref.shape
    level, line, _ = place()
    levels = peers // 2
    first_ref[count:, width:] = jnp.zeros((levels * rows, first_ref.shape[1] - width), bf16)
    for i in range(levels):
        at = count + i * rows
        first_ref[at : at + rows, :width] = slots_ref[(level ^ (levels - 1 - i)) * 2 + 1 - line]


def near_kernel(
    variables, loss_ref, normed_t_ref, active_t_ref, inner_ref, pred_ref, arrived_ref, out_ref, hold_ref
):
    weight_parts(normed_t_ref, active_t_ref, inner_ref, pred_ref[...], loss_ref[0], variables, 0, 1, hold_ref)
    out_ref[...] = hold_ref[...] + arrived_ref[...].astype(f32)


def early_kernel(variables, kept_ref, ride_ref, slots_ref, *out_refs):
    peers, rows, width = slots_ref.shape
    level, line, _ = place()
    levels = peers // 2
    block = kept_ref.shape[0] // levels
    for i, out_ref in enumerate(out_refs):
        here = slice(i * block, (i + 1) * block)
        total = kept_ref[here, :] + ride_ref[here, :].astype(f32)
        out_ref[0:block, :width] = total[:, :width].astype(bf16)
        out_ref[0:block, width:] = split_loss(total[:, width:], variables).astype(bf16)
        out_ref[block:, width:] = jnp.zeros((2 * rows, out_ref.shape[1] - width), bf16)
        out_ref[block : block + rows, :width] = slots_ref[(level ^ (levels - 1 - i)) * 2 + line]
        at = levels // 2 * block + i * rows
        out_ref[block + rows :, :width] = ride_ref[at : at + rows, :width]


def late_kernel(variables, early, kept_ref, message_ref, arrived_ref, ride_ref, slots_ref, *out_refs):
    hidden_ref, own_ref = out_refs[-2:]
    peers, rows, width = slots_ref.shape
    level, line, _ = place()
    levels = peers // 2
    block = kept_ref.shape[0] // levels
    count = (levels - early) * block
    part = unpack(arrived_ref, count, count, kept_ref.shape[1] - width)
    for i in range(early, levels):
        here, there = slice(i * block, (i + 1) * block), slice((i - early) * block, (i - early + 1) * block)
        total = kept_ref[here, :width] + arrived_ref[there, :].astype(f32)
        out = split_loss(kept_ref[here, width:] + part[there], variables)
        if i == levels - 1:
            hidden_ref[:, :width] = total
            hidden_ref[:, width:] = out
            continue
        out_ref = out_refs[i - early]
        out_ref[0:block, :] = total.astype(bf16)
        at = 2 * block
        out_ref[at : at + rows, :] = slots_ref[(level ^ (levels - 1 - i)) * 2 + line]
        ride = early * block + i * rows
        out_ref[at + rows : at + 2 * rows, :] = ride_ref[ride : ride + rows, :width]
        out_ref[at + 2 * rows :, :] = jnp.zeros((packed, width), bf16)
        pack(out_ref, at + 2 * rows, out.astype(bf16))
    for i in range(levels):
        here = slice(i * block, (i + 1) * block)
        at = count + packed + i * block
        total = message_ref[here, :] + arrived_ref[at : at + block, :].astype(f32)
        if i == levels - 1:
            own_ref[...] = total
        elif i >= early:
            out_refs[i - early][block : 2 * block, :] = total.astype(bf16)
        else:
            out_refs[levels - 1 - early + i][...] = total.astype(bf16)


def back_kernel(inner_ref, w_hidden_ref, gain_ref, unit_ref, inverse_ref, grad_ref, scaled_ref):
    rows_all, width = inner_ref.shape
    gain = gain_ref[...].reshape(1, width)
    for begin_row in range(0, rows_all, tile):
        rows = slice(begin_row, begin_row + tile)
        dots = jnp.zeros((tile, 1), f32)
        for begin in range(0, width, tile):
            columns = slice(begin, begin + tile)
            scaled = mm(inner_ref[rows, :], w_hidden_ref[columns, :], 1, 1) * gain[:, columns]
            dots = dots + jnp.sum(scaled * unit_ref[rows, columns], axis=-1, keepdims=True)
            scaled_ref[rows, columns] = scaled
        dots = dots * (1.0 / width)
        inverse = inverse_ref[rows, :]
        for begin in range(0, width, tile):
            columns = slice(begin, begin + tile)
            grad_ref[rows, columns] = (
                (scaled_ref[rows, columns] - unit_ref[rows, columns] * dots) * inverse
            ).astype(bf16)


def slot_kernel(share_ref, grad_ref, slots_ref):
    peers, each, width = slots_ref.shape
    rows = peers * each
    for begin in range(0, width, tile):
        columns = slice(begin, begin + tile)
        both = mm(share_ref[...], grad_ref[:, columns], 1, 0)
        slots_ref[:, :, columns] = (both[:rows] + both[rows:]).astype(bf16).reshape(peers, each, tile)


def owner_kernel(early, block, pick_ref, w_msg_ref, slots_ref, ride_ref, *rest):
    arrived_refs, (grad_ref, token_ref, held_ref) = rest[:-3], rest[-3:]
    token_ref[...] = jnp.zeros_like(token_ref)
    peers, rows, width = slots_ref.shape
    level, line, _ = place()
    levels = peers // 2
    mine = level * 2 + line
    held_ref[mine] = slots_ref[mine]
    held_ref[mine ^ 1] = ride_ref[ride_ref.shape[0] - rows :, :width]
    for i, arrived_ref in enumerate(arrived_refs):
        spot = (level ^ (levels - 1 - i)) * 2 + line
        at = block if i < early else 2 * block
        held_ref[spot] = arrived_ref[at : at + rows, :width]
        held_ref[spot ^ 1] = arrived_ref[at + rows : at + 2 * rows, :width]
    nodes = mm(pick_ref[...], held_ref[...].reshape(peers * rows, width), 0, 0).astype(bf16)
    grad_ref[...] = mm(nodes, w_msg_ref[...], 1, 1).astype(bf16).reshape(grad_ref.shape)


def message_kernel(keep_ref, give_ref, slots_ref, other_ref, second_ref, far_ref, near_ref):
    depth, width = keep_ref.shape[-1], near_ref.shape[1]
    begin_far = second_ref.shape[0]
    far_ref[0:begin_far, :] = second_ref[...]
    for half in range(2):
        own = keep_ref[half].reshape(-1, depth)
        other = give_ref[half].reshape(-1, depth)
        for begin in range(0, width, tile):
            columns = slice(begin, begin + tile)
            here = slots_ref[:, :, columns].reshape(depth, tile)
            there = other_ref[:, :, columns].reshape(depth, tile)
            total = mm(own, here, 1, 0) + mm(other, there, 1, 0)
            if half == 0:
                far_ref[begin_far:, columns] = total.astype(bf16)
            else:
                near_ref[:, columns] = total


def hidden_sum_kernel(variables, scale, early, own_ref, *rest):
    hidden_ref, out_ref, loss_ref, token_ref = rest[-4:]
    token_ref[...] = jnp.zeros_like(token_ref)
    block, width = hidden_ref.shape
    total = own_ref[:, :width]
    part = own_ref[:, width:]
    for i, r in enumerate(rest[:-4]):
        total = total + r[0:block, :width].astype(f32)
        if i < early:
            part = part + r[0:block, width:].astype(f32)
        else:
            part = part + unpack(r, r.shape[0] - packed, block, part.shape[1])
    hidden_ref[...] = total
    out_ref[...] = part[:, :variables]
    column = lax.broadcasted_iota(jnp.int32, (8, part.shape[1]), 1)
    spots = (column == variables) | (column == variables + 1)
    first = lax.broadcasted_iota(jnp.int32, (8, part.shape[1]), 0) == 0
    loss_ref[0] = jnp.sum(jnp.where(spots & first, part[:8], 0.0)) * scale


def sum_kernel(early, own_ref, *rest):
    block = own_ref.shape[0]
    total = own_ref[...]
    for i, r in enumerate(rest[:-1]):
        begin = 0 if i < early else block
        total = total + r[begin : begin + block, :].astype(f32)
    rest[-1][...] = total


def on_device(
    latents, grid_embed, norm_gain, w_msg, w_hidden, variable_projection, present_condition, verifying_field,
    cell_surface, send_rows, edge_slot, edge_dst, edge_weight,
):
    members, nodes, width = latents.shape
    points = grid_embed.shape[0]
    variables = variable_projection.shape[1]
    peers = lax.axis_size("space")
    cores = lax.axis_size("member")
    cap = send_rows.shape[2]
    rows_peer = members * cap
    rows_slot = peers * rows_peer
    rows_all = members * points
    levels = peers // 2
    block = width // (peers * cores)
    half = levels * block
    wide = width + -(-(variables + 2) // lanes) * lanes
    project = variable_projection.T

    exchange = functools.partial(
        lax.all_to_all, axis_name="space", split_axis=0, concat_axis=0, tiled=True
    )
    send, pick = call(
        select_kernel,
        [((peers, rows_peer, width), bf16), ((rows_slot, members * nodes), bf16)],
        [send_rows, latents],
        scratch=[
            pltpu.SMEM(send_rows.shape, jnp.int32),
            pltpu.VMEM(latents.shape, bf16),
            pltpu.SemaphoreType.DMA((2,)),
        ],
        limit=4,
        places=(0, 1),
    )
    received = exchange(send).reshape(rows_slot, width)
    present = present_condition.transpose(1, 0, 2)
    fixed = [w_msg, grid_embed, norm_gain, project, present]
    edges = [edge_slot, edge_dst, edge_weight]
    share, *staged = call(
        functools.partial(stage_kernel, cap, members, len(fixed)),
        [((2 * rows_slot, rows_all), bf16)] + [(x.shape, x.dtype) for x in fixed],
        edges + fixed,
        scratch=[pltpu.VMEM(x.shape, x.dtype) for x in edges]
        + [pltpu.SemaphoreType.DMA((3 + len(fixed),))],
        limit=16,
        places=tuple(range(3 + len(fixed))),
        after=[pick],
    )
    w_msg_near, embed, gain, project_near, present = staged
    field, sent, normed, active, slope, unit, inverse = call(
        forward_kernel,
        [
            ((members, variables, points), f32),
            ((members, variables, points), bf16),
            ((rows_all, width), bf16),
            ((rows_all, width), bf16),
            ((rows_all, width), f32),
            ((rows_all, width), f32),
            ((rows_all, 1), f32),
        ],
        [received, w_msg_near, share, embed, gain, w_hidden, project_near, present],
        scratch=[pltpu.VMEM(w_hidden.shape, bf16), pltpu.SemaphoreType.DMA],
        limit=22,
        places=(5,),
    )
    other = swap(sent, "member", cores, 1)
    normed_t, active_t, received_keep, received_give = call(
        turn_kernel,
        [((cores, 2, levels, block, rows_all), bf16)] * 2 + [((2, levels, block, rows_slot), bf16)] * 2,
        [normed, active, received],
        limit=8,
    )
    received_other = swap(received_give, "member", cores, 1)
    grad_inner, pred, loss_part, far, near = call(
        score_kernel,
        [
            ((rows_all, width), bf16),
            ((lanes, rows_all), bf16),
            ((1,), f32),
            ((half, wide), bf16),
            ((half, wide), bf16),
        ],
        [field, other, verifying_field, cell_surface, project_near, slope, normed_t, active_t],
        scratch=[pltpu.VMEM((lanes, rows_all), f32)],
        limit=16,
        scalar_outs=(2,),
    )
    far_other = swap(far, "member", cores, 1)
    near_other = swap(near, "member", cores, 1)
    (grad_hidden,) = call(
        back_kernel,
        [((rows_all, width), bf16)],
        [grad_inner, w_hidden, gain, unit, inverse],
        scratch=[pltpu.VMEM((rows_all, width), f32)],
        limit=14,
    )
    parts = [loss_part, normed_t, active_t, grad_inner, pred]
    (slots,) = call(
        slot_kernel, [((peers, rows_peer, width), bf16)], [share, grad_hidden], limit=6
    )
    early_count = levels // 2
    count = half // 2
    first, second = call(
        functools.partial(far_kernel, variables),
        [((count + levels * rows_peer, wide), bf16), ((count + packed, width), bf16)],
        parts + [far_other, slots],
        scratch=[pltpu.VMEM((half, wide), f32)],
        limit=12,
        scalars=(0,),
    )
    ride = swap(first, "space", peers, 1)
    slots_other = swap(slots, "member", cores, 1)
    (hidden_near,) = call(
        functools.partial(near_kernel, variables),
        [((half, wide), f32)],
        parts + [near_other],
        scratch=[pltpu.VMEM((half, wide), f32)],
        limit=12,
        scalars=(0,),
        after=[first],
    )
    message_far, message_near = call(
        message_kernel,
        [((count + packed + half, width), bf16), ((half, width), f32)],
        [received_keep, received_other, slots, slots_other, second],
        limit=8,
        after=[hidden_near],
    )
    arrived = swap(message_far, "space", peers, 1)
    steps = [2 * (levels - 1 - i) for i in range(levels - 1)]
    early = call(
        functools.partial(early_kernel, variables),
        [((block + 2 * rows_peer, wide), bf16)] * early_count,
        [hidden_near, ride, slots],
        limit=6,
        cost=2 * 10**10,
    )
    early_parts = [swap(x, "space", peers, k) for x, k in zip(early, steps[:early_count], strict=True)]
    *rest, hidden_own, message_own = call(
        functools.partial(late_kernel, variables, early_count),
        [((2 * block + 2 * rows_peer + packed, width), bf16)] * (levels - 1 - early_count)
        + [((block, width), bf16)] * early_count
        + [((block, wide), f32), ((block, width), f32)],
        [hidden_near, message_near, arrived, ride, slots],
        limit=8,
        after=early_parts,
    )
    late_parts = [
        swap(x, "space", peers, k)
        for x, k in zip(rest[: levels - 1 - early_count], steps[early_count:], strict=True)
    ]
    message_parts = [
        swap(x, "space", peers, k)
        for x, k in zip(rest[levels - 1 - early_count :], steps[:early_count], strict=True)
    ]
    token = ((8, lanes), f32)
    latent_grad, latent_done = call(
        functools.partial(owner_kernel, early_count, block),
        [(latents.shape, bf16), token],
        [pick, w_msg, slots, ride] + early_parts + late_parts,
        scratch=[pltpu.VMEM((peers, rows_peer, width), bf16)],
        limit=8,
        after=[message_own],
    )
    hidden_weight_grad, out_weight_grad, loss, hidden_done = call(
        functools.partial(
            hidden_sum_kernel, variables, 1.0 / (points * peers * variables), early_count
        ),
        [((block, width), f32), ((block, variables), f32), ((1,), f32), token],
        [hidden_own] + early_parts + late_parts,
        limit=6,
        scalar_outs=(2,),
        after=[latent_done],
    )
    (msg_weight_grad,) = call(
        functools.partial(sum_kernel, early_count),
        [((block, width), f32)],
        [message_own] + message_parts + late_parts,
        limit=6,
        after=[hidden_done],
    )
    return (latent_grad, loss, msg_weight_grad, hidden_weight_grad, out_weight_grad)


def solution(mesh):
    placed = (
        P(("groups", "member"), "space", None),
        P(("groups", "space"), None),
        P(),
        P(),
        P(),
        P(),
        P(("groups", "member"), None, "space"),
        P(None, ("groups", "space")),
        P(("groups", "space")),
        P("space", None, None),
        P("space"),
        P("space"),
        P("space"),
    )
    return jax.shard_map(
        on_device,
        mesh=mesh,
        in_specs=placed,
        out_specs=(
            P(("groups", "member"), "space", None),
            P("groups"),
            P(("groups", "space", "member"), None),
            P(("groups", "space", "member"), None),
            P(("groups", "space", "member"), None),
        ),
        check_vma=False,
    )
```

```python
import functools

import jax
import jax.numpy as jnp
from jax import lax
from jax.experimental import pallas as pl
from jax.experimental.pallas import tpu as pltpu
from jax.sharding import PartitionSpec as P

smoothing = 0.1
epsilon = 1e-06
tile = 256
lanes = 128
packed = 16
cost_hints = {
    "back_kernel": 8,
    "slot_kernel": 4,
    "hidden_early_kernel": 4,
    "message_early_kernel": 4,
    "late_kernel": 4,
    "message_sum_kernel": 8,
}
f32 = jnp.float32
bf16 = jnp.bfloat16


def mm(left, right, left_dim, right_dim):
    return lax.dot_general(
        left, right, (((left_dim,), (right_dim,)), ((), ())), preferred_element_type=f32
    )


def call(body, outs, args, scratch=(), limit=16, scalars=(), scalar_outs=(), places=(), after=()):
    whole = pl.BlockSpec(memory_space=pltpu.VMEM)
    small = pl.BlockSpec(memory_space=pltpu.SMEM)
    far_place = pl.BlockSpec(memory_space=pltpu.HBM)
    any_place = pl.BlockSpec(memory_space=pl.ANY)
    count = len(after)
    cost = cost_hints.get(getattr(body, "func", body).__name__, 0) * 10**9
    args = [pltpu.with_memory_space_constraint(x, pltpu.HBM) if i in places else x for i, x in enumerate(args)]

    def inner(*refs):
        body(*refs[count:])

    specs = [small if i in scalars else far_place if i in places else whole for i in range(len(args))]
    return pl.pallas_call(
        inner if count else body,
        out_shape=[jax.ShapeDtypeStruct(dims, kind) for dims, kind in outs],
        in_specs=[any_place] * count + specs,
        out_specs=[small if i in scalar_outs else whole for i in range(len(outs))],
        scratch_shapes=scratch,
        compiler_params=pltpu.CompilerParams(vmem_limit_bytes=limit * 2**20),
        cost_estimate=pl.CostEstimate(flops=cost, bytes_accessed=0, transcendentals=0),
    )(*after, *args)


def place():
    space = lax.axis_index("space")
    return lax.div(space, 2), lax.rem(space, 2), lax.axis_index("member")


def swap(value, axis, size, step):
    return lax.ppermute(value, axis, [(i, i ^ step) for i in range(size)])


def select_kernel(lists_ref, latents_ref, send_ref, pick_ref, small_ref, table_ref, sems):
    _, peers, cap = lists_ref.shape
    members, nodes, width = latents_ref.shape
    lists = pltpu.make_async_copy(lists_ref, small_ref, sems.at[0])
    table = pltpu.make_async_copy(latents_ref, table_ref, sems.at[1])
    lists.start()
    table.start()
    lists.wait()
    at = lax.broadcasted_iota(jnp.int32, (cap, members * nodes), 0)
    column = lax.broadcasted_iota(jnp.int32, (cap, members * nodes), 1)
    rows = []
    for peer in range(peers):
        wanted = jnp.zeros((cap, members * nodes), jnp.int32)
        for j in range(cap):
            wanted = jnp.where(at == j, small_ref[0, peer, j], wanted)
        for member in range(members):
            rows.append((column == wanted + member * nodes).astype(f32))
    pick = jnp.concatenate(rows, axis=0).astype(bf16)
    pick_ref[...] = pick
    table.wait()
    sent = mm(pick, table_ref[...].reshape(members * nodes, width), 1, 0)
    send_ref[...] = sent.astype(bf16).reshape(send_ref.shape)


def stage_kernel(cap, members, count, *refs):
    edge_refs, source_refs, share_ref = refs[:3], refs[3 : 3 + count], refs[3 + count]
    staged_refs, held_refs, sems = refs[4 + count : 4 + 2 * count], refs[4 + 2 * count : -1], refs[-1]
    copies = [
        pltpu.make_async_copy(source, target, sems.at[i])
        for i, (source, target) in enumerate(
            zip(edge_refs + source_refs, held_refs + staged_refs, strict=True)
        )
    ]
    for copy in copies:
        copy.start()
    for copy in copies[:3]:
        copy.wait()
    edge_part(cap, members, *held_refs, share_ref)
    for copy in copies[3:]:
        copy.wait()


def edge_part(cap, members, slot_ref, dst_ref, weight_ref, share_ref):
    edges = slot_ref.shape[0]
    slot = slot_ref[...].reshape(1, edges)
    dst = dst_ref[...].reshape(1, edges)
    weight = weight_ref[...].reshape(1, edges)
    rows = share_ref.shape[0] // 2
    points = share_ref.shape[1] // members
    sender = lax.div(slot, cap)
    spot = sender * (members * cap) + (slot - sender * cap)
    hit = lax.broadcasted_iota(jnp.int32, (rows, edges), 0) == spot
    into = (lax.broadcasted_iota(jnp.int32, (points, edges), 0) == dst).astype(f32).astype(bf16)
    high = weight.astype(bf16).astype(f32)
    table = mm(jnp.where(hit, high, 0.0).astype(bf16), into, 1, 1) + mm(
        jnp.where(hit, weight - high, 0.0).astype(bf16), into, 1, 1
    )
    table = table / jnp.sum(table, axis=0, keepdims=True)
    for member in range(members):
        high = table.astype(bf16)
        columns = slice(member * points, (member + 1) * points)
        share_ref[0:rows, columns] = high
        share_ref[rows : 2 * rows, columns] = (table - high.astype(f32)).astype(bf16)
        table = jnp.concatenate([table[rows - cap :], table[: rows - cap]], axis=0)


def forward_kernel(
    received_ref, w_msg_ref, share_ref, gain_ref, embed_hbm, w_hidden_hbm, project_hbm, present_hbm,
    field_ref, sent_ref, normed_ref, active_ref, slope_ref, unit_ref, inverse_ref,
    embed_ref, weights_ref, project_ref, present_ref, sems,
):
    points, width = embed_ref.shape
    far = (embed_hbm, w_hidden_hbm, project_hbm, present_hbm)
    close = (embed_ref, weights_ref, project_ref, present_ref)
    copies = [pltpu.make_async_copy(x, y, sems.at[i]) for i, (x, y) in enumerate(zip(far, close, strict=True))]
    for copy in copies:
        copy.start()
    variables, members, _ = present_ref.shape
    messages = mm(received_ref[...], w_msg_ref[...], 1, 0).astype(bf16)
    messages = jnp.concatenate([messages, messages], axis=0)
    gain = gain_ref[...].reshape(1, width)
    copies[0].wait()
    for begin in range(0, members * points, lanes):
        rows = slice(begin, begin + lanes)
        source = slice(begin % points, begin % points + lanes)
        hidden = embed_ref[source, :].astype(f32) + mm(share_ref[:, rows], messages, 0, 0)
        inverse = lax.rsqrt(jnp.mean(hidden * hidden, axis=-1, keepdims=True) + epsilon)
        unit = hidden * inverse
        unit_ref[rows, :] = unit
        inverse_ref[rows, :] = inverse
        normed_ref[rows, :] = (unit * gain).astype(bf16)
    for copy in copies[1:]:
        copy.wait()
    root = 0.7978845608028654
    cubic = 0.044715
    for member in range(members):
        rows = slice(member * points, (member + 1) * points)
        for begin in range(0, width, tile):
            columns = slice(begin, begin + tile)
            inner = mm(normed_ref[rows, :], weights_ref[:, columns], 1, 0)
            square = inner * inner
            bend = jnp.tanh(inner * (root + root * cubic * square))
            half = 0.5 + 0.5 * bend
            active_ref[rows, columns] = (inner * half).astype(bf16)
            slope_ref[rows, columns] = half + (0.5 * inner) * (1.0 - bend * bend) * (
                root + 3.0 * root * cubic * square
            )
        field = present_ref[:, member, :] + mm(project_ref[...], active_ref[rows, :], 1, 1)
        field_ref[member] = field
        sent_ref[member] = field.astype(bf16)


def turn_kernel(normed_ref, active_ref, received_ref, normed_t_ref, active_t_ref, keep_ref, give_ref):
    _, _, levels, block, _ = normed_t_ref.shape
    width = normed_ref.shape[1]
    level, line, core = place()
    for source, targets in (
        (received_ref, (keep_ref, give_ref)), (normed_ref, normed_t_ref), (active_ref, active_t_ref)
    ):
        for begin in range(0, width, tile):
            turned = source[:, begin : begin + tile].T
            for piece in range(0, tile, block):
                index = (begin + piece) // block
                far = (index // 2 % 2) ^ line
                step = (index // 4) ^ level
                side = (index % 2) ^ core
                value = turned[piece : piece + block]
                if source is received_ref:
                    for which in range(2):
                        @pl.when(side == which)
                        def _(target=targets[which]):
                            target[1 - far, levels - 1 - step] = value
                else:
                    targets[side, 1 - far, levels - 1 - step] = value


def split_loss(part, variables):
    column = lax.broadcasted_iota(jnp.int32, part.shape, 1)
    spots = (column == variables) | (column == variables + 1)
    total = jnp.sum(jnp.where(spots, part, 0.0), axis=1, keepdims=True)
    high = total.astype(bf16).astype(f32)
    return jnp.where(column == variables, high, jnp.where(column == variables + 1, total - high, part))


def score_kernel(
    own_ref, other_ref, truth_ref, cell_ref, project_ref, slope_ref, normed_t_ref, active_t_ref,
    inner_ref, pred_ref, loss_ref, far_ref, near_ref, hold_ref,
):
    members, variables, points = own_ref.shape
    width = slope_ref.shape[1]
    total = 2 * members
    pairs = total * (total - 1)

    def eased(delta):
        square = delta * delta + smoothing * smoothing
        inverse = lax.rsqrt(square)
        return square * inverse, delta * inverse

    truth, cell = truth_ref[...], cell_ref[...].reshape(1, points)
    own = [own_ref[m] for m in range(members)]
    other = [other_ref[m].astype(f32) for m in range(members)]
    score = jnp.zeros_like(truth)
    pulls = [jnp.zeros_like(truth) for _ in own]
    grads = []
    for m in range(members):
        size, sign = eased(own[m] - truth)
        score = score + size * (1.0 / total)
        grads.append(sign * (1.0 / total))
    for m in range(members):
        for n in range(m + 1, members):
            size, sign = eased(own[m] - own[n])
            score = score - size * (1.0 / pairs)
            pulls[m] = pulls[m] + sign
            pulls[n] = pulls[n] - sign
        for n in range(members):
            size, sign = eased(own[m] - other[n])
            score = score - size * (0.5 / pairs)
            pulls[m] = pulls[m] + sign
    loss = jnp.sum(score * cell)
    loss_ref[0] = loss
    hold_ref[...] = jnp.zeros_like(hold_ref)
    for m in range(members):
        grad = (grads[m] - pulls[m] * (1.0 / pairs)) * cell
        hold_ref[0:variables, m * points : (m + 1) * points] = grad
    pred = hold_ref[...].astype(bf16)
    pred_ref[...] = pred
    for m in range(members):
        rows = slice(m * points, (m + 1) * points)
        part = pred[:variables, rows]
        for begin in range(0, width, tile):
            columns = slice(begin, begin + tile)
            grad = mm(part, project_ref[:, columns], 0, 0)
            inner_ref[rows, columns] = (grad * slope_ref[rows, columns]).astype(bf16)
    weight_parts(normed_t_ref, active_t_ref, inner_ref, pred, loss, variables, 1, 0, far_ref)
    weight_parts(normed_t_ref, active_t_ref, inner_ref, pred, loss, variables, 1, 1, near_ref)


def weight_parts(normed_t_ref, active_t_ref, inner_ref, pred, loss, variables, side, half, out_ref):
    width = inner_ref.shape[1]
    depth = normed_t_ref.shape[-1]
    normed = normed_t_ref[side, half].reshape(-1, depth)
    for begin in range(0, width, tile):
        columns = slice(begin, begin + tile)
        out_ref[:, columns] = mm(normed, inner_ref[:, columns], 1, 0).astype(out_ref.dtype)
    part = mm(active_t_ref[side, half].reshape(-1, depth), pred, 1, 1)
    part = jnp.where(lax.broadcasted_iota(jnp.int32, part.shape, 1) == variables, loss, part)
    out_ref[:, width:] = split_loss(part, variables).astype(out_ref.dtype)


def pack(out_ref, begin, part):
    pad = part.shape[1]
    for i in range(part.shape[0] // packed):
        out_ref[begin : begin + packed, i * pad : (i + 1) * pad] = part[i * packed : (i + 1) * packed]


def unpack(in_ref, begin, count, pad):
    parts = [in_ref[begin : begin + packed, i * pad : (i + 1) * pad] for i in range(count // packed)]
    return jnp.concatenate(parts, axis=0).astype(f32)


def local_kernel(variables, loss_ref, normed_t_ref, active_t_ref, inner_ref, pred_ref, far_ref, near_ref):
    for half, out_ref in ((0, far_ref), (1, near_ref)):
        weight_parts(
            normed_t_ref, active_t_ref, inner_ref, pred_ref[...], loss_ref[0], variables, 0, half, out_ref
        )


def pair_sum(variables, width, held_ref, other_ref, begin, count):
    rows = slice(begin, begin + count)
    total = held_ref[rows, :width] + other_ref[rows, :width].astype(f32)
    part = held_ref[rows, width:] + other_ref[rows, width:].astype(f32)
    return total, split_loss(part, variables)


def first_kernel(variables, width, held_ref, other_ref, out_ref):
    total, part = pair_sum(variables, width, held_ref, other_ref, 0, out_ref.shape[0])
    out_ref[:, :width] = total.astype(bf16)
    out_ref[:, width:] = part.astype(bf16)


def message_kernel(
    variables, early, levels, keep_ref, give_ref, slots_ref, other_ref, held_ref, far_other_ref,
    first_ref, middle_ref, last_ref, near_ref,
):
    depth, width = keep_ref.shape[-1], near_ref.shape[1]
    block = near_ref.shape[0] // levels
    count, rest = early * block, (levels - 1 - early) * block
    for begin, size, out_ref in ((count, rest, middle_ref), (count + rest, block, last_ref)):
        total, part = pair_sum(variables, width, held_ref, far_other_ref, begin, size)
        out_ref[0:size, :] = total.astype(bf16)
        out_ref[size : size + packed, :] = jnp.zeros((packed, width), bf16)
        pack(out_ref, size, part.astype(bf16))
    for half in range(2):
        own = keep_ref[half].reshape(-1, depth)
        other = give_ref[half].reshape(-1, depth)
        for begin in range(0, width, tile):
            columns = slice(begin, begin + tile)
            here = slots_ref[:, :, columns].reshape(depth, tile)
            there = other_ref[:, :, columns].reshape(depth, tile)
            total = mm(own, here, 1, 0) + mm(other, there, 1, 0)
            if half == 0:
                total = total.astype(bf16)
                first_ref[:, columns] = total[:count]
                middle_ref[rest + packed :, columns] = total[count : count + rest]
                last_ref[block + packed :, columns] = total[count + rest :]
            else:
                near_ref[:, columns] = total


def ride_kernel(last_ref, slots_ref, *rest):
    arrived_refs, out_ref = rest[:-1], rest[-1]
    rows = slots_ref.shape[1]
    level, line, _ = place()
    begin = last_ref.shape[0]
    out_ref[0:begin, :] = last_ref[...]
    for i, arrived_ref in enumerate(arrived_refs):
        out_ref[begin + i * rows : begin + (i + 1) * rows, :] = arrived_ref[rows:, :]
    out_ref[begin + len(arrived_refs) * rows :, :] = slots_ref[level * 2 + 1 - line]


def hidden_early_kernel(variables, width, held_ref, other_ref, arrived_ref, *out_refs):
    block = out_refs[0].shape[0]
    for i, out_ref in enumerate(out_refs):
        total, part = pair_sum(variables, width, held_ref, other_ref, i * block, block)
        here = slice(i * block, (i + 1) * block)
        out_ref[:, :width] = (total + arrived_ref[here, :width].astype(f32)).astype(bf16)
        part = split_loss(part + arrived_ref[here, width:].astype(f32), variables)
        out_ref[:, width:] = part.astype(bf16)


def message_early_kernel(near_ref, arrived_ref, *out_refs):
    block = out_refs[0].shape[0]
    for i, out_ref in enumerate(out_refs):
        here = slice(i * block, (i + 1) * block)
        out_ref[...] = (near_ref[here, :] + arrived_ref[here, :].astype(f32)).astype(bf16)


def late_kernel(variables, early, held_ref, other_ref, near_ref, arrived_ref, *out_refs):
    width = near_ref.shape[1]
    block = (out_refs[0].shape[0] - packed) // 2
    count = block * len(out_refs)
    parts = unpack(arrived_ref, count, count, held_ref.shape[1] - width)
    for i, out_ref in enumerate(out_refs):
        begin = (early + i) * block
        total, part = pair_sum(variables, width, held_ref, other_ref, begin, block)
        here = slice(i * block, (i + 1) * block)
        out_ref[0:block, :] = (total + arrived_ref[here, :].astype(f32)).astype(bf16)
        there = slice(count + packed + i * block, count + packed + (i + 1) * block)
        total = near_ref[begin : begin + block, :] + arrived_ref[there, :].astype(f32)
        out_ref[block : 2 * block, :] = total.astype(bf16)
        out_ref[2 * block :, :] = jnp.zeros((packed, width), bf16)
        pack(out_ref, 2 * block, split_loss(part + parts[here], variables).astype(bf16))


def back_kernel(inner_ref, w_hidden_ref, gain_ref, unit_ref, inverse_ref, grad_ref, scaled_ref):
    rows_all, width = inner_ref.shape
    gain = gain_ref[...].reshape(1, width)
    for begin_row in range(0, rows_all, tile):
        rows = slice(begin_row, begin_row + tile)
        dots = jnp.zeros((tile, 1), f32)
        for begin in range(0, width, tile):
            columns = slice(begin, begin + tile)
            scaled = mm(inner_ref[rows, :], w_hidden_ref[columns, :], 1, 1) * gain[:, columns]
            dots = dots + jnp.sum(scaled * unit_ref[rows, columns], axis=-1, keepdims=True)
            scaled_ref[rows, columns] = scaled
        dots = dots * (1.0 / width)
        inverse = inverse_ref[rows, :]
        for begin in range(0, width, tile):
            columns = slice(begin, begin + tile)
            grad_ref[rows, columns] = (
                (scaled_ref[rows, columns] - unit_ref[rows, columns] * dots) * inverse
            ).astype(bf16)


def slot_kernel(share_ref, grad_ref, slots_ref, *send_refs):
    peers, each, width = slots_ref.shape
    rows = peers * each
    for begin in range(0, width, tile):
        columns = slice(begin, begin + tile)
        both = mm(share_ref[...], grad_ref[:, columns], 1, 0)
        slots_ref[:, :, columns] = (both[:rows] + both[rows:]).astype(bf16).reshape(peers, each, tile)
    level, line, _ = place()
    levels = peers // 2
    for i, send_ref in enumerate(send_refs):
        spot = (level ^ (levels - 1 - i)) * 2 + line
        send_ref[0:each, :] = slots_ref[spot]
        send_ref[each:, :] = slots_ref[spot ^ 1]


def owner_kernel(pick_ref, w_msg_ref, slots_ref, last_ref, *rest):
    arrived_refs, (grad_ref, token_ref, held_ref) = rest[:-3], rest[-3:]
    token_ref[...] = jnp.zeros_like(token_ref)
    peers, rows, width = slots_ref.shape
    level, line, _ = place()
    levels = peers // 2
    begin = last_ref.shape[0] - levels * rows
    for i in range(levels):
        spot = (level ^ (levels - 1 - i)) * 2 + line
        held_ref[spot] = slots_ref[spot] if i == levels - 1 else arrived_refs[i][0:rows, :]
        held_ref[spot ^ 1] = last_ref[begin + i * rows : begin + (i + 1) * rows, :]
    nodes = mm(pick_ref[...], held_ref[...].reshape(peers * rows, width), 0, 0).astype(bf16)
    grad_ref[...] = mm(nodes, w_msg_ref[...], 1, 1).astype(bf16).reshape(grad_ref.shape)


def hidden_sum_kernel(variables, scale, early, held_ref, other_ref, last_ref, *rest):
    hidden_ref, out_ref, loss_ref, token_ref = rest[-4:]
    token_ref[...] = jnp.zeros_like(token_ref)
    block, width = hidden_ref.shape
    pad = held_ref.shape[1] - width
    total, part = pair_sum(variables, width, held_ref, other_ref, held_ref.shape[0] - block, block)
    total = total + last_ref[0:block, :].astype(f32)
    part = part + unpack(last_ref, block, block, pad)
    for i, r in enumerate(rest[:-4]):
        total = total + r[0:block, :width].astype(f32)
        if i < early:
            part = part + r[:, width:].astype(f32)
        else:
            part = part + unpack(r, 2 * block, block, pad)
    hidden_ref[...] = total
    out_ref[...] = part[:, :variables]
    column = lax.broadcasted_iota(jnp.int32, (8, pad), 1)
    spots = (column == variables) | (column == variables + 1)
    first = lax.broadcasted_iota(jnp.int32, (8, pad), 0) == 0
    loss_ref[0] = jnp.sum(jnp.where(spots & first, part[:8], 0.0)) * scale


def message_sum_kernel(early, near_ref, last_ref, *rest):
    out_ref = rest[-1]
    block = out_ref.shape[0]
    total = near_ref[near_ref.shape[0] - block :, :]
    total = total + last_ref[block + packed : 2 * block + packed, :].astype(f32)
    for i, r in enumerate(rest[:-1]):
        begin = 0 if i < early else block
        total = total + r[begin : begin + block, :].astype(f32)
    out_ref[...] = total


def on_device(
    latents, grid_embed, norm_gain, w_msg, w_hidden, variable_projection, present_condition, verifying_field,
    cell_surface, send_rows, edge_slot, edge_dst, edge_weight,
):
    members, nodes, width = latents.shape
    points = grid_embed.shape[0]
    variables = variable_projection.shape[1]
    peers = lax.axis_size("space")
    cores = lax.axis_size("member")
    cap = send_rows.shape[2]
    rows_peer = members * cap
    rows_slot = peers * rows_peer
    rows_all = members * points
    levels = peers // 2
    block = width // (peers * cores)
    half = levels * block
    wide = width + -(-(variables + 2) // lanes) * lanes
    project = variable_projection.T

    exchange = functools.partial(
        lax.all_to_all, axis_name="space", split_axis=0, concat_axis=0, tiled=True
    )
    send, pick = call(
        select_kernel,
        [((peers, rows_peer, width), bf16), ((rows_slot, members * nodes), bf16)],
        [send_rows, latents],
        scratch=[
            pltpu.SMEM(send_rows.shape, jnp.int32),
            pltpu.VMEM(latents.shape, bf16),
            pltpu.SemaphoreType.DMA((2,)),
        ],
        limit=4,
        places=(0, 1),
    )
    received = exchange(send).reshape(rows_slot, width)
    present = present_condition.transpose(1, 0, 2)
    fixed = [w_msg]
    direct = [grid_embed, w_hidden, project, present]
    edges = [edge_slot, edge_dst, edge_weight]
    share, *staged = call(
        functools.partial(stage_kernel, cap, members, len(fixed)),
        [((2 * rows_slot, rows_all), bf16)] + [(x.shape, x.dtype) for x in fixed],
        edges + fixed,
        scratch=[pltpu.VMEM(x.shape, x.dtype) for x in edges]
        + [pltpu.SemaphoreType.DMA((3 + len(fixed),))],
        limit=16,
        places=tuple(range(3 + len(fixed))),
        after=[pick],
    )
    (w_msg_near,) = staged
    field, sent, normed, active, slope, unit, inverse = call(
        forward_kernel,
        [
            ((members, variables, points), f32),
            ((members, variables, points), bf16),
            ((rows_all, width), bf16),
            ((rows_all, width), bf16),
            ((rows_all, width), f32),
            ((rows_all, width), f32),
            ((rows_all, 1), f32),
        ],
        [received, w_msg_near, share, norm_gain] + direct,
        scratch=[pltpu.VMEM(x.shape, x.dtype) for x in direct] + [pltpu.SemaphoreType.DMA((len(direct),))],
        limit=22,
        places=(4, 5, 6, 7),
    )
    other = swap(sent, "member", cores, 1)
    normed_t, active_t, received_keep, received_give = call(
        turn_kernel,
        [((cores, 2, levels, block, rows_all), bf16)] * 2 + [((2, levels, block, rows_slot), bf16)] * 2,
        [normed, active, received],
        limit=8,
    )
    received_other = swap(received_give, "member", cores, 1)
    grad_inner, pred, loss_part, far, near = call(
        score_kernel,
        [
            ((rows_all, width), bf16),
            ((lanes, rows_all), bf16),
            ((1,), f32),
            ((half, wide), bf16),
            ((half, wide), bf16),
        ],
        [field, other, verifying_field, cell_surface, project, slope, normed_t, active_t],
        scratch=[pltpu.VMEM((lanes, rows_all), f32)],
        limit=16,
        scalar_outs=(2,),
    )
    far_other = swap(far, "member", cores, 1)
    near_other = swap(near, "member", cores, 1)
    held_far, held_near = call(
        functools.partial(local_kernel, variables),
        [((half, wide), f32)] * 2,
        [loss_part, normed_t, active_t, grad_inner, pred],
        limit=12,
        scalars=(0,),
    )
    early = levels // 2
    count, rest = early * block, (levels - 1 - early) * block
    steps = [2 * (levels - 1 - i) for i in range(levels - 1)]

    def spread(values, part):
        return [swap(x, "space", peers, k) for x, k in zip(values, part, strict=True)]

    (first,) = call(
        functools.partial(first_kernel, variables, width),
        [((count, wide), bf16)],
        [held_far, far_other],
        limit=6,
    )
    first_other = swap(first, "space", peers, 1)
    (grad_hidden,) = call(
        back_kernel,
        [((rows_all, width), bf16)],
        [grad_inner, w_hidden, norm_gain, unit, inverse],
        scratch=[pltpu.VMEM((rows_all, width), f32)],
        limit=14,
        after=[first],
    )
    slots, *slots_sent = call(
        slot_kernel,
        [((peers, rows_peer, width), bf16)] + [((2 * rows_peer, width), bf16)] * (levels - 1),
        [share, grad_hidden],
        limit=6,
    )
    slots_other = swap(slots, "member", cores, 1)
    slots_arrived = spread(slots_sent, steps)
    message_first, middle, last, message_near = call(
        functools.partial(message_kernel, variables, early, levels),
        [
            ((count, width), bf16),
            ((2 * rest + packed, width), bf16),
            ((2 * block + packed, width), bf16),
            ((half, width), f32),
        ],
        [received_keep, received_other, slots, slots_other, held_far, far_other],
        limit=10,
    )
    message_first_other = swap(message_first, "space", peers, 1)
    middle_other = swap(middle, "space", peers, 1)
    (last,) = call(
        ride_kernel,
        [((2 * block + packed + levels * rows_peer, width), bf16)],
        [last, slots] + slots_arrived,
        limit=4,
    )
    last_other = swap(last, "space", peers, 1)
    hidden_early = call(
        functools.partial(hidden_early_kernel, variables, width),
        [((block, wide), bf16)] * early,
        [held_near, near_other, first_other],
        limit=6,
    )
    hidden_parts = spread(hidden_early, steps[:early])
    message_early = call(
        message_early_kernel,
        [((block, width), bf16)] * early,
        [message_near, message_first_other],
        limit=6,
    )
    message_parts = spread(message_early, steps[:early])
    late = call(
        functools.partial(late_kernel, variables, early),
        [((2 * block + packed, width), bf16)] * (levels - 1 - early),
        [held_near, near_other, message_near, middle_other],
        limit=6,
    )
    late_parts = spread(late, steps[early:])
    token = ((8, lanes), f32)
    latent_grad, latent_done = call(
        owner_kernel,
        [(latents.shape, bf16), token],
        [pick, w_msg, slots, last_other] + slots_arrived,
        scratch=[pltpu.VMEM((peers, rows_peer, width), bf16)],
        limit=8,
    )
    hidden_weight_grad, out_weight_grad, loss, hidden_done = call(
        functools.partial(hidden_sum_kernel, variables, 1.0 / (points * peers * variables), early),
        [((block, width), f32), ((block, variables), f32), ((1,), f32), token],
        [held_near, near_other, last_other] + hidden_parts + late_parts,
        limit=8,
        scalar_outs=(2,),
        after=[latent_done],
    )
    (msg_weight_grad,) = call(
        functools.partial(message_sum_kernel, early),
        [((block, width), f32)],
        [message_near, last_other] + message_parts + late_parts,
        limit=6,
        after=[hidden_done],
    )
    return (latent_grad, loss, msg_weight_grad, hidden_weight_grad, out_weight_grad)


def solution(mesh):
    placed = (
        P(("groups", "member"), "space", None),
        P(("groups", "space"), None),
        P(),
        P(),
        P(),
        P(),
        P(("groups", "member"), None, "space"),
        P(None, ("groups", "space")),
        P(("groups", "space")),
        P("space", None, None),
        P("space"),
        P("space"),
        P("space"),
    )
    return jax.shard_map(
        on_device,
        mesh=mesh,
        in_specs=placed,
        out_specs=(
            P(("groups", "member"), "space", None),
            P("groups"),
            P(("groups", "space", "member"), None),
            P(("groups", "space", "member"), None),
            P(("groups", "space", "member"), None),
        ),
        check_vma=False,
    )
```

```python
import functools

import jax
import jax.numpy as jnp
from jax import lax
from jax.experimental import pallas as pl
from jax.experimental.pallas import tpu as pltpu
from jax.sharding import PartitionSpec as P

smoothing = 0.1
epsilon = 1e-06
tile = 256
lanes = 128
packed = 16
cost_hints = {
    "back_kernel": 8,
    "slot_kernel": 4,
    "hidden_early_kernel": 4,
    "message_early_kernel": 4,
    "late_kernel": 4,
    "message_sum_kernel": 8,
}
f32 = jnp.float32
bf16 = jnp.bfloat16


def mm(left, right, left_dim, right_dim):
    return lax.dot_general(
        left, right, (((left_dim,), (right_dim,)), ((), ())), preferred_element_type=f32
    )


def call(body, outs, args, scratch=(), limit=16, scalars=(), scalar_outs=(), places=(), after=()):
    whole = pl.BlockSpec(memory_space=pltpu.VMEM)
    small = pl.BlockSpec(memory_space=pltpu.SMEM)
    far_place = pl.BlockSpec(memory_space=pltpu.HBM)
    any_place = pl.BlockSpec(memory_space=pl.ANY)
    count = len(after)
    cost = cost_hints.get(getattr(body, "func", body).__name__, 0) * 10**9
    args = [pltpu.with_memory_space_constraint(x, pltpu.HBM) if i in places else x for i, x in enumerate(args)]

    def inner(*refs):
        body(*refs[count:])

    specs = [small if i in scalars else far_place if i in places else whole for i in range(len(args))]
    return pl.pallas_call(
        inner if count else body,
        out_shape=[jax.ShapeDtypeStruct(dims, kind) for dims, kind in outs],
        in_specs=[any_place] * count + specs,
        out_specs=[small if i in scalar_outs else whole for i in range(len(outs))],
        scratch_shapes=scratch,
        compiler_params=pltpu.CompilerParams(vmem_limit_bytes=limit * 2**20),
        cost_estimate=pl.CostEstimate(flops=cost, bytes_accessed=0, transcendentals=0),
    )(*after, *args)


def place():
    space = lax.axis_index("space")
    return lax.div(space, 2), lax.rem(space, 2), lax.axis_index("member")


def swap(value, axis, size, step):
    return lax.ppermute(value, axis, [(i, i ^ step) for i in range(size)])


def select_kernel(lists_ref, latents_ref, pick_ref, own_ref, send_ref, small_ref, table_ref, sems):
    _, peers, cap = lists_ref.shape
    members, nodes, width = latents_ref.shape
    lists = pltpu.make_async_copy(lists_ref, small_ref, sems.at[0])
    table = pltpu.make_async_copy(latents_ref, table_ref, sems.at[1])
    lists.start()
    table.start()
    lists.wait()
    me = lax.axis_index("space")
    at = lax.broadcasted_iota(jnp.int32, (cap, members * nodes), 0)
    column = lax.broadcasted_iota(jnp.int32, (cap, members * nodes), 1)
    rows = []
    for step in range(peers):
        wanted = jnp.zeros((cap, members * nodes), jnp.int32)
        for j in range(cap):
            wanted = jnp.where(at == j, small_ref[0, me ^ step, j], wanted)
        for member in range(members):
            rows.append((column == wanted + member * nodes).astype(f32))
    pick = jnp.concatenate(rows, axis=0).astype(bf16)
    pick_ref[...] = pick
    table.wait()
    sent = mm(pick, table_ref[...].reshape(members * nodes, width), 1, 0)
    sent = sent.astype(bf16).reshape(peers // 2, 2, members * cap, width)
    own_ref[...] = sent[:, 0]
    send_ref[...] = sent[:, 1]


def merge_kernel(own_ref, arrived_ref, *out_refs):
    rows = own_ref.shape[1]
    for i, out_ref in enumerate(out_refs):
        step = len(out_refs) - i
        out_ref[0:rows, :] = own_ref[step]
        out_ref[rows:, :] = arrived_ref[step]


def stage_kernel(cap, members, count, *refs):
    edge_refs, source_refs, share_ref = refs[:3], refs[3 : 3 + count], refs[3 + count]
    staged_refs, held_refs, sems = refs[4 + count : 4 + 2 * count], refs[4 + 2 * count : -1], refs[-1]
    copies = [
        pltpu.make_async_copy(source, target, sems.at[i])
        for i, (source, target) in enumerate(
            zip(edge_refs + source_refs, held_refs + staged_refs, strict=True)
        )
    ]
    for copy in copies:
        copy.start()
    for copy in copies[:3]:
        copy.wait()
    edge_part(cap, members, *held_refs, share_ref)
    for copy in copies[3:]:
        copy.wait()


def edge_part(cap, members, slot_ref, dst_ref, weight_ref, share_ref):
    edges = slot_ref.shape[0]
    slot = slot_ref[...].reshape(1, edges)
    dst = dst_ref[...].reshape(1, edges)
    weight = weight_ref[...].reshape(1, edges)
    rows = share_ref.shape[0] // 2
    points = share_ref.shape[1] // members
    sender = lax.div(slot, cap)
    spot = (sender ^ lax.axis_index("space")) * (members * cap) + (slot - sender * cap)
    hit = lax.broadcasted_iota(jnp.int32, (rows, edges), 0) == spot
    into = (lax.broadcasted_iota(jnp.int32, (points, edges), 0) == dst).astype(f32).astype(bf16)
    high = weight.astype(bf16).astype(f32)
    table = mm(jnp.where(hit, high, 0.0).astype(bf16), into, 1, 1) + mm(
        jnp.where(hit, weight - high, 0.0).astype(bf16), into, 1, 1
    )
    table = table / jnp.sum(table, axis=0, keepdims=True)
    for member in range(members):
        high = table.astype(bf16)
        columns = slice(member * points, (member + 1) * points)
        share_ref[0:rows, columns] = high
        share_ref[rows : 2 * rows, columns] = (table - high.astype(f32)).astype(bf16)
        table = jnp.concatenate([table[rows - cap :], table[: rows - cap]], axis=0)


def gathered(own_ref, near_ref, far_refs):
    return jnp.concatenate([own_ref[0], near_ref[0]] + [r[...] for r in far_refs[::-1]], axis=0)


def forward_kernel(
    far, w_msg_ref, share_ref, gain_ref, embed_ref, weights_ref, project_ref, present_ref,
    own_ref, near_ref, *rest,
):
    far_refs = rest[:far]
    field_ref, sent_ref, normed_ref, active_ref, slope_ref, unit_ref, inverse_ref = rest[far:]
    points, width = embed_ref.shape
    variables, members, _ = present_ref.shape
    messages = mm(gathered(own_ref, near_ref, far_refs), w_msg_ref[...], 1, 0).astype(bf16)
    messages = jnp.concatenate([messages, messages], axis=0)
    gain = gain_ref[...].reshape(1, width)
    for begin in range(0, members * points, lanes):
        rows = slice(begin, begin + lanes)
        source = slice(begin % points, begin % points + lanes)
        hidden = embed_ref[source, :].astype(f32) + mm(share_ref[:, rows], messages, 0, 0)
        inverse = lax.rsqrt(jnp.mean(hidden * hidden, axis=-1, keepdims=True) + epsilon)
        unit = hidden * inverse
        unit_ref[rows, :] = unit
        inverse_ref[rows, :] = inverse
        normed_ref[rows, :] = (unit * gain).astype(bf16)
    root = 0.7978845608028654
    cubic = 0.044715
    for member in range(members):
        rows = slice(member * points, (member + 1) * points)
        for begin in range(0, width, tile):
            columns = slice(begin, begin + tile)
            inner = mm(normed_ref[rows, :], weights_ref[:, columns], 1, 0)
            square = inner * inner
            bend = jnp.tanh(inner * (root + root * cubic * square))
            half = 0.5 + 0.5 * bend
            active_ref[rows, columns] = (inner * half).astype(bf16)
            slope_ref[rows, columns] = half + (0.5 * inner) * (1.0 - bend * bend) * (
                root + 3.0 * root * cubic * square
            )
        field = present_ref[:, member, :] + mm(project_ref[...], active_ref[rows, :], 1, 1)
        field_ref[member] = field
        sent_ref[member] = field.astype(bf16)


def turn_kernel(normed_ref, active_ref, own_ref, near_ref, *rest):
    far_refs, (normed_t_ref, active_t_ref, keep_ref, give_ref) = rest[:-4], rest[-4:]
    _, _, levels, block, _ = normed_t_ref.shape
    width = normed_ref.shape[1]
    level, line, core = place()
    received = gathered(own_ref, near_ref, far_refs)
    for source, target in ((received, None), (normed_ref, normed_t_ref), (active_ref, active_t_ref)):
        for begin in range(0, width, tile):
            turned = source[:, begin : begin + tile].T
            for piece in range(0, tile, block):
                index = (begin + piece) // block
                far = (index // 2 % 2) ^ line
                step = (index // 4) ^ level
                side = (index % 2) ^ core
                value = turned[piece : piece + block]
                if target is not None:
                    target[side, 1 - far, levels - 1 - step] = value
                    continue
                for which, part_ref in enumerate((keep_ref, give_ref)):
                    @pl.when(side == which)
                    def _(part_ref=part_ref):
                        part_ref[1 - far, levels - 1 - step] = value


def split_loss(part, variables):
    column = lax.broadcasted_iota(jnp.int32, part.shape, 1)
    spots = (column == variables) | (column == variables + 1)
    total = jnp.sum(jnp.where(spots, part, 0.0), axis=1, keepdims=True)
    high = total.astype(bf16).astype(f32)
    return jnp.where(column == variables, high, jnp.where(column == variables + 1, total - high, part))


def score_kernel(
    own_ref, other_ref, truth_ref, cell_ref, project_ref, slope_ref, normed_t_ref, active_t_ref,
    inner_ref, pred_ref, loss_ref, far_ref, near_ref, hold_ref,
):
    members, variables, points = own_ref.shape
    width = slope_ref.shape[1]
    total = 2 * members
    pairs = total * (total - 1)

    def eased(delta):
        square = delta * delta + smoothing * smoothing
        inverse = lax.rsqrt(square)
        return square * inverse, delta * inverse

    truth, cell = truth_ref[...], cell_ref[...].reshape(1, points)
    own = [own_ref[m] for m in range(members)]
    other = [other_ref[m].astype(f32) for m in range(members)]
    score = jnp.zeros_like(truth)
    pulls = [jnp.zeros_like(truth) for _ in own]
    grads = []
    for m in range(members):
        size, sign = eased(own[m] - truth)
        score = score + size * (1.0 / total)
        grads.append(sign * (1.0 / total))
    for m in range(members):
        for n in range(m + 1, members):
            size, sign = eased(own[m] - own[n])
            score = score - size * (1.0 / pairs)
            pulls[m] = pulls[m] + sign
            pulls[n] = pulls[n] - sign
        for n in range(members):
            size, sign = eased(own[m] - other[n])
            score = score - size * (0.5 / pairs)
            pulls[m] = pulls[m] + sign
    loss = jnp.sum(score * cell)
    loss_ref[0] = loss
    hold_ref[...] = jnp.zeros_like(hold_ref)
    for m in range(members):
        grad = (grads[m] - pulls[m] * (1.0 / pairs)) * cell
        hold_ref[0:variables, m * points : (m + 1) * points] = grad
    pred = hold_ref[...].astype(bf16)
    pred_ref[...] = pred
    for m in range(members):
        rows = slice(m * points, (m + 1) * points)
        part = pred[:variables, rows]
        for begin in range(0, width, tile):
            columns = slice(begin, begin + tile)
            grad = mm(part, project_ref[:, columns], 0, 0)
            inner_ref[rows, columns] = (grad * slope_ref[rows, columns]).astype(bf16)
    weight_parts(normed_t_ref, active_t_ref, inner_ref, pred, loss, variables, 1, 0, far_ref)
    weight_parts(normed_t_ref, active_t_ref, inner_ref, pred, loss, variables, 1, 1, near_ref)


def weight_parts(normed_t_ref, active_t_ref, inner_ref, pred, loss, variables, side, half, out_ref):
    width = inner_ref.shape[1]
    depth = normed_t_ref.shape[-1]
    normed = normed_t_ref[side, half].reshape(-1, depth)
    for begin in range(0, width, tile):
        columns = slice(begin, begin + tile)
        out_ref[:, columns] = mm(normed, inner_ref[:, columns], 1, 0).astype(out_ref.dtype)
    part = mm(active_t_ref[side, half].reshape(-1, depth), pred, 1, 1)
    part = jnp.where(lax.broadcasted_iota(jnp.int32, part.shape, 1) == variables, loss, part)
    out_ref[:, width:] = split_loss(part, variables).astype(out_ref.dtype)


def pack(out_ref, begin, part):
    pad = part.shape[1]
    for i in range(part.shape[0] // packed):
        out_ref[begin : begin + packed, i * pad : (i + 1) * pad] = part[i * packed : (i + 1) * packed]


def unpack(in_ref, begin, count, pad):
    parts = [in_ref[begin : begin + packed, i * pad : (i + 1) * pad] for i in range(count // packed)]
    return jnp.concatenate(parts, axis=0).astype(f32)


def local_kernel(variables, loss_ref, normed_t_ref, active_t_ref, inner_ref, pred_ref, far_ref, near_ref):
    for half, out_ref in ((0, far_ref), (1, near_ref)):
        weight_parts(
            normed_t_ref, active_t_ref, inner_ref, pred_ref[...], loss_ref[0], variables, 0, half, out_ref
        )


def pair_sum(variables, width, held_ref, other_ref, begin, count):
    rows = slice(begin, begin + count)
    total = held_ref[rows, :width] + other_ref[rows, :width].astype(f32)
    part = held_ref[rows, width:] + other_ref[rows, width:].astype(f32)
    return total, split_loss(part, variables)


def first_kernel(variables, width, held_ref, other_ref, out_ref):
    total, part = pair_sum(variables, width, held_ref, other_ref, 0, out_ref.shape[0])
    out_ref[:, :width] = total.astype(bf16)
    out_ref[:, width:] = part.astype(bf16)


def message_kernel(
    variables, early, levels, keep_ref, give_ref, slots_ref, other_ref, held_ref, far_other_ref,
    first_ref, middle_ref, last_ref, near_ref,
):
    depth, width = keep_ref.shape[-1], near_ref.shape[1]
    block = near_ref.shape[0] // levels
    count, rest = early * block, (levels - 1 - early) * block
    for begin, size, out_ref in ((count, rest, middle_ref), (count + rest, block, last_ref)):
        total, part = pair_sum(variables, width, held_ref, far_other_ref, begin, size)
        out_ref[0:size, :] = total.astype(bf16)
        out_ref[size : size + packed, :] = jnp.zeros((packed, width), bf16)
        pack(out_ref, size, part.astype(bf16))
    for half in range(2):
        own = keep_ref[half].reshape(-1, depth)
        other = give_ref[half].reshape(-1, depth)
        for begin in range(0, width, tile):
            columns = slice(begin, begin + tile)
            here = slots_ref[:, :, columns].reshape(depth, tile)
            there = other_ref[:, :, columns].reshape(depth, tile)
            total = mm(own, here, 1, 0) + mm(other, there, 1, 0)
            if half == 0:
                total = total.astype(bf16)
                first_ref[:, columns] = total[:count]
                middle_ref[rest + packed :, columns] = total[count : count + rest]
                last_ref[block + packed :, columns] = total[count + rest :]
            else:
                near_ref[:, columns] = total


def ride_kernel(last_ref, slots_ref, *rest):
    arrived_refs, out_ref = rest[:-1], rest[-1]
    rows = slots_ref.shape[1]
    begin = last_ref.shape[0]
    out_ref[0:begin, :] = last_ref[...]
    for i, arrived_ref in enumerate(arrived_refs):
        out_ref[begin + i * rows : begin + (i + 1) * rows, :] = arrived_ref[rows:, :]
    out_ref[begin + len(arrived_refs) * rows :, :] = slots_ref[1]


def hidden_early_kernel(variables, width, held_ref, other_ref, arrived_ref, *out_refs):
    block = out_refs[0].shape[0]
    for i, out_ref in enumerate(out_refs):
        total, part = pair_sum(variables, width, held_ref, other_ref, i * block, block)
        here = slice(i * block, (i + 1) * block)
        out_ref[:, :width] = (total + arrived_ref[here, :width].astype(f32)).astype(bf16)
        part = split_loss(part + arrived_ref[here, width:].astype(f32), variables)
        out_ref[:, width:] = part.astype(bf16)


def message_early_kernel(near_ref, arrived_ref, *out_refs):
    block = out_refs[0].shape[0]
    for i, out_ref in enumerate(out_refs):
        here = slice(i * block, (i + 1) * block)
        out_ref[...] = (near_ref[here, :] + arrived_ref[here, :].astype(f32)).astype(bf16)


def late_kernel(variables, early, held_ref, other_ref, near_ref, arrived_ref, *out_refs):
    width = near_ref.shape[1]
    block = (out_refs[0].shape[0] - packed) // 2
    count = block * len(out_refs)
    parts = unpack(arrived_ref, count, count, held_ref.shape[1] - width)
    for i, out_ref in enumerate(out_refs):
        begin = (early + i) * block
        total, part = pair_sum(variables, width, held_ref, other_ref, begin, block)
        here = slice(i * block, (i + 1) * block)
        out_ref[0:block, :] = (total + arrived_ref[here, :].astype(f32)).astype(bf16)
        there = slice(count + packed + i * block, count + packed + (i + 1) * block)
        total = near_ref[begin : begin + block, :] + arrived_ref[there, :].astype(f32)
        out_ref[block : 2 * block, :] = total.astype(bf16)
        out_ref[2 * block :, :] = jnp.zeros((packed, width), bf16)
        pack(out_ref, 2 * block, split_loss(part + parts[here], variables).astype(bf16))


def back_kernel(inner_ref, w_hidden_ref, gain_ref, unit_ref, inverse_ref, grad_ref, scaled_ref):
    rows_all, width = inner_ref.shape
    gain = gain_ref[...].reshape(1, width)
    for begin_row in range(0, rows_all, tile):
        rows = slice(begin_row, begin_row + tile)
        dots = jnp.zeros((tile, 1), f32)
        for begin in range(0, width, tile):
            columns = slice(begin, begin + tile)
            scaled = mm(inner_ref[rows, :], w_hidden_ref[columns, :], 1, 1) * gain[:, columns]
            dots = dots + jnp.sum(scaled * unit_ref[rows, columns], axis=-1, keepdims=True)
            scaled_ref[rows, columns] = scaled
        dots = dots * (1.0 / width)
        inverse = inverse_ref[rows, :]
        for begin in range(0, width, tile):
            columns = slice(begin, begin + tile)
            grad_ref[rows, columns] = (
                (scaled_ref[rows, columns] - unit_ref[rows, columns] * dots) * inverse
            ).astype(bf16)


def slot_kernel(share_ref, grad_ref, slots_ref, *send_refs):
    peers, each, width = slots_ref.shape
    rows = peers * each
    for begin in range(0, width, tile):
        columns = slice(begin, begin + tile)
        both = mm(share_ref[...], grad_ref[:, columns], 1, 0)
        slots_ref[:, :, columns] = (both[:rows] + both[rows:]).astype(bf16).reshape(peers, each, tile)
    for i, send_ref in enumerate(send_refs):
        step = len(send_refs) - i
        send_ref[0:each, :] = slots_ref[2 * step]
        send_ref[each:, :] = slots_ref[2 * step + 1]


def owner_kernel(pick_ref, w_msg_ref, slots_ref, last_ref, *rest):
    arrived_refs, (grad_ref, token_ref, held_ref) = rest[:-3], rest[-3:]
    token_ref[...] = jnp.zeros_like(token_ref)
    peers, rows, width = slots_ref.shape
    levels = peers // 2
    begin = last_ref.shape[0] - levels * rows
    for i in range(levels):
        spot = 2 * (levels - 1 - i)
        held_ref[spot] = slots_ref[0] if i == levels - 1 else arrived_refs[i][0:rows, :]
        held_ref[spot + 1] = last_ref[begin + i * rows : begin + (i + 1) * rows, :]
    nodes = mm(pick_ref[...], held_ref[...].reshape(peers * rows, width), 0, 0).astype(bf16)
    grad_ref[...] = mm(nodes, w_msg_ref[...], 1, 1).astype(bf16).reshape(grad_ref.shape)


def hidden_sum_kernel(variables, scale, early, held_ref, other_ref, last_ref, *rest):
    hidden_ref, out_ref, loss_ref, token_ref = rest[-4:]
    token_ref[...] = jnp.zeros_like(token_ref)
    block, width = hidden_ref.shape
    pad = held_ref.shape[1] - width
    total, part = pair_sum(variables, width, held_ref, other_ref, held_ref.shape[0] - block, block)
    total = total + last_ref[0:block, :].astype(f32)
    part = part + unpack(last_ref, block, block, pad)
    for i, r in enumerate(rest[:-4]):
        total = total + r[0:block, :width].astype(f32)
        if i < early:
            part = part + r[:, width:].astype(f32)
        else:
            part = part + unpack(r, 2 * block, block, pad)
    hidden_ref[...] = total
    out_ref[...] = part[:, :variables]
    column = lax.broadcasted_iota(jnp.int32, (8, pad), 1)
    spots = (column == variables) | (column == variables + 1)
    first = lax.broadcasted_iota(jnp.int32, (8, pad), 0) == 0
    loss_ref[0] = jnp.sum(jnp.where(spots & first, part[:8], 0.0)) * scale


def message_sum_kernel(early, near_ref, last_ref, *rest):
    out_ref = rest[-1]
    block = out_ref.shape[0]
    total = near_ref[near_ref.shape[0] - block :, :]
    total = total + last_ref[block + packed : 2 * block + packed, :].astype(f32)
    for i, r in enumerate(rest[:-1]):
        begin = 0 if i < early else block
        total = total + r[begin : begin + block, :].astype(f32)
    out_ref[...] = total


def on_device(
    latents, grid_embed, norm_gain, w_msg, w_hidden, variable_projection, present_condition, verifying_field,
    cell_surface, send_rows, edge_slot, edge_dst, edge_weight,
):
    members, nodes, width = latents.shape
    points = grid_embed.shape[0]
    variables = variable_projection.shape[1]
    peers = lax.axis_size("space")
    cores = lax.axis_size("member")
    cap = send_rows.shape[2]
    rows_peer = members * cap
    rows_slot = peers * rows_peer
    rows_all = members * points
    levels = peers // 2
    block = width // (peers * cores)
    half = levels * block
    wide = width + -(-(variables + 2) // lanes) * lanes
    project = variable_projection.T

    early = levels // 2
    count, rest = early * block, (levels - 1 - early) * block
    steps = [2 * (levels - 1 - i) for i in range(levels - 1)]

    def spread(values, part):
        return [swap(x, "space", peers, k) for x, k in zip(values, part, strict=True)]

    pick, own_rows, send = call(
        select_kernel,
        [((rows_slot, members * nodes), bf16)] + [((levels, rows_peer, width), bf16)] * 2,
        [send_rows, latents],
        scratch=[
            pltpu.SMEM(send_rows.shape, jnp.int32),
            pltpu.VMEM(latents.shape, bf16),
            pltpu.SemaphoreType.DMA((2,)),
        ],
        limit=4,
        places=(0, 1),
    )
    near_rows = swap(send, "space", peers, 1)
    fixed = [w_msg, norm_gain, grid_embed, w_hidden, project, present_condition.transpose(1, 0, 2)]
    edges = [edge_slot, edge_dst, edge_weight]
    share, *staged = call(
        functools.partial(stage_kernel, cap, members, len(fixed)),
        [((2 * rows_slot, rows_all), bf16)] + [(x.shape, x.dtype) for x in fixed],
        edges + fixed,
        scratch=[pltpu.VMEM(x.shape, x.dtype) for x in edges]
        + [pltpu.SemaphoreType.DMA((3 + len(fixed),))],
        limit=16,
        places=tuple(range(3 + len(fixed))),
        after=[pick],
    )
    merged = call(
        merge_kernel,
        [((2 * rows_peer, width), bf16)] * (levels - 1),
        [own_rows, near_rows],
        limit=4,
        after=[share],
    )
    received = [own_rows, near_rows] + spread(merged, steps)
    w_msg_near, gain, embed, w_hidden_near, project_near, present = staged
    field, sent, normed, active, slope, unit, inverse = call(
        functools.partial(forward_kernel, levels - 1),
        [
            ((members, variables, points), f32),
            ((members, variables, points), bf16),
            ((rows_all, width), bf16),
            ((rows_all, width), bf16),
            ((rows_all, width), f32),
            ((rows_all, width), f32),
            ((rows_all, 1), f32),
        ],
        [w_msg_near, share, gain, embed, w_hidden_near, project_near, present] + received,
        limit=20,
    )
    other = swap(sent, "member", cores, 1)
    normed_t, active_t, received_keep, received_give = call(
        turn_kernel,
        [((cores, 2, levels, block, rows_all), bf16)] * 2 + [((2, levels, block, rows_slot), bf16)] * 2,
        [normed, active] + received,
        limit=8,
    )
    received_other = swap(received_give, "member", cores, 1)
    grad_inner, pred, loss_part, far, near = call(
        score_kernel,
        [
            ((rows_all, width), bf16),
            ((lanes, rows_all), bf16),
            ((1,), f32),
            ((half, wide), bf16),
            ((half, wide), bf16),
        ],
        [field, other, verifying_field, cell_surface, project_near, slope, normed_t, active_t],
        scratch=[pltpu.VMEM((lanes, rows_all), f32)],
        limit=16,
        scalar_outs=(2,),
    )
    far_other = swap(far, "member", cores, 1)
    near_other = swap(near, "member", cores, 1)
    held_far, held_near = call(
        functools.partial(local_kernel, variables),
        [((half, wide), f32)] * 2,
        [loss_part, normed_t, active_t, grad_inner, pred],
        limit=12,
        scalars=(0,),
    )
    (first,) = call(
        functools.partial(first_kernel, variables, width),
        [((count, wide), bf16)],
        [held_far, far_other],
        limit=6,
    )
    first_other = swap(first, "space", peers, 1)
    (grad_hidden,) = call(
        back_kernel,
        [((rows_all, width), bf16)],
        [grad_inner, w_hidden_near, gain, unit, inverse],
        scratch=[pltpu.VMEM((rows_all, width), f32)],
        limit=14,
        after=[first],
    )
    slots, *slots_sent = call(
        slot_kernel,
        [((peers, rows_peer, width), bf16)] + [((2 * rows_peer, width), bf16)] * (levels - 1),
        [share, grad_hidden],
        limit=6,
        after=[near_other, received_other],
    )
    slots_other = swap(slots, "member", cores, 1)
    slots_arrived = spread(slots_sent, steps)
    message_first, middle, last, message_near = call(
        functools.partial(message_kernel, variables, early, levels),
        [
            ((count, width), bf16),
            ((2 * rest + packed, width), bf16),
            ((2 * block + packed, width), bf16),
            ((half, width), f32),
        ],
        [received_keep, received_other, slots, slots_other, held_far, far_other],
        limit=10,
    )
    message_first_other = swap(message_first, "space", peers, 1)
    middle_other = swap(middle, "space", peers, 1)
    (last,) = call(
        ride_kernel,
        [((2 * block + packed + levels * rows_peer, width), bf16)],
        [last, slots] + slots_arrived,
        limit=4,
    )
    last_other = swap(last, "space", peers, 1)
    hidden_early = call(
        functools.partial(hidden_early_kernel, variables, width),
        [((block, wide), bf16)] * early,
        [held_near, near_other, first_other],
        limit=6,
    )
    hidden_parts = spread(hidden_early, steps[:early])
    message_early = call(
        message_early_kernel,
        [((block, width), bf16)] * early,
        [message_near, message_first_other],
        limit=6,
    )
    message_parts = spread(message_early, steps[:early])
    late = call(
        functools.partial(late_kernel, variables, early),
        [((2 * block + packed, width), bf16)] * (levels - 1 - early),
        [held_near, near_other, message_near, middle_other],
        limit=6,
    )
    late_parts = spread(late, steps[early:])
    token = ((8, lanes), f32)
    latent_grad, latent_done = call(
        owner_kernel,
        [(latents.shape, bf16), token],
        [pick, w_msg, slots, last_other] + slots_arrived,
        scratch=[pltpu.VMEM((peers, rows_peer, width), bf16)],
        limit=8,
    )
    hidden_weight_grad, out_weight_grad, loss, hidden_done = call(
        functools.partial(hidden_sum_kernel, variables, 1.0 / (points * peers * variables), early),
        [((block, width), f32), ((block, variables), f32), ((1,), f32), token],
        [held_near, near_other, last_other] + hidden_parts + late_parts,
        limit=8,
        scalar_outs=(2,),
        after=[latent_done],
    )
    (msg_weight_grad,) = call(
        functools.partial(message_sum_kernel, early),
        [((block, width), f32)],
        [message_near, last_other] + message_parts + late_parts,
        limit=6,
        after=[hidden_done],
    )
    return (latent_grad, loss, msg_weight_grad, hidden_weight_grad, out_weight_grad)


def solution(mesh):
    placed = (
        P(("groups", "member"), "space", None),
        P(("groups", "space"), None),
        P(),
        P(),
        P(),
        P(),
        P(("groups", "member"), None, "space"),
        P(None, ("groups", "space")),
        P(("groups", "space")),
        P("space", None, None),
        P("space"),
        P("space"),
        P("space"),
    )
    return jax.shard_map(
        on_device,
        mesh=mesh,
        in_specs=placed,
        out_specs=(
            P(("groups", "member"), "space", None),
            P("groups"),
            P(("groups", "space", "member"), None),
            P(("groups", "space", "member"), None),
            P(("groups", "space", "member"), None),
        ),
        check_vma=False,
    )
```

```python
import functools

import jax
import jax.numpy as jnp
from jax import lax
from jax.experimental import pallas as pl
from jax.experimental.pallas import tpu as pltpu
from jax.sharding import PartitionSpec as P

smoothing = 0.1
epsilon = 1e-06
tile = 256
lanes = 128
packed = 16
cost_hints = {
    "partial_kernel": 4,
    "hidden_early_kernel": 3,
    "local_kernel": 8,
    "message_sum_kernel": 5,
    "slot_kernel": 5,
    "message_early_kernel": 5,
}
f32 = jnp.float32
bf16 = jnp.bfloat16


def mm(left, right, left_dim, right_dim):
    return lax.dot_general(
        left, right, (((left_dim,), (right_dim,)), ((), ())), preferred_element_type=f32
    )


def call(body, outs, args, scratch=(), limit=16, scalars=(), scalar_outs=(), places=(), after=()):
    whole = pl.BlockSpec(memory_space=pltpu.VMEM)
    small = pl.BlockSpec(memory_space=pltpu.SMEM)
    far_place = pl.BlockSpec(memory_space=pltpu.HBM)
    any_place = pl.BlockSpec(memory_space=pl.ANY)
    count = len(after)
    cost = cost_hints.get(getattr(body, "func", body).__name__, 0) * 10**9
    args = [pltpu.with_memory_space_constraint(x, pltpu.HBM) if i in places else x for i, x in enumerate(args)]

    def inner(*refs):
        body(*refs[count:])

    specs = [small if i in scalars else far_place if i in places else whole for i in range(len(args))]
    return pl.pallas_call(
        inner if count else body,
        out_shape=[jax.ShapeDtypeStruct(dims, kind) for dims, kind in outs],
        in_specs=[any_place] * count + specs,
        out_specs=[small if i in scalar_outs else whole for i in range(len(outs))],
        scratch_shapes=scratch,
        compiler_params=pltpu.CompilerParams(vmem_limit_bytes=limit * 2**20),
        cost_estimate=pl.CostEstimate(flops=cost, bytes_accessed=0, transcendentals=0),
    )(*after, *args)


def place():
    space = lax.axis_index("space")
    return lax.div(space, 2), lax.rem(space, 2), lax.axis_index("member")


def swap(value, axis, size, step):
    return lax.ppermute(value, axis, [(i, i ^ step) for i in range(size)])


def select_kernel(lists_ref, latents_ref, pick_ref, own_ref, send_ref, small_ref, table_ref, sems):
    _, peers, cap = lists_ref.shape
    members, nodes, width = latents_ref.shape
    lists = pltpu.make_async_copy(lists_ref, small_ref, sems.at[0])
    table = pltpu.make_async_copy(latents_ref, table_ref, sems.at[1])
    lists.start()
    table.start()
    lists.wait()
    me = lax.axis_index("space")
    at = lax.broadcasted_iota(jnp.int32, (cap, members * nodes), 0)
    column = lax.broadcasted_iota(jnp.int32, (cap, members * nodes), 1)
    rows = []
    for step in range(peers):
        wanted = jnp.zeros((cap, members * nodes), jnp.int32)
        for j in range(cap):
            wanted = jnp.where(at == j, small_ref[0, me ^ step, j], wanted)
        for member in range(members):
            rows.append((column == wanted + member * nodes).astype(f32))
    pick = jnp.concatenate(rows, axis=0).astype(bf16)
    pick_ref[...] = pick
    table.wait()
    sent = mm(pick, table_ref[...].reshape(members * nodes, width), 1, 0)
    sent = sent.astype(bf16).reshape(peers // 2, 2, members * cap, width)
    own_ref[...] = sent[:, 0]
    send_ref[...] = sent[:, 1]


def merge_kernel(own_ref, arrived_ref, *out_refs):
    rows = own_ref.shape[1]
    for i, out_ref in enumerate(out_refs):
        step = len(out_refs) - i
        out_ref[0:rows, :] = own_ref[step]
        out_ref[rows:, :] = arrived_ref[step]


def stage_kernel(cap, members, count, *refs):
    edge_refs, source_refs, share_ref = refs[:3], refs[3 : 3 + count], refs[3 + count]
    staged_refs, held_refs, sems = refs[4 + count : 4 + 2 * count], refs[4 + 2 * count : -1], refs[-1]
    copies = [
        pltpu.make_async_copy(source, target, sems.at[i])
        for i, (source, target) in enumerate(
            zip(edge_refs + source_refs, held_refs + staged_refs, strict=True)
        )
    ]
    for copy in copies:
        copy.start()
    for copy in copies[:3]:
        copy.wait()
    edge_part(cap, members, *held_refs, share_ref)
    for copy in copies[3:]:
        copy.wait()


def edge_part(cap, members, slot_ref, dst_ref, weight_ref, share_ref):
    edges = slot_ref.shape[0]
    slot = slot_ref[...].reshape(1, edges)
    dst = dst_ref[...].reshape(1, edges)
    weight = weight_ref[...].reshape(1, edges)
    rows = share_ref.shape[0] // 2
    points = share_ref.shape[1] // members
    sender = lax.div(slot, cap)
    spot = (sender ^ lax.axis_index("space")) * (members * cap) + (slot - sender * cap)
    hit = lax.broadcasted_iota(jnp.int32, (rows, edges), 0) == spot
    into = (lax.broadcasted_iota(jnp.int32, (points, edges), 0) == dst).astype(f32).astype(bf16)
    high = weight.astype(bf16).astype(f32)
    table = mm(jnp.where(hit, high, 0.0).astype(bf16), into, 1, 1) + mm(
        jnp.where(hit, weight - high, 0.0).astype(bf16), into, 1, 1
    )
    table = table / jnp.sum(table, axis=0, keepdims=True)
    for member in range(members):
        high = table.astype(bf16)
        columns = slice(member * points, (member + 1) * points)
        share_ref[0:rows, columns] = high
        share_ref[rows : 2 * rows, columns] = (table - high.astype(f32)).astype(bf16)
        table = jnp.concatenate([table[rows - cap :], table[: rows - cap]], axis=0)


def gathered(own_ref, near_ref, far_refs):
    return jnp.concatenate([own_ref[0], near_ref[0]] + [r[...] for r in far_refs[::-1]], axis=0)


def forward_kernel(
    far, w_msg_ref, share_ref, gain_ref, embed_ref, weights_ref, project_ref, present_ref,
    own_ref, near_ref, *rest,
):
    far_refs = rest[:far]
    field_ref, sent_ref, normed_ref, active_ref, slope_ref, unit_ref, inverse_ref = rest[far:]
    points, width = embed_ref.shape
    variables, members, _ = present_ref.shape
    messages = mm(gathered(own_ref, near_ref, far_refs), w_msg_ref[...], 1, 0).astype(bf16)
    messages = jnp.concatenate([messages, messages], axis=0)
    gain = gain_ref[...].reshape(1, width)
    for begin in range(0, members * points, lanes):
        rows = slice(begin, begin + lanes)
        source = slice(begin % points, begin % points + lanes)
        hidden = embed_ref[source, :].astype(f32) + mm(share_ref[:, rows], messages, 0, 0)
        inverse = lax.rsqrt(jnp.mean(hidden * hidden, axis=-1, keepdims=True) + epsilon)
        unit = hidden * inverse
        unit_ref[rows, :] = unit
        inverse_ref[rows, :] = inverse
        normed_ref[rows, :] = (unit * gain).astype(bf16)
    root = 0.7978845608028654
    cubic = 0.044715
    for member in range(members):
        rows = slice(member * points, (member + 1) * points)
        for begin in range(0, width, tile):
            columns = slice(begin, begin + tile)
            inner = mm(normed_ref[rows, :], weights_ref[:, columns], 1, 0)
            square = inner * inner
            bend = jnp.tanh(inner * (root + root * cubic * square))
            half = 0.5 + 0.5 * bend
            active_ref[rows, columns] = (inner * half).astype(bf16)
            slope_ref[rows, columns] = half + (0.5 * inner) * (1.0 - bend * bend) * (
                root + 3.0 * root * cubic * square
            )
        field = present_ref[:, member, :] + mm(project_ref[...], active_ref[rows, :], 1, 1)
        field_ref[member] = field
        sent_ref[member] = field.astype(bf16)


def turn_kernel(normed_ref, active_ref, own_ref, near_ref, *rest):
    far_refs, (normed_t_ref, active_t_ref, keep_ref, give_ref) = rest[:-4], rest[-4:]
    _, _, levels, block, _ = normed_t_ref.shape
    width = normed_ref.shape[1]
    level, line, core = place()
    received = gathered(own_ref, near_ref, far_refs)
    for source, target in ((received, None), (normed_ref, normed_t_ref), (active_ref, active_t_ref)):
        for begin in range(0, width, tile):
            turned = source[:, begin : begin + tile].T
            for piece in range(0, tile, block):
                index = (begin + piece) // block
                far = (index // 2 % 2) ^ line
                step = (index // 4) ^ level
                side = (index % 2) ^ core
                value = turned[piece : piece + block]
                if target is not None:
                    target[side, 1 - far, levels - 1 - step] = value
                    continue
                for which, part_ref in enumerate((keep_ref, give_ref)):
                    @pl.when(side == which)
                    def _(part_ref=part_ref):
                        part_ref[1 - far, levels - 1 - step] = value


def split_loss(part, variables):
    column = lax.broadcasted_iota(jnp.int32, part.shape, 1)
    spots = (column == variables) | (column == variables + 1)
    total = jnp.sum(jnp.where(spots, part, 0.0), axis=1, keepdims=True)
    high = total.astype(bf16).astype(f32)
    return jnp.where(column == variables, high, jnp.where(column == variables + 1, total - high, part))


def score_kernel(
    own_ref, other_ref, truth_ref, cell_ref, project_ref, slope_ref, normed_t_ref, active_t_ref,
    inner_ref, pred_ref, loss_ref, far_ref, near_ref, hold_ref,
):
    members, variables, points = own_ref.shape
    width = slope_ref.shape[1]
    total = 2 * members
    pairs = total * (total - 1)

    def eased(delta):
        square = delta * delta + smoothing * smoothing
        inverse = lax.rsqrt(square)
        return square * inverse, delta * inverse

    truth, cell = truth_ref[...], cell_ref[...].reshape(1, points)
    own = [own_ref[m] for m in range(members)]
    other = [other_ref[m].astype(f32) for m in range(members)]
    score = jnp.zeros_like(truth)
    pulls = [jnp.zeros_like(truth) for _ in own]
    grads = []
    for m in range(members):
        size, sign = eased(own[m] - truth)
        score = score + size * (1.0 / total)
        grads.append(sign * (1.0 / total))
    for m in range(members):
        for n in range(m + 1, members):
            size, sign = eased(own[m] - own[n])
            score = score - size * (1.0 / pairs)
            pulls[m] = pulls[m] + sign
            pulls[n] = pulls[n] - sign
        for n in range(members):
            size, sign = eased(own[m] - other[n])
            score = score - size * (0.5 / pairs)
            pulls[m] = pulls[m] + sign
    loss = jnp.sum(score * cell)
    loss_ref[0] = loss
    hold_ref[...] = jnp.zeros_like(hold_ref)
    for m in range(members):
        grad = (grads[m] - pulls[m] * (1.0 / pairs)) * cell
        hold_ref[0:variables, m * points : (m + 1) * points] = grad
    pred = hold_ref[...].astype(bf16)
    pred_ref[...] = pred
    for m in range(members):
        rows = slice(m * points, (m + 1) * points)
        part = pred[:variables, rows]
        for begin in range(0, width, tile):
            columns = slice(begin, begin + tile)
            grad = mm(part, project_ref[:, columns], 0, 0)
            inner_ref[rows, columns] = (grad * slope_ref[rows, columns]).astype(bf16)
    weight_parts(normed_t_ref, active_t_ref, inner_ref, pred, loss, variables, 1, 0, far_ref)
    weight_parts(normed_t_ref, active_t_ref, inner_ref, pred, loss, variables, 1, 1, near_ref)


def weight_parts(normed_t_ref, active_t_ref, inner_ref, pred, loss, variables, side, half, out_ref):
    width = inner_ref.shape[1]
    depth = normed_t_ref.shape[-1]
    normed = normed_t_ref[side, half].reshape(-1, depth)
    for begin in range(0, width, tile):
        columns = slice(begin, begin + tile)
        out_ref[:, columns] = mm(normed, inner_ref[:, columns], 1, 0).astype(out_ref.dtype)
    part = mm(active_t_ref[side, half].reshape(-1, depth), pred, 1, 1)
    part = jnp.where(lax.broadcasted_iota(jnp.int32, part.shape, 1) == variables, loss, part)
    out_ref[:, width:] = split_loss(part, variables).astype(out_ref.dtype)


def pack(out_ref, begin, part):
    pad = part.shape[1]
    for i in range(part.shape[0] // packed):
        out_ref[begin : begin + packed, i * pad : (i + 1) * pad] = part[i * packed : (i + 1) * packed]


def unpack(in_ref, begin, count, pad):
    parts = [in_ref[begin : begin + packed, i * pad : (i + 1) * pad] for i in range(count // packed)]
    return jnp.concatenate(parts, axis=0).astype(f32)


def local_kernel(variables, loss_ref, normed_t_ref, active_t_ref, inner_ref, pred_ref, far_ref, near_ref):
    for half, out_ref in ((0, far_ref), (1, near_ref)):
        weight_parts(
            normed_t_ref, active_t_ref, inner_ref, pred_ref[...], loss_ref[0], variables, 0, half, out_ref
        )


def pair_sum(variables, width, held_ref, other_ref, begin, count):
    rows = slice(begin, begin + count)
    total = held_ref[rows, :width] + other_ref[rows, :width].astype(f32)
    part = held_ref[rows, width:] + other_ref[rows, width:].astype(f32)
    return total, split_loss(part, variables)


def first_kernel(variables, width, held_ref, other_ref, out_ref):
    total, part = pair_sum(variables, width, held_ref, other_ref, 0, out_ref.shape[0])
    out_ref[:, :width] = total.astype(bf16)
    out_ref[:, width:] = part.astype(bf16)


def across_kernel(variables, begin, near_ref, near_other_ref, far_ref, far_other_ref, *out_refs):
    width = out_refs[0].shape[1]
    block = out_refs[0].shape[0] // 2 - packed
    for i, out_ref in enumerate(out_refs):
        for line, (held_ref, other_ref) in enumerate(((near_ref, near_other_ref), (far_ref, far_other_ref))):
            total, part = pair_sum(variables, width, held_ref, other_ref, begin + i * block, block)
            at = line * (block + packed)
            out_ref[at : at + block, :] = total.astype(bf16)
            out_ref[at + block : at + block + packed, :] = jnp.zeros((packed, width), bf16)
            pack(out_ref, at + block, part.astype(bf16))


def message_kernel(keep_ref, give_ref, slots_ref, other_ref, first_ref, own_ref, near_ref, *out_refs):
    depth, width = keep_ref.shape[-1], near_ref.shape[1]
    rows = slots_ref.shape[1]
    count, block = first_ref.shape[0], own_ref.shape[0]
    for half in range(2):
        own = keep_ref[half].reshape(-1, depth)
        other = give_ref[half].reshape(-1, depth)
        for begin in range(0, width, tile):
            columns = slice(begin, begin + tile)
            here = slots_ref[:, :, columns].reshape(depth, tile)
            there = other_ref[:, :, columns].reshape(depth, tile)
            total = mm(own, here, 1, 0) + mm(other, there, 1, 0)
            if half == 0:
                first_ref[:, columns] = total[:count].astype(bf16)
                own_ref[:, columns] = total[total.shape[0] - block :]
            else:
                near_ref[:, columns] = total
            for i, out_ref in enumerate(out_refs):
                at = (1 - half) * block
                out_ref[at : at + block, columns] = total[count + i * block : count + (i + 1) * block].astype(bf16)
    for i, out_ref in enumerate(out_refs):
        step = len(out_refs) - i
        out_ref[2 * block : 2 * block + rows, :] = slots_ref[2 * step]
        out_ref[2 * block + rows :, :] = slots_ref[2 * step + 1]


def own_kernel(variables, width, held_ref, other_ref, *rest):
    arrived_refs, out_ref = rest[:-1], rest[-1]
    block = out_ref.shape[0]
    total, part = pair_sum(variables, width, held_ref, other_ref, held_ref.shape[0] - block, block)
    for r in arrived_refs:
        at = block + packed
        total = total + r[at : at + block, :].astype(f32)
        part = part + unpack(r, at + block, block, part.shape[1])
    out_ref[:, :width] = total
    out_ref[:, width:] = split_loss(part, variables)


def last_kernel(early, hidden_ref, own_ref, slots_ref, *rest):
    arrived_refs, out_ref = rest[:-1], rest[-1]
    rows, width = slots_ref.shape[1:]
    block = own_ref.shape[0]
    out_ref[0:block, :] = hidden_ref[:, :width].astype(bf16)
    out_ref[block : block + packed, :] = jnp.zeros((packed, width), bf16)
    pack(out_ref, block, hidden_ref[:, width:].astype(bf16))
    total = own_ref[...]
    for r in arrived_refs[early:]:
        total = total + r[block : 2 * block, :].astype(f32)
    at = 2 * block + packed
    out_ref[block + packed : at, :] = total.astype(bf16)
    for i, r in enumerate(arrived_refs):
        begin = rows if i < early else 2 * block + rows
        out_ref[at : at + rows, :] = r[begin : begin + rows, :]
        at += rows
    out_ref[at:, :] = slots_ref[1]


def hidden_early_kernel(variables, width, held_ref, other_ref, arrived_ref, *out_refs):
    block = out_refs[0].shape[0]
    for i, out_ref in enumerate(out_refs):
        total, part = pair_sum(variables, width, held_ref, other_ref, i * block, block)
        here = slice(i * block, (i + 1) * block)
        out_ref[:, :width] = (total + arrived_ref[here, :width].astype(f32)).astype(bf16)
        part = split_loss(part + arrived_ref[here, width:].astype(f32), variables)
        out_ref[:, width:] = part.astype(bf16)


def message_early_kernel(near_ref, arrived_ref, *out_refs):
    block = out_refs[0].shape[0]
    for i, out_ref in enumerate(out_refs):
        here = slice(i * block, (i + 1) * block)
        out_ref[...] = (near_ref[here, :] + arrived_ref[here, :].astype(f32)).astype(bf16)


def back_kernel(inner_ref, w_hidden_ref, gain_ref, unit_ref, inverse_ref, grad_ref, scaled_ref):
    rows_all, width = inner_ref.shape
    gain = gain_ref[...].reshape(1, width)
    for begin_row in range(0, rows_all, tile):
        rows = slice(begin_row, begin_row + tile)
        dots = jnp.zeros((tile, 1), f32)
        for begin in range(0, width, tile):
            columns = slice(begin, begin + tile)
            scaled = mm(inner_ref[rows, :], w_hidden_ref[columns, :], 1, 1) * gain[:, columns]
            dots = dots + jnp.sum(scaled * unit_ref[rows, columns], axis=-1, keepdims=True)
            scaled_ref[rows, columns] = scaled
        dots = dots * (1.0 / width)
        inverse = inverse_ref[rows, :]
        for begin in range(0, width, tile):
            columns = slice(begin, begin + tile)
            grad_ref[rows, columns] = (
                (scaled_ref[rows, columns] - unit_ref[rows, columns] * dots) * inverse
            ).astype(bf16)


def slot_kernel(share_ref, grad_ref, slots_ref, *send_refs):
    peers, each, width = slots_ref.shape
    rows = peers * each
    for begin in range(0, width, tile):
        columns = slice(begin, begin + tile)
        both = mm(share_ref[...], grad_ref[:, columns], 1, 0)
        slots_ref[:, :, columns] = (both[:rows] + both[rows:]).astype(bf16).reshape(peers, each, tile)
    for i, send_ref in enumerate(send_refs):
        step = peers // 2 - 1 - i
        send_ref[0:each, :] = slots_ref[2 * step]
        send_ref[each:, :] = slots_ref[2 * step + 1]


def owner_kernel(early, block, pick_ref, w_msg_ref, slots_ref, last_ref, *rest):
    arrived_refs, (grad_ref, token_ref, held_ref) = rest[:-3], rest[-3:]
    token_ref[...] = jnp.zeros_like(token_ref)
    peers, rows, width = slots_ref.shape
    levels = peers // 2
    begin = last_ref.shape[0] - levels * rows
    for i in range(levels):
        spot = 2 * (levels - 1 - i)
        if i == levels - 1:
            held_ref[spot] = slots_ref[0]
        else:
            at = 0 if i < early else 2 * block
            held_ref[spot] = arrived_refs[i][at : at + rows, :]
        held_ref[spot + 1] = last_ref[begin + i * rows : begin + (i + 1) * rows, :]
    nodes = mm(pick_ref[...], held_ref[...].reshape(peers * rows, width), 0, 0).astype(bf16)
    grad_ref[...] = mm(nodes, w_msg_ref[...], 1, 1).astype(bf16).reshape(grad_ref.shape)


def partial_kernel(variables, width, early, held_ref, other_ref, *rest):
    arrived_refs, out_ref = rest[:-1], rest[-1]
    block = out_ref.shape[0]
    total, part = pair_sum(variables, width, held_ref, other_ref, held_ref.shape[0] - block, block)
    for i, r in enumerate(arrived_refs):
        total = total + r[0:block, :width].astype(f32)
        if i < early:
            part = part + r[:, width:].astype(f32)
        else:
            part = part + unpack(r, block, block, part.shape[1])
    out_ref[:, :width] = total
    out_ref[:, width:] = part


def hidden_sum_kernel(variables, scale, partial_ref, last_ref, hidden_ref, out_ref, loss_ref, token_ref):
    token_ref[...] = jnp.zeros_like(token_ref)
    block, width = hidden_ref.shape
    pad = partial_ref.shape[1] - width
    part = partial_ref[:, width:] + unpack(last_ref, block, block, pad)
    hidden_ref[...] = partial_ref[:, :width] + last_ref[0:block, :].astype(f32)
    out_ref[...] = part[:, :variables]
    column = lax.broadcasted_iota(jnp.int32, (8, pad), 1)
    spots = (column == variables) | (column == variables + 1)
    first = lax.broadcasted_iota(jnp.int32, (8, pad), 0) == 0
    loss_ref[0] = jnp.sum(jnp.where(spots & first, part[:8], 0.0)) * scale


def message_sum_kernel(near_ref, last_ref, *rest):
    out_ref = rest[-1]
    block = out_ref.shape[0]
    total = near_ref[near_ref.shape[0] - block :, :]
    total = total + last_ref[block + packed : 2 * block + packed, :].astype(f32)
    for r in rest[:-1]:
        total = total + r[0:block, :].astype(f32)
    out_ref[...] = total


def on_device(
    latents, grid_embed, norm_gain, w_msg, w_hidden, variable_projection, present_condition, verifying_field,
    cell_surface, send_rows, edge_slot, edge_dst, edge_weight,
):
    members, nodes, width = latents.shape
    points = grid_embed.shape[0]
    variables = variable_projection.shape[1]
    peers = lax.axis_size("space")
    cores = lax.axis_size("member")
    cap = send_rows.shape[2]
    rows_peer = members * cap
    rows_slot = peers * rows_peer
    rows_all = members * points
    levels = peers // 2
    block = width // (peers * cores)
    half = levels * block
    wide = width + -(-(variables + 2) // lanes) * lanes
    project = variable_projection.T

    early = levels // 2
    count, rest = early * block, (levels - 1 - early) * block
    steps = [2 * (levels - 1 - i) for i in range(levels - 1)]

    def spread(values, part):
        return [swap(x, "space", peers, k) for x, k in zip(values, part, strict=True)]

    pick, own_rows, send = call(
        select_kernel,
        [((rows_slot, members * nodes), bf16)] + [((levels, rows_peer, width), bf16)] * 2,
        [send_rows, latents],
        scratch=[
            pltpu.SMEM(send_rows.shape, jnp.int32),
            pltpu.VMEM(latents.shape, bf16),
            pltpu.SemaphoreType.DMA((2,)),
        ],
        limit=4,
        places=(0, 1),
    )
    near_rows = swap(send, "space", peers, 1)
    fixed = [w_msg, norm_gain, grid_embed, w_hidden, project, present_condition.transpose(1, 0, 2)]
    edges = [edge_slot, edge_dst, edge_weight]
    share, *staged = call(
        functools.partial(stage_kernel, cap, members, len(fixed)),
        [((2 * rows_slot, rows_all), bf16)] + [(x.shape, x.dtype) for x in fixed],
        edges + fixed,
        scratch=[pltpu.VMEM(x.shape, x.dtype) for x in edges]
        + [pltpu.SemaphoreType.DMA((3 + len(fixed),))],
        limit=16,
        places=tuple(range(3 + len(fixed))),
        after=[pick],
    )
    merged = call(
        merge_kernel,
        [((2 * rows_peer, width), bf16)] * (levels - 1),
        [own_rows, near_rows],
        limit=4,
        after=[share],
    )
    received = [own_rows, near_rows] + spread(merged, steps)
    w_msg_near, gain, embed, w_hidden_near, project_near, present = staged
    field, sent, normed, active, slope, unit, inverse = call(
        functools.partial(forward_kernel, levels - 1),
        [
            ((members, variables, points), f32),
            ((members, variables, points), bf16),
            ((rows_all, width), bf16),
            ((rows_all, width), bf16),
            ((rows_all, width), f32),
            ((rows_all, width), f32),
            ((rows_all, 1), f32),
        ],
        [w_msg_near, share, gain, embed, w_hidden_near, project_near, present] + received,
        limit=20,
    )
    other = swap(sent, "member", cores, 1)
    normed_t, active_t, received_keep, received_give = call(
        turn_kernel,
        [((cores, 2, levels, block, rows_all), bf16)] * 2 + [((2, levels, block, rows_slot), bf16)] * 2,
        [normed, active] + received,
        limit=8,
    )
    received_other = swap(received_give, "member", cores, 1)
    grad_inner, pred, loss_part, far, near = call(
        score_kernel,
        [
            ((rows_all, width), bf16),
            ((lanes, rows_all), bf16),
            ((1,), f32),
            ((half, wide), bf16),
            ((half, wide), bf16),
        ],
        [field, other, verifying_field, cell_surface, project_near, slope, normed_t, active_t],
        scratch=[pltpu.VMEM((lanes, rows_all), f32)],
        limit=16,
        scalar_outs=(2,),
    )
    far_other = swap(far, "member", cores, 1)
    near_other = swap(near, "member", cores, 1)
    held_far, held_near = call(
        functools.partial(local_kernel, variables),
        [((half, wide), f32)] * 2,
        [loss_part, normed_t, active_t, grad_inner, pred],
        limit=12,
        scalars=(0,),
    )
    (first,) = call(
        functools.partial(first_kernel, variables, width),
        [((count, wide), bf16)],
        [held_far, far_other],
        limit=6,
    )
    first_other = swap(first, "space", peers, 1)
    across = call(
        functools.partial(across_kernel, variables, count),
        [((2 * block + 2 * packed, width), bf16)] * (levels - 1 - early),
        [held_near, near_other, held_far, far_other],
        limit=6,
        after=[first],
    )
    across_parts = spread(across, steps[early:])
    (grad_hidden,) = call(
        back_kernel,
        [((rows_all, width), bf16)],
        [grad_inner, w_hidden_near, gain, unit, inverse],
        scratch=[pltpu.VMEM((rows_all, width), f32)],
        limit=14,
        after=[across[0]],
    )
    slots, *slots_sent = call(
        slot_kernel,
        [((peers, rows_peer, width), bf16)] + [((2 * rows_peer, width), bf16)] * early,
        [share, grad_hidden],
        limit=6,
        after=[received_other],
    )
    slots_other = swap(slots, "member", cores, 1)
    slots_arrived = spread(slots_sent, steps[:early])
    message_first, message_own, message_near, *message_across = call(
        message_kernel,
        [((count, width), bf16), ((block, width), f32), ((half, width), f32)]
        + [((2 * block + 2 * rows_peer, width), bf16)] * (levels - 1 - early),
        [received_keep, received_other, slots, slots_other],
        limit=10,
    )
    message_first_other = swap(message_first, "space", peers, 1)
    message_across_parts = spread(message_across, steps[early:])
    slots_arrived += message_across_parts
    (hidden_own,) = call(
        functools.partial(own_kernel, variables, width),
        [((block, wide), f32)],
        [held_far, far_other] + across_parts,
        limit=4,
    )
    hidden_early = call(
        functools.partial(hidden_early_kernel, variables, width),
        [((block, wide), bf16)] * early,
        [held_near, near_other, first_other],
        limit=6,
        after=[message_first, hidden_own, slots_arrived[0]],
    )
    hidden_parts = spread(hidden_early, steps[:early])
    message_early = call(
        message_early_kernel,
        [((block, width), bf16)] * early,
        [message_near, message_first_other],
        limit=6,
        after=hidden_early[:1],
    )
    message_parts = spread(message_early, steps[:early])
    (last,) = call(
        functools.partial(last_kernel, early),
        [((2 * block + packed + levels * rows_peer, width), bf16)],
        [hidden_own, message_own, slots] + slots_arrived,
        limit=4,
    )
    last_other = swap(last, "space", peers, 1)
    (partial,) = call(
        functools.partial(partial_kernel, variables, width, early),
        [((block, wide), f32)],
        [held_near, near_other] + hidden_parts + across_parts,
        limit=4,
    )
    token = ((8, lanes), f32)
    latent_grad, latent_done = call(
        functools.partial(owner_kernel, early, block),
        [(latents.shape, bf16), token],
        [pick, w_msg, slots, last_other] + slots_arrived,
        scratch=[pltpu.VMEM((peers, rows_peer, width), bf16)],
        limit=8,
        after=[partial],
    )
    hidden_weight_grad, out_weight_grad, loss, hidden_done = call(
        functools.partial(hidden_sum_kernel, variables, 1.0 / (points * peers * variables)),
        [((block, width), f32), ((block, variables), f32), ((1,), f32), token],
        [partial, last_other],
        limit=8,
        scalar_outs=(2,),
        after=[latent_done],
    )
    (msg_weight_grad,) = call(
        message_sum_kernel,
        [((block, width), f32)],
        [message_near, last_other] + message_parts + message_across_parts,
        limit=6,
        after=[hidden_done],
    )
    return (latent_grad, loss, msg_weight_grad, hidden_weight_grad, out_weight_grad)


def solution(mesh):
    placed = (
        P(("groups", "member"), "space", None),
        P(("groups", "space"), None),
        P(),
        P(),
        P(),
        P(),
        P(("groups", "member"), None, "space"),
        P(None, ("groups", "space")),
        P(("groups", "space")),
        P("space", None, None),
        P("space"),
        P("space"),
        P("space"),
    )
    return jax.shard_map(
        on_device,
        mesh=mesh,
        in_specs=placed,
        out_specs=(
            P(("groups", "member"), "space", None),
            P("groups"),
            P(("groups", "space", "member"), None),
            P(("groups", "space", "member"), None),
            P(("groups", "space", "member"), None),
        ),
        check_vma=False,
    )
```

```python
import functools

import jax
import jax.numpy as jnp
from jax import lax
from jax.experimental import pallas as pl
from jax.experimental.pallas import tpu as pltpu
from jax.sharding import PartitionSpec as P

smoothing = 0.1
epsilon = 1e-06
tile = 256
lanes = 128
packed = 16
cost_hints = {"partial_kernel": 8, "hidden_early_kernel": 6}
f32 = jnp.float32
bf16 = jnp.bfloat16


def mm(left, right, left_dim, right_dim):
    return lax.dot_general(
        left, right, (((left_dim,), (right_dim,)), ((), ())), preferred_element_type=f32
    )


def call(body, outs, args, scratch=(), limit=16, scalars=(), scalar_outs=(), places=(), after=()):
    whole = pl.BlockSpec(memory_space=pltpu.VMEM)
    small = pl.BlockSpec(memory_space=pltpu.SMEM)
    far_place = pl.BlockSpec(memory_space=pltpu.HBM)
    any_place = pl.BlockSpec(memory_space=pl.ANY)
    count = len(after)
    cost = cost_hints.get(getattr(body, "func", body).__name__, 0) * 10**9
    args = [pltpu.with_memory_space_constraint(x, pltpu.HBM) if i in places else x for i, x in enumerate(args)]

    def inner(*refs):
        body(*refs[count:])

    specs = [small if i in scalars else far_place if i in places else whole for i in range(len(args))]
    return pl.pallas_call(
        inner if count else body,
        out_shape=[jax.ShapeDtypeStruct(dims, kind) for dims, kind in outs],
        in_specs=[any_place] * count + specs,
        out_specs=[small if i in scalar_outs else whole for i in range(len(outs))],
        scratch_shapes=scratch,
        compiler_params=pltpu.CompilerParams(vmem_limit_bytes=limit * 2**20),
        cost_estimate=pl.CostEstimate(flops=cost, bytes_accessed=0, transcendentals=0),
    )(*after, *args)


def place():
    space = lax.axis_index("space")
    return lax.div(space, 2), lax.rem(space, 2), lax.axis_index("member")


def swap(value, axis, size, step):
    return lax.ppermute(value, axis, [(i, i ^ step) for i in range(size)])


def select_kernel(lists_ref, latents_ref, pick_ref, own_ref, send_ref, small_ref, table_ref, sems):
    _, peers, cap = lists_ref.shape
    members, nodes, width = latents_ref.shape
    lists = pltpu.make_async_copy(lists_ref, small_ref, sems.at[0])
    table = pltpu.make_async_copy(latents_ref, table_ref, sems.at[1])
    lists.start()
    table.start()
    lists.wait()
    me = lax.axis_index("space")
    at = lax.broadcasted_iota(jnp.int32, (cap, members * nodes), 0)
    column = lax.broadcasted_iota(jnp.int32, (cap, members * nodes), 1)
    rows = []
    for step in range(peers):
        wanted = jnp.zeros((cap, members * nodes), jnp.int32)
        for j in range(cap):
            wanted = jnp.where(at == j, small_ref[0, me ^ step, j], wanted)
        for member in range(members):
            rows.append((column == wanted + member * nodes).astype(f32))
    pick = jnp.concatenate(rows, axis=0).astype(bf16)
    pick_ref[...] = pick
    table.wait()
    sent = mm(pick, table_ref[...].reshape(members * nodes, width), 1, 0)
    sent = sent.astype(bf16).reshape(peers // 2, 2, members * cap, width)
    own_ref[...] = sent[:, 0]
    send_ref[...] = sent[:, 1]


def merge_kernel(own_ref, arrived_ref, *out_refs):
    rows = own_ref.shape[1]
    for i, out_ref in enumerate(out_refs):
        step = len(out_refs) - i
        out_ref[0:rows, :] = own_ref[step]
        out_ref[rows:, :] = arrived_ref[step]


def stage_kernel(cap, members, count, *refs):
    edge_refs, source_refs, share_ref = refs[:3], refs[3 : 3 + count], refs[3 + count]
    staged_refs, held_refs, sems = refs[4 + count : 4 + 2 * count], refs[4 + 2 * count : -1], refs[-1]
    copies = [
        pltpu.make_async_copy(source, target, sems.at[i])
        for i, (source, target) in enumerate(
            zip(edge_refs + source_refs, held_refs + staged_refs, strict=True)
        )
    ]
    for copy in copies:
        copy.start()
    for copy in copies[:3]:
        copy.wait()
    edge_part(cap, members, *held_refs, share_ref)
    for copy in copies[3:]:
        copy.wait()


def edge_part(cap, members, slot_ref, dst_ref, weight_ref, share_ref):
    edges = slot_ref.shape[0]
    slot = slot_ref[...].reshape(1, edges)
    dst = dst_ref[...].reshape(1, edges)
    weight = weight_ref[...].reshape(1, edges)
    rows = share_ref.shape[0] // 2
    points = share_ref.shape[1] // members
    sender = lax.div(slot, cap)
    spot = (sender ^ lax.axis_index("space")) * (members * cap) + (slot - sender * cap)
    hit = lax.broadcasted_iota(jnp.int32, (rows, edges), 0) == spot
    into = (lax.broadcasted_iota(jnp.int32, (points, edges), 0) == dst).astype(f32).astype(bf16)
    high = weight.astype(bf16).astype(f32)
    table = mm(jnp.where(hit, high, 0.0).astype(bf16), into, 1, 1) + mm(
        jnp.where(hit, weight - high, 0.0).astype(bf16), into, 1, 1
    )
    table = table / jnp.sum(table, axis=0, keepdims=True)
    for member in range(members):
        high = table.astype(bf16)
        columns = slice(member * points, (member + 1) * points)
        share_ref[0:rows, columns] = high
        share_ref[rows : 2 * rows, columns] = (table - high.astype(f32)).astype(bf16)
        table = jnp.concatenate([table[rows - cap :], table[: rows - cap]], axis=0)


def gathered(own_ref, near_ref, far_refs):
    return jnp.concatenate([own_ref[0], near_ref[0]] + [r[...] for r in far_refs[::-1]], axis=0)


def forward_kernel(
    far, w_msg_ref, share_ref, gain_ref, embed_ref, weights_ref, project_ref, present_ref,
    own_ref, near_ref, *rest,
):
    far_refs = rest[:far]
    field_ref, sent_ref, normed_ref, active_ref, slope_ref, unit_ref, inverse_ref = rest[far:]
    points, width = embed_ref.shape
    variables, members, _ = present_ref.shape
    messages = mm(gathered(own_ref, near_ref, far_refs), w_msg_ref[...], 1, 0).astype(bf16)
    messages = jnp.concatenate([messages, messages], axis=0)
    gain = gain_ref[...].reshape(1, width)
    for begin in range(0, members * points, lanes):
        rows = slice(begin, begin + lanes)
        source = slice(begin % points, begin % points + lanes)
        hidden = embed_ref[source, :].astype(f32) + mm(share_ref[:, rows], messages, 0, 0)
        inverse = lax.rsqrt(jnp.mean(hidden * hidden, axis=-1, keepdims=True) + epsilon)
        unit = hidden * inverse
        unit_ref[rows, :] = unit
        inverse_ref[rows, :] = inverse
        normed_ref[rows, :] = (unit * gain).astype(bf16)
    root = 0.7978845608028654
    cubic = 0.044715
    for member in range(members):
        rows = slice(member * points, (member + 1) * points)
        for begin in range(0, width, tile):
            columns = slice(begin, begin + tile)
            inner = mm(normed_ref[rows, :], weights_ref[:, columns], 1, 0)
            square = inner * inner
            bend = jnp.tanh(inner * (root + root * cubic * square))
            half = 0.5 + 0.5 * bend
            active_ref[rows, columns] = (inner * half).astype(bf16)
            slope_ref[rows, columns] = half + (0.5 * inner) * (1.0 - bend * bend) * (
                root + 3.0 * root * cubic * square
            )
        field = present_ref[:, member, :] + mm(project_ref[...], active_ref[rows, :], 1, 1)
        field_ref[member] = field
        sent_ref[member] = field.astype(bf16)


def halving_place(step, levels):
    bits = levels.bit_length() - 1
    return sum((1 - ((step >> bit) & 1)) << (bits - 1 - bit) for bit in range(bits))


def turn_kernel(normed_ref, active_ref, own_ref, near_ref, *rest):
    far_refs, (normed_t_ref, active_t_ref, keep_ref, give_ref) = rest[:-4], rest[-4:]
    _, _, levels, block, _ = normed_t_ref.shape
    width = normed_ref.shape[1]
    level, line, core = place()
    received = gathered(own_ref, near_ref, far_refs)
    for source, target in ((received, None), (normed_ref, normed_t_ref), (active_ref, active_t_ref)):
        for begin in range(0, width, tile):
            turned = source[:, begin : begin + tile].T
            for piece in range(0, tile, block):
                index = (begin + piece) // block
                far = (index // 2 % 2) ^ line
                step = (index // 4) ^ level
                side = (index % 2) ^ core
                value = turned[piece : piece + block]
                if target is not None:
                    target[side, 1 - far, levels - 1 - step] = value
                    continue
                spot = halving_place(step, levels)
                for which, part_ref in enumerate((keep_ref, give_ref)):
                    @pl.when(side == which)
                    def _(part_ref=part_ref):
                        part_ref[1 - far, spot] = value


def split_loss(part, variables):
    column = lax.broadcasted_iota(jnp.int32, part.shape, 1)
    spots = (column == variables) | (column == variables + 1)
    total = jnp.sum(jnp.where(spots, part, 0.0), axis=1, keepdims=True)
    high = total.astype(bf16).astype(f32)
    return jnp.where(column == variables, high, jnp.where(column == variables + 1, total - high, part))


def score_kernel(
    own_ref, other_ref, truth_ref, cell_ref, project_ref, slope_ref, normed_t_ref, active_t_ref,
    inner_ref, pred_ref, loss_ref, far_ref, near_ref, hold_ref,
):
    members, variables, points = own_ref.shape
    width = slope_ref.shape[1]
    total = 2 * members
    pairs = total * (total - 1)

    def eased(delta):
        square = delta * delta + smoothing * smoothing
        inverse = lax.rsqrt(square)
        return square * inverse, delta * inverse

    truth, cell = truth_ref[...], cell_ref[...].reshape(1, points)
    own = [own_ref[m] for m in range(members)]
    other = [other_ref[m].astype(f32) for m in range(members)]
    score = jnp.zeros_like(truth)
    pulls = [jnp.zeros_like(truth) for _ in own]
    grads = []
    for m in range(members):
        size, sign = eased(own[m] - truth)
        score = score + size * (1.0 / total)
        grads.append(sign * (1.0 / total))
    for m in range(members):
        for n in range(m + 1, members):
            size, sign = eased(own[m] - own[n])
            score = score - size * (1.0 / pairs)
            pulls[m] = pulls[m] + sign
            pulls[n] = pulls[n] - sign
        for n in range(members):
            size, sign = eased(own[m] - other[n])
            score = score - size * (0.5 / pairs)
            pulls[m] = pulls[m] + sign
    loss = jnp.sum(score * cell)
    loss_ref[0] = loss
    hold_ref[...] = jnp.zeros_like(hold_ref)
    for m in range(members):
        grad = (grads[m] - pulls[m] * (1.0 / pairs)) * cell
        hold_ref[0:variables, m * points : (m + 1) * points] = grad
    pred = hold_ref[...].astype(bf16)
    pred_ref[...] = pred
    for m in range(members):
        rows = slice(m * points, (m + 1) * points)
        part = pred[:variables, rows]
        for begin in range(0, width, tile):
            columns = slice(begin, begin + tile)
            grad = mm(part, project_ref[:, columns], 0, 0)
            inner_ref[rows, columns] = (grad * slope_ref[rows, columns]).astype(bf16)
    weight_parts(normed_t_ref, active_t_ref, inner_ref, pred, loss, variables, 1, 0, far_ref)
    weight_parts(normed_t_ref, active_t_ref, inner_ref, pred, loss, variables, 1, 1, near_ref)


def weight_parts(normed_t_ref, active_t_ref, inner_ref, pred, loss, variables, side, half, out_ref):
    width = inner_ref.shape[1]
    depth = normed_t_ref.shape[-1]
    normed = normed_t_ref[side, half].reshape(-1, depth)
    for begin in range(0, width, tile):
        columns = slice(begin, begin + tile)
        out_ref[:, columns] = mm(normed, inner_ref[:, columns], 1, 0).astype(out_ref.dtype)
    part = mm(active_t_ref[side, half].reshape(-1, depth), pred, 1, 1)
    part = jnp.where(lax.broadcasted_iota(jnp.int32, part.shape, 1) == variables, loss, part)
    out_ref[:, width:] = split_loss(part, variables).astype(out_ref.dtype)


def pack(out_ref, begin, part):
    pad = part.shape[1]
    for i in range(part.shape[0] // packed):
        out_ref[begin : begin + packed, i * pad : (i + 1) * pad] = part[i * packed : (i + 1) * packed]


def unpack(in_ref, begin, count, pad):
    parts = [in_ref[begin : begin + packed, i * pad : (i + 1) * pad] for i in range(count // packed)]
    return jnp.concatenate(parts, axis=0).astype(f32)


def local_kernel(variables, loss_ref, normed_t_ref, active_t_ref, inner_ref, pred_ref, far_ref, near_ref):
    for half, out_ref in ((0, far_ref), (1, near_ref)):
        weight_parts(
            normed_t_ref, active_t_ref, inner_ref, pred_ref[...], loss_ref[0], variables, 0, half, out_ref
        )


def pair_sum(variables, width, held_ref, other_ref, begin, count):
    rows = slice(begin, begin + count)
    total = held_ref[rows, :width] + other_ref[rows, :width].astype(f32)
    part = held_ref[rows, width:] + other_ref[rows, width:].astype(f32)
    return total, split_loss(part, variables)


def first_kernel(variables, width, held_ref, other_ref, out_ref):
    total, part = pair_sum(variables, width, held_ref, other_ref, 0, out_ref.shape[0])
    out_ref[:, :width] = total.astype(bf16)
    out_ref[:, width:] = part.astype(bf16)


def across_kernel(variables, begin, near_ref, near_other_ref, far_ref, far_other_ref, *out_refs):
    width = out_refs[0].shape[1]
    block = out_refs[0].shape[0] // 2 - packed
    for i, out_ref in enumerate(out_refs):
        for line, (held_ref, other_ref) in enumerate(((near_ref, near_other_ref), (far_ref, far_other_ref))):
            total, part = pair_sum(variables, width, held_ref, other_ref, begin + i * block, block)
            at = line * (block + packed)
            out_ref[at : at + block, :] = total.astype(bf16)
            out_ref[at + block : at + block + packed, :] = jnp.zeros((packed, width), bf16)
            pack(out_ref, at + block, part.astype(bf16))


def message_kernel(keep_ref, give_ref, slots_ref, other_ref, first_ref, second_ref, near_ref):
    depth, width = keep_ref.shape[-1], near_ref.shape[1]
    count = first_ref.shape[0]
    for half in range(2):
        own = keep_ref[half].reshape(-1, depth)
        other = give_ref[half].reshape(-1, depth)
        for begin in range(0, width, tile):
            columns = slice(begin, begin + tile)
            here = slots_ref[:, :, columns].reshape(depth, tile)
            there = other_ref[:, :, columns].reshape(depth, tile)
            total = mm(own, here, 1, 0) + mm(other, there, 1, 0)
            if half == 0:
                first_ref[:, columns] = total[:count].astype(bf16)
                second_ref[:, columns] = total[count:].astype(bf16)
            else:
                near_ref[:, columns] = total


def second_kernel(source_ref, out_ref):
    out_ref[...] = source_ref[...]


def step_kernel(near_ref, arrived_ref, slots_ref, out_ref):
    rows = slots_ref.shape[1]
    count = arrived_ref.shape[0]
    out_ref[0:count, :] = (near_ref[0:count, :] + arrived_ref[...].astype(f32)).astype(bf16)
    out_ref[count : count + rows, :] = slots_ref[2]
    out_ref[count + rows :, :] = slots_ref[3]


def halve_kernel(begin, near_ref, *rest):
    arrived_refs, (send_ref, keep_ref) = rest[:-2], rest[-2:]
    count = send_ref.shape[0]
    for at, out_ref in ((0, send_ref), (count, keep_ref)):
        total = near_ref[begin + at : begin + at + count, :]
        for r in arrived_refs:
            total = total + r[at : at + count, :].astype(f32)
        out_ref[...] = total.astype(out_ref.dtype)


def own_kernel(variables, width, held_ref, other_ref, *rest):
    arrived_refs, out_ref = rest[:-1], rest[-1]
    block = out_ref.shape[0]
    total, part = pair_sum(variables, width, held_ref, other_ref, held_ref.shape[0] - block, block)
    for r in arrived_refs:
        at = block + packed
        total = total + r[at : at + block, :].astype(f32)
        part = part + unpack(r, at + block, block, part.shape[1])
    out_ref[:, :width] = total
    out_ref[:, width:] = split_loss(part, variables)


def last_kernel(hidden_ref, slots_ref, *rest):
    arrived_refs, out_ref = rest[:-1], rest[-1]
    rows, width = slots_ref.shape[1:]
    block = hidden_ref.shape[0]
    out_ref[0:block, :] = hidden_ref[:, :width].astype(bf16)
    out_ref[block : block + packed, :] = jnp.zeros((packed, width), bf16)
    pack(out_ref, block, hidden_ref[:, width:].astype(bf16))
    at = block + packed
    for r in arrived_refs:
        out_ref[at : at + rows, :] = r[r.shape[0] - rows :, :]
        at += rows
    out_ref[at:, :] = slots_ref[1]


def hidden_early_kernel(variables, width, held_ref, other_ref, arrived_ref, *out_refs):
    block = out_refs[0].shape[0]
    for i, out_ref in enumerate(out_refs):
        total, part = pair_sum(variables, width, held_ref, other_ref, i * block, block)
        here = slice(i * block, (i + 1) * block)
        out_ref[:, :width] = (total + arrived_ref[here, :width].astype(f32)).astype(bf16)
        part = split_loss(part + arrived_ref[here, width:].astype(f32), variables)
        out_ref[:, width:] = part.astype(bf16)


def back_kernel(inner_ref, w_hidden_ref, gain_ref, unit_ref, inverse_ref, grad_ref, scaled_ref):
    rows_all, width = inner_ref.shape
    gain = gain_ref[...].reshape(1, width)
    for begin_row in range(0, rows_all, tile):
        rows = slice(begin_row, begin_row + tile)
        dots = jnp.zeros((tile, 1), f32)
        for begin in range(0, width, tile):
            columns = slice(begin, begin + tile)
            scaled = mm(inner_ref[rows, :], w_hidden_ref[columns, :], 1, 1) * gain[:, columns]
            dots = dots + jnp.sum(scaled * unit_ref[rows, columns], axis=-1, keepdims=True)
            scaled_ref[rows, columns] = scaled
        dots = dots * (1.0 / width)
        inverse = inverse_ref[rows, :]
        for begin in range(0, width, tile):
            columns = slice(begin, begin + tile)
            grad_ref[rows, columns] = (
                (scaled_ref[rows, columns] - unit_ref[rows, columns] * dots) * inverse
            ).astype(bf16)


def slot_kernel(share_ref, grad_ref, slots_ref, *send_refs):
    peers, each, width = slots_ref.shape
    rows = peers * each
    for begin in range(0, width, tile):
        columns = slice(begin, begin + tile)
        both = mm(share_ref[...], grad_ref[:, columns], 1, 0)
        slots_ref[:, :, columns] = (both[:rows] + both[rows:]).astype(bf16).reshape(peers, each, tile)
    for i, send_ref in enumerate(send_refs):
        step = peers // 2 - 1 - i
        send_ref[0:each, :] = slots_ref[2 * step]
        send_ref[each:, :] = slots_ref[2 * step + 1]


def owner_kernel(pick_ref, w_msg_ref, slots_ref, last_ref, *rest):
    arrived_refs, (grad_ref, token_ref, held_ref) = rest[:-3], rest[-3:]
    token_ref[...] = jnp.zeros_like(token_ref)
    peers, rows, width = slots_ref.shape
    levels = peers // 2
    begin = last_ref.shape[0] - levels * rows
    for i in range(levels):
        spot = 2 * (levels - 1 - i)
        if i == levels - 1:
            held_ref[spot] = slots_ref[0]
        else:
            at = arrived_refs[i].shape[0] - 2 * rows
            held_ref[spot] = arrived_refs[i][at : at + rows, :]
        held_ref[spot + 1] = last_ref[begin + i * rows : begin + (i + 1) * rows, :]
    nodes = mm(pick_ref[...], held_ref[...].reshape(peers * rows, width), 0, 0).astype(bf16)
    grad_ref[...] = mm(nodes, w_msg_ref[...], 1, 1).astype(bf16).reshape(grad_ref.shape)


def partial_kernel(variables, width, early, held_ref, other_ref, *rest):
    arrived_refs, out_ref = rest[:-1], rest[-1]
    block = out_ref.shape[0]
    total, part = pair_sum(variables, width, held_ref, other_ref, held_ref.shape[0] - block, block)
    for i, r in enumerate(arrived_refs):
        total = total + r[0:block, :width].astype(f32)
        if i < early:
            part = part + r[:, width:].astype(f32)
        else:
            part = part + unpack(r, block, block, part.shape[1])
    out_ref[:, :width] = total
    out_ref[:, width:] = part


def hidden_sum_kernel(variables, scale, partial_ref, last_ref, hidden_ref, out_ref, loss_ref, token_ref):
    token_ref[...] = jnp.zeros_like(token_ref)
    block, width = hidden_ref.shape
    pad = partial_ref.shape[1] - width
    part = partial_ref[:, width:] + unpack(last_ref, block, block, pad)
    hidden_ref[...] = partial_ref[:, :width] + last_ref[0:block, :].astype(f32)
    out_ref[...] = part[:, :variables]
    column = lax.broadcasted_iota(jnp.int32, (8, pad), 1)
    spots = (column == variables) | (column == variables + 1)
    first = lax.broadcasted_iota(jnp.int32, (8, pad), 0) == 0
    loss_ref[0] = jnp.sum(jnp.where(spots & first, part[:8], 0.0)) * scale


def message_sum_kernel(keep_ref, arrived_ref, out_ref):
    out_ref[...] = keep_ref[...] + arrived_ref[...].astype(f32)


def on_device(
    latents, grid_embed, norm_gain, w_msg, w_hidden, variable_projection, present_condition, verifying_field,
    cell_surface, send_rows, edge_slot, edge_dst, edge_weight,
):
    members, nodes, width = latents.shape
    points = grid_embed.shape[0]
    variables = variable_projection.shape[1]
    peers = lax.axis_size("space")
    cores = lax.axis_size("member")
    cap = send_rows.shape[2]
    rows_peer = members * cap
    rows_slot = peers * rows_peer
    rows_all = members * points
    levels = peers // 2
    block = width // (peers * cores)
    half = levels * block
    wide = width + -(-(variables + 2) // lanes) * lanes
    project = variable_projection.T

    early = levels // 2
    count, rest = early * block, (levels - 1 - early) * block
    steps = [2 * (levels - 1 - i) for i in range(levels - 1)]

    def spread(values, part):
        return [swap(x, "space", peers, k) for x, k in zip(values, part, strict=True)]

    pick, own_rows, send = call(
        select_kernel,
        [((rows_slot, members * nodes), bf16)] + [((levels, rows_peer, width), bf16)] * 2,
        [send_rows, latents],
        scratch=[
            pltpu.SMEM(send_rows.shape, jnp.int32),
            pltpu.VMEM(latents.shape, bf16),
            pltpu.SemaphoreType.DMA((2,)),
        ],
        limit=4,
        places=(0, 1),
    )
    near_rows = swap(send, "space", peers, 1)
    fixed = [w_msg, norm_gain, grid_embed, w_hidden, project, present_condition.transpose(1, 0, 2)]
    edges = [edge_slot, edge_dst, edge_weight]
    share, *staged = call(
        functools.partial(stage_kernel, cap, members, len(fixed)),
        [((2 * rows_slot, rows_all), bf16)] + [(x.shape, x.dtype) for x in fixed],
        edges + fixed,
        scratch=[pltpu.VMEM(x.shape, x.dtype) for x in edges]
        + [pltpu.SemaphoreType.DMA((3 + len(fixed),))],
        limit=16,
        places=tuple(range(3 + len(fixed))),
        after=[pick],
    )
    merged = call(
        merge_kernel,
        [((2 * rows_peer, width), bf16)] * (levels - 1),
        [own_rows, near_rows],
        limit=4,
        after=[share],
    )
    received = [own_rows, near_rows] + spread(merged, steps)
    w_msg_near, gain, embed, w_hidden_near, project_near, present = staged
    field, sent, normed, active, slope, unit, inverse = call(
        functools.partial(forward_kernel, levels - 1),
        [
            ((members, variables, points), f32),
            ((members, variables, points), bf16),
            ((rows_all, width), bf16),
            ((rows_all, width), bf16),
            ((rows_all, width), f32),
            ((rows_all, width), f32),
            ((rows_all, 1), f32),
        ],
        [w_msg_near, share, gain, embed, w_hidden_near, project_near, present] + received,
        limit=20,
    )
    other = swap(sent, "member", cores, 1)
    normed_t, active_t, received_keep, received_give = call(
        turn_kernel,
        [((cores, 2, levels, block, rows_all), bf16)] * 2 + [((2, levels, block, rows_slot), bf16)] * 2,
        [normed, active] + received,
        limit=8,
    )
    received_other = swap(received_give, "member", cores, 1)
    grad_inner, pred, loss_part, far, near = call(
        score_kernel,
        [
            ((rows_all, width), bf16),
            ((lanes, rows_all), bf16),
            ((1,), f32),
            ((half, wide), bf16),
            ((half, wide), bf16),
        ],
        [field, other, verifying_field, cell_surface, project_near, slope, normed_t, active_t],
        scratch=[pltpu.VMEM((lanes, rows_all), f32)],
        limit=16,
        scalar_outs=(2,),
    )
    far_other = swap(far, "member", cores, 1)
    near_other = swap(near, "member", cores, 1)
    held_far, held_near = call(
        functools.partial(local_kernel, variables),
        [((half, wide), f32)] * 2,
        [loss_part, normed_t, active_t, grad_inner, pred],
        limit=12,
        scalars=(0,),
    )
    (first,) = call(
        functools.partial(first_kernel, variables, width),
        [((count, wide), bf16)],
        [held_far, far_other],
        limit=6,
    )
    first_other = swap(first, "space", peers, 1)
    across = call(
        functools.partial(across_kernel, variables, count),
        [((2 * block + 2 * packed, width), bf16)] * (levels - 1 - early),
        [held_near, near_other, held_far, far_other],
        limit=6,
        after=[first],
    )
    across_parts = spread(across, steps[early:])
    (grad_hidden,) = call(
        back_kernel,
        [((rows_all, width), bf16)],
        [grad_inner, w_hidden_near, gain, unit, inverse],
        scratch=[pltpu.VMEM((rows_all, width), f32)],
        limit=14,
        after=[across[0]],
    )
    slots, *slots_sent = call(
        slot_kernel,
        [((peers, rows_peer, width), bf16)] + [((2 * rows_peer, width), bf16)] * (levels - 2),
        [share, grad_hidden],
        limit=6,
        after=[received_other],
    )
    slots_other = swap(slots, "member", cores, 1)
    slots_arrived = spread(slots_sent, steps[:-1])
    message_first, message_second, message_near = call(
        message_kernel,
        [((half // 2, width), bf16)] * 2 + [((half, width), f32)],
        [received_keep, received_other, slots, slots_other],
        limit=10,
    )
    message_first_other = swap(message_first, "space", peers, 1)
    (hidden_own,) = call(
        functools.partial(own_kernel, variables, width),
        [((block, wide), f32)],
        [held_far, far_other] + across_parts,
        limit=4,
    )
    hidden_early = call(
        functools.partial(hidden_early_kernel, variables, width),
        [((block, wide), bf16)] * early,
        [held_near, near_other, first_other],
        limit=6,
        after=[message_first, hidden_own] + slots_arrived,
    )
    hidden_parts = spread(hidden_early, steps[:early])
    (message_step,) = call(
        step_kernel,
        [((half // 2 + 2 * rows_peer, width), bf16)],
        [message_near, message_first_other, slots],
        limit=4,
        after=hidden_early[:1],
    )
    message_other = swap(message_step, "space", peers, 2)
    (message_second,) = call(
        second_kernel, [((half // 2, width), bf16)], [message_second], limit=4, after=[message_step]
    )
    message_second_other = swap(message_second, "space", peers, 1)
    slots_arrived.append(message_other)
    (partial,) = call(
        functools.partial(partial_kernel, variables, width, early),
        [((block, wide), f32)],
        [held_near, near_other] + hidden_parts + across_parts,
        limit=4,
    )
    (last,) = call(
        last_kernel,
        [((block + packed + levels * rows_peer, width), bf16)],
        [hidden_own, slots] + slots_arrived,
        limit=4,
        after=[partial],
    )
    last_other = swap(last, "space", peers, 1)
    message_send, message_keep = call(
        functools.partial(halve_kernel, half // 2),
        [((half // 4, width), bf16), ((half // 4, width), f32)],
        [message_near, message_second_other, message_other],
        limit=4,
        after=[partial],
    )
    bit = 4
    while bit < peers // 2:
        message_other = swap(message_send, "space", peers, bit)
        rows_left = message_send.shape[0] // 2
        message_send, message_keep = call(
            functools.partial(halve_kernel, 0),
            [((rows_left, width), bf16), ((rows_left, width), f32)],
            [message_keep, message_other],
            limit=4,
        )
        bit *= 2
    message_other = swap(message_send, "space", peers, bit)
    token = ((8, lanes), f32)
    latent_grad, latent_done = call(
        owner_kernel,
        [(latents.shape, bf16), token],
        [pick, w_msg, slots, last_other] + slots_arrived,
        scratch=[pltpu.VMEM((peers, rows_peer, width), bf16)],
        limit=8,
    )
    hidden_weight_grad, out_weight_grad, loss, hidden_done = call(
        functools.partial(hidden_sum_kernel, variables, 1.0 / (points * peers * variables)),
        [((block, width), f32), ((block, variables), f32), ((1,), f32), token],
        [partial, last_other],
        limit=8,
        scalar_outs=(2,),
        after=[latent_done],
    )
    (msg_weight_grad,) = call(
        message_sum_kernel,
        [((block, width), f32)],
        [message_keep, message_other],
        limit=6,
        after=[hidden_done],
    )
    return (latent_grad, loss, msg_weight_grad, hidden_weight_grad, out_weight_grad)


def solution(mesh):
    placed = (
        P(("groups", "member"), "space", None),
        P(("groups", "space"), None),
        P(),
        P(),
        P(),
        P(),
        P(("groups", "member"), None, "space"),
        P(None, ("groups", "space")),
        P(("groups", "space")),
        P("space", None, None),
        P("space"),
        P("space"),
        P("space"),
    )
    return jax.shard_map(
        on_device,
        mesh=mesh,
        in_specs=placed,
        out_specs=(
            P(("groups", "member"), "space", None),
            P("groups"),
            P(("groups", "space", "member"), None),
            P(("groups", "space", "member"), None),
            P(("groups", "space", "member"), None),
        ),
        check_vma=False,
    )
```

```python
import functools

import jax
import jax.numpy as jnp
from jax import lax
from jax.experimental import pallas as pl
from jax.experimental.pallas import tpu as pltpu
from jax.sharding import PartitionSpec as P

smoothing = 0.1
epsilon = 1e-06
tile = 256
lanes = 128
packed = 16
cost_hints = {"partial_kernel": 8, "hidden_early_kernel": 6}
f32 = jnp.float32
bf16 = jnp.bfloat16


def mm(left, right, left_dim, right_dim):
    return lax.dot_general(
        left, right, (((left_dim,), (right_dim,)), ((), ())), preferred_element_type=f32
    )


def call(body, outs, args, scratch=(), limit=16, scalars=(), scalar_outs=(), places=(), after=()):
    whole = pl.BlockSpec(memory_space=pltpu.VMEM)
    small = pl.BlockSpec(memory_space=pltpu.SMEM)
    far_place = pl.BlockSpec(memory_space=pltpu.HBM)
    any_place = pl.BlockSpec(memory_space=pl.ANY)
    count = len(after)
    cost = cost_hints.get(getattr(body, "func", body).__name__, 0) * 10**9
    args = [pltpu.with_memory_space_constraint(x, pltpu.HBM) if i in places else x for i, x in enumerate(args)]

    def inner(*refs):
        body(*refs[count:])

    specs = [small if i in scalars else far_place if i in places else whole for i in range(len(args))]
    return pl.pallas_call(
        inner if count else body,
        out_shape=[jax.ShapeDtypeStruct(dims, kind) for dims, kind in outs],
        in_specs=[any_place] * count + specs,
        out_specs=[small if i in scalar_outs else whole for i in range(len(outs))],
        scratch_shapes=scratch,
        compiler_params=pltpu.CompilerParams(vmem_limit_bytes=limit * 2**20),
        cost_estimate=pl.CostEstimate(flops=cost, bytes_accessed=0, transcendentals=0),
    )(*after, *args)


def place():
    space = lax.axis_index("space")
    return lax.div(space, 2), lax.rem(space, 2), lax.axis_index("member")


def swap(value, axis, size, step):
    return lax.ppermute(value, axis, [(i, i ^ step) for i in range(size)])


def select_kernel(lists_ref, latents_ref, pick_ref, own_ref, send_ref, small_ref, table_ref, sems):
    _, peers, cap = lists_ref.shape
    members, nodes, width = latents_ref.shape
    lists = pltpu.make_async_copy(lists_ref, small_ref, sems.at[0])
    table = pltpu.make_async_copy(latents_ref, table_ref, sems.at[1])
    lists.start()
    table.start()
    lists.wait()
    me = lax.axis_index("space")
    at = lax.broadcasted_iota(jnp.int32, (cap, members * nodes), 0)
    column = lax.broadcasted_iota(jnp.int32, (cap, members * nodes), 1)
    rows = []
    for step in range(peers):
        wanted = jnp.zeros((cap, members * nodes), jnp.int32)
        for j in range(cap):
            wanted = jnp.where(at == j, small_ref[0, me ^ step, j], wanted)
        for member in range(members):
            rows.append((column == wanted + member * nodes).astype(f32))
    pick = jnp.concatenate(rows, axis=0).astype(bf16)
    pick_ref[...] = pick
    table.wait()
    sent = mm(pick, table_ref[...].reshape(members * nodes, width), 1, 0)
    sent = sent.astype(bf16).reshape(peers // 2, 2, members * cap, width)
    own_ref[...] = sent[:, 0]
    send_ref[...] = sent[:, 1]


def merge_kernel(own_ref, arrived_ref, *out_refs):
    rows = own_ref.shape[1]
    for i, out_ref in enumerate(out_refs):
        step = len(out_refs) - i
        out_ref[0:rows, :] = own_ref[step]
        out_ref[rows:, :] = arrived_ref[step]


def stage_kernel(cap, members, count, *refs):
    edge_refs, source_refs, share_ref = refs[:3], refs[3 : 3 + count], refs[3 + count]
    staged_refs, held_refs, sems = refs[4 + count : 4 + 2 * count], refs[4 + 2 * count : -1], refs[-1]
    copies = [
        pltpu.make_async_copy(source, target, sems.at[i])
        for i, (source, target) in enumerate(
            zip(edge_refs + source_refs, held_refs + staged_refs, strict=True)
        )
    ]
    for copy in copies:
        copy.start()
    for copy in copies[:3]:
        copy.wait()
    edge_part(cap, members, *held_refs, share_ref)
    for copy in copies[3:]:
        copy.wait()


def edge_part(cap, members, slot_ref, dst_ref, weight_ref, share_ref):
    edges = slot_ref.shape[0]
    slot = slot_ref[...].reshape(1, edges)
    dst = dst_ref[...].reshape(1, edges)
    weight = weight_ref[...].reshape(1, edges)
    rows = share_ref.shape[0] // 2
    points = share_ref.shape[1] // members
    sender = lax.div(slot, cap)
    spot = (sender ^ lax.axis_index("space")) * (members * cap) + (slot - sender * cap)
    hit = lax.broadcasted_iota(jnp.int32, (rows, edges), 0) == spot
    into = (lax.broadcasted_iota(jnp.int32, (points, edges), 0) == dst).astype(f32).astype(bf16)
    high = weight.astype(bf16).astype(f32)
    table = mm(jnp.where(hit, high, 0.0).astype(bf16), into, 1, 1) + mm(
        jnp.where(hit, weight - high, 0.0).astype(bf16), into, 1, 1
    )
    table = table / jnp.sum(table, axis=0, keepdims=True)
    for member in range(members):
        high = table.astype(bf16)
        columns = slice(member * points, (member + 1) * points)
        share_ref[0:rows, columns] = high
        share_ref[rows : 2 * rows, columns] = (table - high.astype(f32)).astype(bf16)
        table = jnp.concatenate([table[rows - cap :], table[: rows - cap]], axis=0)


def gathered(own_ref, near_ref, far_refs):
    return jnp.concatenate([own_ref[0], near_ref[0]] + [r[...] for r in far_refs[::-1]], axis=0)


def forward_kernel(
    far, w_msg_ref, share_ref, gain_ref, embed_ref, weights_ref, project_ref, present_ref,
    own_ref, near_ref, *rest,
):
    far_refs = rest[:far]
    field_ref, sent_ref, normed_ref, active_ref, slope_ref, unit_ref, inverse_ref = rest[far:]
    points, width = embed_ref.shape
    variables, members, _ = present_ref.shape
    messages = mm(gathered(own_ref, near_ref, far_refs), w_msg_ref[...], 1, 0).astype(bf16)
    messages = jnp.concatenate([messages, messages], axis=0)
    gain = gain_ref[...].reshape(1, width)
    for begin in range(0, members * points, lanes):
        rows = slice(begin, begin + lanes)
        source = slice(begin % points, begin % points + lanes)
        hidden = embed_ref[source, :].astype(f32) + mm(share_ref[:, rows], messages, 0, 0)
        inverse = lax.rsqrt(jnp.mean(hidden * hidden, axis=-1, keepdims=True) + epsilon)
        unit = hidden * inverse
        unit_ref[rows, :] = unit
        inverse_ref[rows, :] = inverse
        normed_ref[rows, :] = (unit * gain).astype(bf16)
    root = 0.7978845608028654
    cubic = 0.044715
    for member in range(members):
        rows = slice(member * points, (member + 1) * points)
        for begin in range(0, width, tile):
            columns = slice(begin, begin + tile)
            inner = mm(normed_ref[rows, :], weights_ref[:, columns], 1, 0)
            square = inner * inner
            bend = jnp.tanh(inner * (root + root * cubic * square))
            half = 0.5 + 0.5 * bend
            active_ref[rows, columns] = (inner * half).astype(bf16)
            slope_ref[rows, columns] = half + (0.5 * inner) * (1.0 - bend * bend) * (
                root + 3.0 * root * cubic * square
            )
        field = present_ref[:, member, :] + mm(project_ref[...], active_ref[rows, :], 1, 1)
        field_ref[member] = field
        sent_ref[member] = field.astype(bf16)


def halving_place(step, levels):
    bits = levels.bit_length() - 1
    return sum((1 - ((step >> bit) & 1)) << (bits - 1 - bit) for bit in range(bits))


def turn_kernel(normed_ref, active_ref, own_ref, near_ref, *rest):
    far_refs, (normed_t_ref, active_t_ref, keep_ref, give_ref) = rest[:-4], rest[-4:]
    _, _, levels, block, _ = normed_t_ref.shape
    width = normed_ref.shape[1]
    level, line, core = place()
    received = gathered(own_ref, near_ref, far_refs)
    for source, target in ((received, None), (normed_ref, normed_t_ref), (active_ref, active_t_ref)):
        for begin in range(0, width, tile):
            turned = source[:, begin : begin + tile].T
            for piece in range(0, tile, block):
                index = (begin + piece) // block
                far = (index // 2 % 2) ^ line
                step = (index // 4) ^ level
                side = (index % 2) ^ core
                value = turned[piece : piece + block]
                if target is not None:
                    target[side, 1 - far, levels - 1 - step] = value
                    continue
                spot = halving_place(step, levels)
                for which, part_ref in enumerate((keep_ref, give_ref)):
                    @pl.when(side == which)
                    def _(part_ref=part_ref):
                        part_ref[1 - far, spot] = value


def split_loss(part, variables):
    column = lax.broadcasted_iota(jnp.int32, part.shape, 1)
    spots = (column == variables) | (column == variables + 1)
    total = jnp.sum(jnp.where(spots, part, 0.0), axis=1, keepdims=True)
    high = total.astype(bf16).astype(f32)
    return jnp.where(column == variables, high, jnp.where(column == variables + 1, total - high, part))


def score_kernel(
    own_ref, other_ref, truth_ref, cell_ref, project_ref, slope_ref, normed_t_ref, active_t_ref,
    inner_ref, pred_ref, loss_ref, far_ref, near_ref, hold_ref,
):
    members, variables, points = own_ref.shape
    width = slope_ref.shape[1]
    total = 2 * members
    pairs = total * (total - 1)

    def eased(delta):
        square = delta * delta + smoothing * smoothing
        inverse = lax.rsqrt(square)
        return square * inverse, delta * inverse

    truth, cell = truth_ref[...], cell_ref[...].reshape(1, points)
    own = [own_ref[m] for m in range(members)]
    other = [other_ref[m].astype(f32) for m in range(members)]
    score = jnp.zeros_like(truth)
    pulls = [jnp.zeros_like(truth) for _ in own]
    grads = []
    for m in range(members):
        size, sign = eased(own[m] - truth)
        score = score + size * (1.0 / total)
        grads.append(sign * (1.0 / total))
    for m in range(members):
        for n in range(m + 1, members):
            size, sign = eased(own[m] - own[n])
            score = score - size * (1.0 / pairs)
            pulls[m] = pulls[m] + sign
            pulls[n] = pulls[n] - sign
        for n in range(members):
            size, sign = eased(own[m] - other[n])
            score = score - size * (0.5 / pairs)
            pulls[m] = pulls[m] + sign
    loss = jnp.sum(score * cell)
    loss_ref[0] = loss
    hold_ref[...] = jnp.zeros_like(hold_ref)
    for m in range(members):
        grad = (grads[m] - pulls[m] * (1.0 / pairs)) * cell
        hold_ref[0:variables, m * points : (m + 1) * points] = grad
    pred = hold_ref[...].astype(bf16)
    pred_ref[...] = pred
    for m in range(members):
        rows = slice(m * points, (m + 1) * points)
        part = pred[:variables, rows]
        for begin in range(0, width, tile):
            columns = slice(begin, begin + tile)
            grad = mm(part, project_ref[:, columns], 0, 0)
            inner_ref[rows, columns] = (grad * slope_ref[rows, columns]).astype(bf16)
    weight_parts(normed_t_ref, active_t_ref, inner_ref, pred, loss, variables, 1, 0, far_ref)
    weight_parts(normed_t_ref, active_t_ref, inner_ref, pred, loss, variables, 1, 1, near_ref)


def weight_parts(normed_t_ref, active_t_ref, inner_ref, pred, loss, variables, side, half, out_ref):
    width = inner_ref.shape[1]
    depth = normed_t_ref.shape[-1]
    normed = normed_t_ref[side, half].reshape(-1, depth)
    for begin in range(0, width, tile):
        columns = slice(begin, begin + tile)
        out_ref[:, columns] = mm(normed, inner_ref[:, columns], 1, 0).astype(out_ref.dtype)
    part = mm(active_t_ref[side, half].reshape(-1, depth), pred, 1, 1)
    part = jnp.where(lax.broadcasted_iota(jnp.int32, part.shape, 1) == variables, loss, part)
    out_ref[:, width:] = split_loss(part, variables).astype(out_ref.dtype)


def pack(out_ref, begin, part):
    pad = part.shape[1]
    for i in range(part.shape[0] // packed):
        out_ref[begin : begin + packed, i * pad : (i + 1) * pad] = part[i * packed : (i + 1) * packed]


def unpack(in_ref, begin, count, pad):
    parts = [in_ref[begin : begin + packed, i * pad : (i + 1) * pad] for i in range(count // packed)]
    return jnp.concatenate(parts, axis=0).astype(f32)


def local_kernel(variables, loss_ref, normed_t_ref, active_t_ref, inner_ref, pred_ref, far_ref, near_ref):
    for half, out_ref in ((0, far_ref), (1, near_ref)):
        weight_parts(
            normed_t_ref, active_t_ref, inner_ref, pred_ref[...], loss_ref[0], variables, 0, half, out_ref
        )


def pair_sum(variables, width, held_ref, other_ref, begin, count):
    rows = slice(begin, begin + count)
    total = held_ref[rows, :width] + other_ref[rows, :width].astype(f32)
    part = held_ref[rows, width:] + other_ref[rows, width:].astype(f32)
    return total, split_loss(part, variables)


def first_kernel(variables, width, held_ref, other_ref, out_ref):
    total, part = pair_sum(variables, width, held_ref, other_ref, 0, out_ref.shape[0])
    out_ref[:, :width] = total.astype(bf16)
    out_ref[:, width:] = part.astype(bf16)


def across_kernel(variables, begin, near_ref, near_other_ref, far_ref, far_other_ref, *out_refs):
    width = out_refs[0].shape[1]
    block = out_refs[0].shape[0] // 2 - packed
    for i, out_ref in enumerate(out_refs):
        for line, (held_ref, other_ref) in enumerate(((near_ref, near_other_ref), (far_ref, far_other_ref))):
            total, part = pair_sum(variables, width, held_ref, other_ref, begin + i * block, block)
            at = line * (block + packed)
            out_ref[at : at + block, :] = total.astype(bf16)
            out_ref[at + block : at + block + packed, :] = jnp.zeros((packed, width), bf16)
            pack(out_ref, at + block, part.astype(bf16))


def message_kernel(keep_ref, give_ref, slots_ref, other_ref, first_ref, second_ref, near_ref, slot_far_ref):
    depth, width = keep_ref.shape[-1], near_ref.shape[1]
    slot_far_ref[...] = slots_ref[slots_ref.shape[0] // 2 :]
    count = first_ref.shape[0]
    for half in range(2):
        own = keep_ref[half].reshape(-1, depth)
        other = give_ref[half].reshape(-1, depth)
        for begin in range(0, width, tile):
            columns = slice(begin, begin + tile)
            here = slots_ref[:, :, columns].reshape(depth, tile)
            there = other_ref[:, :, columns].reshape(depth, tile)
            total = mm(own, here, 1, 0) + mm(other, there, 1, 0)
            if half == 0:
                first_ref[:, columns] = total[:count].astype(bf16)
                second_ref[:, columns] = total[count:].astype(bf16)
            else:
                near_ref[:, columns] = total


def second_kernel(source_ref, out_ref):
    out_ref[...] = source_ref[...]


def step_kernel(near_ref, arrived_ref, out_ref):
    count = out_ref.shape[0]
    out_ref[...] = (near_ref[0:count, :] + arrived_ref[...].astype(f32)).astype(bf16)


def halve_kernel(begin, near_ref, *rest):
    arrived_refs, (send_ref, keep_ref) = rest[:-2], rest[-2:]
    count = send_ref.shape[0]
    for at, out_ref in ((0, send_ref), (count, keep_ref)):
        total = near_ref[begin + at : begin + at + count, :]
        for r in arrived_refs:
            total = total + r[at : at + count, :].astype(f32)
        out_ref[...] = total.astype(out_ref.dtype)


def own_kernel(variables, width, held_ref, other_ref, *rest):
    arrived_refs, out_ref = rest[:-1], rest[-1]
    block = out_ref.shape[0]
    total, part = pair_sum(variables, width, held_ref, other_ref, held_ref.shape[0] - block, block)
    for r in arrived_refs:
        at = block + packed
        total = total + r[at : at + block, :].astype(f32)
        part = part + unpack(r, at + block, block, part.shape[1])
    out_ref[:, :width] = total
    out_ref[:, width:] = split_loss(part, variables)


def fold_kernel(kept_ref, arrived_ref, send_ref, keep_ref):
    half, _, rows, _ = keep_ref.shape
    count = arrived_ref.shape[1]
    for at, out_ref in ((0, keep_ref), (half, send_ref)):
        for i in range(half):
            for j in range(count):
                out_ref[i, j] = kept_ref[at + i, j]
                out_ref[i, count + j] = arrived_ref[at + i, j]


def last_kernel(hidden_ref, kept_ref, arrived_ref, out_ref):
    count, rows, width = kept_ref.shape[1:]
    block = hidden_ref.shape[0]
    out_ref[0:block, :] = hidden_ref[:, :width].astype(bf16)
    out_ref[block : block + packed, :] = jnp.zeros((packed, width), bf16)
    pack(out_ref, block, hidden_ref[:, width:].astype(bf16))
    at = block + packed
    for source_ref in (kept_ref, arrived_ref):
        for j in range(count):
            out_ref[at : at + rows, :] = source_ref[1, j]
            at += rows


def hidden_early_kernel(variables, width, held_ref, other_ref, arrived_ref, *out_refs):
    block = out_refs[0].shape[0]
    for i, out_ref in enumerate(out_refs):
        total, part = pair_sum(variables, width, held_ref, other_ref, i * block, block)
        here = slice(i * block, (i + 1) * block)
        out_ref[:, :width] = (total + arrived_ref[here, :width].astype(f32)).astype(bf16)
        part = split_loss(part + arrived_ref[here, width:].astype(f32), variables)
        out_ref[:, width:] = part.astype(bf16)


def back_kernel(inner_ref, w_hidden_ref, gain_ref, unit_ref, inverse_ref, grad_ref, scaled_ref):
    rows_all, width = inner_ref.shape
    gain = gain_ref[...].reshape(1, width)
    for begin_row in range(0, rows_all, tile):
        rows = slice(begin_row, begin_row + tile)
        dots = jnp.zeros((tile, 1), f32)
        for begin in range(0, width, tile):
            columns = slice(begin, begin + tile)
            scaled = mm(inner_ref[rows, :], w_hidden_ref[columns, :], 1, 1) * gain[:, columns]
            dots = dots + jnp.sum(scaled * unit_ref[rows, columns], axis=-1, keepdims=True)
            scaled_ref[rows, columns] = scaled
        dots = dots * (1.0 / width)
        inverse = inverse_ref[rows, :]
        for begin in range(0, width, tile):
            columns = slice(begin, begin + tile)
            grad_ref[rows, columns] = (
                (scaled_ref[rows, columns] - unit_ref[rows, columns] * dots) * inverse
            ).astype(bf16)


def slot_kernel(share_ref, grad_ref, slots_ref):
    peers, each, width = slots_ref.shape
    rows = peers * each
    for begin in range(0, width, tile):
        columns = slice(begin, begin + tile)
        both = mm(share_ref[...], grad_ref[:, columns], 1, 0)
        slots_ref[:, :, columns] = (both[:rows] + both[rows:]).astype(bf16).reshape(peers, each, tile)


def owner_kernel(pick_ref, w_msg_ref, kept_ref, arrived_ref, last_ref, grad_ref, token_ref, held_ref):
    token_ref[...] = jnp.zeros_like(token_ref)
    peers, rows, width = held_ref.shape
    count = kept_ref.shape[1]
    begin = last_ref.shape[0] - 2 * count * rows
    order = [0]
    for bit in reversed(range(peers.bit_length() - 1)):
        order += [x ^ (1 << bit) for x in order]
    for j in range(count):
        held_ref[order[j]] = kept_ref[0, j]
        held_ref[order[count + j]] = arrived_ref[0, j]
    for j in range(2 * count):
        held_ref[order[2 * count + j]] = last_ref[begin + j * rows : begin + (j + 1) * rows, :]
    nodes = mm(pick_ref[...], held_ref[...].reshape(peers * rows, width), 0, 0).astype(bf16)
    grad_ref[...] = mm(nodes, w_msg_ref[...], 1, 1).astype(bf16).reshape(grad_ref.shape)


def partial_kernel(variables, width, early, held_ref, other_ref, *rest):
    arrived_refs, out_ref = rest[:-1], rest[-1]
    block = out_ref.shape[0]
    total, part = pair_sum(variables, width, held_ref, other_ref, held_ref.shape[0] - block, block)
    for i, r in enumerate(arrived_refs):
        total = total + r[0:block, :width].astype(f32)
        if i < early:
            part = part + r[:, width:].astype(f32)
        else:
            part = part + unpack(r, block, block, part.shape[1])
    out_ref[:, :width] = total
    out_ref[:, width:] = part


def hidden_sum_kernel(variables, scale, partial_ref, last_ref, hidden_ref, out_ref, loss_ref, token_ref):
    token_ref[...] = jnp.zeros_like(token_ref)
    block, width = hidden_ref.shape
    pad = partial_ref.shape[1] - width
    part = partial_ref[:, width:] + unpack(last_ref, block, block, pad)
    hidden_ref[...] = partial_ref[:, :width] + last_ref[0:block, :].astype(f32)
    out_ref[...] = part[:, :variables]
    column = lax.broadcasted_iota(jnp.int32, (8, pad), 1)
    spots = (column == variables) | (column == variables + 1)
    first = lax.broadcasted_iota(jnp.int32, (8, pad), 0) == 0
    loss_ref[0] = jnp.sum(jnp.where(spots & first, part[:8], 0.0)) * scale


def message_sum_kernel(keep_ref, arrived_ref, out_ref):
    out_ref[...] = keep_ref[...] + arrived_ref[...].astype(f32)


def on_device(
    latents, grid_embed, norm_gain, w_msg, w_hidden, variable_projection, present_condition, verifying_field,
    cell_surface, send_rows, edge_slot, edge_dst, edge_weight,
):
    members, nodes, width = latents.shape
    points = grid_embed.shape[0]
    variables = variable_projection.shape[1]
    peers = lax.axis_size("space")
    cores = lax.axis_size("member")
    cap = send_rows.shape[2]
    rows_peer = members * cap
    rows_slot = peers * rows_peer
    rows_all = members * points
    levels = peers // 2
    block = width // (peers * cores)
    half = levels * block
    wide = width + -(-(variables + 2) // lanes) * lanes
    project = variable_projection.T

    early = levels // 2
    count, rest = early * block, (levels - 1 - early) * block
    steps = [2 * (levels - 1 - i) for i in range(levels - 1)]

    def spread(values, part):
        return [swap(x, "space", peers, k) for x, k in zip(values, part, strict=True)]

    pick, own_rows, send = call(
        select_kernel,
        [((rows_slot, members * nodes), bf16)] + [((levels, rows_peer, width), bf16)] * 2,
        [send_rows, latents],
        scratch=[
            pltpu.SMEM(send_rows.shape, jnp.int32),
            pltpu.VMEM(latents.shape, bf16),
            pltpu.SemaphoreType.DMA((2,)),
        ],
        limit=4,
        places=(0, 1),
    )
    near_rows = swap(send, "space", peers, 1)
    fixed = [w_msg, norm_gain, grid_embed, w_hidden, project, present_condition.transpose(1, 0, 2)]
    edges = [edge_slot, edge_dst, edge_weight]
    share, *staged = call(
        functools.partial(stage_kernel, cap, members, len(fixed)),
        [((2 * rows_slot, rows_all), bf16)] + [(x.shape, x.dtype) for x in fixed],
        edges + fixed,
        scratch=[pltpu.VMEM(x.shape, x.dtype) for x in edges]
        + [pltpu.SemaphoreType.DMA((3 + len(fixed),))],
        limit=16,
        places=tuple(range(3 + len(fixed))),
        after=[pick],
    )
    merged = call(
        merge_kernel,
        [((2 * rows_peer, width), bf16)] * (levels - 1),
        [own_rows, near_rows],
        limit=4,
        after=[share],
    )
    received = [own_rows, near_rows] + spread(merged, steps)
    w_msg_near, gain, embed, w_hidden_near, project_near, present = staged
    field, sent, normed, active, slope, unit, inverse = call(
        functools.partial(forward_kernel, levels - 1),
        [
            ((members, variables, points), f32),
            ((members, variables, points), bf16),
            ((rows_all, width), bf16),
            ((rows_all, width), bf16),
            ((rows_all, width), f32),
            ((rows_all, width), f32),
            ((rows_all, 1), f32),
        ],
        [w_msg_near, share, gain, embed, w_hidden_near, project_near, present] + received,
        limit=20,
    )
    other = swap(sent, "member", cores, 1)
    normed_t, active_t, received_keep, received_give = call(
        turn_kernel,
        [((cores, 2, levels, block, rows_all), bf16)] * 2 + [((2, levels, block, rows_slot), bf16)] * 2,
        [normed, active] + received,
        limit=8,
    )
    received_other = swap(received_give, "member", cores, 1)
    grad_inner, pred, loss_part, far, near = call(
        score_kernel,
        [
            ((rows_all, width), bf16),
            ((lanes, rows_all), bf16),
            ((1,), f32),
            ((half, wide), bf16),
            ((half, wide), bf16),
        ],
        [field, other, verifying_field, cell_surface, project_near, slope, normed_t, active_t],
        scratch=[pltpu.VMEM((lanes, rows_all), f32)],
        limit=16,
        scalar_outs=(2,),
    )
    far_other = swap(far, "member", cores, 1)
    near_other = swap(near, "member", cores, 1)
    held_far, held_near = call(
        functools.partial(local_kernel, variables),
        [((half, wide), f32)] * 2,
        [loss_part, normed_t, active_t, grad_inner, pred],
        limit=12,
        scalars=(0,),
    )
    (first,) = call(
        functools.partial(first_kernel, variables, width),
        [((count, wide), bf16)],
        [held_far, far_other],
        limit=6,
    )
    first_other = swap(first, "space", peers, 1)
    across = call(
        functools.partial(across_kernel, variables, count),
        [((2 * block + 2 * packed, width), bf16)] * (levels - 1 - early),
        [held_near, near_other, held_far, far_other],
        limit=6,
        after=[first],
    )
    across_parts = spread(across, steps[early:])
    (grad_hidden,) = call(
        back_kernel,
        [((rows_all, width), bf16)],
        [grad_inner, w_hidden_near, gain, unit, inverse],
        scratch=[pltpu.VMEM((rows_all, width), f32)],
        limit=14,
        after=[across[0]],
    )
    (slots,) = call(
        slot_kernel,
        [((peers, rows_peer, width), bf16)],
        [share, grad_hidden],
        limit=6,
        after=[received_other],
    )
    slots_other = swap(slots, "member", cores, 1)
    message_first, message_second, message_near, slots_sent = call(
        message_kernel,
        [((half // 2, width), bf16)] * 2
        + [((half, width), f32)]
        + [((levels, rows_peer, width), bf16)],
        [received_keep, received_other, slots, slots_other],
        limit=10,
    )
    message_first_other = swap(message_first, "space", peers, 1)
    (hidden_own,) = call(
        functools.partial(own_kernel, variables, width),
        [((block, wide), f32)],
        [held_far, far_other] + across_parts,
        limit=4,
    )
    hidden_early = call(
        functools.partial(hidden_early_kernel, variables, width),
        [((block, wide), bf16)] * early,
        [held_near, near_other, first_other],
        limit=6,
        after=[message_first, hidden_own],
    )
    hidden_parts = spread(hidden_early, steps[:early])
    (message_step,) = call(
        step_kernel,
        [((half // 2, width), bf16)],
        [message_near, message_first_other],
        limit=4,
        after=hidden_early[:1],
    )
    message_other = swap(message_step, "space", peers, 2)
    (message_second,) = call(
        second_kernel, [((half // 2, width), bf16)], [message_second], limit=4, after=[message_step]
    )
    message_second_other = swap(message_second, "space", peers, 1)
    slots_kept = slots.reshape(peers, 1, rows_peer, width)
    slots_sent = slots_sent.reshape(levels, 1, rows_peer, width)
    bit = levels
    while True:
        slots_other = swap(slots_sent, "space", peers, bit)
        if bit == 2:
            break
        folded = (bit // 2, 2 * levels // bit, rows_peer, width)
        slots_sent, slots_kept = call(
            fold_kernel, [(folded, bf16)] * 2, [slots_kept, slots_other], limit=4, after=[message_second]
        )
        bit //= 2
    (partial,) = call(
        functools.partial(partial_kernel, variables, width, early),
        [((block, wide), f32)],
        [held_near, near_other] + hidden_parts + across_parts,
        limit=4,
    )
    (last,) = call(
        last_kernel,
        [((block + packed + levels * rows_peer, width), bf16)],
        [hidden_own, slots_kept, slots_other],
        limit=4,
        after=[message_second],
    )
    last_other = swap(last, "space", peers, 1)
    message_send, message_keep = call(
        functools.partial(halve_kernel, half // 2),
        [((half // 4, width), bf16), ((half // 4, width), f32)],
        [message_near, message_second_other, message_other],
        limit=4,
        after=[partial],
    )
    bit = 4
    while bit < peers // 2:
        message_other = swap(message_send, "space", peers, bit)
        rows_left = message_send.shape[0] // 2
        message_send, message_keep = call(
            functools.partial(halve_kernel, 0),
            [((rows_left, width), bf16), ((rows_left, width), f32)],
            [message_keep, message_other],
            limit=4,
        )
        bit *= 2
    message_other = swap(message_send, "space", peers, bit)
    token = ((8, lanes), f32)
    latent_grad, latent_done = call(
        owner_kernel,
        [(latents.shape, bf16), token],
        [pick, w_msg, slots_kept, slots_other, last_other],
        scratch=[pltpu.VMEM((peers, rows_peer, width), bf16)],
        limit=8,
    )
    hidden_weight_grad, out_weight_grad, loss, hidden_done = call(
        functools.partial(hidden_sum_kernel, variables, 1.0 / (points * peers * variables)),
        [((block, width), f32), ((block, variables), f32), ((1,), f32), token],
        [partial, last_other],
        limit=8,
        scalar_outs=(2,),
        after=[latent_done],
    )
    (msg_weight_grad,) = call(
        message_sum_kernel,
        [((block, width), f32)],
        [message_keep, message_other],
        limit=6,
        after=[hidden_done],
    )
    return (latent_grad, loss, msg_weight_grad, hidden_weight_grad, out_weight_grad)


def solution(mesh):
    placed = (
        P(("groups", "member"), "space", None),
        P(("groups", "space"), None),
        P(),
        P(),
        P(),
        P(),
        P(("groups", "member"), None, "space"),
        P(None, ("groups", "space")),
        P(("groups", "space")),
        P("space", None, None),
        P("space"),
        P("space"),
        P("space"),
    )
    return jax.shard_map(
        on_device,
        mesh=mesh,
        in_specs=placed,
        out_specs=(
            P(("groups", "member"), "space", None),
            P("groups"),
            P(("groups", "space", "member"), None),
            P(("groups", "space", "member"), None),
            P(("groups", "space", "member"), None),
        ),
        check_vma=False,
    )
```

```python
import functools

import jax
import jax.numpy as jnp
from jax import lax
from jax.experimental import pallas as pl
from jax.experimental.pallas import tpu as pltpu
from jax.sharding import PartitionSpec as P

smoothing = 0.1
epsilon = 1e-06
tile = 256
lanes = 128
packed = 16
cost_hints = {
    "back_kernel": 8,
    "slot_kernel": 4,
    "hidden_early_kernel": 4,
    "message_early_kernel": 4,
    "late_kernel": 4,
    "message_sum_kernel": 8,
}
f32 = jnp.float32
bf16 = jnp.bfloat16


def mm(left, right, left_dim, right_dim):
    return lax.dot_general(
        left, right, (((left_dim,), (right_dim,)), ((), ())), preferred_element_type=f32
    )


def call(body, outs, args, scratch=(), limit=16, scalars=(), scalar_outs=(), places=(), after=()):
    whole = pl.BlockSpec(memory_space=pltpu.VMEM)
    small = pl.BlockSpec(memory_space=pltpu.SMEM)
    far_place = pl.BlockSpec(memory_space=pltpu.HBM)
    any_place = pl.BlockSpec(memory_space=pl.ANY)
    count = len(after)
    cost = cost_hints.get(getattr(body, "func", body).__name__, 0) * 10**9
    args = [pltpu.with_memory_space_constraint(x, pltpu.HBM) if i in places else x for i, x in enumerate(args)]

    def inner(*refs):
        body(*refs[count:])

    specs = [small if i in scalars else far_place if i in places else whole for i in range(len(args))]
    return pl.pallas_call(
        inner if count else body,
        out_shape=[jax.ShapeDtypeStruct(dims, kind) for dims, kind in outs],
        in_specs=[any_place] * count + specs,
        out_specs=[small if i in scalar_outs else whole for i in range(len(outs))],
        scratch_shapes=scratch,
        compiler_params=pltpu.CompilerParams(vmem_limit_bytes=limit * 2**20),
        cost_estimate=pl.CostEstimate(flops=cost, bytes_accessed=0, transcendentals=0),
    )(*after, *args)


def place():
    space = lax.axis_index("space")
    return lax.div(space, 2), lax.rem(space, 2), lax.axis_index("member")


def swap(value, axis, size, step):
    return lax.ppermute(value, axis, [(i, i ^ step) for i in range(size)])


def select_kernel(lists_ref, latents_ref, *refs):
    (pick_ref, send_ref, own_ref), direct_refs, (small_ref, table_ref, sems) = refs[:3], refs[3:-3], refs[-3:]
    _, peers, cap = lists_ref.shape
    members, nodes, width = latents_ref.shape
    lists = pltpu.make_async_copy(lists_ref, small_ref, sems.at[0])
    table = pltpu.make_async_copy(latents_ref, table_ref, sems.at[1])
    lists.start()
    table.start()
    lists.wait()
    me = lax.axis_index("space")
    at = lax.broadcasted_iota(jnp.int32, (cap, members * nodes), 0)
    column = lax.broadcasted_iota(jnp.int32, (cap, members * nodes), 1)
    rows = []
    for step in range(peers):
        wanted = jnp.zeros((cap, members * nodes), jnp.int32)
        for j in range(cap):
            wanted = jnp.where(at == j, small_ref[0, me ^ step, j], wanted)
        for member in range(members):
            rows.append((column == wanted + member * nodes).astype(f32))
    pick = jnp.concatenate(rows, axis=0).astype(bf16)
    pick_ref[...] = pick
    table.wait()
    sent = mm(pick, table_ref[...].reshape(members * nodes, width), 1, 0)
    sent = sent.astype(bf16).reshape(peers // 2, 2, members * cap, width)
    send_ref[...] = sent[:, 1]
    own_ref[...] = sent[0, 0]
    for i, direct_ref in enumerate(direct_refs):
        direct_ref[...] = sent[len(direct_refs) - i, 0]


def split_kernel(arrived_ref, own_ref, *out_refs):
    own_ref[...] = arrived_ref[0]
    for i, out_ref in enumerate(out_refs):
        out_ref[...] = arrived_ref[len(out_refs) - i]


def stage_kernel(cap, members, count, *refs):
    edge_refs, source_refs, share_ref = refs[:3], refs[3 : 3 + count], refs[3 + count]
    staged_refs, held_refs, sems = refs[4 + count : 4 + 2 * count], refs[4 + 2 * count : -1], refs[-1]
    copies = [
        pltpu.make_async_copy(source, target, sems.at[i])
        for i, (source, target) in enumerate(
            zip(edge_refs + source_refs, held_refs + staged_refs, strict=True)
        )
    ]
    for copy in copies:
        copy.start()
    for copy in copies[:3]:
        copy.wait()
    edge_part(cap, members, *held_refs, share_ref)
    for copy in copies[3:]:
        copy.wait()


def edge_part(cap, members, slot_ref, dst_ref, weight_ref, share_ref):
    edges = slot_ref.shape[0]
    slot = slot_ref[...].reshape(1, edges)
    dst = dst_ref[...].reshape(1, edges)
    weight = weight_ref[...].reshape(1, edges)
    rows = share_ref.shape[0] // 2
    points = share_ref.shape[1] // members
    sender = lax.div(slot, cap)
    spot = (sender ^ lax.axis_index("space")) * (members * cap) + (slot - sender * cap)
    hit = lax.broadcasted_iota(jnp.int32, (rows, edges), 0) == spot
    into = (lax.broadcasted_iota(jnp.int32, (points, edges), 0) == dst).astype(f32).astype(bf16)
    high = weight.astype(bf16).astype(f32)
    table = mm(jnp.where(hit, high, 0.0).astype(bf16), into, 1, 1) + mm(
        jnp.where(hit, weight - high, 0.0).astype(bf16), into, 1, 1
    )
    table = table / jnp.sum(table, axis=0, keepdims=True)
    for member in range(members):
        high = table.astype(bf16)
        columns = slice(member * points, (member + 1) * points)
        share_ref[0:rows, columns] = high
        share_ref[rows : 2 * rows, columns] = (table - high.astype(f32)).astype(bf16)
        table = jnp.concatenate([table[rows - cap :], table[: rows - cap]], axis=0)


def gathered(refs):
    return jnp.concatenate([r[...] for r in refs], axis=0)


def forward_kernel(
    peers, w_msg_ref, share_ref, gain_ref, embed_ref, weights_ref, project_ref, present_ref, *rest
):
    field_ref, sent_ref, normed_ref, active_ref, slope_ref, unit_ref, inverse_ref = rest[peers:]
    points, width = embed_ref.shape
    variables, members, _ = present_ref.shape
    messages = mm(gathered(rest[:peers]), w_msg_ref[...], 1, 0).astype(bf16)
    messages = jnp.concatenate([messages, messages], axis=0)
    gain = gain_ref[...].reshape(1, width)
    for begin in range(0, members * points, lanes):
        rows = slice(begin, begin + lanes)
        source = slice(begin % points, begin % points + lanes)
        hidden = embed_ref[source, :].astype(f32) + mm(share_ref[:, rows], messages, 0, 0)
        inverse = lax.rsqrt(jnp.mean(hidden * hidden, axis=-1, keepdims=True) + epsilon)
        unit = hidden * inverse
        unit_ref[rows, :] = unit
        inverse_ref[rows, :] = inverse
        normed_ref[rows, :] = (unit * gain).astype(bf16)
    root = 0.7978845608028654
    cubic = 0.044715
    for member in range(members):
        rows = slice(member * points, (member + 1) * points)
        for begin in range(0, width, tile):
            columns = slice(begin, begin + tile)
            inner = mm(normed_ref[rows, :], weights_ref[:, columns], 1, 0)
            square = inner * inner
            bend = jnp.tanh(inner * (root + root * cubic * square))
            half = 0.5 + 0.5 * bend
            active_ref[rows, columns] = (inner * half).astype(bf16)
            slope_ref[rows, columns] = half + (0.5 * inner) * (1.0 - bend * bend) * (
                root + 3.0 * root * cubic * square
            )
        field = present_ref[:, member, :] + mm(project_ref[...], active_ref[rows, :], 1, 1)
        field_ref[member] = field
        sent_ref[member] = field.astype(bf16)


def turn_kernel(normed_ref, active_ref, *rest):
    normed_t_ref, active_t_ref, keep_ref, give_ref = rest[-4:]
    _, _, levels, block, _ = normed_t_ref.shape
    width = normed_ref.shape[1]
    level, line, core = place()
    received = gathered(rest[:-4])
    for source, target in ((received, None), (normed_ref, normed_t_ref), (active_ref, active_t_ref)):
        for begin in range(0, width, tile):
            turned = source[:, begin : begin + tile].T
            for piece in range(0, tile, block):
                index = (begin + piece) // block
                far = (index // 2 % 2) ^ line
                step = (index // 4) ^ level
                side = (index % 2) ^ core
                value = turned[piece : piece + block]
                if target is not None:
                    target[side, 1 - far, levels - 1 - step] = value
                    continue
                for which, part_ref in enumerate((keep_ref, give_ref)):
                    @pl.when(side == which)
                    def _(part_ref=part_ref):
                        part_ref[1 - far, levels - 1 - step] = value


def split_loss(part, variables):
    column = lax.broadcasted_iota(jnp.int32, part.shape, 1)
    spots = (column == variables) | (column == variables + 1)
    total = jnp.sum(jnp.where(spots, part, 0.0), axis=1, keepdims=True)
    high = total.astype(bf16).astype(f32)
    return jnp.where(column == variables, high, jnp.where(column == variables + 1, total - high, part))


def score_kernel(
    own_ref, other_ref, truth_ref, cell_ref, project_ref, slope_ref, normed_t_ref, active_t_ref,
    inner_ref, pred_ref, loss_ref, far_ref, near_ref, hold_ref,
):
    members, variables, points = own_ref.shape
    width = slope_ref.shape[1]
    total = 2 * members
    pairs = total * (total - 1)

    def eased(delta):
        square = delta * delta + smoothing * smoothing
        inverse = lax.rsqrt(square)
        return square * inverse, delta * inverse

    truth, cell = truth_ref[...], cell_ref[...].reshape(1, points)
    own = [own_ref[m] for m in range(members)]
    other = [other_ref[m].astype(f32) for m in range(members)]
    score = jnp.zeros_like(truth)
    pulls = [jnp.zeros_like(truth) for _ in own]
    grads = []
    for m in range(members):
        size, sign = eased(own[m] - truth)
        score = score + size * (1.0 / total)
        grads.append(sign * (1.0 / total))
    for m in range(members):
        for n in range(m + 1, members):
            size, sign = eased(own[m] - own[n])
            score = score - size * (1.0 / pairs)
            pulls[m] = pulls[m] + sign
            pulls[n] = pulls[n] - sign
        for n in range(members):
            size, sign = eased(own[m] - other[n])
            score = score - size * (0.5 / pairs)
            pulls[m] = pulls[m] + sign
    loss = jnp.sum(score * cell)
    loss_ref[0] = loss
    hold_ref[...] = jnp.zeros_like(hold_ref)
    for m in range(members):
        grad = (grads[m] - pulls[m] * (1.0 / pairs)) * cell
        hold_ref[0:variables, m * points : (m + 1) * points] = grad
    pred = hold_ref[...].astype(bf16)
    pred_ref[...] = pred
    for m in range(members):
        rows = slice(m * points, (m + 1) * points)
        part = pred[:variables, rows]
        for begin in range(0, width, tile):
            columns = slice(begin, begin + tile)
            grad = mm(part, project_ref[:, columns], 0, 0)
            inner_ref[rows, columns] = (grad * slope_ref[rows, columns]).astype(bf16)
    weight_parts(normed_t_ref, active_t_ref, inner_ref, pred, loss, variables, 1, 0, far_ref)
    weight_parts(normed_t_ref, active_t_ref, inner_ref, pred, loss, variables, 1, 1, near_ref)


def weight_parts(normed_t_ref, active_t_ref, inner_ref, pred, loss, variables, side, half, out_ref):
    width = inner_ref.shape[1]
    depth = normed_t_ref.shape[-1]
    normed = normed_t_ref[side, half].reshape(-1, depth)
    for begin in range(0, width, tile):
        columns = slice(begin, begin + tile)
        out_ref[:, columns] = mm(normed, inner_ref[:, columns], 1, 0).astype(out_ref.dtype)
    part = mm(active_t_ref[side, half].reshape(-1, depth), pred, 1, 1)
    part = jnp.where(lax.broadcasted_iota(jnp.int32, part.shape, 1) == variables, loss, part)
    out_ref[:, width:] = split_loss(part, variables).astype(out_ref.dtype)


def pack(out_ref, begin, part):
    pad = part.shape[1]
    for i in range(part.shape[0] // packed):
        out_ref[begin : begin + packed, i * pad : (i + 1) * pad] = part[i * packed : (i + 1) * packed]


def unpack(in_ref, begin, count, pad):
    parts = [in_ref[begin : begin + packed, i * pad : (i + 1) * pad] for i in range(count // packed)]
    return jnp.concatenate(parts, axis=0).astype(f32)


def local_kernel(variables, loss_ref, normed_t_ref, active_t_ref, inner_ref, pred_ref, far_ref, near_ref):
    for half, out_ref in ((0, far_ref), (1, near_ref)):
        weight_parts(
            normed_t_ref, active_t_ref, inner_ref, pred_ref[...], loss_ref[0], variables, 0, half, out_ref
        )


def pair_sum(variables, width, held_ref, other_ref, begin, count):
    rows = slice(begin, begin + count)
    total = held_ref[rows, :width] + other_ref[rows, :width].astype(f32)
    part = held_ref[rows, width:] + other_ref[rows, width:].astype(f32)
    return total, split_loss(part, variables)


def first_kernel(variables, width, held_ref, other_ref, out_ref):
    total, part = pair_sum(variables, width, held_ref, other_ref, 0, out_ref.shape[0])
    out_ref[:, :width] = total.astype(bf16)
    out_ref[:, width:] = part.astype(bf16)


def message_kernel(
    variables, early, levels, keep_ref, give_ref, slots_ref, other_ref, held_ref, far_other_ref,
    first_ref, middle_ref, last_ref, near_ref,
):
    depth, width = keep_ref.shape[-1], near_ref.shape[1]
    block = near_ref.shape[0] // levels
    count, rest = early * block, (levels - 1 - early) * block
    for begin, size, out_ref in ((count, rest, middle_ref), (count + rest, block, last_ref)):
        total, part = pair_sum(variables, width, held_ref, far_other_ref, begin, size)
        out_ref[0:size, :] = total.astype(bf16)
        out_ref[size : size + packed, :] = jnp.zeros((packed, width), bf16)
        pack(out_ref, size, part.astype(bf16))
    for half in range(2):
        own = keep_ref[half].reshape(-1, depth)
        other = give_ref[half].reshape(-1, depth)
        for begin in range(0, width, tile):
            columns = slice(begin, begin + tile)
            here = slots_ref[:, :, columns].reshape(depth, tile)
            there = other_ref[:, :, columns].reshape(depth, tile)
            total = mm(own, here, 1, 0) + mm(other, there, 1, 0)
            if half == 0:
                total = total.astype(bf16)
                first_ref[:, columns] = total[:count]
                middle_ref[rest + packed :, columns] = total[count : count + rest]
                last_ref[block + packed :, columns] = total[count + rest :]
            else:
                near_ref[:, columns] = total


def ride_kernel(last_ref, slots_ref, *rest):
    arrived_refs, out_ref = rest[:-1], rest[-1]
    rows = slots_ref.shape[1]
    begin = last_ref.shape[0]
    out_ref[0:begin, :] = last_ref[...]
    for i, arrived_ref in enumerate(arrived_refs):
        out_ref[begin + i * rows : begin + (i + 1) * rows, :] = arrived_ref[rows:, :]
    out_ref[begin + len(arrived_refs) * rows :, :] = slots_ref[1]


def hidden_early_kernel(variables, width, held_ref, other_ref, arrived_ref, *out_refs):
    block = out_refs[0].shape[0]
    for i, out_ref in enumerate(out_refs):
        total, part = pair_sum(variables, width, held_ref, other_ref, i * block, block)
        here = slice(i * block, (i + 1) * block)
        out_ref[:, :width] = (total + arrived_ref[here, :width].astype(f32)).astype(bf16)
        part = split_loss(part + arrived_ref[here, width:].astype(f32), variables)
        out_ref[:, width:] = part.astype(bf16)


def message_early_kernel(near_ref, arrived_ref, *out_refs):
    block = out_refs[0].shape[0]
    for i, out_ref in enumerate(out_refs):
        here = slice(i * block, (i + 1) * block)
        out_ref[...] = (near_ref[here, :] + arrived_ref[here, :].astype(f32)).astype(bf16)


def late_kernel(variables, early, held_ref, other_ref, near_ref, arrived_ref, *out_refs):
    width = near_ref.shape[1]
    block = (out_refs[0].shape[0] - packed) // 2
    count = block * len(out_refs)
    parts = unpack(arrived_ref, count, count, held_ref.shape[1] - width)
    for i, out_ref in enumerate(out_refs):
        begin = (early + i) * block
        total, part = pair_sum(variables, width, held_ref, other_ref, begin, block)
        here = slice(i * block, (i + 1) * block)
        out_ref[0:block, :] = (total + arrived_ref[here, :].astype(f32)).astype(bf16)
        there = slice(count + packed + i * block, count + packed + (i + 1) * block)
        total = near_ref[begin : begin + block, :] + arrived_ref[there, :].astype(f32)
        out_ref[block : 2 * block, :] = total.astype(bf16)
        out_ref[2 * block :, :] = jnp.zeros((packed, width), bf16)
        pack(out_ref, 2 * block, split_loss(part + parts[here], variables).astype(bf16))


def back_kernel(inner_ref, w_hidden_ref, gain_ref, unit_ref, inverse_ref, grad_ref, scaled_ref):
    rows_all, width = inner_ref.shape
    gain = gain_ref[...].reshape(1, width)
    for begin_row in range(0, rows_all, tile):
        rows = slice(begin_row, begin_row + tile)
        dots = jnp.zeros((tile, 1), f32)
        for begin in range(0, width, tile):
            columns = slice(begin, begin + tile)
            scaled = mm(inner_ref[rows, :], w_hidden_ref[columns, :], 1, 1) * gain[:, columns]
            dots = dots + jnp.sum(scaled * unit_ref[rows, columns], axis=-1, keepdims=True)
            scaled_ref[rows, columns] = scaled
        dots = dots * (1.0 / width)
        inverse = inverse_ref[rows, :]
        for begin in range(0, width, tile):
            columns = slice(begin, begin + tile)
            grad_ref[rows, columns] = (
                (scaled_ref[rows, columns] - unit_ref[rows, columns] * dots) * inverse
            ).astype(bf16)


def slot_kernel(share_ref, grad_ref, slots_ref, *send_refs):
    peers, each, width = slots_ref.shape
    rows = peers * each
    for begin in range(0, width, tile):
        columns = slice(begin, begin + tile)
        both = mm(share_ref[...], grad_ref[:, columns], 1, 0)
        slots_ref[:, :, columns] = (both[:rows] + both[rows:]).astype(bf16).reshape(peers, each, tile)
    for i, send_ref in enumerate(send_refs):
        step = len(send_refs) - i
        send_ref[0:each, :] = slots_ref[2 * step]
        send_ref[each:, :] = slots_ref[2 * step + 1]


def owner_kernel(pick_ref, w_msg_ref, slots_ref, last_ref, *rest):
    arrived_refs, (grad_ref, token_ref, held_ref) = rest[:-3], rest[-3:]
    token_ref[...] = jnp.zeros_like(token_ref)
    peers, rows, width = slots_ref.shape
    levels = peers // 2
    begin = last_ref.shape[0] - levels * rows
    for i in range(levels):
        spot = 2 * (levels - 1 - i)
        held_ref[spot] = slots_ref[0] if i == levels - 1 else arrived_refs[i][0:rows, :]
        held_ref[spot + 1] = last_ref[begin + i * rows : begin + (i + 1) * rows, :]
    nodes = mm(pick_ref[...], held_ref[...].reshape(peers * rows, width), 0, 0).astype(bf16)
    grad_ref[...] = mm(nodes, w_msg_ref[...], 1, 1).astype(bf16).reshape(grad_ref.shape)


def hidden_sum_kernel(variables, scale, early, held_ref, other_ref, last_ref, *rest):
    hidden_ref, out_ref, loss_ref, token_ref = rest[-4:]
    token_ref[...] = jnp.zeros_like(token_ref)
    block, width = hidden_ref.shape
    pad = held_ref.shape[1] - width
    total, part = pair_sum(variables, width, held_ref, other_ref, held_ref.shape[0] - block, block)
    total = total + last_ref[0:block, :].astype(f32)
    part = part + unpack(last_ref, block, block, pad)
    for i, r in enumerate(rest[:-4]):
        total = total + r[0:block, :width].astype(f32)
        if i < early:
            part = part + r[:, width:].astype(f32)
        else:
            part = part + unpack(r, 2 * block, block, pad)
    hidden_ref[...] = total
    out_ref[...] = part[:, :variables]
    column = lax.broadcasted_iota(jnp.int32, (8, pad), 1)
    spots = (column == variables) | (column == variables + 1)
    first = lax.broadcasted_iota(jnp.int32, (8, pad), 0) == 0
    loss_ref[0] = jnp.sum(jnp.where(spots & first, part[:8], 0.0)) * scale


def message_sum_kernel(early, near_ref, last_ref, *rest):
    out_ref = rest[-1]
    block = out_ref.shape[0]
    total = near_ref[near_ref.shape[0] - block :, :]
    total = total + last_ref[block + packed : 2 * block + packed, :].astype(f32)
    for i, r in enumerate(rest[:-1]):
        begin = 0 if i < early else block
        total = total + r[begin : begin + block, :].astype(f32)
    out_ref[...] = total


def on_device(
    latents, grid_embed, norm_gain, w_msg, w_hidden, variable_projection, present_condition, verifying_field,
    cell_surface, send_rows, edge_slot, edge_dst, edge_weight,
):
    members, nodes, width = latents.shape
    points = grid_embed.shape[0]
    variables = variable_projection.shape[1]
    peers = lax.axis_size("space")
    cores = lax.axis_size("member")
    cap = send_rows.shape[2]
    rows_peer = members * cap
    rows_slot = peers * rows_peer
    rows_all = members * points
    levels = peers // 2
    block = width // (peers * cores)
    half = levels * block
    wide = width + -(-(variables + 2) // lanes) * lanes
    project = variable_projection.T

    early = levels // 2
    count, rest = early * block, (levels - 1 - early) * block
    steps = [2 * (levels - 1 - i) for i in range(levels - 1)]

    def spread(values, part):
        return [swap(x, "space", peers, k) for x, k in zip(values, part, strict=True)]

    pick, send, own_rows, *direct = call(
        select_kernel,
        [((rows_slot, members * nodes), bf16), ((levels, rows_peer, width), bf16)]
        + [((rows_peer, width), bf16)] * levels,
        [send_rows, latents],
        scratch=[
            pltpu.SMEM(send_rows.shape, jnp.int32),
            pltpu.VMEM(latents.shape, bf16),
            pltpu.SemaphoreType.DMA((2,)),
        ],
        limit=4,
        places=(0, 1),
    )
    near_rows = swap(send, "space", peers, 1)
    direct = spread(direct, steps)
    fixed = [w_msg, norm_gain, grid_embed, w_hidden, project, present_condition.transpose(1, 0, 2)]
    edges = [edge_slot, edge_dst, edge_weight]
    share, *staged = call(
        functools.partial(stage_kernel, cap, members, len(fixed)),
        [((2 * rows_slot, rows_all), bf16)] + [(x.shape, x.dtype) for x in fixed],
        edges + fixed,
        scratch=[pltpu.VMEM(x.shape, x.dtype) for x in edges]
        + [pltpu.SemaphoreType.DMA((3 + len(fixed),))],
        limit=16,
        places=tuple(range(3 + len(fixed))),
        after=[pick],
    )
    near_own, *forwarded = call(
        split_kernel,
        [((rows_peer, width), bf16)] * levels,
        [near_rows],
        limit=4,
        after=[share] + direct,
    )
    forwarded = spread(forwarded, steps)
    received = [own_rows, near_own]
    for x, y in zip(direct[::-1], forwarded[::-1], strict=True):
        received += [x, y]
    w_msg_near, gain, embed, w_hidden_near, project_near, present = staged
    field, sent, normed, active, slope, unit, inverse = call(
        functools.partial(forward_kernel, peers),
        [
            ((members, variables, points), f32),
            ((members, variables, points), bf16),
            ((rows_all, width), bf16),
            ((rows_all, width), bf16),
            ((rows_all, width), f32),
            ((rows_all, width), f32),
            ((rows_all, 1), f32),
        ],
        [w_msg_near, share, gain, embed, w_hidden_near, project_near, present] + received,
        limit=20,
    )
    other = swap(sent, "member", cores, 1)
    normed_t, active_t, received_keep, received_give = call(
        turn_kernel,
        [((cores, 2, levels, block, rows_all), bf16)] * 2 + [((2, levels, block, rows_slot), bf16)] * 2,
        [normed, active] + received,
        limit=8,
    )
    received_other = swap(received_give, "member", cores, 1)
    grad_inner, pred, loss_part, far, near = call(
        score_kernel,
        [
            ((rows_all, width), bf16),
            ((lanes, rows_all), bf16),
            ((1,), f32),
            ((half, wide), bf16),
            ((half, wide), bf16),
        ],
        [field, other, verifying_field, cell_surface, project_near, slope, normed_t, active_t],
        scratch=[pltpu.VMEM((lanes, rows_all), f32)],
        limit=16,
        scalar_outs=(2,),
    )
    far_other = swap(far, "member", cores, 1)
    near_other = swap(near, "member", cores, 1)
    held_far, held_near = call(
        functools.partial(local_kernel, variables),
        [((half, wide), f32)] * 2,
        [loss_part, normed_t, active_t, grad_inner, pred],
        limit=12,
        scalars=(0,),
    )
    (first,) = call(
        functools.partial(first_kernel, variables, width),
        [((count, wide), bf16)],
        [held_far, far_other],
        limit=6,
    )
    first_other = swap(first, "space", peers, 1)
    (grad_hidden,) = call(
        back_kernel,
        [((rows_all, width), bf16)],
        [grad_inner, w_hidden_near, gain, unit, inverse],
        scratch=[pltpu.VMEM((rows_all, width), f32)],
        limit=14,
        after=[first],
    )
    slots, *slots_sent = call(
        slot_kernel,
        [((peers, rows_peer, width), bf16)] + [((2 * rows_peer, width), bf16)] * (levels - 1),
        [share, grad_hidden],
        limit=6,
        after=[near_other, received_other],
    )
    slots_other = swap(slots, "member", cores, 1)
    slots_arrived = spread(slots_sent, steps)
    message_first, middle, last, message_near = call(
        functools.partial(message_kernel, variables, early, levels),
        [
            ((count, width), bf16),
            ((2 * rest + packed, width), bf16),
            ((2 * block + packed, width), bf16),
            ((half, width), f32),
        ],
        [received_keep, received_other, slots, slots_other, held_far, far_other],
        limit=10,
    )
    message_first_other = swap(message_first, "space", peers, 1)
    middle_other = swap(middle, "space", peers, 1)
    (last,) = call(
        ride_kernel,
        [((2 * block + packed + levels * rows_peer, width), bf16)],
        [last, slots] + slots_arrived,
        limit=4,
    )
    last_other = swap(last, "space", peers, 1)
    hidden_early = call(
        functools.partial(hidden_early_kernel, variables, width),
        [((block, wide), bf16)] * early,
        [held_near, near_other, first_other],
        limit=6,
    )
    hidden_parts = spread(hidden_early, steps[:early])
    message_early = call(
        message_early_kernel,
        [((block, width), bf16)] * early,
        [message_near, message_first_other],
        limit=6,
    )
    message_parts = spread(message_early, steps[:early])
    late = call(
        functools.partial(late_kernel, variables, early),
        [((2 * block + packed, width), bf16)] * (levels - 1 - early),
        [held_near, near_other, message_near, middle_other],
        limit=6,
    )
    late_parts = spread(late, steps[early:])
    token = ((8, lanes), f32)
    latent_grad, latent_done = call(
        owner_kernel,
        [(latents.shape, bf16), token],
        [pick, w_msg, slots, last_other] + slots_arrived,
        scratch=[pltpu.VMEM((peers, rows_peer, width), bf16)],
        limit=8,
    )
    hidden_weight_grad, out_weight_grad, loss, hidden_done = call(
        functools.partial(hidden_sum_kernel, variables, 1.0 / (points * peers * variables), early),
        [((block, width), f32), ((block, variables), f32), ((1,), f32), token],
        [held_near, near_other, last_other] + hidden_parts + late_parts,
        limit=8,
        scalar_outs=(2,),
        after=[latent_done],
    )
    (msg_weight_grad,) = call(
        functools.partial(message_sum_kernel, early),
        [((block, width), f32)],
        [message_near, last_other] + message_parts + late_parts,
        limit=6,
        after=[hidden_done],
    )
    return (latent_grad, loss, msg_weight_grad, hidden_weight_grad, out_weight_grad)


def solution(mesh):
    placed = (
        P(("groups", "member"), "space", None),
        P(("groups", "space"), None),
        P(),
        P(),
        P(),
        P(),
        P(("groups", "member"), None, "space"),
        P(None, ("groups", "space")),
        P(("groups", "space")),
        P("space", None, None),
        P("space"),
        P("space"),
        P("space"),
    )
    return jax.shard_map(
        on_device,
        mesh=mesh,
        in_specs=placed,
        out_specs=(
            P(("groups", "member"), "space", None),
            P("groups"),
            P(("groups", "space", "member"), None),
            P(("groups", "space", "member"), None),
            P(("groups", "space", "member"), None),
        ),
        check_vma=False,
    )
```

```python
import functools

import jax
import jax.numpy as jnp
from jax import lax
from jax.experimental import pallas as pl
from jax.experimental.pallas import tpu as pltpu
from jax.sharding import PartitionSpec as P

smoothing = 0.1
epsilon = 1e-06
tile = 256
lanes = 128
packed = 16
cost_hints = {"back_kernel": 8, "slot_kernel": 4, "hidden_early_kernel": 4}
f32 = jnp.float32
bf16 = jnp.bfloat16


def mm(left, right, left_dim, right_dim):
    return lax.dot_general(
        left, right, (((left_dim,), (right_dim,)), ((), ())), preferred_element_type=f32
    )


def call(body, outs, args, scratch=(), limit=16, scalars=(), scalar_outs=(), places=(), after=()):
    whole = pl.BlockSpec(memory_space=pltpu.VMEM)
    small = pl.BlockSpec(memory_space=pltpu.SMEM)
    far_place = pl.BlockSpec(memory_space=pltpu.HBM)
    any_place = pl.BlockSpec(memory_space=pl.ANY)
    count = len(after)
    cost = cost_hints.get(getattr(body, "func", body).__name__, 0) * 10**9
    args = [pltpu.with_memory_space_constraint(x, pltpu.HBM) if i in places else x for i, x in enumerate(args)]

    def inner(*refs):
        body(*refs[count:])

    specs = [small if i in scalars else far_place if i in places else whole for i in range(len(args))]
    return pl.pallas_call(
        inner if count else body,
        out_shape=[jax.ShapeDtypeStruct(dims, kind) for dims, kind in outs],
        in_specs=[any_place] * count + specs,
        out_specs=[small if i in scalar_outs else whole for i in range(len(outs))],
        scratch_shapes=scratch,
        compiler_params=pltpu.CompilerParams(vmem_limit_bytes=limit * 2**20),
        cost_estimate=pl.CostEstimate(flops=cost, bytes_accessed=0, transcendentals=0),
    )(*after, *args)


def place():
    space = lax.axis_index("space")
    return lax.div(space, 2), lax.rem(space, 2), lax.axis_index("member")


def swap(value, axis, size, step):
    return lax.ppermute(value, axis, [(i, i ^ step) for i in range(size)])


def select_kernel(lists_ref, latents_ref, pick_ref, own_ref, send_ref, small_ref, table_ref, sems):
    _, peers, cap = lists_ref.shape
    members, nodes, width = latents_ref.shape
    lists = pltpu.make_async_copy(lists_ref, small_ref, sems.at[0])
    table = pltpu.make_async_copy(latents_ref, table_ref, sems.at[1])
    lists.start()
    table.start()
    lists.wait()
    me = lax.axis_index("space")
    at = lax.broadcasted_iota(jnp.int32, (cap, members * nodes), 0)
    column = lax.broadcasted_iota(jnp.int32, (cap, members * nodes), 1)
    rows = []
    for step in range(peers):
        wanted = jnp.zeros((cap, members * nodes), jnp.int32)
        for j in range(cap):
            wanted = jnp.where(at == j, small_ref[0, me ^ step, j], wanted)
        for member in range(members):
            rows.append((column == wanted + member * nodes).astype(f32))
    pick = jnp.concatenate(rows, axis=0).astype(bf16)
    pick_ref[...] = pick
    table.wait()
    sent = mm(pick, table_ref[...].reshape(members * nodes, width), 1, 0)
    sent = sent.astype(bf16).reshape(peers // 2, 2, members * cap, width)
    own_ref[...] = sent[:, 0]
    send_ref[...] = sent[:, 1]


def merge_kernel(own_ref, arrived_ref, *out_refs):
    rows = own_ref.shape[1]
    for i, out_ref in enumerate(out_refs):
        step = len(out_refs) - i
        out_ref[0:rows, :] = own_ref[step]
        out_ref[rows:, :] = arrived_ref[step]


def stage_kernel(cap, members, count, *refs):
    edge_refs, source_refs, share_ref = refs[:3], refs[3 : 3 + count], refs[3 + count]
    staged_refs, held_refs, sems = refs[4 + count : 4 + 2 * count], refs[4 + 2 * count : -1], refs[-1]
    copies = [
        pltpu.make_async_copy(source, target, sems.at[i])
        for i, (source, target) in enumerate(
            zip(edge_refs + source_refs, held_refs + staged_refs, strict=True)
        )
    ]
    for copy in copies:
        copy.start()
    for copy in copies[:3]:
        copy.wait()
    edge_part(cap, members, *held_refs, share_ref)
    for copy in copies[3:]:
        copy.wait()


def edge_part(cap, members, slot_ref, dst_ref, weight_ref, share_ref):
    edges = slot_ref.shape[0]
    slot = slot_ref[...].reshape(1, edges)
    dst = dst_ref[...].reshape(1, edges)
    weight = weight_ref[...].reshape(1, edges)
    rows = share_ref.shape[0] // 2
    points = share_ref.shape[1] // members
    sender = lax.div(slot, cap)
    spot = (sender ^ lax.axis_index("space")) * (members * cap) + (slot - sender * cap)
    hit = lax.broadcasted_iota(jnp.int32, (rows, edges), 0) == spot
    into = (lax.broadcasted_iota(jnp.int32, (points, edges), 0) == dst).astype(f32).astype(bf16)
    high = weight.astype(bf16).astype(f32)
    table = mm(jnp.where(hit, high, 0.0).astype(bf16), into, 1, 1) + mm(
        jnp.where(hit, weight - high, 0.0).astype(bf16), into, 1, 1
    )
    table = table / jnp.sum(table, axis=0, keepdims=True)
    for member in range(members):
        high = table.astype(bf16)
        columns = slice(member * points, (member + 1) * points)
        share_ref[0:rows, columns] = high
        share_ref[rows : 2 * rows, columns] = (table - high.astype(f32)).astype(bf16)
        table = jnp.concatenate([table[rows - cap :], table[: rows - cap]], axis=0)


def gathered(own_ref, near_ref, far_refs):
    return jnp.concatenate([own_ref[0], near_ref[0]] + [r[...] for r in far_refs[::-1]], axis=0)


def forward_kernel(
    far, w_msg_ref, share_ref, gain_ref, embed_ref, weights_ref, project_ref, present_ref,
    own_ref, near_ref, *rest,
):
    far_refs = rest[:far]
    field_ref, sent_ref, normed_ref, active_ref, slope_ref, unit_ref, inverse_ref = rest[far:]
    points, width = embed_ref.shape
    variables, members, _ = present_ref.shape
    messages = mm(gathered(own_ref, near_ref, far_refs), w_msg_ref[...], 1, 0).astype(bf16)
    messages = jnp.concatenate([messages, messages], axis=0)
    gain = gain_ref[...].reshape(1, width)
    for begin in range(0, members * points, lanes):
        rows = slice(begin, begin + lanes)
        source = slice(begin % points, begin % points + lanes)
        hidden = embed_ref[source, :].astype(f32) + mm(share_ref[:, rows], messages, 0, 0)
        inverse = lax.rsqrt(jnp.mean(hidden * hidden, axis=-1, keepdims=True) + epsilon)
        unit = hidden * inverse
        unit_ref[rows, :] = unit
        inverse_ref[rows, :] = inverse
        normed_ref[rows, :] = (unit * gain).astype(bf16)
    root = 0.7978845608028654
    cubic = 0.044715
    for member in range(members):
        rows = slice(member * points, (member + 1) * points)
        for begin in range(0, width, tile):
            columns = slice(begin, begin + tile)
            inner = mm(normed_ref[rows, :], weights_ref[:, columns], 1, 0)
            square = inner * inner
            bend = jnp.tanh(inner * (root + root * cubic * square))
            half = 0.5 + 0.5 * bend
            active_ref[rows, columns] = (inner * half).astype(bf16)
            slope_ref[rows, columns] = half + (0.5 * inner) * (1.0 - bend * bend) * (
                root + 3.0 * root * cubic * square
            )
        field = present_ref[:, member, :] + mm(project_ref[...], active_ref[rows, :], 1, 1)
        field_ref[member] = field
        sent_ref[member] = field.astype(bf16)


def turn_kernel(normed_ref, active_ref, own_ref, near_ref, *rest):
    far_refs, (normed_t_ref, active_t_ref, keep_ref, give_ref) = rest[:-4], rest[-4:]
    _, _, levels, block, _ = normed_t_ref.shape
    width = normed_ref.shape[1]
    level, line, core = place()
    received = gathered(own_ref, near_ref, far_refs)
    for source, target in ((received, None), (normed_ref, normed_t_ref), (active_ref, active_t_ref)):
        for begin in range(0, width, tile):
            turned = source[:, begin : begin + tile].T
            for piece in range(0, tile, block):
                index = (begin + piece) // block
                far = (index // 2 % 2) ^ line
                step = (index // 4) ^ level
                side = (index % 2) ^ core
                value = turned[piece : piece + block]
                if target is not None:
                    target[side, 1 - far, levels - 1 - step] = value
                    continue
                for which, part_ref in enumerate((keep_ref, give_ref)):
                    @pl.when(side == which)
                    def _(part_ref=part_ref):
                        part_ref[1 - far, levels - 1 - step] = value


def split_loss(part, variables):
    column = lax.broadcasted_iota(jnp.int32, part.shape, 1)
    spots = (column == variables) | (column == variables + 1)
    total = jnp.sum(jnp.where(spots, part, 0.0), axis=1, keepdims=True)
    high = total.astype(bf16).astype(f32)
    return jnp.where(column == variables, high, jnp.where(column == variables + 1, total - high, part))


def score_kernel(
    own_ref, other_ref, truth_ref, cell_ref, project_ref, slope_ref, normed_t_ref, active_t_ref,
    inner_ref, pred_ref, loss_ref, far_ref, near_ref, hold_ref,
):
    members, variables, points = own_ref.shape
    width = slope_ref.shape[1]
    total = 2 * members
    pairs = total * (total - 1)

    def eased(delta):
        square = delta * delta + smoothing * smoothing
        inverse = lax.rsqrt(square)
        return square * inverse, delta * inverse

    truth, cell = truth_ref[...], cell_ref[...].reshape(1, points)
    own = [own_ref[m] for m in range(members)]
    other = [other_ref[m].astype(f32) for m in range(members)]
    score = jnp.zeros_like(truth)
    pulls = [jnp.zeros_like(truth) for _ in own]
    grads = []
    for m in range(members):
        size, sign = eased(own[m] - truth)
        score = score + size * (1.0 / total)
        grads.append(sign * (1.0 / total))
    for m in range(members):
        for n in range(m + 1, members):
            size, sign = eased(own[m] - own[n])
            score = score - size * (1.0 / pairs)
            pulls[m] = pulls[m] + sign
            pulls[n] = pulls[n] - sign
        for n in range(members):
            size, sign = eased(own[m] - other[n])
            score = score - size * (0.5 / pairs)
            pulls[m] = pulls[m] + sign
    loss = jnp.sum(score * cell)
    loss_ref[0] = loss
    hold_ref[...] = jnp.zeros_like(hold_ref)
    for m in range(members):
        grad = (grads[m] - pulls[m] * (1.0 / pairs)) * cell
        hold_ref[0:variables, m * points : (m + 1) * points] = grad
    pred = hold_ref[...].astype(bf16)
    pred_ref[...] = pred
    for m in range(members):
        rows = slice(m * points, (m + 1) * points)
        part = pred[:variables, rows]
        for begin in range(0, width, tile):
            columns = slice(begin, begin + tile)
            grad = mm(part, project_ref[:, columns], 0, 0)
            inner_ref[rows, columns] = (grad * slope_ref[rows, columns]).astype(bf16)
    weight_parts(normed_t_ref, active_t_ref, inner_ref, pred, loss, variables, 1, 0, far_ref)
    weight_parts(normed_t_ref, active_t_ref, inner_ref, pred, loss, variables, 1, 1, near_ref)


def weight_parts(normed_t_ref, active_t_ref, inner_ref, pred, loss, variables, side, half, out_ref):
    width = inner_ref.shape[1]
    depth = normed_t_ref.shape[-1]
    normed = normed_t_ref[side, half].reshape(-1, depth)
    for begin in range(0, width, tile):
        columns = slice(begin, begin + tile)
        out_ref[:, columns] = mm(normed, inner_ref[:, columns], 1, 0).astype(out_ref.dtype)
    part = mm(active_t_ref[side, half].reshape(-1, depth), pred, 1, 1)
    part = jnp.where(lax.broadcasted_iota(jnp.int32, part.shape, 1) == variables, loss, part)
    out_ref[:, width:] = split_loss(part, variables).astype(out_ref.dtype)


def pack(out_ref, begin, part):
    pad = part.shape[1]
    for i in range(part.shape[0] // packed):
        out_ref[begin : begin + packed, i * pad : (i + 1) * pad] = part[i * packed : (i + 1) * packed]


def unpack(in_ref, begin, count, pad):
    parts = [in_ref[begin : begin + packed, i * pad : (i + 1) * pad] for i in range(count // packed)]
    return jnp.concatenate(parts, axis=0).astype(f32)


def local_kernel(variables, loss_ref, normed_t_ref, active_t_ref, inner_ref, pred_ref, far_ref, near_ref):
    for half, out_ref in ((0, far_ref), (1, near_ref)):
        weight_parts(
            normed_t_ref, active_t_ref, inner_ref, pred_ref[...], loss_ref[0], variables, 0, half, out_ref
        )


def pair_sum(variables, width, held_ref, other_ref, begin, count):
    rows = slice(begin, begin + count)
    total = held_ref[rows, :width] + other_ref[rows, :width].astype(f32)
    part = held_ref[rows, width:] + other_ref[rows, width:].astype(f32)
    return total, split_loss(part, variables)


def first_kernel(variables, width, held_ref, other_ref, out_ref):
    total, part = pair_sum(variables, width, held_ref, other_ref, 0, out_ref.shape[0])
    out_ref[:, :width] = total.astype(bf16)
    out_ref[:, width:] = part.astype(bf16)


def message_kernel(
    variables, early, levels, keep_ref, give_ref, slots_ref, other_ref, held_ref, far_other_ref,
    first_ref, middle_ref, last_ref, near_ref,
):
    depth, width = keep_ref.shape[-1], near_ref.shape[1]
    block = near_ref.shape[0] // levels
    count, rest = early * block, (levels - 1 - early) * block
    for begin, size, out_ref in ((count, rest, middle_ref), (count + rest, block, last_ref)):
        total, part = pair_sum(variables, width, held_ref, far_other_ref, begin, size)
        out_ref[0:size, :] = total.astype(bf16)
        out_ref[size : size + packed, :] = jnp.zeros((packed, width), bf16)
        pack(out_ref, size, part.astype(bf16))
    for half in range(2):
        own = keep_ref[half].reshape(-1, depth)
        other = give_ref[half].reshape(-1, depth)
        for begin in range(0, width, tile):
            columns = slice(begin, begin + tile)
            here = slots_ref[:, :, columns].reshape(depth, tile)
            there = other_ref[:, :, columns].reshape(depth, tile)
            total = mm(own, here, 1, 0) + mm(other, there, 1, 0)
            if half == 0:
                total = total.astype(bf16)
                first_ref[:, columns] = total[:count]
                middle_ref[rest + packed :, columns] = total[count : count + rest]
                last_ref[block + packed :, columns] = total[count + rest :]
            else:
                near_ref[:, columns] = total


def ride_kernel(last_ref, slots_ref, *rest):
    arrived_refs, out_ref = rest[:-1], rest[-1]
    rows = slots_ref.shape[1]
    begin = last_ref.shape[0]
    out_ref[0:begin, :] = last_ref[...]
    for i, arrived_ref in enumerate(arrived_refs):
        out_ref[begin + i * rows : begin + (i + 1) * rows, :] = arrived_ref[rows:, :]
    out_ref[begin + len(arrived_refs) * rows :, :] = slots_ref[1]


def hidden_early_kernel(variables, width, held_ref, other_ref, arrived_ref, *out_refs):
    block = out_refs[0].shape[0]
    for i, out_ref in enumerate(out_refs):
        total, part = pair_sum(variables, width, held_ref, other_ref, i * block, block)
        here = slice(i * block, (i + 1) * block)
        out_ref[:, :width] = (total + arrived_ref[here, :width].astype(f32)).astype(bf16)
        part = split_loss(part + arrived_ref[here, width:].astype(f32), variables)
        out_ref[:, width:] = part.astype(bf16)


def message_early_kernel(begin, near_ref, arrived_ref, out_ref):
    here = slice(begin, begin + out_ref.shape[0])
    out_ref[...] = (near_ref[here, :] + arrived_ref[here, :].astype(f32)).astype(bf16)


def late_kernel(variables, early, held_ref, other_ref, near_ref, arrived_ref, *out_refs):
    width = near_ref.shape[1]
    block = (out_refs[0].shape[0] - packed) // 2
    count = block * len(out_refs)
    parts = unpack(arrived_ref, count, count, held_ref.shape[1] - width)
    for i, out_ref in enumerate(out_refs):
        begin = (early + i) * block
        total, part = pair_sum(variables, width, held_ref, other_ref, begin, block)
        here = slice(i * block, (i + 1) * block)
        out_ref[0:block, :] = (total + arrived_ref[here, :].astype(f32)).astype(bf16)
        there = slice(count + packed + i * block, count + packed + (i + 1) * block)
        total = near_ref[begin : begin + block, :] + arrived_ref[there, :].astype(f32)
        out_ref[block : 2 * block, :] = total.astype(bf16)
        out_ref[2 * block :, :] = jnp.zeros((packed, width), bf16)
        pack(out_ref, 2 * block, split_loss(part + parts[here], variables).astype(bf16))


def back_kernel(inner_ref, w_hidden_ref, gain_ref, unit_ref, inverse_ref, grad_ref, scaled_ref):
    rows_all, width = inner_ref.shape
    gain = gain_ref[...].reshape(1, width)
    for begin_row in range(0, rows_all, tile):
        rows = slice(begin_row, begin_row + tile)
        dots = jnp.zeros((tile, 1), f32)
        for begin in range(0, width, tile):
            columns = slice(begin, begin + tile)
            scaled = mm(inner_ref[rows, :], w_hidden_ref[columns, :], 1, 1) * gain[:, columns]
            dots = dots + jnp.sum(scaled * unit_ref[rows, columns], axis=-1, keepdims=True)
            scaled_ref[rows, columns] = scaled
        dots = dots * (1.0 / width)
        inverse = inverse_ref[rows, :]
        for begin in range(0, width, tile):
            columns = slice(begin, begin + tile)
            grad_ref[rows, columns] = (
                (scaled_ref[rows, columns] - unit_ref[rows, columns] * dots) * inverse
            ).astype(bf16)


def slot_kernel(share_ref, grad_ref, slots_ref, *send_refs):
    peers, each, width = slots_ref.shape
    rows = peers * each
    for begin in range(0, width, tile):
        columns = slice(begin, begin + tile)
        both = mm(share_ref[...], grad_ref[:, columns], 1, 0)
        slots_ref[:, :, columns] = (both[:rows] + both[rows:]).astype(bf16).reshape(peers, each, tile)
    for i, send_ref in enumerate(send_refs):
        step = len(send_refs) - i
        send_ref[0:each, :] = slots_ref[2 * step]
        send_ref[each:, :] = slots_ref[2 * step + 1]


def owner_kernel(pick_ref, w_msg_ref, slots_ref, last_ref, *rest):
    arrived_refs, (grad_ref, token_ref, held_ref) = rest[:-3], rest[-3:]
    token_ref[...] = jnp.zeros_like(token_ref)
    peers, rows, width = slots_ref.shape
    levels = peers // 2
    begin = last_ref.shape[0] - levels * rows
    for i in range(levels):
        spot = 2 * (levels - 1 - i)
        held_ref[spot] = slots_ref[0] if i == levels - 1 else arrived_refs[i][0:rows, :]
        held_ref[spot + 1] = last_ref[begin + i * rows : begin + (i + 1) * rows, :]
    nodes = mm(pick_ref[...], held_ref[...].reshape(peers * rows, width), 0, 0).astype(bf16)
    grad_ref[...] = mm(nodes, w_msg_ref[...], 1, 1).astype(bf16).reshape(grad_ref.shape)


def hidden_sum_kernel(variables, scale, early, held_ref, other_ref, last_ref, *rest):
    hidden_ref, out_ref, loss_ref, token_ref = rest[-4:]
    token_ref[...] = jnp.zeros_like(token_ref)
    block, width = hidden_ref.shape
    pad = held_ref.shape[1] - width
    total, part = pair_sum(variables, width, held_ref, other_ref, held_ref.shape[0] - block, block)
    total = total + last_ref[0:block, :].astype(f32)
    part = part + unpack(last_ref, block, block, pad)
    for i, r in enumerate(rest[:-4]):
        total = total + r[0:block, :width].astype(f32)
        if i < early:
            part = part + r[:, width:].astype(f32)
        else:
            part = part + unpack(r, 2 * block, block, pad)
    hidden_ref[...] = total
    out_ref[...] = part[:, :variables]
    column = lax.broadcasted_iota(jnp.int32, (8, pad), 1)
    spots = (column == variables) | (column == variables + 1)
    first = lax.broadcasted_iota(jnp.int32, (8, pad), 0) == 0
    loss_ref[0] = jnp.sum(jnp.where(spots & first, part[:8], 0.0)) * scale


def message_sum_kernel(early, near_ref, last_ref, *rest):
    out_ref = rest[-1]
    block = out_ref.shape[0]
    total = near_ref[near_ref.shape[0] - block :, :]
    total = total + last_ref[block + packed : 2 * block + packed, :].astype(f32)
    for i, r in enumerate(rest[:-1]):
        begin = 0 if i < early else block
        total = total + r[begin : begin + block, :].astype(f32)
    out_ref[...] = total


def on_device(
    latents, grid_embed, norm_gain, w_msg, w_hidden, variable_projection, present_condition, verifying_field,
    cell_surface, send_rows, edge_slot, edge_dst, edge_weight,
):
    members, nodes, width = latents.shape
    points = grid_embed.shape[0]
    variables = variable_projection.shape[1]
    peers = lax.axis_size("space")
    cores = lax.axis_size("member")
    cap = send_rows.shape[2]
    rows_peer = members * cap
    rows_slot = peers * rows_peer
    rows_all = members * points
    levels = peers // 2
    block = width // (peers * cores)
    half = levels * block
    wide = width + -(-(variables + 2) // lanes) * lanes
    project = variable_projection.T

    early = levels // 2
    count, rest = early * block, (levels - 1 - early) * block
    steps = [2 * (levels - 1 - i) for i in range(levels - 1)]

    def spread(values, part):
        return [swap(x, "space", peers, k) for x, k in zip(values, part, strict=True)]

    pick, own_rows, send = call(
        select_kernel,
        [((rows_slot, members * nodes), bf16)] + [((levels, rows_peer, width), bf16)] * 2,
        [send_rows, latents],
        scratch=[
            pltpu.SMEM(send_rows.shape, jnp.int32),
            pltpu.VMEM(latents.shape, bf16),
            pltpu.SemaphoreType.DMA((2,)),
        ],
        limit=4,
        places=(0, 1),
    )
    near_rows = swap(send, "space", peers, 1)
    fixed = [w_msg, norm_gain, grid_embed, w_hidden, project, present_condition.transpose(1, 0, 2)]
    edges = [edge_slot, edge_dst, edge_weight]
    share, *staged = call(
        functools.partial(stage_kernel, cap, members, len(fixed)),
        [((2 * rows_slot, rows_all), bf16)] + [(x.shape, x.dtype) for x in fixed],
        edges + fixed,
        scratch=[pltpu.VMEM(x.shape, x.dtype) for x in edges]
        + [pltpu.SemaphoreType.DMA((3 + len(fixed),))],
        limit=16,
        places=tuple(range(3 + len(fixed))),
        after=[pick],
    )
    merged = call(
        merge_kernel,
        [((2 * rows_peer, width), bf16)] * (levels - 1),
        [own_rows, near_rows],
        limit=4,
        after=[share],
    )
    received = [own_rows, near_rows] + spread(merged, steps)
    w_msg_near, gain, embed, w_hidden_near, project_near, present = staged
    field, sent, normed, active, slope, unit, inverse = call(
        functools.partial(forward_kernel, levels - 1),
        [
            ((members, variables, points), f32),
            ((members, variables, points), bf16),
            ((rows_all, width), bf16),
            ((rows_all, width), bf16),
            ((rows_all, width), f32),
            ((rows_all, width), f32),
            ((rows_all, 1), f32),
        ],
        [w_msg_near, share, gain, embed, w_hidden_near, project_near, present] + received,
        limit=20,
    )
    other = swap(sent, "member", cores, 1)
    normed_t, active_t, received_keep, received_give = call(
        turn_kernel,
        [((cores, 2, levels, block, rows_all), bf16)] * 2 + [((2, levels, block, rows_slot), bf16)] * 2,
        [normed, active] + received,
        limit=8,
    )
    received_other = swap(received_give, "member", cores, 1)
    grad_inner, pred, loss_part, far, near = call(
        score_kernel,
        [
            ((rows_all, width), bf16),
            ((lanes, rows_all), bf16),
            ((1,), f32),
            ((half, wide), bf16),
            ((half, wide), bf16),
        ],
        [field, other, verifying_field, cell_surface, project_near, slope, normed_t, active_t],
        scratch=[pltpu.VMEM((lanes, rows_all), f32)],
        limit=16,
        scalar_outs=(2,),
    )
    far_other = swap(far, "member", cores, 1)
    near_other = swap(near, "member", cores, 1)
    held_far, held_near = call(
        functools.partial(local_kernel, variables),
        [((half, wide), f32)] * 2,
        [loss_part, normed_t, active_t, grad_inner, pred],
        limit=12,
        scalars=(0,),
    )
    (first,) = call(
        functools.partial(first_kernel, variables, width),
        [((count, wide), bf16)],
        [held_far, far_other],
        limit=6,
    )
    first_other = swap(first, "space", peers, 1)
    (grad_hidden,) = call(
        back_kernel,
        [((rows_all, width), bf16)],
        [grad_inner, w_hidden_near, gain, unit, inverse],
        scratch=[pltpu.VMEM((rows_all, width), f32)],
        limit=14,
        after=[first],
    )
    slots, *slots_sent = call(
        slot_kernel,
        [((peers, rows_peer, width), bf16)] + [((2 * rows_peer, width), bf16)] * (levels - 1),
        [share, grad_hidden],
        limit=6,
        after=[near_other, received_other],
    )
    slots_other = swap(slots, "member", cores, 1)
    slots_arrived = spread(slots_sent, steps)
    message_first, middle, last, message_near = call(
        functools.partial(message_kernel, variables, early, levels),
        [
            ((count, width), bf16),
            ((2 * rest + packed, width), bf16),
            ((2 * block + packed, width), bf16),
            ((half, width), f32),
        ],
        [received_keep, received_other, slots, slots_other, held_far, far_other],
        limit=10,
    )
    message_first_other = swap(message_first, "space", peers, 1)
    middle_other = swap(middle, "space", peers, 1)
    hidden_early = call(
        functools.partial(hidden_early_kernel, variables, width),
        [((block, wide), bf16)] * early,
        [held_near, near_other, first_other],
        limit=6,
        after=[message_first] + slots_arrived,
    )
    hidden_parts = spread(hidden_early, steps[:early])
    message_parts, pieces = [], []
    for i in range(early):
        (piece,) = call(
            functools.partial(message_early_kernel, i * block),
            [((block, width), bf16)],
            [message_near, message_first_other],
            limit=6,
        )
        pieces.append(piece)
        message_parts.append(swap(piece, "space", peers, steps[i]))
    (last,) = call(
        ride_kernel,
        [((2 * block + packed + levels * rows_peer, width), bf16)],
        [last, slots] + slots_arrived,
        limit=4,
        after=[middle_other],
    )
    last_other = swap(last, "space", peers, 1)
    late = call(
        functools.partial(late_kernel, variables, early),
        [((2 * block + packed, width), bf16)] * (levels - 1 - early),
        [held_near, near_other, message_near, middle_other],
        limit=6,
        after=hidden_parts + pieces,
    )
    late_parts = spread(late, steps[early:])
    token = ((8, lanes), f32)
    latent_grad, latent_done = call(
        owner_kernel,
        [(latents.shape, bf16), token],
        [pick, w_msg, slots, last_other] + slots_arrived,
        scratch=[pltpu.VMEM((peers, rows_peer, width), bf16)],
        limit=8,
    )
    hidden_weight_grad, out_weight_grad, loss, hidden_done = call(
        functools.partial(hidden_sum_kernel, variables, 1.0 / (points * peers * variables), early),
        [((block, width), f32), ((block, variables), f32), ((1,), f32), token],
        [held_near, near_other, last_other] + hidden_parts + late_parts,
        limit=8,
        scalar_outs=(2,),
        after=[latent_done],
    )
    (msg_weight_grad,) = call(
        functools.partial(message_sum_kernel, early),
        [((block, width), f32)],
        [message_near, last_other] + message_parts + late_parts,
        limit=6,
        after=[hidden_done],
    )
    return (latent_grad, loss, msg_weight_grad, hidden_weight_grad, out_weight_grad)


def solution(mesh):
    placed = (
        P(("groups", "member"), "space", None),
        P(("groups", "space"), None),
        P(),
        P(),
        P(),
        P(),
        P(("groups", "member"), None, "space"),
        P(None, ("groups", "space")),
        P(("groups", "space")),
        P("space", None, None),
        P("space"),
        P("space"),
        P("space"),
    )
    return jax.shard_map(
        on_device,
        mesh=mesh,
        in_specs=placed,
        out_specs=(
            P(("groups", "member"), "space", None),
            P("groups"),
            P(("groups", "space", "member"), None),
            P(("groups", "space", "member"), None),
            P(("groups", "space", "member"), None),
        ),
        check_vma=False,
    )
```

```python
import functools

import jax
import jax.numpy as jnp
from jax import lax
from jax.experimental import pallas as pl
from jax.experimental.pallas import tpu as pltpu
from jax.sharding import PartitionSpec as P

smoothing = 0.1
epsilon = 1e-06
tile = 256
lanes = 128
packed = 16
cost_hints = {"partial_kernel": 4, "hidden_early_kernel": 4, "own_kernel": 8}
f32 = jnp.float32
bf16 = jnp.bfloat16


def mm(left, right, left_dim, right_dim):
    return lax.dot_general(
        left, right, (((left_dim,), (right_dim,)), ((), ())), preferred_element_type=f32
    )


def call(body, outs, args, scratch=(), limit=16, scalars=(), scalar_outs=(), places=(), after=()):
    whole = pl.BlockSpec(memory_space=pltpu.VMEM)
    small = pl.BlockSpec(memory_space=pltpu.SMEM)
    far_place = pl.BlockSpec(memory_space=pltpu.HBM)
    any_place = pl.BlockSpec(memory_space=pl.ANY)
    count = len(after)
    cost = cost_hints.get(getattr(body, "func", body).__name__, 0) * 10**9
    args = [pltpu.with_memory_space_constraint(x, pltpu.HBM) if i in places else x for i, x in enumerate(args)]

    def inner(*refs):
        body(*refs[count:])

    specs = [small if i in scalars else far_place if i in places else whole for i in range(len(args))]
    return pl.pallas_call(
        inner if count else body,
        out_shape=[jax.ShapeDtypeStruct(dims, kind) for dims, kind in outs],
        in_specs=[any_place] * count + specs,
        out_specs=[small if i in scalar_outs else whole for i in range(len(outs))],
        scratch_shapes=scratch,
        compiler_params=pltpu.CompilerParams(vmem_limit_bytes=limit * 2**20),
        cost_estimate=pl.CostEstimate(flops=cost, bytes_accessed=0, transcendentals=0),
    )(*after, *args)


def place():
    space = lax.axis_index("space")
    return lax.div(space, 2), lax.rem(space, 2), lax.axis_index("member")


def swap(value, axis, size, step):
    return lax.ppermute(value, axis, [(i, i ^ step) for i in range(size)])


def select_kernel(lists_ref, latents_ref, pick_ref, own_ref, send_ref, small_ref, table_ref, sems):
    _, peers, cap = lists_ref.shape
    members, nodes, width = latents_ref.shape
    lists = pltpu.make_async_copy(lists_ref, small_ref, sems.at[0])
    table = pltpu.make_async_copy(latents_ref, table_ref, sems.at[1])
    lists.start()
    table.start()
    lists.wait()
    me = lax.axis_index("space")
    at = lax.broadcasted_iota(jnp.int32, (cap, members * nodes), 0)
    column = lax.broadcasted_iota(jnp.int32, (cap, members * nodes), 1)
    rows = []
    for step in range(peers):
        wanted = jnp.zeros((cap, members * nodes), jnp.int32)
        for j in range(cap):
            wanted = jnp.where(at == j, small_ref[0, me ^ step, j], wanted)
        for member in range(members):
            rows.append((column == wanted + member * nodes).astype(f32))
    pick = jnp.concatenate(rows, axis=0).astype(bf16)
    pick_ref[...] = pick
    table.wait()
    sent = mm(pick, table_ref[...].reshape(members * nodes, width), 1, 0)
    sent = sent.astype(bf16).reshape(peers // 2, 2, members * cap, width)
    own_ref[...] = sent[:, 0]
    send_ref[...] = sent[:, 1]


def merge_kernel(own_ref, arrived_ref, *out_refs):
    rows = own_ref.shape[1]
    for i, out_ref in enumerate(out_refs):
        step = len(out_refs) - i
        out_ref[0:rows, :] = own_ref[step]
        out_ref[rows:, :] = arrived_ref[step]


def stage_kernel(cap, members, count, *refs):
    edge_refs, source_refs, share_ref = refs[:3], refs[3 : 3 + count], refs[3 + count]
    staged_refs, held_refs, sems = refs[4 + count : 4 + 2 * count], refs[4 + 2 * count : -1], refs[-1]
    copies = [
        pltpu.make_async_copy(source, target, sems.at[i])
        for i, (source, target) in enumerate(
            zip(edge_refs + source_refs, held_refs + staged_refs, strict=True)
        )
    ]
    for copy in copies:
        copy.start()
    for copy in copies[:3]:
        copy.wait()
    edge_part(cap, members, *held_refs, share_ref)
    for copy in copies[3:]:
        copy.wait()


def edge_part(cap, members, slot_ref, dst_ref, weight_ref, share_ref):
    edges = slot_ref.shape[0]
    slot = slot_ref[...].reshape(1, edges)
    dst = dst_ref[...].reshape(1, edges)
    weight = weight_ref[...].reshape(1, edges)
    rows = share_ref.shape[0] // 2
    points = share_ref.shape[1] // members
    sender = lax.div(slot, cap)
    spot = (sender ^ lax.axis_index("space")) * (members * cap) + (slot - sender * cap)
    hit = lax.broadcasted_iota(jnp.int32, (rows, edges), 0) == spot
    into = (lax.broadcasted_iota(jnp.int32, (points, edges), 0) == dst).astype(f32).astype(bf16)
    high = weight.astype(bf16).astype(f32)
    table = mm(jnp.where(hit, high, 0.0).astype(bf16), into, 1, 1) + mm(
        jnp.where(hit, weight - high, 0.0).astype(bf16), into, 1, 1
    )
    table = table / jnp.sum(table, axis=0, keepdims=True)
    for member in range(members):
        high = table.astype(bf16)
        columns = slice(member * points, (member + 1) * points)
        share_ref[0:rows, columns] = high
        share_ref[rows : 2 * rows, columns] = (table - high.astype(f32)).astype(bf16)
        table = jnp.concatenate([table[rows - cap :], table[: rows - cap]], axis=0)


def gathered(own_ref, near_ref, far_refs):
    return jnp.concatenate([own_ref[0], near_ref[0]] + [r[...] for r in far_refs[::-1]], axis=0)


def forward_kernel(
    far, w_msg_ref, share_ref, gain_ref, embed_ref, weights_ref, project_ref, present_ref,
    own_ref, near_ref, *rest,
):
    far_refs = rest[:far]
    field_ref, sent_ref, normed_ref, active_ref, slope_ref, unit_ref, inverse_ref = rest[far:]
    points, width = embed_ref.shape
    variables, members, _ = present_ref.shape
    messages = mm(gathered(own_ref, near_ref, far_refs), w_msg_ref[...], 1, 0).astype(bf16)
    messages = jnp.concatenate([messages, messages], axis=0)
    gain = gain_ref[...].reshape(1, width)
    for begin in range(0, members * points, lanes):
        rows = slice(begin, begin + lanes)
        source = slice(begin % points, begin % points + lanes)
        hidden = embed_ref[source, :].astype(f32) + mm(share_ref[:, rows], messages, 0, 0)
        inverse = lax.rsqrt(jnp.mean(hidden * hidden, axis=-1, keepdims=True) + epsilon)
        unit = hidden * inverse
        unit_ref[rows, :] = unit
        inverse_ref[rows, :] = inverse
        normed_ref[rows, :] = (unit * gain).astype(bf16)
    root = 0.7978845608028654
    cubic = 0.044715
    for member in range(members):
        rows = slice(member * points, (member + 1) * points)
        for begin in range(0, width, tile):
            columns = slice(begin, begin + tile)
            inner = mm(normed_ref[rows, :], weights_ref[:, columns], 1, 0)
            square = inner * inner
            bend = jnp.tanh(inner * (root + root * cubic * square))
            half = 0.5 + 0.5 * bend
            active_ref[rows, columns] = (inner * half).astype(bf16)
            slope_ref[rows, columns] = half + (0.5 * inner) * (1.0 - bend * bend) * (
                root + 3.0 * root * cubic * square
            )
        field = present_ref[:, member, :] + mm(project_ref[...], active_ref[rows, :], 1, 1)
        field_ref[member] = field
        sent_ref[member] = field.astype(bf16)


def halving_place(step, levels):
    bits = levels.bit_length() - 1
    return sum((1 - ((step >> bit) & 1)) << (bits - 1 - bit) for bit in range(bits))


def turn_kernel(normed_ref, active_ref, own_ref, near_ref, *rest):
    far_refs, (normed_t_ref, active_t_ref, keep_ref, give_ref) = rest[:-4], rest[-4:]
    _, _, levels, block, _ = normed_t_ref.shape
    width = normed_ref.shape[1]
    level, line, core = place()
    received = gathered(own_ref, near_ref, far_refs)
    for source, target in ((received, None), (normed_ref, normed_t_ref), (active_ref, active_t_ref)):
        for begin in range(0, width, tile):
            turned = source[:, begin : begin + tile].T
            for piece in range(0, tile, block):
                index = (begin + piece) // block
                far = (index // 2 % 2) ^ line
                step = (index // 4) ^ level
                side = (index % 2) ^ core
                value = turned[piece : piece + block]
                if target is not None:
                    target[side, 1 - far, levels - 1 - step] = value
                    continue
                spot = halving_place(step, levels)
                for which, part_ref in enumerate((keep_ref, give_ref)):
                    @pl.when(side == which)
                    def _(part_ref=part_ref):
                        part_ref[1 - far, spot] = value


def split_loss(part, variables):
    column = lax.broadcasted_iota(jnp.int32, part.shape, 1)
    spots = (column == variables) | (column == variables + 1)
    total = jnp.sum(jnp.where(spots, part, 0.0), axis=1, keepdims=True)
    high = total.astype(bf16).astype(f32)
    return jnp.where(column == variables, high, jnp.where(column == variables + 1, total - high, part))


def score_kernel(
    own_ref, other_ref, truth_ref, cell_ref, project_ref, slope_ref, normed_t_ref, active_t_ref,
    inner_ref, pred_ref, loss_ref, far_ref, near_ref, hold_ref,
):
    members, variables, points = own_ref.shape
    width = slope_ref.shape[1]
    total = 2 * members
    pairs = total * (total - 1)

    def eased(delta):
        square = delta * delta + smoothing * smoothing
        inverse = lax.rsqrt(square)
        return square * inverse, delta * inverse

    truth, cell = truth_ref[...], cell_ref[...].reshape(1, points)
    own = [own_ref[m] for m in range(members)]
    other = [other_ref[m].astype(f32) for m in range(members)]
    score = jnp.zeros_like(truth)
    pulls = [jnp.zeros_like(truth) for _ in own]
    grads = []
    for m in range(members):
        size, sign = eased(own[m] - truth)
        score = score + size * (1.0 / total)
        grads.append(sign * (1.0 / total))
    for m in range(members):
        for n in range(m + 1, members):
            size, sign = eased(own[m] - own[n])
            score = score - size * (1.0 / pairs)
            pulls[m] = pulls[m] + sign
            pulls[n] = pulls[n] - sign
        for n in range(members):
            size, sign = eased(own[m] - other[n])
            score = score - size * (0.5 / pairs)
            pulls[m] = pulls[m] + sign
    loss = jnp.sum(score * cell)
    loss_ref[0] = loss
    hold_ref[...] = jnp.zeros_like(hold_ref)
    for m in range(members):
        grad = (grads[m] - pulls[m] * (1.0 / pairs)) * cell
        hold_ref[0:variables, m * points : (m + 1) * points] = grad
    pred = hold_ref[...].astype(bf16)
    pred_ref[...] = pred
    for m in range(members):
        rows = slice(m * points, (m + 1) * points)
        part = pred[:variables, rows]
        for begin in range(0, width, tile):
            columns = slice(begin, begin + tile)
            grad = mm(part, project_ref[:, columns], 0, 0)
            inner_ref[rows, columns] = (grad * slope_ref[rows, columns]).astype(bf16)
    weight_parts(normed_t_ref, active_t_ref, inner_ref, pred, loss, variables, 1, 0, far_ref)
    weight_parts(normed_t_ref, active_t_ref, inner_ref, pred, loss, variables, 1, 1, near_ref)


def weight_parts(normed_t_ref, active_t_ref, inner_ref, pred, loss, variables, side, half, out_ref):
    width = inner_ref.shape[1]
    depth = normed_t_ref.shape[-1]
    normed = normed_t_ref[side, half].reshape(-1, depth)
    for begin in range(0, width, tile):
        columns = slice(begin, begin + tile)
        out_ref[:, columns] = mm(normed, inner_ref[:, columns], 1, 0).astype(out_ref.dtype)
    part = mm(active_t_ref[side, half].reshape(-1, depth), pred, 1, 1)
    part = jnp.where(lax.broadcasted_iota(jnp.int32, part.shape, 1) == variables, loss, part)
    out_ref[:, width:] = split_loss(part, variables).astype(out_ref.dtype)


def pack(out_ref, begin, part):
    pad = part.shape[1]
    for i in range(part.shape[0] // packed):
        out_ref[begin : begin + packed, i * pad : (i + 1) * pad] = part[i * packed : (i + 1) * packed]


def unpack(in_ref, begin, count, pad):
    parts = [in_ref[begin : begin + packed, i * pad : (i + 1) * pad] for i in range(count // packed)]
    return jnp.concatenate(parts, axis=0).astype(f32)


def local_kernel(variables, loss_ref, normed_t_ref, active_t_ref, inner_ref, pred_ref, far_ref, near_ref):
    for half, out_ref in ((0, far_ref), (1, near_ref)):
        weight_parts(
            normed_t_ref, active_t_ref, inner_ref, pred_ref[...], loss_ref[0], variables, 0, half, out_ref
        )


def pair_sum(variables, width, held_ref, other_ref, begin, count):
    rows = slice(begin, begin + count)
    total = held_ref[rows, :width] + other_ref[rows, :width].astype(f32)
    part = held_ref[rows, width:] + other_ref[rows, width:].astype(f32)
    return total, split_loss(part, variables)


def first_kernel(variables, width, held_ref, other_ref, out_ref):
    total, part = pair_sum(variables, width, held_ref, other_ref, 0, out_ref.shape[0])
    out_ref[:, :width] = total.astype(bf16)
    out_ref[:, width:] = part.astype(bf16)


def across_kernel(variables, begin, near_ref, near_other_ref, far_ref, far_other_ref, *out_refs):
    width = out_refs[0].shape[1]
    block = out_refs[0].shape[0] // 2 - packed
    for i, out_ref in enumerate(out_refs):
        for line, (held_ref, other_ref) in enumerate(((near_ref, near_other_ref), (far_ref, far_other_ref))):
            total, part = pair_sum(variables, width, held_ref, other_ref, begin + i * block, block)
            at = line * (block + packed)
            out_ref[at : at + block, :] = total.astype(bf16)
            out_ref[at + block : at + block + packed, :] = jnp.zeros((packed, width), bf16)
            pack(out_ref, at + block, part.astype(bf16))


def message_kernel(keep_ref, give_ref, slots_ref, other_ref, first_ref, second_ref, near_ref, slot_far_ref):
    depth, width = keep_ref.shape[-1], near_ref.shape[1]
    slot_far_ref[...] = slots_ref[slots_ref.shape[0] // 2 :]
    count = first_ref.shape[0]
    for half in range(2):
        own = keep_ref[half].reshape(-1, depth)
        other = give_ref[half].reshape(-1, depth)
        for begin in range(0, width, tile):
            columns = slice(begin, begin + tile)
            here = slots_ref[:, :, columns].reshape(depth, tile)
            there = other_ref[:, :, columns].reshape(depth, tile)
            total = mm(own, here, 1, 0) + mm(other, there, 1, 0)
            if half == 0:
                first_ref[:, columns] = total[:count].astype(bf16)
                second_ref[:, columns] = total[count:].astype(bf16)
            else:
                near_ref[:, columns] = total


def second_kernel(source_ref, out_ref):
    out_ref[...] = source_ref[...]


def step_kernel(near_ref, arrived_ref, out_ref):
    count = out_ref.shape[0]
    out_ref[...] = (near_ref[0:count, :] + arrived_ref[...].astype(f32)).astype(bf16)


def halve_kernel(begin, near_ref, *rest):
    arrived_refs, (send_ref, keep_ref) = rest[:-2], rest[-2:]
    count = send_ref.shape[0]
    for at, out_ref in ((0, send_ref), (count, keep_ref)):
        total = near_ref[begin + at : begin + at + count, :]
        for r in arrived_refs:
            total = total + r[at : at + count, :].astype(f32)
        out_ref[...] = total.astype(out_ref.dtype)


def own_kernel(variables, width, held_ref, other_ref, *rest):
    arrived_refs, out_ref = rest[:-1], rest[-1]
    block = out_ref.shape[0]
    total, part = pair_sum(variables, width, held_ref, other_ref, held_ref.shape[0] - block, block)
    for r in arrived_refs:
        at = block + packed
        total = total + r[at : at + block, :].astype(f32)
        part = part + unpack(r, at + block, block, part.shape[1])
    out_ref[:, :width] = total
    out_ref[:, width:] = split_loss(part, variables)


def fold_kernel(kept_ref, arrived_ref, send_ref, keep_ref):
    half, _, rows, _ = keep_ref.shape
    count = arrived_ref.shape[1]
    for at, out_ref in ((0, keep_ref), (half, send_ref)):
        for i in range(half):
            for j in range(count):
                out_ref[i, j] = kept_ref[at + i, j]
                out_ref[i, count + j] = arrived_ref[at + i, j]


def last_kernel(hidden_ref, out_ref):
    width = out_ref.shape[1]
    block = hidden_ref.shape[0]
    out_ref[0:block, :] = hidden_ref[:, :width].astype(bf16)
    out_ref[block:, :] = jnp.zeros((packed, width), bf16)
    pack(out_ref, block, hidden_ref[:, width:].astype(bf16))


def across_line_kernel(kept_ref, arrived_ref, out_ref):
    count = kept_ref.shape[1]
    for j in range(count):
        out_ref[j] = kept_ref[1, j]
        out_ref[count + j] = arrived_ref[1, j]


def hidden_early_kernel(variables, width, held_ref, other_ref, arrived_ref, *out_refs):
    block = out_refs[0].shape[0]
    for i, out_ref in enumerate(out_refs):
        total, part = pair_sum(variables, width, held_ref, other_ref, i * block, block)
        here = slice(i * block, (i + 1) * block)
        out_ref[:, :width] = (total + arrived_ref[here, :width].astype(f32)).astype(bf16)
        part = split_loss(part + arrived_ref[here, width:].astype(f32), variables)
        out_ref[:, width:] = part.astype(bf16)


def back_kernel(inner_ref, w_hidden_ref, gain_ref, unit_ref, inverse_ref, grad_ref, scaled_ref):
    rows_all, width = inner_ref.shape
    gain = gain_ref[...].reshape(1, width)
    for begin_row in range(0, rows_all, tile):
        rows = slice(begin_row, begin_row + tile)
        dots = jnp.zeros((tile, 1), f32)
        for begin in range(0, width, tile):
            columns = slice(begin, begin + tile)
            scaled = mm(inner_ref[rows, :], w_hidden_ref[columns, :], 1, 1) * gain[:, columns]
            dots = dots + jnp.sum(scaled * unit_ref[rows, columns], axis=-1, keepdims=True)
            scaled_ref[rows, columns] = scaled
        dots = dots * (1.0 / width)
        inverse = inverse_ref[rows, :]
        for begin in range(0, width, tile):
            columns = slice(begin, begin + tile)
            grad_ref[rows, columns] = (
                (scaled_ref[rows, columns] - unit_ref[rows, columns] * dots) * inverse
            ).astype(bf16)


def slot_kernel(share_ref, grad_ref, slots_ref):
    peers, each, width = slots_ref.shape
    rows = peers * each
    for begin in range(0, width, tile):
        columns = slice(begin, begin + tile)
        both = mm(share_ref[...], grad_ref[:, columns], 1, 0)
        slots_ref[:, :, columns] = (both[:rows] + both[rows:]).astype(bf16).reshape(peers, each, tile)


def owner_kernel(pick_ref, w_msg_ref, kept_ref, arrived_ref, line_ref, grad_ref, token_ref, held_ref):
    token_ref[...] = jnp.zeros_like(token_ref)
    peers, rows, width = held_ref.shape
    count = kept_ref.shape[1]
    order = [0]
    for bit in reversed(range(peers.bit_length() - 1)):
        order += [x ^ (1 << bit) for x in order]
    for j in range(count):
        held_ref[order[j]] = kept_ref[0, j]
        held_ref[order[count + j]] = arrived_ref[0, j]
    for j in range(2 * count):
        held_ref[order[2 * count + j]] = line_ref[j]
    nodes = mm(pick_ref[...], held_ref[...].reshape(peers * rows, width), 0, 0).astype(bf16)
    grad_ref[...] = mm(nodes, w_msg_ref[...], 1, 1).astype(bf16).reshape(grad_ref.shape)


def partial_kernel(variables, width, early, held_ref, other_ref, *rest):
    arrived_refs, out_ref = rest[:-1], rest[-1]
    block = out_ref.shape[0]
    total, part = pair_sum(variables, width, held_ref, other_ref, held_ref.shape[0] - block, block)
    for i, r in enumerate(arrived_refs):
        total = total + r[0:block, :width].astype(f32)
        if i < early:
            part = part + r[:, width:].astype(f32)
        else:
            part = part + unpack(r, block, block, part.shape[1])
    out_ref[:, :width] = total
    out_ref[:, width:] = part


def hidden_sum_kernel(variables, scale, partial_ref, last_ref, hidden_ref, out_ref, loss_ref, token_ref):
    token_ref[...] = jnp.zeros_like(token_ref)
    block, width = hidden_ref.shape
    pad = partial_ref.shape[1] - width
    part = partial_ref[:, width:] + unpack(last_ref, block, block, pad)
    hidden_ref[...] = partial_ref[:, :width] + last_ref[0:block, :].astype(f32)
    out_ref[...] = part[:, :variables]
    column = lax.broadcasted_iota(jnp.int32, (8, pad), 1)
    spots = (column == variables) | (column == variables + 1)
    first = lax.broadcasted_iota(jnp.int32, (8, pad), 0) == 0
    loss_ref[0] = jnp.sum(jnp.where(spots & first, part[:8], 0.0)) * scale


def message_sum_kernel(keep_ref, arrived_ref, out_ref):
    out_ref[...] = keep_ref[...] + arrived_ref[...].astype(f32)


def on_device(
    latents, grid_embed, norm_gain, w_msg, w_hidden, variable_projection, present_condition, verifying_field,
    cell_surface, send_rows, edge_slot, edge_dst, edge_weight,
):
    members, nodes, width = latents.shape
    points = grid_embed.shape[0]
    variables = variable_projection.shape[1]
    peers = lax.axis_size("space")
    cores = lax.axis_size("member")
    cap = send_rows.shape[2]
    rows_peer = members * cap
    rows_slot = peers * rows_peer
    rows_all = members * points
    levels = peers // 2
    block = width // (peers * cores)
    half = levels * block
    wide = width + -(-(variables + 2) // lanes) * lanes
    project = variable_projection.T

    early = levels // 2
    count, rest = early * block, (levels - 1 - early) * block
    steps = [2 * (levels - 1 - i) for i in range(levels - 1)]

    def spread(values, part):
        return [swap(x, "space", peers, k) for x, k in zip(values, part, strict=True)]

    pick, own_rows, send = call(
        select_kernel,
        [((rows_slot, members * nodes), bf16)] + [((levels, rows_peer, width), bf16)] * 2,
        [send_rows, latents],
        scratch=[
            pltpu.SMEM(send_rows.shape, jnp.int32),
            pltpu.VMEM(latents.shape, bf16),
            pltpu.SemaphoreType.DMA((2,)),
        ],
        limit=4,
        places=(0, 1),
    )
    near_rows = swap(send, "space", peers, 1)
    fixed = [w_msg, norm_gain, grid_embed, w_hidden, project, present_condition.transpose(1, 0, 2)]
    edges = [edge_slot, edge_dst, edge_weight]
    share, *staged = call(
        functools.partial(stage_kernel, cap, members, len(fixed)),
        [((2 * rows_slot, rows_all), bf16)] + [(x.shape, x.dtype) for x in fixed],
        edges + fixed,
        scratch=[pltpu.VMEM(x.shape, x.dtype) for x in edges]
        + [pltpu.SemaphoreType.DMA((3 + len(fixed),))],
        limit=16,
        places=tuple(range(3 + len(fixed))),
        after=[pick],
    )
    merged = call(
        merge_kernel,
        [((2 * rows_peer, width), bf16)] * (levels - 1),
        [own_rows, near_rows],
        limit=4,
        after=[share],
    )
    received = [own_rows, near_rows] + spread(merged, steps)
    w_msg_near, gain, embed, w_hidden_near, project_near, present = staged
    field, sent, normed, active, slope, unit, inverse = call(
        functools.partial(forward_kernel, levels - 1),
        [
            ((members, variables, points), f32),
            ((members, variables, points), bf16),
            ((rows_all, width), bf16),
            ((rows_all, width), bf16),
            ((rows_all, width), f32),
            ((rows_all, width), f32),
            ((rows_all, 1), f32),
        ],
        [w_msg_near, share, gain, embed, w_hidden_near, project_near, present] + received,
        limit=20,
    )
    other = swap(sent, "member", cores, 1)
    normed_t, active_t, received_keep, received_give = call(
        turn_kernel,
        [((cores, 2, levels, block, rows_all), bf16)] * 2 + [((2, levels, block, rows_slot), bf16)] * 2,
        [normed, active] + received,
        limit=8,
    )
    received_other = swap(received_give, "member", cores, 1)
    grad_inner, pred, loss_part, far, near = call(
        score_kernel,
        [
            ((rows_all, width), bf16),
            ((lanes, rows_all), bf16),
            ((1,), f32),
            ((half, wide), bf16),
            ((half, wide), bf16),
        ],
        [field, other, verifying_field, cell_surface, project_near, slope, normed_t, active_t],
        scratch=[pltpu.VMEM((lanes, rows_all), f32)],
        limit=16,
        scalar_outs=(2,),
    )
    far_other = swap(far, "member", cores, 1)
    near_other = swap(near, "member", cores, 1)
    held_far, held_near = call(
        functools.partial(local_kernel, variables),
        [((half, wide), f32)] * 2,
        [loss_part, normed_t, active_t, grad_inner, pred],
        limit=12,
        scalars=(0,),
    )
    (first,) = call(
        functools.partial(first_kernel, variables, width),
        [((count, wide), bf16)],
        [held_far, far_other],
        limit=6,
    )
    first_other = swap(first, "space", peers, 1)
    across = call(
        functools.partial(across_kernel, variables, count),
        [((2 * block + 2 * packed, width), bf16)] * (levels - 1 - early),
        [held_near, near_other, held_far, far_other],
        limit=6,
        after=[first],
    )
    across_parts = spread(across, steps[early:])
    (grad_hidden,) = call(
        back_kernel,
        [((rows_all, width), bf16)],
        [grad_inner, w_hidden_near, gain, unit, inverse],
        scratch=[pltpu.VMEM((rows_all, width), f32)],
        limit=14,
        after=[across[0]],
    )
    (slots,) = call(
        slot_kernel,
        [((peers, rows_peer, width), bf16)],
        [share, grad_hidden],
        limit=6,
        after=[received_other],
    )
    slots_other = swap(slots, "member", cores, 1)
    message_first, message_second, message_near, slots_sent = call(
        message_kernel,
        [((half // 2, width), bf16)] * 2
        + [((half, width), f32)]
        + [((levels, rows_peer, width), bf16)],
        [received_keep, received_other, slots, slots_other],
        limit=10,
    )
    message_first_other = swap(message_first, "space", peers, 1)
    (hidden_own,) = call(
        functools.partial(own_kernel, variables, width),
        [((block, wide), f32)],
        [held_far, far_other] + across_parts,
        limit=4,
        after=[first_other],
    )
    slots_kept = slots.reshape(peers, 1, rows_peer, width)
    slots_sent = slots_sent.reshape(levels, 1, rows_peer, width)
    bit = levels
    slots_other = swap(slots_sent, "space", peers, bit)
    hidden_early = call(
        functools.partial(hidden_early_kernel, variables, width),
        [((block, wide), bf16)] * early,
        [held_near, near_other, first_other],
        limit=6,
        after=[message_first, hidden_own, slots_other],
    )
    hidden_parts = spread(hidden_early, steps[:early])
    (message_step,) = call(
        step_kernel,
        [((half // 2, width), bf16)],
        [message_near, message_first_other],
        limit=4,
        after=hidden_early[:1],
    )
    message_other = swap(message_step, "space", peers, 2)
    (message_second,) = call(
        second_kernel, [((half // 2, width), bf16)], [message_second], limit=4, after=[message_step]
    )
    message_second_other = swap(message_second, "space", peers, 1)
    while bit > 2:
        folded = (bit // 2, 2 * levels // bit, rows_peer, width)
        slots_sent, slots_kept = call(
            fold_kernel, [(folded, bf16)] * 2, [slots_kept, slots_other], limit=4, after=[message_second]
        )
        bit //= 2
        slots_other = swap(slots_sent, "space", peers, bit)
    (partial,) = call(
        functools.partial(partial_kernel, variables, width, early),
        [((block, wide), f32)],
        [held_near, near_other] + hidden_parts + across_parts,
        limit=4,
    )
    (last,) = call(
        last_kernel,
        [((block + packed, width), bf16)],
        [hidden_own],
        limit=4,
        after=[message_second],
    )
    (line_slots,) = call(
        across_line_kernel,
        [((levels, rows_peer, width), bf16)],
        [slots_kept, slots_other],
        limit=4,
    )
    line_other = swap(line_slots, "space", peers, 1)
    last_other = swap(last, "space", peers, 1)
    message_send, message_keep = call(
        functools.partial(halve_kernel, half // 2),
        [((half // 4, width), bf16), ((half // 4, width), f32)],
        [message_near, message_second_other, message_other],
        limit=4,
        after=[partial],
    )
    bit = 4
    while bit < peers // 2:
        message_other = swap(message_send, "space", peers, bit)
        rows_left = message_send.shape[0] // 2
        message_send, message_keep = call(
            functools.partial(halve_kernel, 0),
            [((rows_left, width), bf16), ((rows_left, width), f32)],
            [message_keep, message_other],
            limit=4,
        )
        bit *= 2
    message_other = swap(message_send, "space", peers, bit)
    token = ((8, lanes), f32)
    latent_grad, latent_done = call(
        owner_kernel,
        [(latents.shape, bf16), token],
        [pick, w_msg, slots_kept, slots_other, line_other],
        scratch=[pltpu.VMEM((peers, rows_peer, width), bf16)],
        limit=8,
    )
    hidden_weight_grad, out_weight_grad, loss, hidden_done = call(
        functools.partial(hidden_sum_kernel, variables, 1.0 / (points * peers * variables)),
        [((block, width), f32), ((block, variables), f32), ((1,), f32), token],
        [partial, last_other],
        limit=8,
        scalar_outs=(2,),
        after=[latent_done],
    )
    (msg_weight_grad,) = call(
        message_sum_kernel,
        [((block, width), f32)],
        [message_keep, message_other],
        limit=6,
        after=[hidden_done],
    )
    return (latent_grad, loss, msg_weight_grad, hidden_weight_grad, out_weight_grad)


def solution(mesh):
    placed = (
        P(("groups", "member"), "space", None),
        P(("groups", "space"), None),
        P(),
        P(),
        P(),
        P(),
        P(("groups", "member"), None, "space"),
        P(None, ("groups", "space")),
        P(("groups", "space")),
        P("space", None, None),
        P("space"),
        P("space"),
        P("space"),
    )
    return jax.shard_map(
        on_device,
        mesh=mesh,
        in_specs=placed,
        out_specs=(
            P(("groups", "member"), "space", None),
            P("groups"),
            P(("groups", "space", "member"), None),
            P(("groups", "space", "member"), None),
            P(("groups", "space", "member"), None),
        ),
        check_vma=False,
    )
```

```python
import functools

import jax
import jax.numpy as jnp
from jax import lax
from jax.experimental import pallas as pl
from jax.experimental.pallas import tpu as pltpu
from jax.sharding import PartitionSpec as P

smoothing = 0.1
epsilon = 1e-06
tile = 256
lanes = 128
packed = 16
cost_hints = {
    "back_kernel": 8,
    "slot_kernel": 4,
    "hidden_early_kernel": 4,
    "message_early_kernel": 4,
    "late_kernel": 4,
    "message_sum_kernel": 8,
}
f32 = jnp.float32
bf16 = jnp.bfloat16


def mm(left, right, left_dim, right_dim):
    return lax.dot_general(
        left, right, (((left_dim,), (right_dim,)), ((), ())), preferred_element_type=f32
    )


def call(body, outs, args, scratch=(), limit=16, scalars=(), scalar_outs=(), places=(), after=()):
    whole = pl.BlockSpec(memory_space=pltpu.VMEM)
    small = pl.BlockSpec(memory_space=pltpu.SMEM)
    far_place = pl.BlockSpec(memory_space=pltpu.HBM)
    any_place = pl.BlockSpec(memory_space=pl.ANY)
    count = len(after)
    cost = cost_hints.get(getattr(body, "func", body).__name__, 0) * 10**9
    args = [pltpu.with_memory_space_constraint(x, pltpu.HBM) if i in places else x for i, x in enumerate(args)]

    def inner(*refs):
        body(*refs[count:])

    specs = [small if i in scalars else far_place if i in places else whole for i in range(len(args))]
    return pl.pallas_call(
        inner if count else body,
        out_shape=[jax.ShapeDtypeStruct(dims, kind) for dims, kind in outs],
        in_specs=[any_place] * count + specs,
        out_specs=[small if i in scalar_outs else whole for i in range(len(outs))],
        scratch_shapes=scratch,
        compiler_params=pltpu.CompilerParams(vmem_limit_bytes=limit * 2**20),
        cost_estimate=pl.CostEstimate(flops=cost, bytes_accessed=0, transcendentals=0),
    )(*after, *args)


def place():
    space = lax.axis_index("space")
    return lax.div(space, 2), lax.rem(space, 2), lax.axis_index("member")


def swap(value, axis, size, step):
    return lax.ppermute(value, axis, [(i, i ^ step) for i in range(size)])


def select_kernel(lists_ref, latents_ref, pick_ref, own_ref, send_ref, small_ref, table_ref, sems):
    _, peers, cap = lists_ref.shape
    members, nodes, width = latents_ref.shape
    lists = pltpu.make_async_copy(lists_ref, small_ref, sems.at[0])
    table = pltpu.make_async_copy(latents_ref, table_ref, sems.at[1])
    lists.start()
    table.start()
    lists.wait()
    me = lax.axis_index("space")
    at = lax.broadcasted_iota(jnp.int32, (cap, members * nodes), 0)
    column = lax.broadcasted_iota(jnp.int32, (cap, members * nodes), 1)
    rows = []
    for step in range(peers):
        wanted = jnp.zeros((cap, members * nodes), jnp.int32)
        for j in range(cap):
            wanted = jnp.where(at == j, small_ref[0, me ^ step, j], wanted)
        for member in range(members):
            rows.append((column == wanted + member * nodes).astype(f32))
    pick = jnp.concatenate(rows, axis=0).astype(bf16)
    pick_ref[...] = pick
    table.wait()
    sent = mm(pick, table_ref[...].reshape(members * nodes, width), 1, 0)
    sent = sent.astype(bf16).reshape(peers // 2, 2, members * cap, width)
    own_ref[...] = sent[:, 0]
    send_ref[...] = sent[:, 1]


def merge_kernel(own_ref, arrived_ref, *out_refs):
    rows = own_ref.shape[1]
    for i, out_ref in enumerate(out_refs):
        step = len(out_refs) - i
        out_ref[0:rows, :] = own_ref[step]
        out_ref[rows:, :] = arrived_ref[step]


def stage_kernel(cap, members, count, *refs):
    edge_refs, source_refs, share_ref = refs[:3], refs[3 : 3 + count], refs[3 + count]
    staged_refs, held_refs, sems = refs[4 + count : 4 + 2 * count], refs[4 + 2 * count : -1], refs[-1]
    copies = [
        pltpu.make_async_copy(source, target, sems.at[i])
        for i, (source, target) in enumerate(
            zip(edge_refs + source_refs, held_refs + staged_refs, strict=True)
        )
    ]
    for copy in copies:
        copy.start()
    for copy in copies[:3]:
        copy.wait()
    edge_part(cap, members, *held_refs, share_ref)
    for copy in copies[3:]:
        copy.wait()


def edge_part(cap, members, slot_ref, dst_ref, weight_ref, share_ref):
    edges = slot_ref.shape[0]
    slot = slot_ref[...].reshape(1, edges)
    dst = dst_ref[...].reshape(1, edges)
    weight = weight_ref[...].reshape(1, edges)
    rows = share_ref.shape[0] // 2
    points = share_ref.shape[1] // members
    sender = lax.div(slot, cap)
    spot = (sender ^ lax.axis_index("space")) * (members * cap) + (slot - sender * cap)
    hit = lax.broadcasted_iota(jnp.int32, (rows, edges), 0) == spot
    into = (lax.broadcasted_iota(jnp.int32, (points, edges), 0) == dst).astype(f32).astype(bf16)
    high = weight.astype(bf16).astype(f32)
    table = mm(jnp.where(hit, high, 0.0).astype(bf16), into, 1, 1) + mm(
        jnp.where(hit, weight - high, 0.0).astype(bf16), into, 1, 1
    )
    table = table / jnp.sum(table, axis=0, keepdims=True)
    for member in range(members):
        high = table.astype(bf16)
        columns = slice(member * points, (member + 1) * points)
        share_ref[0:rows, columns] = high
        share_ref[rows : 2 * rows, columns] = (table - high.astype(f32)).astype(bf16)
        table = jnp.concatenate([table[rows - cap :], table[: rows - cap]], axis=0)


def gathered(own_ref, near_ref, far_refs):
    return jnp.concatenate([own_ref[0], near_ref[0]] + [r[...] for r in far_refs[::-1]], axis=0)


def forward_kernel(
    far, w_msg_ref, share_ref, gain_ref, embed_ref, weights_ref, project_ref, present_ref,
    own_ref, near_ref, *rest,
):
    far_refs = rest[:far]
    field_ref, sent_ref, normed_ref, active_ref, slope_ref, unit_ref, inverse_ref = rest[far:]
    points, width = embed_ref.shape
    variables, members, _ = present_ref.shape
    messages = mm(gathered(own_ref, near_ref, far_refs), w_msg_ref[...], 1, 0).astype(bf16)
    messages = jnp.concatenate([messages, messages], axis=0)
    gain = gain_ref[...].reshape(1, width)
    for begin in range(0, members * points, lanes):
        rows = slice(begin, begin + lanes)
        source = slice(begin % points, begin % points + lanes)
        hidden = embed_ref[source, :].astype(f32) + mm(share_ref[:, rows], messages, 0, 0)
        inverse = lax.rsqrt(jnp.mean(hidden * hidden, axis=-1, keepdims=True) + epsilon)
        unit = hidden * inverse
        unit_ref[rows, :] = unit
        inverse_ref[rows, :] = inverse
        normed_ref[rows, :] = (unit * gain).astype(bf16)
    root = 0.7978845608028654
    cubic = 0.044715
    for member in range(members):
        rows = slice(member * points, (member + 1) * points)
        for begin in range(0, width, tile):
            columns = slice(begin, begin + tile)
            inner = mm(normed_ref[rows, :], weights_ref[:, columns], 1, 0)
            square = inner * inner
            bend = jnp.tanh(inner * (root + root * cubic * square))
            half = 0.5 + 0.5 * bend
            active_ref[rows, columns] = (inner * half).astype(bf16)
            slope_ref[rows, columns] = half + (0.5 * inner) * (1.0 - bend * bend) * (
                root + 3.0 * root * cubic * square
            )
        field = present_ref[:, member, :] + mm(project_ref[...], active_ref[rows, :], 1, 1)
        field_ref[member] = field
        sent_ref[member] = field.astype(bf16)


def turn_kernel(normed_ref, active_ref, own_ref, near_ref, *rest):
    far_refs, (normed_t_ref, active_t_ref, keep_ref, give_ref) = rest[:-4], rest[-4:]
    _, _, levels, block, _ = normed_t_ref.shape
    width = normed_ref.shape[1]
    level, line, core = place()
    received = gathered(own_ref, near_ref, far_refs)
    for source, target in ((received, None), (normed_ref, normed_t_ref), (active_ref, active_t_ref)):
        for begin in range(0, width, tile):
            turned = source[:, begin : begin + tile].T
            for piece in range(0, tile, block):
                index = (begin + piece) // block
                far = (index // 2 % 2) ^ line
                step = (index // 4) ^ level
                side = (index % 2) ^ core
                value = turned[piece : piece + block]
                if target is not None:
                    target[side, 1 - far, levels - 1 - step] = value
                    continue
                for which, part_ref in enumerate((keep_ref, give_ref)):
                    @pl.when(side == which)
                    def _(part_ref=part_ref):
                        part_ref[1 - far, levels - 1 - step] = value


def split_loss(part, variables):
    column = lax.broadcasted_iota(jnp.int32, part.shape, 1)
    spots = (column == variables) | (column == variables + 1)
    total = jnp.sum(jnp.where(spots, part, 0.0), axis=1, keepdims=True)
    high = total.astype(bf16).astype(f32)
    return jnp.where(column == variables, high, jnp.where(column == variables + 1, total - high, part))


def score_kernel(
    own_ref, other_ref, truth_ref, cell_ref, project_ref, slope_ref, normed_t_ref, active_t_ref,
    inner_ref, pred_ref, loss_ref, far_ref, near_ref, hold_ref,
):
    members, variables, points = own_ref.shape
    width = slope_ref.shape[1]
    total = 2 * members
    pairs = total * (total - 1)

    def eased(delta):
        square = delta * delta + smoothing * smoothing
        inverse = lax.rsqrt(square)
        return square * inverse, delta * inverse

    truth, cell = truth_ref[...], cell_ref[...].reshape(1, points)
    own = [own_ref[m] for m in range(members)]
    other = [other_ref[m].astype(f32) for m in range(members)]
    score = jnp.zeros_like(truth)
    pulls = [jnp.zeros_like(truth) for _ in own]
    grads = []
    for m in range(members):
        size, sign = eased(own[m] - truth)
        score = score + size * (1.0 / total)
        grads.append(sign * (1.0 / total))
    for m in range(members):
        for n in range(m + 1, members):
            size, sign = eased(own[m] - own[n])
            score = score - size * (1.0 / pairs)
            pulls[m] = pulls[m] + sign
            pulls[n] = pulls[n] - sign
        for n in range(members):
            size, sign = eased(own[m] - other[n])
            score = score - size * (0.5 / pairs)
            pulls[m] = pulls[m] + sign
    loss = jnp.sum(score * cell)
    loss_ref[0] = loss
    hold_ref[...] = jnp.zeros_like(hold_ref)
    for m in range(members):
        grad = (grads[m] - pulls[m] * (1.0 / pairs)) * cell
        hold_ref[0:variables, m * points : (m + 1) * points] = grad
    pred = hold_ref[...].astype(bf16)
    pred_ref[...] = pred
    for m in range(members):
        rows = slice(m * points, (m + 1) * points)
        part = pred[:variables, rows]
        for begin in range(0, width, tile):
            columns = slice(begin, begin + tile)
            grad = mm(part, project_ref[:, columns], 0, 0)
            inner_ref[rows, columns] = (grad * slope_ref[rows, columns]).astype(bf16)
    weight_parts(normed_t_ref, active_t_ref, inner_ref, pred, loss, variables, 1, 0, far_ref)
    weight_parts(normed_t_ref, active_t_ref, inner_ref, pred, loss, variables, 1, 1, near_ref)


def weight_parts(normed_t_ref, active_t_ref, inner_ref, pred, loss, variables, side, half, out_ref):
    width = inner_ref.shape[1]
    depth = normed_t_ref.shape[-1]
    normed = normed_t_ref[side, half].reshape(-1, depth)
    for begin in range(0, width, tile):
        columns = slice(begin, begin + tile)
        out_ref[:, columns] = mm(normed, inner_ref[:, columns], 1, 0).astype(out_ref.dtype)
    part = mm(active_t_ref[side, half].reshape(-1, depth), pred, 1, 1)
    part = jnp.where(lax.broadcasted_iota(jnp.int32, part.shape, 1) == variables, loss, part)
    out_ref[:, width:] = split_loss(part, variables).astype(out_ref.dtype)


def pack(out_ref, begin, part):
    pad = part.shape[1]
    for i in range(part.shape[0] // packed):
        out_ref[begin : begin + packed, i * pad : (i + 1) * pad] = part[i * packed : (i + 1) * packed]


def unpack(in_ref, begin, count, pad):
    parts = [in_ref[begin : begin + packed, i * pad : (i + 1) * pad] for i in range(count // packed)]
    return jnp.concatenate(parts, axis=0).astype(f32)


def local_kernel(variables, loss_ref, normed_t_ref, active_t_ref, inner_ref, pred_ref, far_ref, near_ref):
    for half, out_ref in ((0, far_ref), (1, near_ref)):
        weight_parts(
            normed_t_ref, active_t_ref, inner_ref, pred_ref[...], loss_ref[0], variables, 0, half, out_ref
        )


def pair_sum(variables, width, held_ref, other_ref, begin, count):
    rows = slice(begin, begin + count)
    total = held_ref[rows, :width] + other_ref[rows, :width].astype(f32)
    part = held_ref[rows, width:] + other_ref[rows, width:].astype(f32)
    return total, split_loss(part, variables)


def first_kernel(variables, width, held_ref, other_ref, out_ref):
    total, part = pair_sum(variables, width, held_ref, other_ref, 0, out_ref.shape[0])
    out_ref[:, :width] = total.astype(bf16)
    out_ref[:, width:] = part.astype(bf16)


def message_kernel(
    variables, early, levels, keep_ref, give_ref, slots_ref, other_ref, held_ref, far_other_ref,
    first_ref, middle_ref, last_ref, near_ref,
):
    depth, width = keep_ref.shape[-1], near_ref.shape[1]
    block = near_ref.shape[0] // levels
    count, rest = early * block, (levels - 1 - early) * block
    for begin, size, out_ref in ((count, rest, middle_ref), (count + rest, block, last_ref)):
        total, part = pair_sum(variables, width, held_ref, far_other_ref, begin, size)
        out_ref[0:size, :] = total.astype(bf16)
        out_ref[size : size + packed, :] = jnp.zeros((packed, width), bf16)
        pack(out_ref, size, part.astype(bf16))
    for half in range(2):
        own = keep_ref[half].reshape(-1, depth)
        other = give_ref[half].reshape(-1, depth)
        for begin in range(0, width, tile):
            columns = slice(begin, begin + tile)
            here = slots_ref[:, :, columns].reshape(depth, tile)
            there = other_ref[:, :, columns].reshape(depth, tile)
            total = mm(own, here, 1, 0) + mm(other, there, 1, 0)
            if half == 0:
                total = total.astype(bf16)
                first_ref[:, columns] = total[:count]
                middle_ref[rest + packed :, columns] = total[count : count + rest]
                last_ref[block + packed :, columns] = total[count + rest :]
            else:
                near_ref[:, columns] = total


def ride_kernel(last_ref, slots_ref, *rest):
    arrived_refs, out_ref = rest[:-1], rest[-1]
    rows = slots_ref.shape[1]
    begin = last_ref.shape[0]
    out_ref[0:begin, :] = last_ref[...]
    for i, arrived_ref in enumerate(arrived_refs):
        out_ref[begin + i * rows : begin + (i + 1) * rows, :] = arrived_ref[rows:, :]
    out_ref[begin + len(arrived_refs) * rows :, :] = slots_ref[1]


def hidden_early_kernel(variables, width, held_ref, other_ref, arrived_ref, *out_refs):
    block = out_refs[0].shape[0]
    for i, out_ref in enumerate(out_refs):
        total, part = pair_sum(variables, width, held_ref, other_ref, i * block, block)
        here = slice(i * block, (i + 1) * block)
        out_ref[:, :width] = (total + arrived_ref[here, :width].astype(f32)).astype(bf16)
        part = split_loss(part + arrived_ref[here, width:].astype(f32), variables)
        out_ref[:, width:] = part.astype(bf16)


def message_early_kernel(begin, near_ref, arrived_ref, out_ref):
    here = slice(begin, begin + out_ref.shape[0])
    out_ref[...] = (near_ref[here, :] + arrived_ref[here, :].astype(f32)).astype(bf16)


def late_kernel(variables, early, held_ref, other_ref, near_ref, arrived_ref, *out_refs):
    width = near_ref.shape[1]
    block = (out_refs[0].shape[0] - packed) // 2
    count = block * len(out_refs)
    parts = unpack(arrived_ref, count, count, held_ref.shape[1] - width)
    for i, out_ref in enumerate(out_refs):
        begin = (early + i) * block
        total, part = pair_sum(variables, width, held_ref, other_ref, begin, block)
        here = slice(i * block, (i + 1) * block)
        out_ref[0:block, :] = (total + arrived_ref[here, :].astype(f32)).astype(bf16)
        there = slice(count + packed + i * block, count + packed + (i + 1) * block)
        total = near_ref[begin : begin + block, :] + arrived_ref[there, :].astype(f32)
        out_ref[block : 2 * block, :] = total.astype(bf16)
        out_ref[2 * block :, :] = jnp.zeros((packed, width), bf16)
        pack(out_ref, 2 * block, split_loss(part + parts[here], variables).astype(bf16))


def back_kernel(inner_ref, w_hidden_ref, gain_ref, unit_ref, inverse_ref, grad_ref, scaled_ref):
    rows_all, width = inner_ref.shape
    gain = gain_ref[...].reshape(1, width)
    for begin_row in range(0, rows_all, tile):
        rows = slice(begin_row, begin_row + tile)
        dots = jnp.zeros((tile, 1), f32)
        for begin in range(0, width, tile):
            columns = slice(begin, begin + tile)
            scaled = mm(inner_ref[rows, :], w_hidden_ref[columns, :], 1, 1) * gain[:, columns]
            dots = dots + jnp.sum(scaled * unit_ref[rows, columns], axis=-1, keepdims=True)
            scaled_ref[rows, columns] = scaled
        dots = dots * (1.0 / width)
        inverse = inverse_ref[rows, :]
        for begin in range(0, width, tile):
            columns = slice(begin, begin + tile)
            grad_ref[rows, columns] = (
                (scaled_ref[rows, columns] - unit_ref[rows, columns] * dots) * inverse
            ).astype(bf16)


def slot_kernel(share_ref, grad_ref, slots_ref, *send_refs):
    peers, each, width = slots_ref.shape
    rows = peers * each
    for begin in range(0, width, tile):
        columns = slice(begin, begin + tile)
        both = mm(share_ref[...], grad_ref[:, columns], 1, 0)
        slots_ref[:, :, columns] = (both[:rows] + both[rows:]).astype(bf16).reshape(peers, each, tile)
    for i, send_ref in enumerate(send_refs):
        step = len(send_refs) - i
        send_ref[0:each, :] = slots_ref[2 * step]
        send_ref[each:, :] = slots_ref[2 * step + 1]


def owner_kernel(pick_ref, w_msg_ref, slots_ref, last_ref, *rest):
    arrived_refs, (grad_ref, token_ref, held_ref) = rest[:-3], rest[-3:]
    token_ref[...] = jnp.zeros_like(token_ref)
    peers, rows, width = slots_ref.shape
    levels = peers // 2
    begin = last_ref.shape[0] - levels * rows
    for i in range(levels):
        spot = 2 * (levels - 1 - i)
        held_ref[spot] = slots_ref[0] if i == levels - 1 else arrived_refs[i][0:rows, :]
        held_ref[spot + 1] = last_ref[begin + i * rows : begin + (i + 1) * rows, :]
    nodes = mm(pick_ref[...], held_ref[...].reshape(peers * rows, width), 0, 0).astype(bf16)
    grad_ref[...] = mm(nodes, w_msg_ref[...], 1, 1).astype(bf16).reshape(grad_ref.shape)


def hidden_sum_kernel(variables, scale, early, held_ref, other_ref, last_ref, *rest):
    hidden_ref, out_ref, loss_ref, token_ref = rest[-4:]
    token_ref[...] = jnp.zeros_like(token_ref)
    block, width = hidden_ref.shape
    pad = held_ref.shape[1] - width
    total, part = pair_sum(variables, width, held_ref, other_ref, held_ref.shape[0] - block, block)
    total = total + last_ref[0:block, :].astype(f32)
    part = part + unpack(last_ref, block, block, pad)
    for i, r in enumerate(rest[:-4]):
        total = total + r[0:block, :width].astype(f32)
        if i < early:
            part = part + r[:, width:].astype(f32)
        else:
            part = part + unpack(r, 2 * block, block, pad)
    hidden_ref[...] = total
    out_ref[...] = part[:, :variables]
    column = lax.broadcasted_iota(jnp.int32, (8, pad), 1)
    spots = (column == variables) | (column == variables + 1)
    first = lax.broadcasted_iota(jnp.int32, (8, pad), 0) == 0
    loss_ref[0] = jnp.sum(jnp.where(spots & first, part[:8], 0.0)) * scale


def message_sum_kernel(early, near_ref, last_ref, *rest):
    out_ref = rest[-1]
    block = out_ref.shape[0]
    total = near_ref[near_ref.shape[0] - block :, :]
    total = total + last_ref[block + packed : 2 * block + packed, :].astype(f32)
    for i, r in enumerate(rest[:-1]):
        begin = 0 if i < early else block
        total = total + r[begin : begin + block, :].astype(f32)
    out_ref[...] = total


def on_device(
    latents, grid_embed, norm_gain, w_msg, w_hidden, variable_projection, present_condition, verifying_field,
    cell_surface, send_rows, edge_slot, edge_dst, edge_weight,
):
    members, nodes, width = latents.shape
    points = grid_embed.shape[0]
    variables = variable_projection.shape[1]
    peers = lax.axis_size("space")
    cores = lax.axis_size("member")
    cap = send_rows.shape[2]
    rows_peer = members * cap
    rows_slot = peers * rows_peer
    rows_all = members * points
    levels = peers // 2
    block = width // (peers * cores)
    half = levels * block
    wide = width + -(-(variables + 2) // lanes) * lanes
    project = variable_projection.T

    early = levels // 2
    count, rest = early * block, (levels - 1 - early) * block
    steps = [2 * (levels - 1 - i) for i in range(levels - 1)]

    def spread(values, part):
        return [swap(x, "space", peers, k) for x, k in zip(values, part, strict=True)]

    pick, own_rows, send = call(
        select_kernel,
        [((rows_slot, members * nodes), bf16)] + [((levels, rows_peer, width), bf16)] * 2,
        [send_rows, latents],
        scratch=[
            pltpu.SMEM(send_rows.shape, jnp.int32),
            pltpu.VMEM(latents.shape, bf16),
            pltpu.SemaphoreType.DMA((2,)),
        ],
        limit=4,
        places=(0, 1),
    )
    near_rows = swap(send, "space", peers, 1)
    fixed = [w_msg, norm_gain, grid_embed, w_hidden, project, present_condition.transpose(1, 0, 2)]
    edges = [edge_slot, edge_dst, edge_weight]
    share, *staged = call(
        functools.partial(stage_kernel, cap, members, len(fixed)),
        [((2 * rows_slot, rows_all), bf16)] + [(x.shape, x.dtype) for x in fixed],
        edges + fixed,
        scratch=[pltpu.VMEM(x.shape, x.dtype) for x in edges]
        + [pltpu.SemaphoreType.DMA((3 + len(fixed),))],
        limit=16,
        places=tuple(range(3 + len(fixed))),
        after=[pick],
    )
    merged = call(
        merge_kernel,
        [((2 * rows_peer, width), bf16)] * (levels - 1),
        [own_rows, near_rows],
        limit=4,
        after=[share],
    )
    received = [own_rows, near_rows] + spread(merged, steps)
    w_msg_near, gain, embed, w_hidden_near, project_near, present = staged
    field, sent, normed, active, slope, unit, inverse = call(
        functools.partial(forward_kernel, levels - 1),
        [
            ((members, variables, points), f32),
            ((members, variables, points), bf16),
            ((rows_all, width), bf16),
            ((rows_all, width), bf16),
            ((rows_all, width), f32),
            ((rows_all, width), f32),
            ((rows_all, 1), f32),
        ],
        [w_msg_near, share, gain, embed, w_hidden_near, project_near, present] + received,
        limit=20,
    )
    other = swap(sent, "member", cores, 1)
    normed_t, active_t, received_keep, received_give = call(
        turn_kernel,
        [((cores, 2, levels, block, rows_all), bf16)] * 2 + [((2, levels, block, rows_slot), bf16)] * 2,
        [normed, active] + received,
        limit=8,
    )
    received_other = swap(received_give, "member", cores, 1)
    grad_inner, pred, loss_part, far, near = call(
        score_kernel,
        [
            ((rows_all, width), bf16),
            ((lanes, rows_all), bf16),
            ((1,), f32),
            ((half, wide), bf16),
            ((half, wide), bf16),
        ],
        [field, other, verifying_field, cell_surface, project_near, slope, normed_t, active_t],
        scratch=[pltpu.VMEM((lanes, rows_all), f32)],
        limit=16,
        scalar_outs=(2,),
    )
    far_other = swap(far, "member", cores, 1)
    near_other = swap(near, "member", cores, 1)
    held_far, held_near = call(
        functools.partial(local_kernel, variables),
        [((half, wide), f32)] * 2,
        [loss_part, normed_t, active_t, grad_inner, pred],
        limit=12,
        scalars=(0,),
    )
    (first,) = call(
        functools.partial(first_kernel, variables, width),
        [((count, wide), bf16)],
        [held_far, far_other],
        limit=6,
    )
    first_other = swap(first, "space", peers, 1)
    (grad_hidden,) = call(
        back_kernel,
        [((rows_all, width), bf16)],
        [grad_inner, w_hidden_near, gain, unit, inverse],
        scratch=[pltpu.VMEM((rows_all, width), f32)],
        limit=14,
        after=[first],
    )
    slots, *slots_sent = call(
        slot_kernel,
        [((peers, rows_peer, width), bf16)] + [((2 * rows_peer, width), bf16)] * (levels - 1),
        [share, grad_hidden],
        limit=6,
        after=[near_other, received_other],
    )
    slots_other = swap(slots, "member", cores, 1)
    slots_arrived = spread(slots_sent, steps)
    message_first, middle, last, message_near = call(
        functools.partial(message_kernel, variables, early, levels),
        [
            ((count, width), bf16),
            ((2 * rest + packed, width), bf16),
            ((2 * block + packed, width), bf16),
            ((half, width), f32),
        ],
        [received_keep, received_other, slots, slots_other, held_far, far_other],
        limit=10,
    )
    message_first_other = swap(message_first, "space", peers, 1)
    middle_other = swap(middle, "space", peers, 1)
    (last,) = call(
        ride_kernel,
        [((2 * block + packed + levels * rows_peer, width), bf16)],
        [last, slots] + slots_arrived,
        limit=4,
    )
    last_other = swap(last, "space", peers, 1)
    hidden_early = call(
        functools.partial(hidden_early_kernel, variables, width),
        [((block, wide), bf16)] * early,
        [held_near, near_other, first_other],
        limit=6,
    )
    hidden_parts = spread(hidden_early, steps[:early])
    message_parts = []
    for i in range(early):
        (piece,) = call(
            functools.partial(message_early_kernel, i * block),
            [((block, width), bf16)],
            [message_near, message_first_other],
            limit=6,
            after=hidden_parts[:i],
        )
        message_parts.append(swap(piece, "space", peers, steps[i]))
    late = call(
        functools.partial(late_kernel, variables, early),
        [((2 * block + packed, width), bf16)] * (levels - 1 - early),
        [held_near, near_other, message_near, middle_other],
        limit=6,
    )
    late_parts = spread(late, steps[early:])
    token = ((8, lanes), f32)
    latent_grad, latent_done = call(
        owner_kernel,
        [(latents.shape, bf16), token],
        [pick, w_msg, slots, last_other] + slots_arrived,
        scratch=[pltpu.VMEM((peers, rows_peer, width), bf16)],
        limit=8,
    )
    hidden_weight_grad, out_weight_grad, loss, hidden_done = call(
        functools.partial(hidden_sum_kernel, variables, 1.0 / (points * peers * variables), early),
        [((block, width), f32), ((block, variables), f32), ((1,), f32), token],
        [held_near, near_other, last_other] + hidden_parts + late_parts,
        limit=8,
        scalar_outs=(2,),
        after=[latent_done],
    )
    (msg_weight_grad,) = call(
        functools.partial(message_sum_kernel, early),
        [((block, width), f32)],
        [message_near, last_other] + message_parts + late_parts,
        limit=6,
        after=[hidden_done],
    )
    return (latent_grad, loss, msg_weight_grad, hidden_weight_grad, out_weight_grad)


def solution(mesh):
    placed = (
        P(("groups", "member"), "space", None),
        P(("groups", "space"), None),
        P(),
        P(),
        P(),
        P(),
        P(("groups", "member"), None, "space"),
        P(None, ("groups", "space")),
        P(("groups", "space")),
        P("space", None, None),
        P("space"),
        P("space"),
        P("space"),
    )
    return jax.shard_map(
        on_device,
        mesh=mesh,
        in_specs=placed,
        out_specs=(
            P(("groups", "member"), "space", None),
            P("groups"),
            P(("groups", "space", "member"), None),
            P(("groups", "space", "member"), None),
            P(("groups", "space", "member"), None),
        ),
        check_vma=False,
    )
```

```python
import functools

import jax
import jax.numpy as jnp
from jax import lax
from jax.experimental import pallas as pl
from jax.experimental.pallas import tpu as pltpu
from jax.sharding import PartitionSpec as P

smoothing = 0.1
epsilon = 1e-06
tile = 256
lanes = 128
packed = 16
cost_hints = {
    "back_kernel": 8,
    "slot_kernel": 4,
    "hidden_early_kernel": 4,
    "message_early_kernel": 4,
    "late_kernel": 4,
    "message_sum_kernel": 8,
}
f32 = jnp.float32
bf16 = jnp.bfloat16


def mm(left, right, left_dim, right_dim):
    return lax.dot_general(
        left, right, (((left_dim,), (right_dim,)), ((), ())), preferred_element_type=f32
    )


def call(body, outs, args, scratch=(), limit=16, scalars=(), scalar_outs=(), places=(), after=()):
    whole = pl.BlockSpec(memory_space=pltpu.VMEM)
    small = pl.BlockSpec(memory_space=pltpu.SMEM)
    far_place = pl.BlockSpec(memory_space=pltpu.HBM)
    any_place = pl.BlockSpec(memory_space=pl.ANY)
    count = len(after)
    cost = cost_hints.get(getattr(body, "func", body).__name__, 0) * 10**9
    args = [pltpu.with_memory_space_constraint(x, pltpu.HBM) if i in places else x for i, x in enumerate(args)]

    def inner(*refs):
        body(*refs[count:])

    specs = [small if i in scalars else far_place if i in places else whole for i in range(len(args))]
    return pl.pallas_call(
        inner if count else body,
        out_shape=[jax.ShapeDtypeStruct(dims, kind) for dims, kind in outs],
        in_specs=[any_place] * count + specs,
        out_specs=[small if i in scalar_outs else whole for i in range(len(outs))],
        scratch_shapes=scratch,
        compiler_params=pltpu.CompilerParams(vmem_limit_bytes=limit * 2**20),
        cost_estimate=pl.CostEstimate(flops=cost, bytes_accessed=0, transcendentals=0),
    )(*after, *args)


def place():
    space = lax.axis_index("space")
    return lax.div(space, 2), lax.rem(space, 2), lax.axis_index("member")


def swap(value, axis, size, step):
    return lax.ppermute(value, axis, [(i, i ^ step) for i in range(size)])


def select_kernel(lists_ref, latents_ref, pick_ref, own_ref, send_ref, small_ref, table_ref, sems):
    _, peers, cap = lists_ref.shape
    members, nodes, width = latents_ref.shape
    lists = pltpu.make_async_copy(lists_ref, small_ref, sems.at[0])
    table = pltpu.make_async_copy(latents_ref, table_ref, sems.at[1])
    lists.start()
    table.start()
    lists.wait()
    me = lax.axis_index("space")
    at = lax.broadcasted_iota(jnp.int32, (cap, members * nodes), 0)
    column = lax.broadcasted_iota(jnp.int32, (cap, members * nodes), 1)
    rows = []
    for step in range(peers):
        wanted = jnp.zeros((cap, members * nodes), jnp.int32)
        for j in range(cap):
            wanted = jnp.where(at == j, small_ref[0, me ^ step, j], wanted)
        for member in range(members):
            rows.append((column == wanted + member * nodes).astype(f32))
    pick = jnp.concatenate(rows, axis=0).astype(bf16)
    pick_ref[...] = pick
    table.wait()
    sent = mm(pick, table_ref[...].reshape(members * nodes, width), 1, 0)
    sent = sent.astype(bf16).reshape(peers // 2, 2, members * cap, width)
    own_ref[...] = sent[:, 0]
    send_ref[...] = sent[:, 1]


def merge_kernel(own_ref, arrived_ref, *out_refs):
    rows = own_ref.shape[1]
    for i, out_ref in enumerate(out_refs):
        step = len(out_refs) - i
        out_ref[0:rows, :] = own_ref[step]
        out_ref[rows:, :] = arrived_ref[step]


def stage_kernel(cap, members, count, *refs):
    edge_refs, source_refs, share_ref = refs[:3], refs[3 : 3 + count], refs[3 + count]
    staged_refs, held_refs, sems = refs[4 + count : 4 + 2 * count], refs[4 + 2 * count : -1], refs[-1]
    copies = [
        pltpu.make_async_copy(source, target, sems.at[i])
        for i, (source, target) in enumerate(
            zip(edge_refs + source_refs, held_refs + staged_refs, strict=True)
        )
    ]
    for copy in copies:
        copy.start()
    for copy in copies[:3]:
        copy.wait()
    edge_part(cap, members, *held_refs, share_ref)
    for copy in copies[3:]:
        copy.wait()


def edge_part(cap, members, slot_ref, dst_ref, weight_ref, share_ref):
    edges = slot_ref.shape[0]
    slot = slot_ref[...].reshape(1, edges)
    dst = dst_ref[...].reshape(1, edges)
    weight = weight_ref[...].reshape(1, edges)
    rows = share_ref.shape[0] // 2
    points = share_ref.shape[1] // members
    sender = lax.div(slot, cap)
    spot = (sender ^ lax.axis_index("space")) * (members * cap) + (slot - sender * cap)
    hit = lax.broadcasted_iota(jnp.int32, (rows, edges), 0) == spot
    into = (lax.broadcasted_iota(jnp.int32, (points, edges), 0) == dst).astype(f32).astype(bf16)
    high = weight.astype(bf16).astype(f32)
    table = mm(jnp.where(hit, high, 0.0).astype(bf16), into, 1, 1) + mm(
        jnp.where(hit, weight - high, 0.0).astype(bf16), into, 1, 1
    )
    table = table / jnp.sum(table, axis=0, keepdims=True)
    for member in range(members):
        high = table.astype(bf16)
        columns = slice(member * points, (member + 1) * points)
        share_ref[0:rows, columns] = high
        share_ref[rows : 2 * rows, columns] = (table - high.astype(f32)).astype(bf16)
        table = jnp.concatenate([table[rows - cap :], table[: rows - cap]], axis=0)


def gathered(own_ref, near_ref, far_refs):
    return jnp.concatenate([own_ref[0], near_ref[0]] + [r[...] for r in far_refs[::-1]], axis=0)


def forward_kernel(
    far, w_msg_ref, share_ref, gain_ref, embed_ref, weights_ref, project_ref, present_ref,
    own_ref, near_ref, *rest,
):
    far_refs = rest[:far]
    field_ref, sent_ref, normed_ref, active_ref, slope_ref, unit_ref, inverse_ref = rest[far:]
    points, width = embed_ref.shape
    variables, members, _ = present_ref.shape
    messages = mm(gathered(own_ref, near_ref, far_refs), w_msg_ref[...], 1, 0).astype(bf16)
    messages = jnp.concatenate([messages, messages], axis=0)
    gain = gain_ref[...].reshape(1, width)
    for begin in range(0, members * points, lanes):
        rows = slice(begin, begin + lanes)
        source = slice(begin % points, begin % points + lanes)
        hidden = embed_ref[source, :].astype(f32) + mm(share_ref[:, rows], messages, 0, 0)
        inverse = lax.rsqrt(jnp.mean(hidden * hidden, axis=-1, keepdims=True) + epsilon)
        unit = hidden * inverse
        unit_ref[rows, :] = unit
        inverse_ref[rows, :] = inverse
        normed_ref[rows, :] = (unit * gain).astype(bf16)
    root = 0.7978845608028654
    cubic = 0.044715
    for member in range(members):
        rows = slice(member * points, (member + 1) * points)
        for begin in range(0, width, tile):
            columns = slice(begin, begin + tile)
            inner = mm(normed_ref[rows, :], weights_ref[:, columns], 1, 0)
            square = inner * inner
            bend = jnp.tanh(inner * (root + root * cubic * square))
            half = 0.5 + 0.5 * bend
            active_ref[rows, columns] = (inner * half).astype(bf16)
            slope_ref[rows, columns] = half + (0.5 * inner) * (1.0 - bend * bend) * (
                root + 3.0 * root * cubic * square
            )
        field = present_ref[:, member, :] + mm(project_ref[...], active_ref[rows, :], 1, 1)
        field_ref[member] = field
        sent_ref[member] = field.astype(bf16)


def turn_kernel(normed_ref, active_ref, own_ref, near_ref, *rest):
    far_refs, (normed_t_ref, active_t_ref, keep_ref, give_ref) = rest[:-4], rest[-4:]
    _, _, levels, block, _ = normed_t_ref.shape
    width = normed_ref.shape[1]
    level, line, core = place()
    received = gathered(own_ref, near_ref, far_refs)
    for source, target in ((received, None), (normed_ref, normed_t_ref), (active_ref, active_t_ref)):
        for begin in range(0, width, tile):
            turned = source[:, begin : begin + tile].T
            for piece in range(0, tile, block):
                index = (begin + piece) // block
                far = (index // 2 % 2) ^ line
                step = (index // 4) ^ level
                side = (index % 2) ^ core
                value = turned[piece : piece + block]
                if target is not None:
                    target[side, 1 - far, levels - 1 - step] = value
                    continue
                for which, part_ref in enumerate((keep_ref, give_ref)):
                    @pl.when(side == which)
                    def _(part_ref=part_ref):
                        part_ref[1 - far, levels - 1 - step] = value


def split_loss(part, variables):
    column = lax.broadcasted_iota(jnp.int32, part.shape, 1)
    spots = (column == variables) | (column == variables + 1)
    total = jnp.sum(jnp.where(spots, part, 0.0), axis=1, keepdims=True)
    high = total.astype(bf16).astype(f32)
    return jnp.where(column == variables, high, jnp.where(column == variables + 1, total - high, part))


def score_kernel(
    own_ref, other_ref, truth_ref, cell_ref, project_ref, slope_ref, normed_t_ref, active_t_ref,
    inner_ref, pred_ref, loss_ref, far_ref, near_ref, hold_ref,
):
    members, variables, points = own_ref.shape
    width = slope_ref.shape[1]
    total = 2 * members
    pairs = total * (total - 1)

    def eased(delta):
        square = delta * delta + smoothing * smoothing
        inverse = lax.rsqrt(square)
        return square * inverse, delta * inverse

    truth, cell = truth_ref[...], cell_ref[...].reshape(1, points)
    own = [own_ref[m] for m in range(members)]
    other = [other_ref[m].astype(f32) for m in range(members)]
    score = jnp.zeros_like(truth)
    pulls = [jnp.zeros_like(truth) for _ in own]
    grads = []
    for m in range(members):
        size, sign = eased(own[m] - truth)
        score = score + size * (1.0 / total)
        grads.append(sign * (1.0 / total))
    for m in range(members):
        for n in range(m + 1, members):
            size, sign = eased(own[m] - own[n])
            score = score - size * (1.0 / pairs)
            pulls[m] = pulls[m] + sign
            pulls[n] = pulls[n] - sign
        for n in range(members):
            size, sign = eased(own[m] - other[n])
            score = score - size * (0.5 / pairs)
            pulls[m] = pulls[m] + sign
    loss = jnp.sum(score * cell)
    loss_ref[0] = loss
    hold_ref[...] = jnp.zeros_like(hold_ref)
    for m in range(members):
        grad = (grads[m] - pulls[m] * (1.0 / pairs)) * cell
        hold_ref[0:variables, m * points : (m + 1) * points] = grad
    pred = hold_ref[...].astype(bf16)
    pred_ref[...] = pred
    for m in range(members):
        rows = slice(m * points, (m + 1) * points)
        part = pred[:variables, rows]
        for begin in range(0, width, tile):
            columns = slice(begin, begin + tile)
            grad = mm(part, project_ref[:, columns], 0, 0)
            inner_ref[rows, columns] = (grad * slope_ref[rows, columns]).astype(bf16)
    weight_parts(normed_t_ref, active_t_ref, inner_ref, pred, loss, variables, 1, 0, far_ref)
    weight_parts(normed_t_ref, active_t_ref, inner_ref, pred, loss, variables, 1, 1, near_ref)


def weight_parts(normed_t_ref, active_t_ref, inner_ref, pred, loss, variables, side, half, out_ref):
    width = inner_ref.shape[1]
    depth = normed_t_ref.shape[-1]
    normed = normed_t_ref[side, half].reshape(-1, depth)
    for begin in range(0, width, tile):
        columns = slice(begin, begin + tile)
        out_ref[:, columns] = mm(normed, inner_ref[:, columns], 1, 0).astype(out_ref.dtype)
    part = mm(active_t_ref[side, half].reshape(-1, depth), pred, 1, 1)
    part = jnp.where(lax.broadcasted_iota(jnp.int32, part.shape, 1) == variables, loss, part)
    out_ref[:, width:] = split_loss(part, variables).astype(out_ref.dtype)


def pack(out_ref, begin, part):
    pad = part.shape[1]
    for i in range(part.shape[0] // packed):
        out_ref[begin : begin + packed, i * pad : (i + 1) * pad] = part[i * packed : (i + 1) * packed]


def unpack(in_ref, begin, count, pad):
    parts = [in_ref[begin : begin + packed, i * pad : (i + 1) * pad] for i in range(count // packed)]
    return jnp.concatenate(parts, axis=0).astype(f32)


def local_kernel(variables, loss_ref, normed_t_ref, active_t_ref, inner_ref, pred_ref, far_ref, near_ref):
    for half, out_ref in ((0, far_ref), (1, near_ref)):
        weight_parts(
            normed_t_ref, active_t_ref, inner_ref, pred_ref[...], loss_ref[0], variables, 0, half, out_ref
        )


def pair_sum(variables, width, held_ref, other_ref, begin, count):
    rows = slice(begin, begin + count)
    total = held_ref[rows, :width] + other_ref[rows, :width].astype(f32)
    part = held_ref[rows, width:] + other_ref[rows, width:].astype(f32)
    return total, split_loss(part, variables)


def first_kernel(variables, width, held_ref, other_ref, out_ref):
    total, part = pair_sum(variables, width, held_ref, other_ref, 0, out_ref.shape[0])
    out_ref[:, :width] = total.astype(bf16)
    out_ref[:, width:] = part.astype(bf16)


def message_kernel(
    variables, early, levels, keep_ref, give_ref, slots_ref, other_ref, held_ref, far_other_ref,
    first_ref, middle_ref, last_ref, near_ref,
):
    depth, width = keep_ref.shape[-1], near_ref.shape[1]
    block = near_ref.shape[0] // levels
    count, rest = early * block, (levels - 1 - early) * block
    for begin, size, out_ref in ((count, rest, middle_ref), (count + rest, block, last_ref)):
        total, part = pair_sum(variables, width, held_ref, far_other_ref, begin, size)
        out_ref[0:size, :] = total.astype(bf16)
        out_ref[size : size + packed, :] = jnp.zeros((packed, width), bf16)
        pack(out_ref, size, part.astype(bf16))
    for half in range(2):
        own = keep_ref[half].reshape(-1, depth)
        other = give_ref[half].reshape(-1, depth)
        for begin in range(0, width, tile):
            columns = slice(begin, begin + tile)
            here = slots_ref[:, :, columns].reshape(depth, tile)
            there = other_ref[:, :, columns].reshape(depth, tile)
            total = mm(own, here, 1, 0) + mm(other, there, 1, 0)
            if half == 0:
                total = total.astype(bf16)
                first_ref[:, columns] = total[:count]
                middle_ref[rest + packed :, columns] = total[count : count + rest]
                last_ref[block + packed :, columns] = total[count + rest :]
            else:
                near_ref[:, columns] = total


def ride_kernel(last_ref, slots_ref, *rest):
    arrived_refs, out_ref = rest[:-1], rest[-1]
    rows = slots_ref.shape[1]
    begin = last_ref.shape[0]
    out_ref[0:begin, :] = last_ref[...]
    for i, arrived_ref in enumerate(arrived_refs):
        out_ref[begin + i * rows : begin + (i + 1) * rows, :] = arrived_ref[rows:, :]
    out_ref[begin + len(arrived_refs) * rows :, :] = slots_ref[1]


def hidden_early_kernel(variables, width, held_ref, other_ref, arrived_ref, *out_refs):
    block = out_refs[0].shape[0]
    for i, out_ref in enumerate(out_refs):
        total, part = pair_sum(variables, width, held_ref, other_ref, i * block, block)
        here = slice(i * block, (i + 1) * block)
        out_ref[:, :width] = (total + arrived_ref[here, :width].astype(f32)).astype(bf16)
        part = split_loss(part + arrived_ref[here, width:].astype(f32), variables)
        out_ref[:, width:] = part.astype(bf16)


def message_early_kernel(begin, near_ref, arrived_ref, out_ref):
    here = slice(begin, begin + out_ref.shape[0])
    out_ref[...] = (near_ref[here, :] + arrived_ref[here, :].astype(f32)).astype(bf16)


def late_kernel(variables, early, held_ref, other_ref, near_ref, arrived_ref, *out_refs):
    width = near_ref.shape[1]
    block = (out_refs[0].shape[0] - packed) // 2
    count = block * len(out_refs)
    parts = unpack(arrived_ref, count, count, held_ref.shape[1] - width)
    for i, out_ref in enumerate(out_refs):
        begin = (early + i) * block
        total, part = pair_sum(variables, width, held_ref, other_ref, begin, block)
        here = slice(i * block, (i + 1) * block)
        out_ref[0:block, :] = (total + arrived_ref[here, :].astype(f32)).astype(bf16)
        there = slice(count + packed + i * block, count + packed + (i + 1) * block)
        total = near_ref[begin : begin + block, :] + arrived_ref[there, :].astype(f32)
        out_ref[block : 2 * block, :] = total.astype(bf16)
        out_ref[2 * block :, :] = jnp.zeros((packed, width), bf16)
        pack(out_ref, 2 * block, split_loss(part + parts[here], variables).astype(bf16))


def back_kernel(inner_ref, w_hidden_ref, gain_ref, unit_ref, inverse_ref, grad_ref, scaled_ref):
    rows_all, width = inner_ref.shape
    gain = gain_ref[...].reshape(1, width)
    for begin_row in range(0, rows_all, tile):
        rows = slice(begin_row, begin_row + tile)
        dots = jnp.zeros((tile, 1), f32)
        for begin in range(0, width, tile):
            columns = slice(begin, begin + tile)
            scaled = mm(inner_ref[rows, :], w_hidden_ref[columns, :], 1, 1) * gain[:, columns]
            dots = dots + jnp.sum(scaled * unit_ref[rows, columns], axis=-1, keepdims=True)
            scaled_ref[rows, columns] = scaled
        dots = dots * (1.0 / width)
        inverse = inverse_ref[rows, :]
        for begin in range(0, width, tile):
            columns = slice(begin, begin + tile)
            grad_ref[rows, columns] = (
                (scaled_ref[rows, columns] - unit_ref[rows, columns] * dots) * inverse
            ).astype(bf16)


def slot_kernel(share_ref, grad_ref, slots_ref, *send_refs):
    peers, each, width = slots_ref.shape
    rows = peers * each
    for begin in range(0, width, tile):
        columns = slice(begin, begin + tile)
        both = mm(share_ref[...], grad_ref[:, columns], 1, 0)
        slots_ref[:, :, columns] = (both[:rows] + both[rows:]).astype(bf16).reshape(peers, each, tile)
    for i, send_ref in enumerate(send_refs):
        step = len(send_refs) - i
        send_ref[0:each, :] = slots_ref[2 * step]
        send_ref[each:, :] = slots_ref[2 * step + 1]


def owner_kernel(pick_ref, w_msg_ref, slots_ref, last_ref, *rest):
    arrived_refs, (grad_ref, token_ref, held_ref) = rest[:-3], rest[-3:]
    token_ref[...] = jnp.zeros_like(token_ref)
    peers, rows, width = slots_ref.shape
    levels = peers // 2
    begin = last_ref.shape[0] - levels * rows
    for i in range(levels):
        spot = 2 * (levels - 1 - i)
        held_ref[spot] = slots_ref[0] if i == levels - 1 else arrived_refs[i][0:rows, :]
        held_ref[spot + 1] = last_ref[begin + i * rows : begin + (i + 1) * rows, :]
    nodes = mm(pick_ref[...], held_ref[...].reshape(peers * rows, width), 0, 0).astype(bf16)
    grad_ref[...] = mm(nodes, w_msg_ref[...], 1, 1).astype(bf16).reshape(grad_ref.shape)


def hidden_sum_kernel(variables, scale, early, held_ref, other_ref, last_ref, *rest):
    hidden_ref, out_ref, loss_ref, token_ref = rest[-4:]
    token_ref[...] = jnp.zeros_like(token_ref)
    block, width = hidden_ref.shape
    pad = held_ref.shape[1] - width
    total, part = pair_sum(variables, width, held_ref, other_ref, held_ref.shape[0] - block, block)
    total = total + last_ref[0:block, :].astype(f32)
    part = part + unpack(last_ref, block, block, pad)
    for i, r in enumerate(rest[:-4]):
        total = total + r[0:block, :width].astype(f32)
        if i < early:
            part = part + r[:, width:].astype(f32)
        else:
            part = part + unpack(r, 2 * block, block, pad)
    hidden_ref[...] = total
    out_ref[...] = part[:, :variables]
    column = lax.broadcasted_iota(jnp.int32, (8, pad), 1)
    spots = (column == variables) | (column == variables + 1)
    first = lax.broadcasted_iota(jnp.int32, (8, pad), 0) == 0
    loss_ref[0] = jnp.sum(jnp.where(spots & first, part[:8], 0.0)) * scale


def message_sum_kernel(early, near_ref, last_ref, *rest):
    out_ref = rest[-1]
    block = out_ref.shape[0]
    total = near_ref[near_ref.shape[0] - block :, :]
    total = total + last_ref[block + packed : 2 * block + packed, :].astype(f32)
    for i, r in enumerate(rest[:-1]):
        begin = 0 if i < early else block
        total = total + r[begin : begin + block, :].astype(f32)
    out_ref[...] = total


def on_device(
    latents, grid_embed, norm_gain, w_msg, w_hidden, variable_projection, present_condition, verifying_field,
    cell_surface, send_rows, edge_slot, edge_dst, edge_weight,
):
    members, nodes, width = latents.shape
    points = grid_embed.shape[0]
    variables = variable_projection.shape[1]
    peers = lax.axis_size("space")
    cores = lax.axis_size("member")
    cap = send_rows.shape[2]
    rows_peer = members * cap
    rows_slot = peers * rows_peer
    rows_all = members * points
    levels = peers // 2
    block = width // (peers * cores)
    half = levels * block
    wide = width + -(-(variables + 2) // lanes) * lanes
    project = variable_projection.T

    early = levels // 2
    count, rest = early * block, (levels - 1 - early) * block
    steps = [2 * (levels - 1 - i) for i in range(levels - 1)]

    def spread(values, part):
        return [swap(x, "space", peers, k) for x, k in zip(values, part, strict=True)]

    pick, own_rows, send = call(
        select_kernel,
        [((rows_slot, members * nodes), bf16)] + [((levels, rows_peer, width), bf16)] * 2,
        [send_rows, latents],
        scratch=[
            pltpu.SMEM(send_rows.shape, jnp.int32),
            pltpu.VMEM(latents.shape, bf16),
            pltpu.SemaphoreType.DMA((2,)),
        ],
        limit=4,
        places=(0, 1),
    )
    near_rows = swap(send, "space", peers, 1)
    fixed = [w_msg, norm_gain, grid_embed, w_hidden, project, present_condition.transpose(1, 0, 2)]
    edges = [edge_slot, edge_dst, edge_weight]
    share, *staged = call(
        functools.partial(stage_kernel, cap, members, len(fixed)),
        [((2 * rows_slot, rows_all), bf16)] + [(x.shape, x.dtype) for x in fixed],
        edges + fixed,
        scratch=[pltpu.VMEM(x.shape, x.dtype) for x in edges]
        + [pltpu.SemaphoreType.DMA((3 + len(fixed),))],
        limit=16,
        places=tuple(range(3 + len(fixed))),
        after=[pick],
    )
    merged = call(
        merge_kernel,
        [((2 * rows_peer, width), bf16)] * (levels - 1),
        [own_rows, near_rows],
        limit=4,
        after=[share],
    )
    received = [own_rows, near_rows] + spread(merged, steps)
    w_msg_near, gain, embed, w_hidden_near, project_near, present = staged
    field, sent, normed, active, slope, unit, inverse = call(
        functools.partial(forward_kernel, levels - 1),
        [
            ((members, variables, points), f32),
            ((members, variables, points), bf16),
            ((rows_all, width), bf16),
            ((rows_all, width), bf16),
            ((rows_all, width), f32),
            ((rows_all, width), f32),
            ((rows_all, 1), f32),
        ],
        [w_msg_near, share, gain, embed, w_hidden_near, project_near, present] + received,
        limit=20,
    )
    other = swap(sent, "member", cores, 1)
    normed_t, active_t, received_keep, received_give = call(
        turn_kernel,
        [((cores, 2, levels, block, rows_all), bf16)] * 2 + [((2, levels, block, rows_slot), bf16)] * 2,
        [normed, active] + received,
        limit=8,
    )
    received_other = swap(received_give, "member", cores, 1)
    grad_inner, pred, loss_part, far, near = call(
        score_kernel,
        [
            ((rows_all, width), bf16),
            ((lanes, rows_all), bf16),
            ((1,), f32),
            ((half, wide), bf16),
            ((half, wide), bf16),
        ],
        [field, other, verifying_field, cell_surface, project_near, slope, normed_t, active_t],
        scratch=[pltpu.VMEM((lanes, rows_all), f32)],
        limit=16,
        scalar_outs=(2,),
    )
    far_other = swap(far, "member", cores, 1)
    near_other = swap(near, "member", cores, 1)
    held_far, held_near = call(
        functools.partial(local_kernel, variables),
        [((half, wide), f32)] * 2,
        [loss_part, normed_t, active_t, grad_inner, pred],
        limit=12,
        scalars=(0,),
    )
    (first,) = call(
        functools.partial(first_kernel, variables, width),
        [((count, wide), bf16)],
        [held_far, far_other],
        limit=6,
    )
    first_other = swap(first, "space", peers, 1)
    (grad_hidden,) = call(
        back_kernel,
        [((rows_all, width), bf16)],
        [grad_inner, w_hidden_near, gain, unit, inverse],
        scratch=[pltpu.VMEM((rows_all, width), f32)],
        limit=14,
        after=[first],
    )
    slots, *slots_sent = call(
        slot_kernel,
        [((peers, rows_peer, width), bf16)] + [((2 * rows_peer, width), bf16)] * (levels - 1),
        [share, grad_hidden],
        limit=6,
        after=[near_other, received_other],
    )
    slots_other = swap(slots, "member", cores, 1)
    slots_arrived = spread(slots_sent, steps)
    message_first, middle, last, message_near = call(
        functools.partial(message_kernel, variables, early, levels),
        [
            ((count, width), bf16),
            ((2 * rest + packed, width), bf16),
            ((2 * block + packed, width), bf16),
            ((half, width), f32),
        ],
        [received_keep, received_other, slots, slots_other, held_far, far_other],
        limit=10,
    )
    message_first_other = swap(message_first, "space", peers, 1)
    middle_other = swap(middle, "space", peers, 1)
    hidden_early = call(
        functools.partial(hidden_early_kernel, variables, width),
        [((block, wide), bf16)] * early,
        [held_near, near_other, first_other],
        limit=6,
    )
    hidden_parts = spread(hidden_early, steps[:early])
    (last,) = call(
        ride_kernel,
        [((2 * block + packed + levels * rows_peer, width), bf16)],
        [last, slots] + slots_arrived,
        limit=4,
        after=hidden_early[:1],
    )
    last_other = swap(last, "space", peers, 1)
    message_parts = []
    for i in range(early):
        (piece,) = call(
            functools.partial(message_early_kernel, i * block),
            [((block, width), bf16)],
            [message_near, message_first_other],
            limit=6,
            after=hidden_parts[:i],
        )
        message_parts.append(swap(piece, "space", peers, steps[i]))
    late = call(
        functools.partial(late_kernel, variables, early),
        [((2 * block + packed, width), bf16)] * (levels - 1 - early),
        [held_near, near_other, message_near, middle_other],
        limit=6,
    )
    late_parts = spread(late, steps[early:])
    token = ((8, lanes), f32)
    latent_grad, latent_done = call(
        owner_kernel,
        [(latents.shape, bf16), token],
        [pick, w_msg, slots, last_other] + slots_arrived,
        scratch=[pltpu.VMEM((peers, rows_peer, width), bf16)],
        limit=8,
    )
    hidden_weight_grad, out_weight_grad, loss, hidden_done = call(
        functools.partial(hidden_sum_kernel, variables, 1.0 / (points * peers * variables), early),
        [((block, width), f32), ((block, variables), f32), ((1,), f32), token],
        [held_near, near_other, last_other] + hidden_parts + late_parts,
        limit=8,
        scalar_outs=(2,),
        after=[latent_done],
    )
    (msg_weight_grad,) = call(
        functools.partial(message_sum_kernel, early),
        [((block, width), f32)],
        [message_near, last_other] + message_parts + late_parts,
        limit=6,
        after=[hidden_done],
    )
    return (latent_grad, loss, msg_weight_grad, hidden_weight_grad, out_weight_grad)


def solution(mesh):
    placed = (
        P(("groups", "member"), "space", None),
        P(("groups", "space"), None),
        P(),
        P(),
        P(),
        P(),
        P(("groups", "member"), None, "space"),
        P(None, ("groups", "space")),
        P(("groups", "space")),
        P("space", None, None),
        P("space"),
        P("space"),
        P("space"),
    )
    return jax.shard_map(
        on_device,
        mesh=mesh,
        in_specs=placed,
        out_specs=(
            P(("groups", "member"), "space", None),
            P("groups"),
            P(("groups", "space", "member"), None),
            P(("groups", "space", "member"), None),
            P(("groups", "space", "member"), None),
        ),
        check_vma=False,
    )
```

```python
import functools

import jax
import jax.numpy as jnp
from jax import lax
from jax.experimental import pallas as pl
from jax.experimental.pallas import tpu as pltpu
from jax.sharding import PartitionSpec as P

smoothing = 0.1
epsilon = 1e-06
tile = 256
lanes = 128
packed = 16
cost_hints = {
    "back_kernel": 8,
    "slot_kernel": 4,
    "hidden_early_kernel": 4,
    "message_early_kernel": 4,
    "late_kernel": 4,
    "message_sum_kernel": 8,
}
f32 = jnp.float32
bf16 = jnp.bfloat16


def mm(left, right, left_dim, right_dim):
    return lax.dot_general(
        left, right, (((left_dim,), (right_dim,)), ((), ())), preferred_element_type=f32
    )


def call(body, outs, args, scratch=(), limit=16, scalars=(), scalar_outs=(), places=(), after=()):
    whole = pl.BlockSpec(memory_space=pltpu.VMEM)
    small = pl.BlockSpec(memory_space=pltpu.SMEM)
    far_place = pl.BlockSpec(memory_space=pltpu.HBM)
    any_place = pl.BlockSpec(memory_space=pl.ANY)
    count = len(after)
    cost = cost_hints.get(getattr(body, "func", body).__name__, 0) * 10**9
    args = [pltpu.with_memory_space_constraint(x, pltpu.HBM) if i in places else x for i, x in enumerate(args)]

    def inner(*refs):
        body(*refs[count:])

    specs = [small if i in scalars else far_place if i in places else whole for i in range(len(args))]
    return pl.pallas_call(
        inner if count else body,
        out_shape=[jax.ShapeDtypeStruct(dims, kind) for dims, kind in outs],
        in_specs=[any_place] * count + specs,
        out_specs=[small if i in scalar_outs else whole for i in range(len(outs))],
        scratch_shapes=scratch,
        compiler_params=pltpu.CompilerParams(vmem_limit_bytes=limit * 2**20),
        cost_estimate=pl.CostEstimate(flops=cost, bytes_accessed=0, transcendentals=0),
    )(*after, *args)


def place():
    space = lax.axis_index("space")
    return lax.div(space, 2), lax.rem(space, 2), lax.axis_index("member")


def swap(value, axis, size, step):
    return lax.ppermute(value, axis, [(i, i ^ step) for i in range(size)])


def select_kernel(lists_ref, latents_ref, pick_ref, own_ref, send_ref, small_ref, table_ref, sems):
    _, peers, cap = lists_ref.shape
    members, nodes, width = latents_ref.shape
    lists = pltpu.make_async_copy(lists_ref, small_ref, sems.at[0])
    table = pltpu.make_async_copy(latents_ref, table_ref, sems.at[1])
    lists.start()
    table.start()
    lists.wait()
    me = lax.axis_index("space")
    at = lax.broadcasted_iota(jnp.int32, (cap, members * nodes), 0)
    column = lax.broadcasted_iota(jnp.int32, (cap, members * nodes), 1)
    rows = []
    for step in range(peers):
        wanted = jnp.zeros((cap, members * nodes), jnp.int32)
        for j in range(cap):
            wanted = jnp.where(at == j, small_ref[0, me ^ step, j], wanted)
        for member in range(members):
            rows.append((column == wanted + member * nodes).astype(f32))
    pick = jnp.concatenate(rows, axis=0).astype(bf16)
    pick_ref[...] = pick
    table.wait()
    sent = mm(pick, table_ref[...].reshape(members * nodes, width), 1, 0)
    sent = sent.astype(bf16).reshape(peers // 2, 2, members * cap, width)
    own_ref[...] = sent[:, 0]
    send_ref[...] = sent[:, 1]


def merge_kernel(own_ref, arrived_ref, *out_refs):
    rows = own_ref.shape[1]
    for i, out_ref in enumerate(out_refs):
        step = len(out_refs) - i
        out_ref[0:rows, :] = own_ref[step]
        out_ref[rows:, :] = arrived_ref[step]


def stage_kernel(cap, members, count, *refs):
    edge_refs, source_refs, share_ref = refs[:3], refs[3 : 3 + count], refs[3 + count]
    staged_refs, held_refs, sems = refs[4 + count : 4 + 2 * count], refs[4 + 2 * count : -1], refs[-1]
    copies = [
        pltpu.make_async_copy(source, target, sems.at[i])
        for i, (source, target) in enumerate(
            zip(edge_refs + source_refs, held_refs + staged_refs, strict=True)
        )
    ]
    for copy in copies:
        copy.start()
    for copy in copies[:3]:
        copy.wait()
    edge_part(cap, members, *held_refs, share_ref)
    for copy in copies[3:]:
        copy.wait()


def edge_part(cap, members, slot_ref, dst_ref, weight_ref, share_ref):
    edges = slot_ref.shape[0]
    slot = slot_ref[...].reshape(1, edges)
    dst = dst_ref[...].reshape(1, edges)
    weight = weight_ref[...].reshape(1, edges)
    rows = share_ref.shape[0] // 2
    points = share_ref.shape[1] // members
    sender = lax.div(slot, cap)
    spot = (sender ^ lax.axis_index("space")) * (members * cap) + (slot - sender * cap)
    hit = lax.broadcasted_iota(jnp.int32, (rows, edges), 0) == spot
    into = (lax.broadcasted_iota(jnp.int32, (points, edges), 0) == dst).astype(f32).astype(bf16)
    high = weight.astype(bf16).astype(f32)
    table = mm(jnp.where(hit, high, 0.0).astype(bf16), into, 1, 1) + mm(
        jnp.where(hit, weight - high, 0.0).astype(bf16), into, 1, 1
    )
    table = table / jnp.sum(table, axis=0, keepdims=True)
    for member in range(members):
        high = table.astype(bf16)
        columns = slice(member * points, (member + 1) * points)
        share_ref[0:rows, columns] = high
        share_ref[rows : 2 * rows, columns] = (table - high.astype(f32)).astype(bf16)
        table = jnp.concatenate([table[rows - cap :], table[: rows - cap]], axis=0)


def gathered(own_ref, near_ref, far_refs):
    return jnp.concatenate([own_ref[0], near_ref[0]] + [r[...] for r in far_refs[::-1]], axis=0)


def forward_kernel(
    far, w_msg_ref, share_ref, gain_ref, embed_ref, weights_ref, project_ref, present_ref,
    own_ref, near_ref, *rest,
):
    far_refs = rest[:far]
    field_ref, sent_ref, normed_ref, active_ref, slope_ref, unit_ref, inverse_ref = rest[far:]
    points, width = embed_ref.shape
    variables, members, _ = present_ref.shape
    messages = mm(gathered(own_ref, near_ref, far_refs), w_msg_ref[...], 1, 0).astype(bf16)
    messages = jnp.concatenate([messages, messages], axis=0)
    gain = gain_ref[...].reshape(1, width)
    for begin in range(0, members * points, lanes):
        rows = slice(begin, begin + lanes)
        source = slice(begin % points, begin % points + lanes)
        hidden = embed_ref[source, :].astype(f32) + mm(share_ref[:, rows], messages, 0, 0)
        inverse = lax.rsqrt(jnp.mean(hidden * hidden, axis=-1, keepdims=True) + epsilon)
        unit = hidden * inverse
        unit_ref[rows, :] = unit
        inverse_ref[rows, :] = inverse
        normed_ref[rows, :] = (unit * gain).astype(bf16)
    root = 0.7978845608028654
    cubic = 0.044715
    for member in range(members):
        rows = slice(member * points, (member + 1) * points)
        for begin in range(0, width, tile):
            columns = slice(begin, begin + tile)
            inner = mm(normed_ref[rows, :], weights_ref[:, columns], 1, 0)
            square = inner * inner
            bend = jnp.tanh(inner * (root + root * cubic * square))
            half = 0.5 + 0.5 * bend
            active_ref[rows, columns] = (inner * half).astype(bf16)
            slope_ref[rows, columns] = half + (0.5 * inner) * (1.0 - bend * bend) * (
                root + 3.0 * root * cubic * square
            )
        field = present_ref[:, member, :] + mm(project_ref[...], active_ref[rows, :], 1, 1)
        field_ref[member] = field
        sent_ref[member] = field.astype(bf16)


def turn_kernel(normed_ref, active_ref, own_ref, near_ref, *rest):
    far_refs, (normed_t_ref, active_t_ref, keep_ref, give_ref) = rest[:-4], rest[-4:]
    _, _, levels, block, _ = normed_t_ref.shape
    width = normed_ref.shape[1]
    level, line, core = place()
    received = gathered(own_ref, near_ref, far_refs)
    for source, target in ((received, None), (normed_ref, normed_t_ref), (active_ref, active_t_ref)):
        for begin in range(0, width, tile):
            turned = source[:, begin : begin + tile].T
            for piece in range(0, tile, block):
                index = (begin + piece) // block
                far = (index // 2 % 2) ^ line
                step = (index // 4) ^ level
                side = (index % 2) ^ core
                value = turned[piece : piece + block]
                if target is not None:
                    target[side, 1 - far, levels - 1 - step] = value
                    continue
                for which, part_ref in enumerate((keep_ref, give_ref)):
                    @pl.when(side == which)
                    def _(part_ref=part_ref):
                        part_ref[1 - far, levels - 1 - step] = value


def split_loss(part, variables):
    column = lax.broadcasted_iota(jnp.int32, part.shape, 1)
    spots = (column == variables) | (column == variables + 1)
    total = jnp.sum(jnp.where(spots, part, 0.0), axis=1, keepdims=True)
    high = total.astype(bf16).astype(f32)
    return jnp.where(column == variables, high, jnp.where(column == variables + 1, total - high, part))


def score_kernel(
    own_ref, other_ref, truth_ref, cell_ref, project_ref, slope_ref, normed_t_ref, active_t_ref,
    inner_ref, pred_ref, loss_ref, far_ref, near_ref, hold_ref,
):
    members, variables, points = own_ref.shape
    width = slope_ref.shape[1]
    total = 2 * members
    pairs = total * (total - 1)

    def eased(delta):
        square = delta * delta + smoothing * smoothing
        inverse = lax.rsqrt(square)
        return square * inverse, delta * inverse

    truth, cell = truth_ref[...], cell_ref[...].reshape(1, points)
    own = [own_ref[m] for m in range(members)]
    other = [other_ref[m].astype(f32) for m in range(members)]
    score = jnp.zeros_like(truth)
    pulls = [jnp.zeros_like(truth) for _ in own]
    grads = []
    for m in range(members):
        size, sign = eased(own[m] - truth)
        score = score + size * (1.0 / total)
        grads.append(sign * (1.0 / total))
    for m in range(members):
        for n in range(m + 1, members):
            size, sign = eased(own[m] - own[n])
            score = score - size * (1.0 / pairs)
            pulls[m] = pulls[m] + sign
            pulls[n] = pulls[n] - sign
        for n in range(members):
            size, sign = eased(own[m] - other[n])
            score = score - size * (0.5 / pairs)
            pulls[m] = pulls[m] + sign
    loss = jnp.sum(score * cell)
    loss_ref[0] = loss
    hold_ref[...] = jnp.zeros_like(hold_ref)
    for m in range(members):
        grad = (grads[m] - pulls[m] * (1.0 / pairs)) * cell
        hold_ref[0:variables, m * points : (m + 1) * points] = grad
    pred = hold_ref[...].astype(bf16)
    pred_ref[...] = pred
    for m in range(members):
        rows = slice(m * points, (m + 1) * points)
        part = pred[:variables, rows]
        for begin in range(0, width, tile):
            columns = slice(begin, begin + tile)
            grad = mm(part, project_ref[:, columns], 0, 0)
            inner_ref[rows, columns] = (grad * slope_ref[rows, columns]).astype(bf16)
    weight_parts(normed_t_ref, active_t_ref, inner_ref, pred, loss, variables, 1, 0, far_ref)
    weight_parts(normed_t_ref, active_t_ref, inner_ref, pred, loss, variables, 1, 1, near_ref)


def weight_parts(normed_t_ref, active_t_ref, inner_ref, pred, loss, variables, side, half, out_ref):
    width = inner_ref.shape[1]
    depth = normed_t_ref.shape[-1]
    normed = normed_t_ref[side, half].reshape(-1, depth)
    for begin in range(0, width, tile):
        columns = slice(begin, begin + tile)
        out_ref[:, columns] = mm(normed, inner_ref[:, columns], 1, 0).astype(out_ref.dtype)
    part = mm(active_t_ref[side, half].reshape(-1, depth), pred, 1, 1)
    part = jnp.where(lax.broadcasted_iota(jnp.int32, part.shape, 1) == variables, loss, part)
    out_ref[:, width:] = split_loss(part, variables).astype(out_ref.dtype)


def pack(out_ref, begin, part):
    pad = part.shape[1]
    for i in range(part.shape[0] // packed):
        out_ref[begin : begin + packed, i * pad : (i + 1) * pad] = part[i * packed : (i + 1) * packed]


def unpack(in_ref, begin, count, pad):
    parts = [in_ref[begin : begin + packed, i * pad : (i + 1) * pad] for i in range(count // packed)]
    return jnp.concatenate(parts, axis=0).astype(f32)


def local_kernel(variables, loss_ref, normed_t_ref, active_t_ref, inner_ref, pred_ref, far_ref, near_ref):
    for half, out_ref in ((0, far_ref), (1, near_ref)):
        weight_parts(
            normed_t_ref, active_t_ref, inner_ref, pred_ref[...], loss_ref[0], variables, 0, half, out_ref
        )


def pair_sum(variables, width, held_ref, other_ref, begin, count):
    rows = slice(begin, begin + count)
    total = held_ref[rows, :width] + other_ref[rows, :width].astype(f32)
    part = held_ref[rows, width:] + other_ref[rows, width:].astype(f32)
    return total, split_loss(part, variables)


def first_kernel(variables, width, held_ref, other_ref, out_ref):
    total, part = pair_sum(variables, width, held_ref, other_ref, 0, out_ref.shape[0])
    out_ref[:, :width] = total.astype(bf16)
    out_ref[:, width:] = part.astype(bf16)


def message_kernel(
    variables, early, levels, keep_ref, give_ref, slots_ref, other_ref, held_ref, far_other_ref,
    first_ref, middle_ref, last_ref, near_ref,
):
    depth, width = keep_ref.shape[-1], near_ref.shape[1]
    block = near_ref.shape[0] // levels
    count, rest = early * block, (levels - 1 - early) * block
    for begin, size, out_ref in ((count, rest, middle_ref), (count + rest, block, last_ref)):
        total, part = pair_sum(variables, width, held_ref, far_other_ref, begin, size)
        out_ref[0:size, :] = total.astype(bf16)
        out_ref[size : size + packed, :] = jnp.zeros((packed, width), bf16)
        pack(out_ref, size, part.astype(bf16))
    for half in range(2):
        own = keep_ref[half].reshape(-1, depth)
        other = give_ref[half].reshape(-1, depth)
        for begin in range(0, width, tile):
            columns = slice(begin, begin + tile)
            here = slots_ref[:, :, columns].reshape(depth, tile)
            there = other_ref[:, :, columns].reshape(depth, tile)
            total = mm(own, here, 1, 0) + mm(other, there, 1, 0)
            if half == 0:
                total = total.astype(bf16)
                first_ref[:, columns] = total[:count]
                middle_ref[rest + packed :, columns] = total[count : count + rest]
                last_ref[block + packed :, columns] = total[count + rest :]
            else:
                near_ref[:, columns] = total


def ride_kernel(last_ref, slots_ref, *rest):
    arrived_refs, out_ref = rest[:-1], rest[-1]
    rows = slots_ref.shape[1]
    begin = last_ref.shape[0]
    out_ref[0:begin, :] = last_ref[...]
    for i, arrived_ref in enumerate(arrived_refs):
        out_ref[begin + i * rows : begin + (i + 1) * rows, :] = arrived_ref[rows:, :]
    out_ref[begin + len(arrived_refs) * rows :, :] = slots_ref[1]


def hidden_early_kernel(variables, width, held_ref, other_ref, arrived_ref, *out_refs):
    block = out_refs[0].shape[0]
    for i, out_ref in enumerate(out_refs):
        total, part = pair_sum(variables, width, held_ref, other_ref, i * block, block)
        here = slice(i * block, (i + 1) * block)
        out_ref[:, :width] = (total + arrived_ref[here, :width].astype(f32)).astype(bf16)
        part = split_loss(part + arrived_ref[here, width:].astype(f32), variables)
        out_ref[:, width:] = part.astype(bf16)


def message_early_kernel(begin, near_ref, arrived_ref, out_ref):
    here = slice(begin, begin + out_ref.shape[0])
    out_ref[...] = (near_ref[here, :] + arrived_ref[here, :].astype(f32)).astype(bf16)


def late_kernel(variables, early, held_ref, other_ref, near_ref, arrived_ref, *out_refs):
    width = near_ref.shape[1]
    block = (out_refs[0].shape[0] - packed) // 2
    count = block * len(out_refs)
    parts = unpack(arrived_ref, count, count, held_ref.shape[1] - width)
    for i, out_ref in enumerate(out_refs):
        begin = (early + i) * block
        total, part = pair_sum(variables, width, held_ref, other_ref, begin, block)
        here = slice(i * block, (i + 1) * block)
        out_ref[0:block, :] = (total + arrived_ref[here, :].astype(f32)).astype(bf16)
        there = slice(count + packed + i * block, count + packed + (i + 1) * block)
        total = near_ref[begin : begin + block, :] + arrived_ref[there, :].astype(f32)
        out_ref[block : 2 * block, :] = total.astype(bf16)
        out_ref[2 * block :, :] = jnp.zeros((packed, width), bf16)
        pack(out_ref, 2 * block, split_loss(part + parts[here], variables).astype(bf16))


def back_kernel(inner_ref, w_hidden_ref, gain_ref, unit_ref, inverse_ref, grad_ref, scaled_ref):
    rows_all, width = inner_ref.shape
    gain = gain_ref[...].reshape(1, width)
    for begin_row in range(0, rows_all, tile):
        rows = slice(begin_row, begin_row + tile)
        dots = jnp.zeros((tile, 1), f32)
        for begin in range(0, width, tile):
            columns = slice(begin, begin + tile)
            scaled = mm(inner_ref[rows, :], w_hidden_ref[columns, :], 1, 1) * gain[:, columns]
            dots = dots + jnp.sum(scaled * unit_ref[rows, columns], axis=-1, keepdims=True)
            scaled_ref[rows, columns] = scaled
        dots = dots * (1.0 / width)
        inverse = inverse_ref[rows, :]
        for begin in range(0, width, tile):
            columns = slice(begin, begin + tile)
            grad_ref[rows, columns] = (
                (scaled_ref[rows, columns] - unit_ref[rows, columns] * dots) * inverse
            ).astype(bf16)


def slot_kernel(share_ref, grad_ref, slots_ref, *send_refs):
    peers, each, width = slots_ref.shape
    rows = peers * each
    for begin in range(0, width, tile):
        columns = slice(begin, begin + tile)
        both = mm(share_ref[...], grad_ref[:, columns], 1, 0)
        slots_ref[:, :, columns] = (both[:rows] + both[rows:]).astype(bf16).reshape(peers, each, tile)
    for i, send_ref in enumerate(send_refs):
        step = len(send_refs) - i
        send_ref[0:each, :] = slots_ref[2 * step]
        send_ref[each:, :] = slots_ref[2 * step + 1]


def owner_kernel(pick_ref, w_msg_ref, slots_ref, last_ref, *rest):
    arrived_refs, (grad_ref, token_ref, held_ref) = rest[:-3], rest[-3:]
    token_ref[...] = jnp.zeros_like(token_ref)
    peers, rows, width = slots_ref.shape
    levels = peers // 2
    begin = last_ref.shape[0] - levels * rows
    for i in range(levels):
        spot = 2 * (levels - 1 - i)
        held_ref[spot] = slots_ref[0] if i == levels - 1 else arrived_refs[i][0:rows, :]
        held_ref[spot + 1] = last_ref[begin + i * rows : begin + (i + 1) * rows, :]
    nodes = mm(pick_ref[...], held_ref[...].reshape(peers * rows, width), 0, 0).astype(bf16)
    grad_ref[...] = mm(nodes, w_msg_ref[...], 1, 1).astype(bf16).reshape(grad_ref.shape)


def hidden_sum_kernel(variables, scale, early, held_ref, other_ref, last_ref, *rest):
    hidden_ref, out_ref, loss_ref, token_ref = rest[-4:]
    token_ref[...] = jnp.zeros_like(token_ref)
    block, width = hidden_ref.shape
    pad = held_ref.shape[1] - width
    total, part = pair_sum(variables, width, held_ref, other_ref, held_ref.shape[0] - block, block)
    total = total + last_ref[0:block, :].astype(f32)
    part = part + unpack(last_ref, block, block, pad)
    for i, r in enumerate(rest[:-4]):
        total = total + r[0:block, :width].astype(f32)
        if i < early:
            part = part + r[:, width:].astype(f32)
        else:
            part = part + unpack(r, 2 * block, block, pad)
    hidden_ref[...] = total
    out_ref[...] = part[:, :variables]
    column = lax.broadcasted_iota(jnp.int32, (8, pad), 1)
    spots = (column == variables) | (column == variables + 1)
    first = lax.broadcasted_iota(jnp.int32, (8, pad), 0) == 0
    loss_ref[0] = jnp.sum(jnp.where(spots & first, part[:8], 0.0)) * scale


def message_sum_kernel(early, near_ref, last_ref, *rest):
    out_ref = rest[-1]
    block = out_ref.shape[0]
    total = near_ref[near_ref.shape[0] - block :, :]
    total = total + last_ref[block + packed : 2 * block + packed, :].astype(f32)
    for i, r in enumerate(rest[:-1]):
        begin = 0 if i < early else block
        total = total + r[begin : begin + block, :].astype(f32)
    out_ref[...] = total


def on_device(
    latents, grid_embed, norm_gain, w_msg, w_hidden, variable_projection, present_condition, verifying_field,
    cell_surface, send_rows, edge_slot, edge_dst, edge_weight,
):
    members, nodes, width = latents.shape
    points = grid_embed.shape[0]
    variables = variable_projection.shape[1]
    peers = lax.axis_size("space")
    cores = lax.axis_size("member")
    cap = send_rows.shape[2]
    rows_peer = members * cap
    rows_slot = peers * rows_peer
    rows_all = members * points
    levels = peers // 2
    block = width // (peers * cores)
    half = levels * block
    wide = width + -(-(variables + 2) // lanes) * lanes
    project = variable_projection.T

    early = levels // 2
    count, rest = early * block, (levels - 1 - early) * block
    steps = [2 * (levels - 1 - i) for i in range(levels - 1)]

    def spread(values, part):
        return [swap(x, "space", peers, k) for x, k in zip(values, part, strict=True)]

    pick, own_rows, send = call(
        select_kernel,
        [((rows_slot, members * nodes), bf16)] + [((levels, rows_peer, width), bf16)] * 2,
        [send_rows, latents],
        scratch=[
            pltpu.SMEM(send_rows.shape, jnp.int32),
            pltpu.VMEM(latents.shape, bf16),
            pltpu.SemaphoreType.DMA((2,)),
        ],
        limit=4,
        places=(0, 1),
    )
    near_rows = swap(send, "space", peers, 1)
    fixed = [w_msg, norm_gain, grid_embed, w_hidden, project, present_condition.transpose(1, 0, 2)]
    edges = [edge_slot, edge_dst, edge_weight]
    share, *staged = call(
        functools.partial(stage_kernel, cap, members, len(fixed)),
        [((2 * rows_slot, rows_all), bf16)] + [(x.shape, x.dtype) for x in fixed],
        edges + fixed,
        scratch=[pltpu.VMEM(x.shape, x.dtype) for x in edges]
        + [pltpu.SemaphoreType.DMA((3 + len(fixed),))],
        limit=16,
        places=tuple(range(3 + len(fixed))),
        after=[pick],
    )
    merged = call(
        merge_kernel,
        [((2 * rows_peer, width), bf16)] * (levels - 1),
        [own_rows, near_rows],
        limit=4,
        after=[share],
    )
    received = [own_rows, near_rows] + spread(merged, steps)
    w_msg_near, gain, embed, w_hidden_near, project_near, present = staged
    field, sent, normed, active, slope, unit, inverse = call(
        functools.partial(forward_kernel, levels - 1),
        [
            ((members, variables, points), f32),
            ((members, variables, points), bf16),
            ((rows_all, width), bf16),
            ((rows_all, width), bf16),
            ((rows_all, width), f32),
            ((rows_all, width), f32),
            ((rows_all, 1), f32),
        ],
        [w_msg_near, share, gain, embed, w_hidden_near, project_near, present] + received,
        limit=20,
    )
    other = swap(sent, "member", cores, 1)
    normed_t, active_t, received_keep, received_give = call(
        turn_kernel,
        [((cores, 2, levels, block, rows_all), bf16)] * 2 + [((2, levels, block, rows_slot), bf16)] * 2,
        [normed, active] + received,
        limit=8,
    )
    received_other = swap(received_give, "member", cores, 1)
    grad_inner, pred, loss_part, far, near = call(
        score_kernel,
        [
            ((rows_all, width), bf16),
            ((lanes, rows_all), bf16),
            ((1,), f32),
            ((half, wide), bf16),
            ((half, wide), bf16),
        ],
        [field, other, verifying_field, cell_surface, project_near, slope, normed_t, active_t],
        scratch=[pltpu.VMEM((lanes, rows_all), f32)],
        limit=16,
        scalar_outs=(2,),
    )
    far_other = swap(far, "member", cores, 1)
    near_other = swap(near, "member", cores, 1)
    held_far, held_near = call(
        functools.partial(local_kernel, variables),
        [((half, wide), f32)] * 2,
        [loss_part, normed_t, active_t, grad_inner, pred],
        limit=12,
        scalars=(0,),
    )
    (first,) = call(
        functools.partial(first_kernel, variables, width),
        [((count, wide), bf16)],
        [held_far, far_other],
        limit=6,
    )
    first_other = swap(first, "space", peers, 1)
    (grad_hidden,) = call(
        back_kernel,
        [((rows_all, width), bf16)],
        [grad_inner, w_hidden_near, gain, unit, inverse],
        scratch=[pltpu.VMEM((rows_all, width), f32)],
        limit=14,
        after=[first],
    )
    slots, *slots_sent = call(
        slot_kernel,
        [((peers, rows_peer, width), bf16)] + [((2 * rows_peer, width), bf16)] * (levels - 1),
        [share, grad_hidden],
        limit=6,
        after=[near_other, received_other],
    )
    slots_other = swap(slots, "member", cores, 1)
    slots_arrived = spread(slots_sent, steps)
    message_first, middle, last, message_near = call(
        functools.partial(message_kernel, variables, early, levels),
        [
            ((count, width), bf16),
            ((2 * rest + packed, width), bf16),
            ((2 * block + packed, width), bf16),
            ((half, width), f32),
        ],
        [received_keep, received_other, slots, slots_other, held_far, far_other],
        limit=10,
    )
    message_first_other = swap(message_first, "space", peers, 1)
    middle_other = swap(middle, "space", peers, 1)
    hidden_early = call(
        functools.partial(hidden_early_kernel, variables, width),
        [((block, wide), bf16)] * early,
        [held_near, near_other, first_other],
        limit=6,
    )
    hidden_parts = spread(hidden_early, steps[:early])
    (last,) = call(
        ride_kernel,
        [((2 * block + packed + levels * rows_peer, width), bf16)],
        [last, slots] + slots_arrived,
        limit=4,
        after=hidden_early[:1],
    )
    last_other = swap(last, "space", peers, 1)
    message_parts = []
    for i in range(early):
        (piece,) = call(
            functools.partial(message_early_kernel, i * block),
            [((block, width), bf16)],
            [message_near, message_first_other],
            limit=6,
            after=hidden_parts[1 : 1 + i],
        )
        message_parts.append(swap(piece, "space", peers, steps[i]))
    late = call(
        functools.partial(late_kernel, variables, early),
        [((2 * block + packed, width), bf16)] * (levels - 1 - early),
        [held_near, near_other, message_near, middle_other],
        limit=6,
    )
    late_parts = spread(late, steps[early:])
    token = ((8, lanes), f32)
    latent_grad, latent_done = call(
        owner_kernel,
        [(latents.shape, bf16), token],
        [pick, w_msg, slots, last_other] + slots_arrived,
        scratch=[pltpu.VMEM((peers, rows_peer, width), bf16)],
        limit=8,
    )
    hidden_weight_grad, out_weight_grad, loss, hidden_done = call(
        functools.partial(hidden_sum_kernel, variables, 1.0 / (points * peers * variables), early),
        [((block, width), f32), ((block, variables), f32), ((1,), f32), token],
        [held_near, near_other, last_other] + hidden_parts + late_parts,
        limit=8,
        scalar_outs=(2,),
        after=[latent_done],
    )
    (msg_weight_grad,) = call(
        functools.partial(message_sum_kernel, early),
        [((block, width), f32)],
        [message_near, last_other] + message_parts + late_parts,
        limit=6,
        after=[hidden_done],
    )
    return (latent_grad, loss, msg_weight_grad, hidden_weight_grad, out_weight_grad)


def solution(mesh):
    placed = (
        P(("groups", "member"), "space", None),
        P(("groups", "space"), None),
        P(),
        P(),
        P(),
        P(),
        P(("groups", "member"), None, "space"),
        P(None, ("groups", "space")),
        P(("groups", "space")),
        P("space", None, None),
        P("space"),
        P("space"),
        P("space"),
    )
    return jax.shard_map(
        on_device,
        mesh=mesh,
        in_specs=placed,
        out_specs=(
            P(("groups", "member"), "space", None),
            P("groups"),
            P(("groups", "space", "member"), None),
            P(("groups", "space", "member"), None),
            P(("groups", "space", "member"), None),
        ),
        check_vma=False,
    )
```

```python
import functools

import jax
import jax.numpy as jnp
from jax import lax
from jax.experimental import pallas as pl
from jax.experimental.pallas import tpu as pltpu
from jax.sharding import PartitionSpec as P

smoothing = 0.1
epsilon = 1e-06
tile = 256
lanes = 128
packed = 16
cost_hints = {
    "back_kernel": 8,
    "slot_kernel": 4,
    "hidden_early_kernel": 8,
    "message_early_kernel": 4,
    "late_kernel": 4,
    "owner_kernel": 8,
}
f32 = jnp.float32
bf16 = jnp.bfloat16


def mm(left, right, left_dim, right_dim):
    return lax.dot_general(
        left, right, (((left_dim,), (right_dim,)), ((), ())), preferred_element_type=f32
    )


def call(body, outs, args, scratch=(), limit=16, scalars=(), scalar_outs=(), places=(), after=()):
    whole = pl.BlockSpec(memory_space=pltpu.VMEM)
    small = pl.BlockSpec(memory_space=pltpu.SMEM)
    far_place = pl.BlockSpec(memory_space=pltpu.HBM)
    any_place = pl.BlockSpec(memory_space=pl.ANY)
    count = len(after)
    cost = cost_hints.get(getattr(body, "func", body).__name__, 0) * 10**9
    args = [pltpu.with_memory_space_constraint(x, pltpu.HBM) if i in places else x for i, x in enumerate(args)]

    def inner(*refs):
        body(*refs[count:])

    specs = [small if i in scalars else far_place if i in places else whole for i in range(len(args))]
    return pl.pallas_call(
        inner if count else body,
        out_shape=[jax.ShapeDtypeStruct(dims, kind) for dims, kind in outs],
        in_specs=[any_place] * count + specs,
        out_specs=[small if i in scalar_outs else whole for i in range(len(outs))],
        scratch_shapes=scratch,
        compiler_params=pltpu.CompilerParams(vmem_limit_bytes=limit * 2**20),
        cost_estimate=pl.CostEstimate(flops=cost, bytes_accessed=0, transcendentals=0),
    )(*after, *args)


def place():
    space = lax.axis_index("space")
    return lax.div(space, 2), lax.rem(space, 2), lax.axis_index("member")


def swap(value, axis, size, step):
    return lax.ppermute(value, axis, [(i, i ^ step) for i in range(size)])


def select_kernel(lists_ref, latents_ref, pick_ref, own_ref, send_ref, small_ref, table_ref, sems):
    _, peers, cap = lists_ref.shape
    members, nodes, width = latents_ref.shape
    lists = pltpu.make_async_copy(lists_ref, small_ref, sems.at[0])
    table = pltpu.make_async_copy(latents_ref, table_ref, sems.at[1])
    lists.start()
    table.start()
    lists.wait()
    me = lax.axis_index("space")
    at = lax.broadcasted_iota(jnp.int32, (cap, members * nodes), 0)
    column = lax.broadcasted_iota(jnp.int32, (cap, members * nodes), 1)
    rows = []
    for step in range(peers):
        wanted = jnp.zeros((cap, members * nodes), jnp.int32)
        for j in range(cap):
            wanted = jnp.where(at == j, small_ref[0, me ^ step, j], wanted)
        for member in range(members):
            rows.append((column == wanted + member * nodes).astype(f32))
    pick = jnp.concatenate(rows, axis=0).astype(bf16)
    pick_ref[...] = pick
    table.wait()
    sent = mm(pick, table_ref[...].reshape(members * nodes, width), 1, 0)
    sent = sent.astype(bf16).reshape(peers // 2, 2, members * cap, width)
    own_ref[...] = sent[:, 0]
    send_ref[...] = sent[:, 1]


def merge_kernel(own_ref, arrived_ref, *out_refs):
    rows = own_ref.shape[1]
    for i, out_ref in enumerate(out_refs):
        step = len(out_refs) - i
        out_ref[0:rows, :] = own_ref[step]
        out_ref[rows:, :] = arrived_ref[step]


def stage_kernel(cap, members, count, *refs):
    edge_refs, source_refs, share_ref = refs[:3], refs[3 : 3 + count], refs[3 + count]
    staged_refs, held_refs, sems = refs[4 + count : 4 + 2 * count], refs[4 + 2 * count : -1], refs[-1]
    copies = [
        pltpu.make_async_copy(source, target, sems.at[i])
        for i, (source, target) in enumerate(
            zip(edge_refs + source_refs, held_refs + staged_refs, strict=True)
        )
    ]
    for copy in copies:
        copy.start()
    for copy in copies[:3]:
        copy.wait()
    edge_part(cap, members, *held_refs, share_ref)
    for copy in copies[3:]:
        copy.wait()


def edge_part(cap, members, slot_ref, dst_ref, weight_ref, share_ref):
    edges = slot_ref.shape[0]
    slot = slot_ref[...].reshape(1, edges)
    dst = dst_ref[...].reshape(1, edges)
    weight = weight_ref[...].reshape(1, edges)
    rows = share_ref.shape[0] // 2
    points = share_ref.shape[1] // members
    sender = lax.div(slot, cap)
    spot = (sender ^ lax.axis_index("space")) * (members * cap) + (slot - sender * cap)
    hit = lax.broadcasted_iota(jnp.int32, (rows, edges), 0) == spot
    into = (lax.broadcasted_iota(jnp.int32, (points, edges), 0) == dst).astype(f32).astype(bf16)
    high = weight.astype(bf16).astype(f32)
    table = mm(jnp.where(hit, high, 0.0).astype(bf16), into, 1, 1) + mm(
        jnp.where(hit, weight - high, 0.0).astype(bf16), into, 1, 1
    )
    table = table / jnp.sum(table, axis=0, keepdims=True)
    for member in range(members):
        high = table.astype(bf16)
        columns = slice(member * points, (member + 1) * points)
        share_ref[0:rows, columns] = high
        share_ref[rows : 2 * rows, columns] = (table - high.astype(f32)).astype(bf16)
        table = jnp.concatenate([table[rows - cap :], table[: rows - cap]], axis=0)


def gathered(own_ref, near_ref, far_refs):
    return jnp.concatenate([own_ref[0], near_ref[0]] + [r[...] for r in far_refs[::-1]], axis=0)


def forward_kernel(
    far, w_msg_ref, share_ref, gain_ref, embed_ref, weights_ref, project_ref, present_ref,
    own_ref, near_ref, *rest,
):
    far_refs = rest[:far]
    field_ref, sent_ref, normed_ref, active_ref, slope_ref, unit_ref, inverse_ref = rest[far:]
    points, width = embed_ref.shape
    variables, members, _ = present_ref.shape
    messages = mm(gathered(own_ref, near_ref, far_refs), w_msg_ref[...], 1, 0).astype(bf16)
    messages = jnp.concatenate([messages, messages], axis=0)
    gain = gain_ref[...].reshape(1, width)
    for begin in range(0, members * points, lanes):
        rows = slice(begin, begin + lanes)
        source = slice(begin % points, begin % points + lanes)
        hidden = embed_ref[source, :].astype(f32) + mm(share_ref[:, rows], messages, 0, 0)
        inverse = lax.rsqrt(jnp.mean(hidden * hidden, axis=-1, keepdims=True) + epsilon)
        unit = hidden * inverse
        unit_ref[rows, :] = unit
        inverse_ref[rows, :] = inverse
        normed_ref[rows, :] = (unit * gain).astype(bf16)
    root = 0.7978845608028654
    cubic = 0.044715
    for member in range(members):
        rows = slice(member * points, (member + 1) * points)
        for begin in range(0, width, tile):
            columns = slice(begin, begin + tile)
            inner = mm(normed_ref[rows, :], weights_ref[:, columns], 1, 0)
            square = inner * inner
            bend = jnp.tanh(inner * (root + root * cubic * square))
            half = 0.5 + 0.5 * bend
            active_ref[rows, columns] = (inner * half).astype(bf16)
            slope_ref[rows, columns] = half + (0.5 * inner) * (1.0 - bend * bend) * (
                root + 3.0 * root * cubic * square
            )
        field = present_ref[:, member, :] + mm(project_ref[...], active_ref[rows, :], 1, 1)
        field_ref[member] = field
        sent_ref[member] = field.astype(bf16)


def turn_kernel(normed_ref, active_ref, own_ref, near_ref, *rest):
    far_refs, (normed_t_ref, active_t_ref, keep_ref, give_ref) = rest[:-4], rest[-4:]
    _, _, levels, block, _ = normed_t_ref.shape
    width = normed_ref.shape[1]
    level, line, core = place()
    received = gathered(own_ref, near_ref, far_refs)
    for source, target in ((received, None), (normed_ref, normed_t_ref), (active_ref, active_t_ref)):
        for begin in range(0, width, tile):
            turned = source[:, begin : begin + tile].T
            for piece in range(0, tile, block):
                index = (begin + piece) // block
                far = (index // 2 % 2) ^ line
                step = (index // 4) ^ level
                side = (index % 2) ^ core
                value = turned[piece : piece + block]
                if target is not None:
                    target[side, 1 - far, levels - 1 - step] = value
                    continue
                for which, part_ref in enumerate((keep_ref, give_ref)):
                    @pl.when(side == which)
                    def _(part_ref=part_ref):
                        part_ref[1 - far, levels - 1 - step] = value


def split_loss(part, variables):
    column = lax.broadcasted_iota(jnp.int32, part.shape, 1)
    spots = (column == variables) | (column == variables + 1)
    total = jnp.sum(jnp.where(spots, part, 0.0), axis=1, keepdims=True)
    high = total.astype(bf16).astype(f32)
    return jnp.where(column == variables, high, jnp.where(column == variables + 1, total - high, part))


def score_kernel(
    own_ref, other_ref, truth_ref, cell_ref, project_ref, slope_ref, normed_t_ref, active_t_ref,
    inner_ref, pred_ref, loss_ref, far_ref, near_ref, hold_ref,
):
    members, variables, points = own_ref.shape
    width = slope_ref.shape[1]
    total = 2 * members
    pairs = total * (total - 1)

    def eased(delta):
        square = delta * delta + smoothing * smoothing
        inverse = lax.rsqrt(square)
        return square * inverse, delta * inverse

    truth, cell = truth_ref[...], cell_ref[...].reshape(1, points)
    own = [own_ref[m] for m in range(members)]
    other = [other_ref[m].astype(f32) for m in range(members)]
    score = jnp.zeros_like(truth)
    pulls = [jnp.zeros_like(truth) for _ in own]
    grads = []
    for m in range(members):
        size, sign = eased(own[m] - truth)
        score = score + size * (1.0 / total)
        grads.append(sign * (1.0 / total))
    for m in range(members):
        for n in range(m + 1, members):
            size, sign = eased(own[m] - own[n])
            score = score - size * (1.0 / pairs)
            pulls[m] = pulls[m] + sign
            pulls[n] = pulls[n] - sign
        for n in range(members):
            size, sign = eased(own[m] - other[n])
            score = score - size * (0.5 / pairs)
            pulls[m] = pulls[m] + sign
    loss = jnp.sum(score * cell)
    loss_ref[0] = loss
    hold_ref[...] = jnp.zeros_like(hold_ref)
    for m in range(members):
        grad = (grads[m] - pulls[m] * (1.0 / pairs)) * cell
        hold_ref[0:variables, m * points : (m + 1) * points] = grad
    pred = hold_ref[...].astype(bf16)
    pred_ref[...] = pred
    for m in range(members):
        rows = slice(m * points, (m + 1) * points)
        part = pred[:variables, rows]
        for begin in range(0, width, tile):
            columns = slice(begin, begin + tile)
            grad = mm(part, project_ref[:, columns], 0, 0)
            inner_ref[rows, columns] = (grad * slope_ref[rows, columns]).astype(bf16)
    weight_parts(normed_t_ref, active_t_ref, inner_ref, pred, loss, variables, 1, 0, far_ref)
    weight_parts(normed_t_ref, active_t_ref, inner_ref, pred, loss, variables, 1, 1, near_ref)


def weight_parts(normed_t_ref, active_t_ref, inner_ref, pred, loss, variables, side, half, out_ref):
    width = inner_ref.shape[1]
    depth = normed_t_ref.shape[-1]
    normed = normed_t_ref[side, half].reshape(-1, depth)
    for begin in range(0, width, tile):
        columns = slice(begin, begin + tile)
        out_ref[:, columns] = mm(normed, inner_ref[:, columns], 1, 0).astype(out_ref.dtype)
    part = mm(active_t_ref[side, half].reshape(-1, depth), pred, 1, 1)
    part = jnp.where(lax.broadcasted_iota(jnp.int32, part.shape, 1) == variables, loss, part)
    out_ref[:, width:] = split_loss(part, variables).astype(out_ref.dtype)


def pack(out_ref, begin, part):
    pad = part.shape[1]
    for i in range(part.shape[0] // packed):
        out_ref[begin : begin + packed, i * pad : (i + 1) * pad] = part[i * packed : (i + 1) * packed]


def unpack(in_ref, begin, count, pad):
    parts = [in_ref[begin : begin + packed, i * pad : (i + 1) * pad] for i in range(count // packed)]
    return jnp.concatenate(parts, axis=0).astype(f32)


def local_kernel(variables, loss_ref, normed_t_ref, active_t_ref, inner_ref, pred_ref, far_ref, near_ref):
    for half, out_ref in ((0, far_ref), (1, near_ref)):
        weight_parts(
            normed_t_ref, active_t_ref, inner_ref, pred_ref[...], loss_ref[0], variables, 0, half, out_ref
        )


def pair_sum(variables, width, held_ref, other_ref, begin, count):
    rows = slice(begin, begin + count)
    total = held_ref[rows, :width] + other_ref[rows, :width].astype(f32)
    part = held_ref[rows, width:] + other_ref[rows, width:].astype(f32)
    return total, split_loss(part, variables)


def first_kernel(variables, width, held_ref, other_ref, out_ref):
    total, part = pair_sum(variables, width, held_ref, other_ref, 0, out_ref.shape[0])
    out_ref[:, :width] = total.astype(bf16)
    out_ref[:, width:] = part.astype(bf16)


def message_kernel(
    variables, early, levels, keep_ref, give_ref, slots_ref, other_ref, held_ref, far_other_ref,
    first_ref, middle_ref, last_ref, near_ref,
):
    depth, width = keep_ref.shape[-1], near_ref.shape[1]
    block = near_ref.shape[0] // levels
    count, rest = early * block, (levels - 1 - early) * block
    for begin, size, out_ref in ((count, rest, middle_ref), (count + rest, block, last_ref)):
        total, part = pair_sum(variables, width, held_ref, far_other_ref, begin, size)
        out_ref[0:size, :] = total.astype(bf16)
        out_ref[size : size + packed, :] = jnp.zeros((packed, width), bf16)
        pack(out_ref, size, part.astype(bf16))
    for half in range(2):
        own = keep_ref[half].reshape(-1, depth)
        other = give_ref[half].reshape(-1, depth)
        for begin in range(0, width, tile):
            columns = slice(begin, begin + tile)
            here = slots_ref[:, :, columns].reshape(depth, tile)
            there = other_ref[:, :, columns].reshape(depth, tile)
            total = mm(own, here, 1, 0) + mm(other, there, 1, 0)
            if half == 0:
                total = total.astype(bf16)
                first_ref[:, columns] = total[:count]
                middle_ref[rest + packed :, columns] = total[count : count + rest]
                last_ref[block + packed :, columns] = total[count + rest :]
            else:
                near_ref[:, columns] = total


def ride_kernel(last_ref, slots_ref, *rest):
    arrived_refs, out_ref = rest[:-1], rest[-1]
    rows = slots_ref.shape[1]
    begin = last_ref.shape[0]
    out_ref[0:begin, :] = last_ref[...]
    for i, arrived_ref in enumerate(arrived_refs):
        out_ref[begin + i * rows : begin + (i + 1) * rows, :] = arrived_ref[rows:, :]
    out_ref[begin + len(arrived_refs) * rows :, :] = slots_ref[1]


def hidden_early_kernel(variables, width, held_ref, other_ref, arrived_ref, *out_refs):
    block = out_refs[0].shape[0]
    for i, out_ref in enumerate(out_refs):
        total, part = pair_sum(variables, width, held_ref, other_ref, i * block, block)
        here = slice(i * block, (i + 1) * block)
        out_ref[:, :width] = (total + arrived_ref[here, :width].astype(f32)).astype(bf16)
        part = split_loss(part + arrived_ref[here, width:].astype(f32), variables)
        out_ref[:, width:] = part.astype(bf16)


def message_early_kernel(begin, near_ref, arrived_ref, out_ref):
    here = slice(begin, begin + out_ref.shape[0])
    out_ref[...] = (near_ref[here, :] + arrived_ref[here, :].astype(f32)).astype(bf16)


def late_kernel(variables, early, held_ref, other_ref, near_ref, arrived_ref, *out_refs):
    width = near_ref.shape[1]
    block = (out_refs[0].shape[0] - packed) // 2
    count = block * len(out_refs)
    parts = unpack(arrived_ref, count, count, held_ref.shape[1] - width)
    for i, out_ref in enumerate(out_refs):
        begin = (early + i) * block
        total, part = pair_sum(variables, width, held_ref, other_ref, begin, block)
        here = slice(i * block, (i + 1) * block)
        out_ref[0:block, :] = (total + arrived_ref[here, :].astype(f32)).astype(bf16)
        there = slice(count + packed + i * block, count + packed + (i + 1) * block)
        total = near_ref[begin : begin + block, :] + arrived_ref[there, :].astype(f32)
        out_ref[block : 2 * block, :] = total.astype(bf16)
        out_ref[2 * block :, :] = jnp.zeros((packed, width), bf16)
        pack(out_ref, 2 * block, split_loss(part + parts[here], variables).astype(bf16))


def back_kernel(inner_ref, w_hidden_ref, gain_ref, unit_ref, inverse_ref, grad_ref, scaled_ref):
    rows_all, width = inner_ref.shape
    gain = gain_ref[...].reshape(1, width)
    for begin_row in range(0, rows_all, tile):
        rows = slice(begin_row, begin_row + tile)
        dots = jnp.zeros((tile, 1), f32)
        for begin in range(0, width, tile):
            columns = slice(begin, begin + tile)
            scaled = mm(inner_ref[rows, :], w_hidden_ref[columns, :], 1, 1) * gain[:, columns]
            dots = dots + jnp.sum(scaled * unit_ref[rows, columns], axis=-1, keepdims=True)
            scaled_ref[rows, columns] = scaled
        dots = dots * (1.0 / width)
        inverse = inverse_ref[rows, :]
        for begin in range(0, width, tile):
            columns = slice(begin, begin + tile)
            grad_ref[rows, columns] = (
                (scaled_ref[rows, columns] - unit_ref[rows, columns] * dots) * inverse
            ).astype(bf16)


def slot_kernel(share_ref, grad_ref, slots_ref, *send_refs):
    peers, each, width = slots_ref.shape
    rows = peers * each
    for begin in range(0, width, tile):
        columns = slice(begin, begin + tile)
        both = mm(share_ref[...], grad_ref[:, columns], 1, 0)
        slots_ref[:, :, columns] = (both[:rows] + both[rows:]).astype(bf16).reshape(peers, each, tile)
    for i, send_ref in enumerate(send_refs):
        step = len(send_refs) - i
        send_ref[0:each, :] = slots_ref[2 * step]
        send_ref[each:, :] = slots_ref[2 * step + 1]


def owner_kernel(pick_ref, w_msg_ref, slots_ref, last_ref, *rest):
    arrived_refs, (grad_ref, token_ref, held_ref) = rest[:-3], rest[-3:]
    token_ref[...] = jnp.zeros_like(token_ref)
    peers, rows, width = slots_ref.shape
    levels = peers // 2
    begin = last_ref.shape[0] - levels * rows
    for i in range(levels):
        spot = 2 * (levels - 1 - i)
        held_ref[spot] = slots_ref[0] if i == levels - 1 else arrived_refs[i][0:rows, :]
        held_ref[spot + 1] = last_ref[begin + i * rows : begin + (i + 1) * rows, :]
    nodes = mm(pick_ref[...], held_ref[...].reshape(peers * rows, width), 0, 0).astype(bf16)
    grad_ref[...] = mm(nodes, w_msg_ref[...], 1, 1).astype(bf16).reshape(grad_ref.shape)


def hidden_sum_kernel(variables, scale, early, held_ref, other_ref, last_ref, *rest):
    hidden_ref, out_ref, loss_ref, token_ref = rest[-4:]
    token_ref[...] = jnp.zeros_like(token_ref)
    block, width = hidden_ref.shape
    pad = held_ref.shape[1] - width
    total, part = pair_sum(variables, width, held_ref, other_ref, held_ref.shape[0] - block, block)
    total = total + last_ref[0:block, :].astype(f32)
    part = part + unpack(last_ref, block, block, pad)
    for i, r in enumerate(rest[:-4]):
        total = total + r[0:block, :width].astype(f32)
        if i < early:
            part = part + r[:, width:].astype(f32)
        else:
            part = part + unpack(r, 2 * block, block, pad)
    hidden_ref[...] = total
    out_ref[...] = part[:, :variables]
    column = lax.broadcasted_iota(jnp.int32, (8, pad), 1)
    spots = (column == variables) | (column == variables + 1)
    first = lax.broadcasted_iota(jnp.int32, (8, pad), 0) == 0
    loss_ref[0] = jnp.sum(jnp.where(spots & first, part[:8], 0.0)) * scale


def message_sum_kernel(early, near_ref, last_ref, *rest):
    out_ref = rest[-1]
    block = out_ref.shape[0]
    total = near_ref[near_ref.shape[0] - block :, :]
    total = total + last_ref[block + packed : 2 * block + packed, :].astype(f32)
    for i, r in enumerate(rest[:-1]):
        begin = 0 if i < early else block
        total = total + r[begin : begin + block, :].astype(f32)
    out_ref[...] = total


def on_device(
    latents, grid_embed, norm_gain, w_msg, w_hidden, variable_projection, present_condition, verifying_field,
    cell_surface, send_rows, edge_slot, edge_dst, edge_weight,
):
    members, nodes, width = latents.shape
    points = grid_embed.shape[0]
    variables = variable_projection.shape[1]
    peers = lax.axis_size("space")
    cores = lax.axis_size("member")
    cap = send_rows.shape[2]
    rows_peer = members * cap
    rows_slot = peers * rows_peer
    rows_all = members * points
    levels = peers // 2
    block = width // (peers * cores)
    half = levels * block
    wide = width + -(-(variables + 2) // lanes) * lanes
    project = variable_projection.T

    early = levels // 2
    count, rest = early * block, (levels - 1 - early) * block
    steps = [2 * (levels - 1 - i) for i in range(levels - 1)]

    def spread(values, part):
        return [swap(x, "space", peers, k) for x, k in zip(values, part, strict=True)]

    pick, own_rows, send = call(
        select_kernel,
        [((rows_slot, members * nodes), bf16)] + [((levels, rows_peer, width), bf16)] * 2,
        [send_rows, latents],
        scratch=[
            pltpu.SMEM(send_rows.shape, jnp.int32),
            pltpu.VMEM(latents.shape, bf16),
            pltpu.SemaphoreType.DMA((2,)),
        ],
        limit=4,
        places=(0, 1),
    )
    near_rows = swap(send, "space", peers, 1)
    fixed = [w_msg, norm_gain, grid_embed, w_hidden, project, present_condition.transpose(1, 0, 2)]
    edges = [edge_slot, edge_dst, edge_weight]
    share, *staged = call(
        functools.partial(stage_kernel, cap, members, len(fixed)),
        [((2 * rows_slot, rows_all), bf16)] + [(x.shape, x.dtype) for x in fixed],
        edges + fixed,
        scratch=[pltpu.VMEM(x.shape, x.dtype) for x in edges]
        + [pltpu.SemaphoreType.DMA((3 + len(fixed),))],
        limit=16,
        places=tuple(range(3 + len(fixed))),
        after=[pick],
    )
    merged = call(
        merge_kernel,
        [((2 * rows_peer, width), bf16)] * (levels - 1),
        [own_rows, near_rows],
        limit=4,
        after=[share],
    )
    received = [own_rows, near_rows] + spread(merged, steps)
    w_msg_near, gain, embed, w_hidden_near, project_near, present = staged
    field, sent, normed, active, slope, unit, inverse = call(
        functools.partial(forward_kernel, levels - 1),
        [
            ((members, variables, points), f32),
            ((members, variables, points), bf16),
            ((rows_all, width), bf16),
            ((rows_all, width), bf16),
            ((rows_all, width), f32),
            ((rows_all, width), f32),
            ((rows_all, 1), f32),
        ],
        [w_msg_near, share, gain, embed, w_hidden_near, project_near, present] + received,
        limit=20,
    )
    other = swap(sent, "member", cores, 1)
    normed_t, active_t, received_keep, received_give = call(
        turn_kernel,
        [((cores, 2, levels, block, rows_all), bf16)] * 2 + [((2, levels, block, rows_slot), bf16)] * 2,
        [normed, active] + received,
        limit=8,
    )
    received_other = swap(received_give, "member", cores, 1)
    grad_inner, pred, loss_part, far, near = call(
        score_kernel,
        [
            ((rows_all, width), bf16),
            ((lanes, rows_all), bf16),
            ((1,), f32),
            ((half, wide), bf16),
            ((half, wide), bf16),
        ],
        [field, other, verifying_field, cell_surface, project_near, slope, normed_t, active_t],
        scratch=[pltpu.VMEM((lanes, rows_all), f32)],
        limit=16,
        scalar_outs=(2,),
    )
    far_other = swap(far, "member", cores, 1)
    near_other = swap(near, "member", cores, 1)
    held_far, held_near = call(
        functools.partial(local_kernel, variables),
        [((half, wide), f32)] * 2,
        [loss_part, normed_t, active_t, grad_inner, pred],
        limit=12,
        scalars=(0,),
    )
    (first,) = call(
        functools.partial(first_kernel, variables, width),
        [((count, wide), bf16)],
        [held_far, far_other],
        limit=6,
    )
    first_other = swap(first, "space", peers, 1)
    (grad_hidden,) = call(
        back_kernel,
        [((rows_all, width), bf16)],
        [grad_inner, w_hidden_near, gain, unit, inverse],
        scratch=[pltpu.VMEM((rows_all, width), f32)],
        limit=14,
        after=[first],
    )
    slots, *slots_sent = call(
        slot_kernel,
        [((peers, rows_peer, width), bf16)] + [((2 * rows_peer, width), bf16)] * (levels - 1),
        [share, grad_hidden],
        limit=6,
        after=[near_other, received_other],
    )
    slots_other = swap(slots, "member", cores, 1)
    slots_arrived = spread(slots_sent, steps)
    message_first, middle, last, message_near = call(
        functools.partial(message_kernel, variables, early, levels),
        [
            ((count, width), bf16),
            ((2 * rest + packed, width), bf16),
            ((2 * block + packed, width), bf16),
            ((half, width), f32),
        ],
        [received_keep, received_other, slots, slots_other, held_far, far_other],
        limit=10,
    )
    message_first_other = swap(message_first, "space", peers, 1)
    middle_other = swap(middle, "space", peers, 1)
    hidden_early = call(
        functools.partial(hidden_early_kernel, variables, width),
        [((block, wide), bf16)] * early,
        [held_near, near_other, first_other],
        limit=6,
    )
    hidden_parts = spread(hidden_early, steps[:early])
    (last,) = call(
        ride_kernel,
        [((2 * block + packed + levels * rows_peer, width), bf16)],
        [last, slots] + slots_arrived,
        limit=4,
        after=hidden_early[:1],
    )
    last_other = swap(last, "space", peers, 1)
    message_parts = []
    for i in range(early):
        (piece,) = call(
            functools.partial(message_early_kernel, i * block),
            [((block, width), bf16)],
            [message_near, message_first_other],
            limit=6,
            after=hidden_parts[1 : 1 + i],
        )
        message_parts.append(swap(piece, "space", peers, steps[i]))
    late = call(
        functools.partial(late_kernel, variables, early),
        [((2 * block + packed, width), bf16)] * (levels - 1 - early),
        [held_near, near_other, message_near, middle_other],
        limit=6,
    )
    late_parts = spread(late, steps[early:])
    token = ((8, lanes), f32)
    latent_grad, latent_done = call(
        owner_kernel,
        [(latents.shape, bf16), token],
        [pick, w_msg, slots, last_other] + slots_arrived,
        scratch=[pltpu.VMEM((peers, rows_peer, width), bf16)],
        limit=8,
    )
    hidden_weight_grad, out_weight_grad, loss, hidden_done = call(
        functools.partial(hidden_sum_kernel, variables, 1.0 / (points * peers * variables), early),
        [((block, width), f32), ((block, variables), f32), ((1,), f32), token],
        [held_near, near_other, last_other] + hidden_parts + late_parts,
        limit=8,
        scalar_outs=(2,),
        after=[latent_done],
    )
    (msg_weight_grad,) = call(
        functools.partial(message_sum_kernel, early),
        [((block, width), f32)],
        [message_near, last_other] + message_parts + late_parts,
        limit=6,
        after=[hidden_done],
    )
    return (latent_grad, loss, msg_weight_grad, hidden_weight_grad, out_weight_grad)


def solution(mesh):
    placed = (
        P(("groups", "member"), "space", None),
        P(("groups", "space"), None),
        P(),
        P(),
        P(),
        P(),
        P(("groups", "member"), None, "space"),
        P(None, ("groups", "space")),
        P(("groups", "space")),
        P("space", None, None),
        P("space"),
        P("space"),
        P("space"),
    )
    return jax.shard_map(
        on_device,
        mesh=mesh,
        in_specs=placed,
        out_specs=(
            P(("groups", "member"), "space", None),
            P("groups"),
            P(("groups", "space", "member"), None),
            P(("groups", "space", "member"), None),
            P(("groups", "space", "member"), None),
        ),
        check_vma=False,
    )
```

```python
import functools

import jax
import jax.numpy as jnp
from jax import lax
from jax.experimental import pallas as pl
from jax.experimental.pallas import tpu as pltpu
from jax.sharding import PartitionSpec as P

smoothing = 0.1
epsilon = 1e-06
tile = 256
lanes = 128
packed = 16
cost_hints = {
    "back_kernel": 8,
    "slot_kernel": 4,
    "hidden_early_kernel": 4,
    "message_early_kernel": 4,
    "late_kernel": 4,
    "message_sum_kernel": 8,
}
f32 = jnp.float32
bf16 = jnp.bfloat16


def mm(left, right, left_dim, right_dim):
    return lax.dot_general(
        left, right, (((left_dim,), (right_dim,)), ((), ())), preferred_element_type=f32
    )


def call(body, outs, args, scratch=(), limit=16, scalars=(), scalar_outs=(), places=(), after=()):
    whole = pl.BlockSpec(memory_space=pltpu.VMEM)
    small = pl.BlockSpec(memory_space=pltpu.SMEM)
    far_place = pl.BlockSpec(memory_space=pltpu.HBM)
    any_place = pl.BlockSpec(memory_space=pl.ANY)
    count = len(after)
    cost = cost_hints.get(getattr(body, "func", body).__name__, 0) * 10**9
    args = [pltpu.with_memory_space_constraint(x, pltpu.HBM) if i in places else x for i, x in enumerate(args)]

    def inner(*refs):
        body(*refs[count:])

    specs = [small if i in scalars else far_place if i in places else whole for i in range(len(args))]
    return pl.pallas_call(
        inner if count else body,
        out_shape=[jax.ShapeDtypeStruct(dims, kind) for dims, kind in outs],
        in_specs=[any_place] * count + specs,
        out_specs=[small if i in scalar_outs else whole for i in range(len(outs))],
        scratch_shapes=scratch,
        compiler_params=pltpu.CompilerParams(vmem_limit_bytes=limit * 2**20),
        cost_estimate=pl.CostEstimate(flops=cost, bytes_accessed=0, transcendentals=0),
    )(*after, *args)


def place():
    space = lax.axis_index("space")
    return lax.div(space, 2), lax.rem(space, 2), lax.axis_index("member")


def swap(value, axis, size, step):
    return lax.ppermute(value, axis, [(i, i ^ step) for i in range(size)])


def select_kernel(lists_ref, latents_ref, pick_ref, own_ref, send_ref, small_ref, table_ref, sems):
    _, peers, cap = lists_ref.shape
    members, nodes, width = latents_ref.shape
    lists = pltpu.make_async_copy(lists_ref, small_ref, sems.at[0])
    table = pltpu.make_async_copy(latents_ref, table_ref, sems.at[1])
    lists.start()
    table.start()
    lists.wait()
    me = lax.axis_index("space")
    at = lax.broadcasted_iota(jnp.int32, (cap, members * nodes), 0)
    column = lax.broadcasted_iota(jnp.int32, (cap, members * nodes), 1)
    rows = []
    for step in range(peers):
        wanted = jnp.zeros((cap, members * nodes), jnp.int32)
        for j in range(cap):
            wanted = jnp.where(at == j, small_ref[0, me ^ step, j], wanted)
        for member in range(members):
            rows.append((column == wanted + member * nodes).astype(f32))
    pick = jnp.concatenate(rows, axis=0).astype(bf16)
    pick_ref[...] = pick
    table.wait()
    sent = mm(pick, table_ref[...].reshape(members * nodes, width), 1, 0)
    sent = sent.astype(bf16).reshape(peers // 2, 2, members * cap, width)
    own_ref[...] = sent[:, 0]
    send_ref[...] = sent[:, 1]


def merge_kernel(own_ref, arrived_ref, *out_refs):
    rows = own_ref.shape[1]
    for i, out_ref in enumerate(out_refs):
        step = len(out_refs) - i
        out_ref[0:rows, :] = own_ref[step]
        out_ref[rows:, :] = arrived_ref[step]


def stage_kernel(cap, members, count, *refs):
    edge_refs, source_refs, share_ref = refs[:3], refs[3 : 3 + count], refs[3 + count]
    staged_refs, held_refs, sems = refs[4 + count : 4 + 2 * count], refs[4 + 2 * count : -1], refs[-1]
    copies = [
        pltpu.make_async_copy(source, target, sems.at[i])
        for i, (source, target) in enumerate(
            zip(edge_refs + source_refs, held_refs + staged_refs, strict=True)
        )
    ]
    for copy in copies:
        copy.start()
    for copy in copies[:3]:
        copy.wait()
    edge_part(cap, members, *held_refs, share_ref)
    for copy in copies[3:]:
        copy.wait()


def edge_part(cap, members, slot_ref, dst_ref, weight_ref, share_ref):
    edges = slot_ref.shape[0]
    slot = slot_ref[...].reshape(1, edges)
    dst = dst_ref[...].reshape(1, edges)
    weight = weight_ref[...].reshape(1, edges)
    rows = share_ref.shape[0] // 2
    points = share_ref.shape[1] // members
    sender = lax.div(slot, cap)
    spot = (sender ^ lax.axis_index("space")) * (members * cap) + (slot - sender * cap)
    hit = lax.broadcasted_iota(jnp.int32, (rows, edges), 0) == spot
    into = (lax.broadcasted_iota(jnp.int32, (points, edges), 0) == dst).astype(f32).astype(bf16)
    high = weight.astype(bf16).astype(f32)
    table = mm(jnp.where(hit, high, 0.0).astype(bf16), into, 1, 1) + mm(
        jnp.where(hit, weight - high, 0.0).astype(bf16), into, 1, 1
    )
    table = table / jnp.sum(table, axis=0, keepdims=True)
    for member in range(members):
        high = table.astype(bf16)
        columns = slice(member * points, (member + 1) * points)
        share_ref[0:rows, columns] = high
        share_ref[rows : 2 * rows, columns] = (table - high.astype(f32)).astype(bf16)
        table = jnp.concatenate([table[rows - cap :], table[: rows - cap]], axis=0)


def gathered(own_ref, near_ref, far_refs):
    return jnp.concatenate([own_ref[0], near_ref[0]] + [r[...] for r in far_refs[::-1]], axis=0)


def forward_kernel(
    far, w_msg_ref, share_ref, gain_ref, embed_ref, weights_ref, project_ref, present_ref,
    own_ref, near_ref, *rest,
):
    far_refs = rest[:far]
    field_ref, sent_ref, normed_ref, active_ref, slope_ref, unit_ref, inverse_ref = rest[far:]
    points, width = embed_ref.shape
    variables, members, _ = present_ref.shape
    messages = mm(gathered(own_ref, near_ref, far_refs), w_msg_ref[...], 1, 0).astype(bf16)
    messages = jnp.concatenate([messages, messages], axis=0)
    gain = gain_ref[...].reshape(1, width)
    for begin in range(0, members * points, lanes):
        rows = slice(begin, begin + lanes)
        source = slice(begin % points, begin % points + lanes)
        hidden = embed_ref[source, :].astype(f32) + mm(share_ref[:, rows], messages, 0, 0)
        inverse = lax.rsqrt(jnp.mean(hidden * hidden, axis=-1, keepdims=True) + epsilon)
        unit = hidden * inverse
        unit_ref[rows, :] = unit
        inverse_ref[rows, :] = inverse
        normed_ref[rows, :] = (unit * gain).astype(bf16)
    root = 0.7978845608028654
    cubic = 0.044715
    for member in range(members):
        rows = slice(member * points, (member + 1) * points)
        for begin in range(0, width, tile):
            columns = slice(begin, begin + tile)
            inner = mm(normed_ref[rows, :], weights_ref[:, columns], 1, 0)
            square = inner * inner
            bend = jnp.tanh(inner * (root + root * cubic * square))
            half = 0.5 + 0.5 * bend
            active_ref[rows, columns] = (inner * half).astype(bf16)
            slope_ref[rows, columns] = half + (0.5 * inner) * (1.0 - bend * bend) * (
                root + 3.0 * root * cubic * square
            )
        field = present_ref[:, member, :] + mm(project_ref[...], active_ref[rows, :], 1, 1)
        field_ref[member] = field
        sent_ref[member] = field.astype(bf16)


def turn_kernel(normed_ref, active_ref, own_ref, near_ref, *rest):
    far_refs, (normed_t_ref, active_t_ref, keep_ref, give_ref) = rest[:-4], rest[-4:]
    _, _, levels, block, _ = normed_t_ref.shape
    width = normed_ref.shape[1]
    level, line, core = place()
    received = gathered(own_ref, near_ref, far_refs)
    for source, target in ((received, None), (normed_ref, normed_t_ref), (active_ref, active_t_ref)):
        for begin in range(0, width, tile):
            turned = source[:, begin : begin + tile].T
            for piece in range(0, tile, block):
                index = (begin + piece) // block
                far = (index // 2 % 2) ^ line
                step = (index // 4) ^ level
                side = (index % 2) ^ core
                value = turned[piece : piece + block]
                if target is not None:
                    target[side, 1 - far, levels - 1 - step] = value
                    continue
                for which, part_ref in enumerate((keep_ref, give_ref)):
                    @pl.when(side == which)
                    def _(part_ref=part_ref):
                        part_ref[1 - far, levels - 1 - step] = value


def split_loss(part, variables):
    column = lax.broadcasted_iota(jnp.int32, part.shape, 1)
    spots = (column == variables) | (column == variables + 1)
    total = jnp.sum(jnp.where(spots, part, 0.0), axis=1, keepdims=True)
    high = total.astype(bf16).astype(f32)
    return jnp.where(column == variables, high, jnp.where(column == variables + 1, total - high, part))


def score_kernel(
    own_ref, other_ref, truth_ref, cell_ref, project_ref, slope_ref, normed_t_ref, active_t_ref,
    inner_ref, pred_ref, loss_ref, far_ref, near_ref, hold_ref,
):
    members, variables, points = own_ref.shape
    width = slope_ref.shape[1]
    total = 2 * members
    pairs = total * (total - 1)

    def eased(delta):
        square = delta * delta + smoothing * smoothing
        inverse = lax.rsqrt(square)
        return square * inverse, delta * inverse

    truth, cell = truth_ref[...], cell_ref[...].reshape(1, points)
    own = [own_ref[m] for m in range(members)]
    other = [other_ref[m].astype(f32) for m in range(members)]
    score = jnp.zeros_like(truth)
    pulls = [jnp.zeros_like(truth) for _ in own]
    grads = []
    for m in range(members):
        size, sign = eased(own[m] - truth)
        score = score + size * (1.0 / total)
        grads.append(sign * (1.0 / total))
    for m in range(members):
        for n in range(m + 1, members):
            size, sign = eased(own[m] - own[n])
            score = score - size * (1.0 / pairs)
            pulls[m] = pulls[m] + sign
            pulls[n] = pulls[n] - sign
        for n in range(members):
            size, sign = eased(own[m] - other[n])
            score = score - size * (0.5 / pairs)
            pulls[m] = pulls[m] + sign
    loss = jnp.sum(score * cell)
    loss_ref[0] = loss
    hold_ref[...] = jnp.zeros_like(hold_ref)
    for m in range(members):
        grad = (grads[m] - pulls[m] * (1.0 / pairs)) * cell
        hold_ref[0:variables, m * points : (m + 1) * points] = grad
    pred = hold_ref[...].astype(bf16)
    pred_ref[...] = pred
    for m in range(members):
        rows = slice(m * points, (m + 1) * points)
        part = pred[:variables, rows]
        for begin in range(0, width, tile):
            columns = slice(begin, begin + tile)
            grad = mm(part, project_ref[:, columns], 0, 0)
            inner_ref[rows, columns] = (grad * slope_ref[rows, columns]).astype(bf16)
    weight_parts(normed_t_ref, active_t_ref, inner_ref, pred, loss, variables, 1, 0, far_ref)
    weight_parts(normed_t_ref, active_t_ref, inner_ref, pred, loss, variables, 1, 1, near_ref)


def weight_parts(normed_t_ref, active_t_ref, inner_ref, pred, loss, variables, side, half, out_ref):
    width = inner_ref.shape[1]
    depth = normed_t_ref.shape[-1]
    normed = normed_t_ref[side, half].reshape(-1, depth)
    for begin in range(0, width, tile):
        columns = slice(begin, begin + tile)
        out_ref[:, columns] = mm(normed, inner_ref[:, columns], 1, 0).astype(out_ref.dtype)
    part = mm(active_t_ref[side, half].reshape(-1, depth), pred, 1, 1)
    part = jnp.where(lax.broadcasted_iota(jnp.int32, part.shape, 1) == variables, loss, part)
    out_ref[:, width:] = split_loss(part, variables).astype(out_ref.dtype)


def pack(out_ref, begin, part):
    pad = part.shape[1]
    for i in range(part.shape[0] // packed):
        out_ref[begin : begin + packed, i * pad : (i + 1) * pad] = part[i * packed : (i + 1) * packed]


def unpack(in_ref, begin, count, pad):
    parts = [in_ref[begin : begin + packed, i * pad : (i + 1) * pad] for i in range(count // packed)]
    return jnp.concatenate(parts, axis=0).astype(f32)


def local_kernel(variables, loss_ref, normed_t_ref, active_t_ref, inner_ref, pred_ref, far_ref, near_ref):
    for half, out_ref in ((0, far_ref), (1, near_ref)):
        weight_parts(
            normed_t_ref, active_t_ref, inner_ref, pred_ref[...], loss_ref[0], variables, 0, half, out_ref
        )


def pair_sum(variables, width, held_ref, other_ref, begin, count):
    rows = slice(begin, begin + count)
    total = held_ref[rows, :width] + other_ref[rows, :width].astype(f32)
    part = held_ref[rows, width:] + other_ref[rows, width:].astype(f32)
    return total, split_loss(part, variables)


def first_kernel(variables, width, held_ref, other_ref, out_ref):
    total, part = pair_sum(variables, width, held_ref, other_ref, 0, out_ref.shape[0])
    out_ref[:, :width] = total.astype(bf16)
    out_ref[:, width:] = part.astype(bf16)


def message_kernel(
    variables, early, levels, keep_ref, give_ref, slots_ref, other_ref, held_ref, far_other_ref,
    first_ref, middle_ref, last_ref, near_ref,
):
    depth, width = keep_ref.shape[-1], near_ref.shape[1]
    block = near_ref.shape[0] // levels
    count, rest = early * block, (levels - 1 - early) * block
    for begin, size, out_ref in ((count, rest, middle_ref), (count + rest, block, last_ref)):
        total, part = pair_sum(variables, width, held_ref, far_other_ref, begin, size)
        out_ref[0:size, :] = total.astype(bf16)
        out_ref[size : size + packed, :] = jnp.zeros((packed, width), bf16)
        pack(out_ref, size, part.astype(bf16))
    for half in range(2):
        own = keep_ref[half].reshape(-1, depth)
        other = give_ref[half].reshape(-1, depth)
        for begin in range(0, width, tile):
            columns = slice(begin, begin + tile)
            here = slots_ref[:, :, columns].reshape(depth, tile)
            there = other_ref[:, :, columns].reshape(depth, tile)
            total = mm(own, here, 1, 0) + mm(other, there, 1, 0)
            if half == 0:
                total = total.astype(bf16)
                first_ref[:, columns] = total[:count]
                middle_ref[rest + packed :, columns] = total[count : count + rest]
                last_ref[block + packed :, columns] = total[count + rest :]
            else:
                near_ref[:, columns] = total


def ride_kernel(last_ref, slots_ref, *rest):
    arrived_refs, out_ref = rest[:-1], rest[-1]
    rows = slots_ref.shape[1]
    begin = last_ref.shape[0]
    out_ref[0:begin, :] = last_ref[...]
    for i, arrived_ref in enumerate(arrived_refs):
        out_ref[begin + i * rows : begin + (i + 1) * rows, :] = arrived_ref[rows:, :]
    out_ref[begin + len(arrived_refs) * rows :, :] = slots_ref[1]


def hidden_early_kernel(variables, width, held_ref, other_ref, arrived_ref, *out_refs):
    block = out_refs[0].shape[0]
    for i, out_ref in enumerate(out_refs):
        total, part = pair_sum(variables, width, held_ref, other_ref, i * block, block)
        here = slice(i * block, (i + 1) * block)
        out_ref[:, :width] = (total + arrived_ref[here, :width].astype(f32)).astype(bf16)
        part = split_loss(part + arrived_ref[here, width:].astype(f32), variables)
        out_ref[:, width:] = part.astype(bf16)


def message_early_kernel(begin, near_ref, arrived_ref, out_ref):
    here = slice(begin, begin + out_ref.shape[0])
    out_ref[...] = (near_ref[here, :] + arrived_ref[here, :].astype(f32)).astype(bf16)


def late_kernel(variables, early, held_ref, other_ref, near_ref, arrived_ref, *out_refs):
    width = near_ref.shape[1]
    block = (out_refs[0].shape[0] - packed) // 2
    count = block * len(out_refs)
    parts = unpack(arrived_ref, count, count, held_ref.shape[1] - width)
    for i, out_ref in enumerate(out_refs):
        begin = (early + i) * block
        total, part = pair_sum(variables, width, held_ref, other_ref, begin, block)
        here = slice(i * block, (i + 1) * block)
        out_ref[0:block, :] = (total + arrived_ref[here, :].astype(f32)).astype(bf16)
        there = slice(count + packed + i * block, count + packed + (i + 1) * block)
        total = near_ref[begin : begin + block, :] + arrived_ref[there, :].astype(f32)
        out_ref[block : 2 * block, :] = total.astype(bf16)
        out_ref[2 * block :, :] = jnp.zeros((packed, width), bf16)
        pack(out_ref, 2 * block, split_loss(part + parts[here], variables).astype(bf16))


def back_kernel(inner_ref, w_hidden_ref, gain_ref, unit_ref, inverse_ref, grad_ref, scaled_ref):
    rows_all, width = inner_ref.shape
    gain = gain_ref[...].reshape(1, width)
    for begin_row in range(0, rows_all, tile):
        rows = slice(begin_row, begin_row + tile)
        dots = jnp.zeros((tile, 1), f32)
        for begin in range(0, width, tile):
            columns = slice(begin, begin + tile)
            scaled = mm(inner_ref[rows, :], w_hidden_ref[columns, :], 1, 1) * gain[:, columns]
            dots = dots + jnp.sum(scaled * unit_ref[rows, columns], axis=-1, keepdims=True)
            scaled_ref[rows, columns] = scaled
        dots = dots * (1.0 / width)
        inverse = inverse_ref[rows, :]
        for begin in range(0, width, tile):
            columns = slice(begin, begin + tile)
            grad_ref[rows, columns] = (
                (scaled_ref[rows, columns] - unit_ref[rows, columns] * dots) * inverse
            ).astype(bf16)


def slot_kernel(share_ref, grad_ref, slots_ref, *send_refs):
    peers, each, width = slots_ref.shape
    rows = peers * each
    for begin in range(0, width, tile):
        columns = slice(begin, begin + tile)
        both = mm(share_ref[...], grad_ref[:, columns], 1, 0)
        slots_ref[:, :, columns] = (both[:rows] + both[rows:]).astype(bf16).reshape(peers, each, tile)
    for i, send_ref in enumerate(send_refs):
        step = len(send_refs) - i
        send_ref[0:each, :] = slots_ref[2 * step]
        send_ref[each:, :] = slots_ref[2 * step + 1]


def owner_kernel(pick_ref, w_msg_ref, slots_ref, last_ref, *rest):
    arrived_refs, (grad_ref, token_ref, held_ref) = rest[:-3], rest[-3:]
    token_ref[...] = jnp.zeros_like(token_ref)
    peers, rows, width = slots_ref.shape
    levels = peers // 2
    begin = last_ref.shape[0] - levels * rows
    for i in range(levels):
        spot = 2 * (levels - 1 - i)
        held_ref[spot] = slots_ref[0] if i == levels - 1 else arrived_refs[i][0:rows, :]
        held_ref[spot + 1] = last_ref[begin + i * rows : begin + (i + 1) * rows, :]
    nodes = mm(pick_ref[...], held_ref[...].reshape(peers * rows, width), 0, 0).astype(bf16)
    grad_ref[...] = mm(nodes, w_msg_ref[...], 1, 1).astype(bf16).reshape(grad_ref.shape)


def hidden_sum_kernel(variables, scale, early, held_ref, other_ref, last_ref, *rest):
    hidden_ref, out_ref, loss_ref, token_ref = rest[-4:]
    token_ref[...] = jnp.zeros_like(token_ref)
    block, width = hidden_ref.shape
    pad = held_ref.shape[1] - width
    total, part = pair_sum(variables, width, held_ref, other_ref, held_ref.shape[0] - block, block)
    total = total + last_ref[0:block, :].astype(f32)
    part = part + unpack(last_ref, block, block, pad)
    for i, r in enumerate(rest[:-4]):
        total = total + r[0:block, :width].astype(f32)
        if i < early:
            part = part + r[:, width:].astype(f32)
        else:
            part = part + unpack(r, 2 * block, block, pad)
    hidden_ref[...] = total
    out_ref[...] = part[:, :variables]
    column = lax.broadcasted_iota(jnp.int32, (8, pad), 1)
    spots = (column == variables) | (column == variables + 1)
    first = lax.broadcasted_iota(jnp.int32, (8, pad), 0) == 0
    loss_ref[0] = jnp.sum(jnp.where(spots & first, part[:8], 0.0)) * scale


def message_partial_kernel(early, near_ref, last_ref, *rest):
    out_ref = rest[-1]
    block = out_ref.shape[0]
    total = near_ref[near_ref.shape[0] - block :, :]
    total = total + last_ref[block + packed : 2 * block + packed, :].astype(f32)
    for i, r in enumerate(rest[:-1]):
        begin = 0 if i < early else block
        total = total + r[begin : begin + block, :].astype(f32)
    out_ref[...] = total


def message_sum_kernel(partial_ref, arrived_ref, out_ref):
    out_ref[...] = partial_ref[...] + arrived_ref[...].astype(f32)


def on_device(
    latents, grid_embed, norm_gain, w_msg, w_hidden, variable_projection, present_condition, verifying_field,
    cell_surface, send_rows, edge_slot, edge_dst, edge_weight,
):
    members, nodes, width = latents.shape
    points = grid_embed.shape[0]
    variables = variable_projection.shape[1]
    peers = lax.axis_size("space")
    cores = lax.axis_size("member")
    cap = send_rows.shape[2]
    rows_peer = members * cap
    rows_slot = peers * rows_peer
    rows_all = members * points
    levels = peers // 2
    block = width // (peers * cores)
    half = levels * block
    wide = width + -(-(variables + 2) // lanes) * lanes
    project = variable_projection.T

    early = levels // 2
    count, rest = early * block, (levels - 1 - early) * block
    steps = [2 * (levels - 1 - i) for i in range(levels - 1)]

    def spread(values, part):
        return [swap(x, "space", peers, k) for x, k in zip(values, part, strict=True)]

    pick, own_rows, send = call(
        select_kernel,
        [((rows_slot, members * nodes), bf16)] + [((levels, rows_peer, width), bf16)] * 2,
        [send_rows, latents],
        scratch=[
            pltpu.SMEM(send_rows.shape, jnp.int32),
            pltpu.VMEM(latents.shape, bf16),
            pltpu.SemaphoreType.DMA((2,)),
        ],
        limit=4,
        places=(0, 1),
    )
    near_rows = swap(send, "space", peers, 1)
    fixed = [w_msg, norm_gain, grid_embed, w_hidden, project, present_condition.transpose(1, 0, 2)]
    edges = [edge_slot, edge_dst, edge_weight]
    share, *staged = call(
        functools.partial(stage_kernel, cap, members, len(fixed)),
        [((2 * rows_slot, rows_all), bf16)] + [(x.shape, x.dtype) for x in fixed],
        edges + fixed,
        scratch=[pltpu.VMEM(x.shape, x.dtype) for x in edges]
        + [pltpu.SemaphoreType.DMA((3 + len(fixed),))],
        limit=16,
        places=tuple(range(3 + len(fixed))),
        after=[pick],
    )
    merged = call(
        merge_kernel,
        [((2 * rows_peer, width), bf16)] * (levels - 1),
        [own_rows, near_rows],
        limit=4,
        after=[share],
    )
    received = [own_rows, near_rows] + spread(merged, steps)
    w_msg_near, gain, embed, w_hidden_near, project_near, present = staged
    field, sent, normed, active, slope, unit, inverse = call(
        functools.partial(forward_kernel, levels - 1),
        [
            ((members, variables, points), f32),
            ((members, variables, points), bf16),
            ((rows_all, width), bf16),
            ((rows_all, width), bf16),
            ((rows_all, width), f32),
            ((rows_all, width), f32),
            ((rows_all, 1), f32),
        ],
        [w_msg_near, share, gain, embed, w_hidden_near, project_near, present] + received,
        limit=20,
    )
    other = swap(sent, "member", cores, 1)
    normed_t, active_t, received_keep, received_give = call(
        turn_kernel,
        [((cores, 2, levels, block, rows_all), bf16)] * 2 + [((2, levels, block, rows_slot), bf16)] * 2,
        [normed, active] + received,
        limit=8,
    )
    received_other = swap(received_give, "member", cores, 1)
    grad_inner, pred, loss_part, far, near = call(
        score_kernel,
        [
            ((rows_all, width), bf16),
            ((lanes, rows_all), bf16),
            ((1,), f32),
            ((half, wide), bf16),
            ((half, wide), bf16),
        ],
        [field, other, verifying_field, cell_surface, project_near, slope, normed_t, active_t],
        scratch=[pltpu.VMEM((lanes, rows_all), f32)],
        limit=16,
        scalar_outs=(2,),
    )
    far_other = swap(far, "member", cores, 1)
    near_other = swap(near, "member", cores, 1)
    held_far, held_near = call(
        functools.partial(local_kernel, variables),
        [((half, wide), f32)] * 2,
        [loss_part, normed_t, active_t, grad_inner, pred],
        limit=12,
        scalars=(0,),
    )
    (first,) = call(
        functools.partial(first_kernel, variables, width),
        [((count, wide), bf16)],
        [held_far, far_other],
        limit=6,
    )
    first_other = swap(first, "space", peers, 1)
    (grad_hidden,) = call(
        back_kernel,
        [((rows_all, width), bf16)],
        [grad_inner, w_hidden_near, gain, unit, inverse],
        scratch=[pltpu.VMEM((rows_all, width), f32)],
        limit=14,
        after=[first],
    )
    slots, *slots_sent = call(
        slot_kernel,
        [((peers, rows_peer, width), bf16)] + [((2 * rows_peer, width), bf16)] * (levels - 1),
        [share, grad_hidden],
        limit=6,
        after=[near_other, received_other],
    )
    slots_other = swap(slots, "member", cores, 1)
    slots_arrived = spread(slots_sent, steps)
    message_first, middle, last, message_near = call(
        functools.partial(message_kernel, variables, early, levels),
        [
            ((count, width), bf16),
            ((2 * rest + packed, width), bf16),
            ((2 * block + packed, width), bf16),
            ((half, width), f32),
        ],
        [received_keep, received_other, slots, slots_other, held_far, far_other],
        limit=10,
    )
    message_first_other = swap(message_first, "space", peers, 1)
    middle_other = swap(middle, "space", peers, 1)
    hidden_early = call(
        functools.partial(hidden_early_kernel, variables, width),
        [((block, wide), bf16)] * early,
        [held_near, near_other, first_other],
        limit=6,
    )
    hidden_parts = spread(hidden_early, steps[:early])
    (last,) = call(
        ride_kernel,
        [((2 * block + packed + levels * rows_peer, width), bf16)],
        [last, slots] + slots_arrived,
        limit=4,
        after=hidden_early[:1],
    )
    last_other = swap(last, "space", peers, 1)
    message_parts = []
    for i in range(early):
        (piece,) = call(
            functools.partial(message_early_kernel, i * block),
            [((block, width), bf16)],
            [message_near, message_first_other],
            limit=6,
            after=hidden_parts[1 : 1 + i],
        )
        message_parts.append(swap(piece, "space", peers, steps[i]))
    late = call(
        functools.partial(late_kernel, variables, early),
        [((2 * block + packed, width), bf16)] * (levels - 1 - early),
        [held_near, near_other, message_near, middle_other],
        limit=6,
    )
    late_parts = spread(late, steps[early:])
    token = ((8, lanes), f32)
    latent_grad, latent_done = call(
        owner_kernel,
        [(latents.shape, bf16), token],
        [pick, w_msg, slots, last_other] + slots_arrived,
        scratch=[pltpu.VMEM((peers, rows_peer, width), bf16)],
        limit=8,
    )
    hidden_weight_grad, out_weight_grad, loss, hidden_done = call(
        functools.partial(hidden_sum_kernel, variables, 1.0 / (points * peers * variables), early),
        [((block, width), f32), ((block, variables), f32), ((1,), f32), token],
        [held_near, near_other, last_other] + hidden_parts + late_parts,
        limit=8,
        scalar_outs=(2,),
        after=[latent_done],
    )
    (message_partial,) = call(
        functools.partial(message_partial_kernel, early - 1),
        [((block, width), f32)],
        [message_near, last_other] + message_parts[:-1] + late_parts,
        limit=6,
        after=[hidden_done],
    )
    (msg_weight_grad,) = call(
        message_sum_kernel, [((block, width), f32)], [message_partial, message_parts[-1]], limit=4
    )
    return (latent_grad, loss, msg_weight_grad, hidden_weight_grad, out_weight_grad)


def solution(mesh):
    placed = (
        P(("groups", "member"), "space", None),
        P(("groups", "space"), None),
        P(),
        P(),
        P(),
        P(),
        P(("groups", "member"), None, "space"),
        P(None, ("groups", "space")),
        P(("groups", "space")),
        P("space", None, None),
        P("space"),
        P("space"),
        P("space"),
    )
    return jax.shard_map(
        on_device,
        mesh=mesh,
        in_specs=placed,
        out_specs=(
            P(("groups", "member"), "space", None),
            P("groups"),
            P(("groups", "space", "member"), None),
            P(("groups", "space", "member"), None),
            P(("groups", "space", "member"), None),
        ),
        check_vma=False,
    )
```

```python
import functools

import jax
import jax.numpy as jnp
from jax import lax
from jax.experimental import pallas as pl
from jax.experimental.pallas import tpu as pltpu
from jax.sharding import PartitionSpec as P

smoothing = 0.1
epsilon = 1e-06
tile = 256
lanes = 128
packed = 16
cost_hints = {
    "back_kernel": 8,
    "slot_kernel": 4,
    "hidden_early_kernel": 4,
    "message_early_kernel": 4,
    "late_kernel": 4,
    "message_sum_kernel": 8,
}
f32 = jnp.float32
bf16 = jnp.bfloat16


def mm(left, right, left_dim, right_dim):
    return lax.dot_general(
        left, right, (((left_dim,), (right_dim,)), ((), ())), preferred_element_type=f32
    )


def call(body, outs, args, scratch=(), limit=16, scalars=(), scalar_outs=(), places=(), after=()):
    whole = pl.BlockSpec(memory_space=pltpu.VMEM)
    small = pl.BlockSpec(memory_space=pltpu.SMEM)
    far_place = pl.BlockSpec(memory_space=pltpu.HBM)
    any_place = pl.BlockSpec(memory_space=pl.ANY)
    count = len(after)
    cost = cost_hints.get(getattr(body, "func", body).__name__, 0) * 10**9
    args = [pltpu.with_memory_space_constraint(x, pltpu.HBM) if i in places else x for i, x in enumerate(args)]

    def inner(*refs):
        body(*refs[count:])

    specs = [small if i in scalars else far_place if i in places else whole for i in range(len(args))]
    return pl.pallas_call(
        inner if count else body,
        out_shape=[jax.ShapeDtypeStruct(dims, kind) for dims, kind in outs],
        in_specs=[any_place] * count + specs,
        out_specs=[small if i in scalar_outs else whole for i in range(len(outs))],
        scratch_shapes=scratch,
        compiler_params=pltpu.CompilerParams(vmem_limit_bytes=limit * 2**20),
        cost_estimate=pl.CostEstimate(flops=cost, bytes_accessed=0, transcendentals=0),
    )(*after, *args)


def place():
    space = lax.axis_index("space")
    return lax.div(space, 2), lax.rem(space, 2), lax.axis_index("member")


def swap(value, axis, size, step):
    return lax.ppermute(value, axis, [(i, i ^ step) for i in range(size)])


def select_kernel(lists_ref, latents_ref, pick_ref, own_ref, send_ref, small_ref, table_ref, sems):
    _, peers, cap = lists_ref.shape
    members, nodes, width = latents_ref.shape
    lists = pltpu.make_async_copy(lists_ref, small_ref, sems.at[0])
    table = pltpu.make_async_copy(latents_ref, table_ref, sems.at[1])
    lists.start()
    table.start()
    lists.wait()
    me = lax.axis_index("space")
    at = lax.broadcasted_iota(jnp.int32, (cap, members * nodes), 0)
    column = lax.broadcasted_iota(jnp.int32, (cap, members * nodes), 1)
    rows = []
    for step in range(peers):
        wanted = jnp.zeros((cap, members * nodes), jnp.int32)
        for j in range(cap):
            wanted = jnp.where(at == j, small_ref[0, me ^ step, j], wanted)
        for member in range(members):
            rows.append((column == wanted + member * nodes).astype(f32))
    pick = jnp.concatenate(rows, axis=0).astype(bf16)
    pick_ref[...] = pick
    table.wait()
    sent = mm(pick, table_ref[...].reshape(members * nodes, width), 1, 0)
    sent = sent.astype(bf16).reshape(peers // 2, 2, members * cap, width)
    own_ref[...] = sent[:, 0]
    send_ref[...] = sent[:, 1]


def merge_kernel(own_ref, arrived_ref, *out_refs):
    rows = own_ref.shape[1]
    for i, out_ref in enumerate(out_refs):
        step = len(out_refs) - i
        out_ref[0:rows, :] = own_ref[step]
        out_ref[rows:, :] = arrived_ref[step]


def stage_kernel(cap, members, count, *refs):
    edge_refs, source_refs, share_ref = refs[:3], refs[3 : 3 + count], refs[3 + count]
    staged_refs, held_refs, sems = refs[4 + count : 4 + 2 * count], refs[4 + 2 * count : -1], refs[-1]
    copies = [
        pltpu.make_async_copy(source, target, sems.at[i])
        for i, (source, target) in enumerate(
            zip(edge_refs + source_refs, held_refs + staged_refs, strict=True)
        )
    ]
    for copy in copies:
        copy.start()
    for copy in copies[:3]:
        copy.wait()
    edge_part(cap, members, *held_refs, share_ref)
    for copy in copies[3:]:
        copy.wait()


def edge_part(cap, members, slot_ref, dst_ref, weight_ref, share_ref):
    edges = slot_ref.shape[0]
    slot = slot_ref[...].reshape(1, edges)
    dst = dst_ref[...].reshape(1, edges)
    weight = weight_ref[...].reshape(1, edges)
    rows = share_ref.shape[0] // 2
    points = share_ref.shape[1] // members
    sender = lax.div(slot, cap)
    spot = (sender ^ lax.axis_index("space")) * (members * cap) + (slot - sender * cap)
    hit = lax.broadcasted_iota(jnp.int32, (rows, edges), 0) == spot
    into = (lax.broadcasted_iota(jnp.int32, (points, edges), 0) == dst).astype(f32).astype(bf16)
    high = weight.astype(bf16).astype(f32)
    table = mm(jnp.where(hit, high, 0.0).astype(bf16), into, 1, 1) + mm(
        jnp.where(hit, weight - high, 0.0).astype(bf16), into, 1, 1
    )
    table = table / jnp.sum(table, axis=0, keepdims=True)
    for member in range(members):
        high = table.astype(bf16)
        columns = slice(member * points, (member + 1) * points)
        share_ref[0:rows, columns] = high
        share_ref[rows : 2 * rows, columns] = (table - high.astype(f32)).astype(bf16)
        table = jnp.concatenate([table[rows - cap :], table[: rows - cap]], axis=0)


def gathered(own_ref, near_ref, far_refs):
    return jnp.concatenate([own_ref[0], near_ref[0]] + [r[...] for r in far_refs[::-1]], axis=0)


def forward_kernel(
    far, w_msg_ref, share_ref, gain_ref, embed_ref, weights_ref, project_ref, present_ref,
    own_ref, near_ref, *rest,
):
    far_refs = rest[:far]
    field_ref, sent_ref, normed_ref, active_ref, slope_ref, unit_ref, inverse_ref = rest[far:]
    points, width = embed_ref.shape
    variables, members, _ = present_ref.shape
    messages = mm(gathered(own_ref, near_ref, far_refs), w_msg_ref[...], 1, 0).astype(bf16)
    messages = jnp.concatenate([messages, messages], axis=0)
    gain = gain_ref[...].reshape(1, width)
    for begin in range(0, members * points, lanes):
        rows = slice(begin, begin + lanes)
        source = slice(begin % points, begin % points + lanes)
        hidden = embed_ref[source, :].astype(f32) + mm(share_ref[:, rows], messages, 0, 0)
        inverse = lax.rsqrt(jnp.mean(hidden * hidden, axis=-1, keepdims=True) + epsilon)
        unit = hidden * inverse
        unit_ref[rows, :] = unit
        inverse_ref[rows, :] = inverse
        normed_ref[rows, :] = (unit * gain).astype(bf16)
    root = 0.7978845608028654
    cubic = 0.044715
    for member in range(members):
        rows = slice(member * points, (member + 1) * points)
        for begin in range(0, width, tile):
            columns = slice(begin, begin + tile)
            inner = mm(normed_ref[rows, :], weights_ref[:, columns], 1, 0)
            square = inner * inner
            bend = jnp.tanh(inner * (root + root * cubic * square))
            half = 0.5 + 0.5 * bend
            active_ref[rows, columns] = (inner * half).astype(bf16)
            slope_ref[rows, columns] = half + (0.5 * inner) * (1.0 - bend * bend) * (
                root + 3.0 * root * cubic * square
            )
        field = present_ref[:, member, :] + mm(project_ref[...], active_ref[rows, :], 1, 1)
        field_ref[member] = field
        sent_ref[member] = field.astype(bf16)


def turn_kernel(normed_ref, active_ref, own_ref, near_ref, *rest):
    far_refs, (normed_t_ref, active_t_ref, keep_ref, give_ref) = rest[:-4], rest[-4:]
    _, _, levels, block, _ = normed_t_ref.shape
    width = normed_ref.shape[1]
    level, line, core = place()
    received = gathered(own_ref, near_ref, far_refs)
    for source, target in ((received, None), (normed_ref, normed_t_ref), (active_ref, active_t_ref)):
        for begin in range(0, width, tile):
            turned = source[:, begin : begin + tile].T
            for piece in range(0, tile, block):
                index = (begin + piece) // block
                far = (index // 2 % 2) ^ line
                step = (index // 4) ^ level
                side = (index % 2) ^ core
                value = turned[piece : piece + block]
                if target is not None:
                    target[side, 1 - far, levels - 1 - step] = value
                    continue
                for which, part_ref in enumerate((keep_ref, give_ref)):
                    @pl.when(side == which)
                    def _(part_ref=part_ref):
                        part_ref[1 - far, levels - 1 - step] = value


def split_loss(part, variables):
    column = lax.broadcasted_iota(jnp.int32, part.shape, 1)
    spots = (column == variables) | (column == variables + 1)
    total = jnp.sum(jnp.where(spots, part, 0.0), axis=1, keepdims=True)
    high = total.astype(bf16).astype(f32)
    return jnp.where(column == variables, high, jnp.where(column == variables + 1, total - high, part))


def score_kernel(
    own_ref, other_ref, truth_ref, cell_ref, project_ref, slope_ref, normed_t_ref, active_t_ref,
    inner_ref, pred_ref, loss_ref, far_ref, near_ref, hold_ref,
):
    members, variables, points = own_ref.shape
    width = slope_ref.shape[1]
    total = 2 * members
    pairs = total * (total - 1)

    def eased(delta):
        square = delta * delta + smoothing * smoothing
        inverse = lax.rsqrt(square)
        return square * inverse, delta * inverse

    truth, cell = truth_ref[...], cell_ref[...].reshape(1, points)
    own = [own_ref[m] for m in range(members)]
    other = [other_ref[m].astype(f32) for m in range(members)]
    score = jnp.zeros_like(truth)
    pulls = [jnp.zeros_like(truth) for _ in own]
    grads = []
    for m in range(members):
        size, sign = eased(own[m] - truth)
        score = score + size * (1.0 / total)
        grads.append(sign * (1.0 / total))
    for m in range(members):
        for n in range(m + 1, members):
            size, sign = eased(own[m] - own[n])
            score = score - size * (1.0 / pairs)
            pulls[m] = pulls[m] + sign
            pulls[n] = pulls[n] - sign
        for n in range(members):
            size, sign = eased(own[m] - other[n])
            score = score - size * (0.5 / pairs)
            pulls[m] = pulls[m] + sign
    loss = jnp.sum(score * cell)
    loss_ref[0] = loss
    hold_ref[...] = jnp.zeros_like(hold_ref)
    for m in range(members):
        grad = (grads[m] - pulls[m] * (1.0 / pairs)) * cell
        hold_ref[0:variables, m * points : (m + 1) * points] = grad
    pred = hold_ref[...].astype(bf16)
    pred_ref[...] = pred
    for m in range(members):
        rows = slice(m * points, (m + 1) * points)
        part = pred[:variables, rows]
        for begin in range(0, width, tile):
            columns = slice(begin, begin + tile)
            grad = mm(part, project_ref[:, columns], 0, 0)
            inner_ref[rows, columns] = (grad * slope_ref[rows, columns]).astype(bf16)
    weight_parts(normed_t_ref, active_t_ref, inner_ref, pred, loss, variables, 1, 0, far_ref)
    weight_parts(normed_t_ref, active_t_ref, inner_ref, pred, loss, variables, 1, 1, near_ref)


def weight_parts(normed_t_ref, active_t_ref, inner_ref, pred, loss, variables, side, half, out_ref):
    width = inner_ref.shape[1]
    depth = normed_t_ref.shape[-1]
    normed = normed_t_ref[side, half].reshape(-1, depth)
    for begin in range(0, width, tile):
        columns = slice(begin, begin + tile)
        out_ref[:, columns] = mm(normed, inner_ref[:, columns], 1, 0).astype(out_ref.dtype)
    part = mm(active_t_ref[side, half].reshape(-1, depth), pred, 1, 1)
    part = jnp.where(lax.broadcasted_iota(jnp.int32, part.shape, 1) == variables, loss, part)
    out_ref[:, width:] = split_loss(part, variables).astype(out_ref.dtype)


def pack(out_ref, begin, part):
    pad = part.shape[1]
    for i in range(part.shape[0] // packed):
        out_ref[begin : begin + packed, i * pad : (i + 1) * pad] = part[i * packed : (i + 1) * packed]


def unpack(in_ref, begin, count, pad):
    parts = [in_ref[begin : begin + packed, i * pad : (i + 1) * pad] for i in range(count // packed)]
    return jnp.concatenate(parts, axis=0).astype(f32)


def local_kernel(variables, half, loss_ref, normed_t_ref, active_t_ref, inner_ref, pred_ref, out_ref):
    weight_parts(
        normed_t_ref, active_t_ref, inner_ref, pred_ref[...], loss_ref[0], variables, 0, half, out_ref
    )


def pair_sum(variables, width, held_ref, other_ref, begin, count):
    rows = slice(begin, begin + count)
    total = held_ref[rows, :width] + other_ref[rows, :width].astype(f32)
    part = held_ref[rows, width:] + other_ref[rows, width:].astype(f32)
    return total, split_loss(part, variables)


def first_kernel(variables, width, held_ref, other_ref, out_ref):
    total, part = pair_sum(variables, width, held_ref, other_ref, 0, out_ref.shape[0])
    out_ref[:, :width] = total.astype(bf16)
    out_ref[:, width:] = part.astype(bf16)


def message_kernel(
    variables, early, levels, keep_ref, give_ref, slots_ref, other_ref, held_ref, far_other_ref,
    first_ref, middle_ref, last_ref, near_ref,
):
    depth, width = keep_ref.shape[-1], near_ref.shape[1]
    block = near_ref.shape[0] // levels
    count, rest = early * block, (levels - 1 - early) * block
    for begin, size, out_ref in ((count, rest, middle_ref), (count + rest, block, last_ref)):
        total, part = pair_sum(variables, width, held_ref, far_other_ref, begin, size)
        out_ref[0:size, :] = total.astype(bf16)
        out_ref[size : size + packed, :] = jnp.zeros((packed, width), bf16)
        pack(out_ref, size, part.astype(bf16))
    for half in range(2):
        own = keep_ref[half].reshape(-1, depth)
        other = give_ref[half].reshape(-1, depth)
        for begin in range(0, width, tile):
            columns = slice(begin, begin + tile)
            here = slots_ref[:, :, columns].reshape(depth, tile)
            there = other_ref[:, :, columns].reshape(depth, tile)
            total = mm(own, here, 1, 0) + mm(other, there, 1, 0)
            if half == 0:
                total = total.astype(bf16)
                first_ref[:, columns] = total[:count]
                middle_ref[rest + packed :, columns] = total[count : count + rest]
                last_ref[block + packed :, columns] = total[count + rest :]
            else:
                near_ref[:, columns] = total


def ride_kernel(last_ref, slots_ref, *rest):
    arrived_refs, out_ref = rest[:-1], rest[-1]
    rows = slots_ref.shape[1]
    begin = last_ref.shape[0]
    out_ref[0:begin, :] = last_ref[...]
    for i, arrived_ref in enumerate(arrived_refs):
        out_ref[begin + i * rows : begin + (i + 1) * rows, :] = arrived_ref[rows:, :]
    out_ref[begin + len(arrived_refs) * rows :, :] = slots_ref[1]


def hidden_early_kernel(variables, width, held_ref, other_ref, arrived_ref, *out_refs):
    block = out_refs[0].shape[0]
    for i, out_ref in enumerate(out_refs):
        total, part = pair_sum(variables, width, held_ref, other_ref, i * block, block)
        here = slice(i * block, (i + 1) * block)
        out_ref[:, :width] = (total + arrived_ref[here, :width].astype(f32)).astype(bf16)
        part = split_loss(part + arrived_ref[here, width:].astype(f32), variables)
        out_ref[:, width:] = part.astype(bf16)


def message_early_kernel(begin, near_ref, arrived_ref, out_ref):
    here = slice(begin, begin + out_ref.shape[0])
    out_ref[...] = (near_ref[here, :] + arrived_ref[here, :].astype(f32)).astype(bf16)


def late_kernel(variables, early, held_ref, other_ref, near_ref, arrived_ref, *out_refs):
    width = near_ref.shape[1]
    block = (out_refs[0].shape[0] - packed) // 2
    count = block * len(out_refs)
    parts = unpack(arrived_ref, count, count, held_ref.shape[1] - width)
    for i, out_ref in enumerate(out_refs):
        begin = (early + i) * block
        total, part = pair_sum(variables, width, held_ref, other_ref, begin, block)
        here = slice(i * block, (i + 1) * block)
        out_ref[0:block, :] = (total + arrived_ref[here, :].astype(f32)).astype(bf16)
        there = slice(count + packed + i * block, count + packed + (i + 1) * block)
        total = near_ref[begin : begin + block, :] + arrived_ref[there, :].astype(f32)
        out_ref[block : 2 * block, :] = total.astype(bf16)
        out_ref[2 * block :, :] = jnp.zeros((packed, width), bf16)
        pack(out_ref, 2 * block, split_loss(part + parts[here], variables).astype(bf16))


def back_kernel(inner_ref, w_hidden_ref, gain_ref, unit_ref, inverse_ref, grad_ref, scaled_ref):
    rows_all, width = inner_ref.shape
    gain = gain_ref[...].reshape(1, width)
    for begin_row in range(0, rows_all, tile):
        rows = slice(begin_row, begin_row + tile)
        dots = jnp.zeros((tile, 1), f32)
        for begin in range(0, width, tile):
            columns = slice(begin, begin + tile)
            scaled = mm(inner_ref[rows, :], w_hidden_ref[columns, :], 1, 1) * gain[:, columns]
            dots = dots + jnp.sum(scaled * unit_ref[rows, columns], axis=-1, keepdims=True)
            scaled_ref[rows, columns] = scaled
        dots = dots * (1.0 / width)
        inverse = inverse_ref[rows, :]
        for begin in range(0, width, tile):
            columns = slice(begin, begin + tile)
            grad_ref[rows, columns] = (
                (scaled_ref[rows, columns] - unit_ref[rows, columns] * dots) * inverse
            ).astype(bf16)


def slot_kernel(share_ref, grad_ref, slots_ref, *send_refs):
    peers, each, width = slots_ref.shape
    rows = peers * each
    for begin in range(0, width, tile):
        columns = slice(begin, begin + tile)
        both = mm(share_ref[...], grad_ref[:, columns], 1, 0)
        slots_ref[:, :, columns] = (both[:rows] + both[rows:]).astype(bf16).reshape(peers, each, tile)
    for i, send_ref in enumerate(send_refs):
        step = len(send_refs) - i
        send_ref[0:each, :] = slots_ref[2 * step]
        send_ref[each:, :] = slots_ref[2 * step + 1]


def owner_kernel(pick_ref, w_msg_ref, slots_ref, last_ref, *rest):
    arrived_refs, (grad_ref, token_ref, held_ref) = rest[:-3], rest[-3:]
    token_ref[...] = jnp.zeros_like(token_ref)
    peers, rows, width = slots_ref.shape
    levels = peers // 2
    begin = last_ref.shape[0] - levels * rows
    for i in range(levels):
        spot = 2 * (levels - 1 - i)
        held_ref[spot] = slots_ref[0] if i == levels - 1 else arrived_refs[i][0:rows, :]
        held_ref[spot + 1] = last_ref[begin + i * rows : begin + (i + 1) * rows, :]
    nodes = mm(pick_ref[...], held_ref[...].reshape(peers * rows, width), 0, 0).astype(bf16)
    grad_ref[...] = mm(nodes, w_msg_ref[...], 1, 1).astype(bf16).reshape(grad_ref.shape)


def hidden_sum_kernel(variables, scale, early, held_ref, other_ref, last_ref, *rest):
    hidden_ref, out_ref, loss_ref, token_ref = rest[-4:]
    token_ref[...] = jnp.zeros_like(token_ref)
    block, width = hidden_ref.shape
    pad = held_ref.shape[1] - width
    total, part = pair_sum(variables, width, held_ref, other_ref, held_ref.shape[0] - block, block)
    total = total + last_ref[0:block, :].astype(f32)
    part = part + unpack(last_ref, block, block, pad)
    for i, r in enumerate(rest[:-4]):
        total = total + r[0:block, :width].astype(f32)
        if i < early:
            part = part + r[:, width:].astype(f32)
        else:
            part = part + unpack(r, 2 * block, block, pad)
    hidden_ref[...] = total
    out_ref[...] = part[:, :variables]
    column = lax.broadcasted_iota(jnp.int32, (8, pad), 1)
    spots = (column == variables) | (column == variables + 1)
    first = lax.broadcasted_iota(jnp.int32, (8, pad), 0) == 0
    loss_ref[0] = jnp.sum(jnp.where(spots & first, part[:8], 0.0)) * scale


def message_partial_kernel(early, near_ref, last_ref, *rest):
    out_ref = rest[-1]
    block = out_ref.shape[0]
    total = near_ref[near_ref.shape[0] - block :, :]
    total = total + last_ref[block + packed : 2 * block + packed, :].astype(f32)
    for i, r in enumerate(rest[:-1]):
        begin = 0 if i < early else block
        total = total + r[begin : begin + block, :].astype(f32)
    out_ref[...] = total


def message_sum_kernel(partial_ref, arrived_ref, out_ref):
    out_ref[...] = partial_ref[...] + arrived_ref[...].astype(f32)


def on_device(
    latents, grid_embed, norm_gain, w_msg, w_hidden, variable_projection, present_condition, verifying_field,
    cell_surface, send_rows, edge_slot, edge_dst, edge_weight,
):
    members, nodes, width = latents.shape
    points = grid_embed.shape[0]
    variables = variable_projection.shape[1]
    peers = lax.axis_size("space")
    cores = lax.axis_size("member")
    cap = send_rows.shape[2]
    rows_peer = members * cap
    rows_slot = peers * rows_peer
    rows_all = members * points
    levels = peers // 2
    block = width // (peers * cores)
    half = levels * block
    wide = width + -(-(variables + 2) // lanes) * lanes
    project = variable_projection.T

    early = levels // 2
    count, rest = early * block, (levels - 1 - early) * block
    steps = [2 * (levels - 1 - i) for i in range(levels - 1)]

    def spread(values, part):
        return [swap(x, "space", peers, k) for x, k in zip(values, part, strict=True)]

    pick, own_rows, send = call(
        select_kernel,
        [((rows_slot, members * nodes), bf16)] + [((levels, rows_peer, width), bf16)] * 2,
        [send_rows, latents],
        scratch=[
            pltpu.SMEM(send_rows.shape, jnp.int32),
            pltpu.VMEM(latents.shape, bf16),
            pltpu.SemaphoreType.DMA((2,)),
        ],
        limit=4,
        places=(0, 1),
    )
    near_rows = swap(send, "space", peers, 1)
    fixed = [w_msg, norm_gain, grid_embed, w_hidden, project, present_condition.transpose(1, 0, 2)]
    edges = [edge_slot, edge_dst, edge_weight]
    share, *staged = call(
        functools.partial(stage_kernel, cap, members, len(fixed)),
        [((2 * rows_slot, rows_all), bf16)] + [(x.shape, x.dtype) for x in fixed],
        edges + fixed,
        scratch=[pltpu.VMEM(x.shape, x.dtype) for x in edges]
        + [pltpu.SemaphoreType.DMA((3 + len(fixed),))],
        limit=16,
        places=tuple(range(3 + len(fixed))),
        after=[pick],
    )
    merged = call(
        merge_kernel,
        [((2 * rows_peer, width), bf16)] * (levels - 1),
        [own_rows, near_rows],
        limit=4,
        after=[share],
    )
    received = [own_rows, near_rows] + spread(merged, steps)
    w_msg_near, gain, embed, w_hidden_near, project_near, present = staged
    field, sent, normed, active, slope, unit, inverse = call(
        functools.partial(forward_kernel, levels - 1),
        [
            ((members, variables, points), f32),
            ((members, variables, points), bf16),
            ((rows_all, width), bf16),
            ((rows_all, width), bf16),
            ((rows_all, width), f32),
            ((rows_all, width), f32),
            ((rows_all, 1), f32),
        ],
        [w_msg_near, share, gain, embed, w_hidden_near, project_near, present] + received,
        limit=20,
    )
    other = swap(sent, "member", cores, 1)
    normed_t, active_t, received_keep, received_give = call(
        turn_kernel,
        [((cores, 2, levels, block, rows_all), bf16)] * 2 + [((2, levels, block, rows_slot), bf16)] * 2,
        [normed, active] + received,
        limit=8,
    )
    received_other = swap(received_give, "member", cores, 1)
    grad_inner, pred, loss_part, far, near = call(
        score_kernel,
        [
            ((rows_all, width), bf16),
            ((lanes, rows_all), bf16),
            ((1,), f32),
            ((half, wide), bf16),
            ((half, wide), bf16),
        ],
        [field, other, verifying_field, cell_surface, project_near, slope, normed_t, active_t],
        scratch=[pltpu.VMEM((lanes, rows_all), f32)],
        limit=16,
        scalar_outs=(2,),
    )
    far_other = swap(far, "member", cores, 1)
    near_other = swap(near, "member", cores, 1)
    def local(half, after):
        (held,) = call(
            functools.partial(local_kernel, variables, half),
            [((levels * block, wide), f32)],
            [loss_part, normed_t, active_t, grad_inner, pred],
            limit=12,
            scalars=(0,),
            after=after,
        )
        return held

    held_far = local(0, [])
    (first,) = call(
        functools.partial(first_kernel, variables, width),
        [((count, wide), bf16)],
        [held_far, far_other],
        limit=6,
    )
    first_other = swap(first, "space", peers, 1)
    held_near = local(1, [first])
    (grad_hidden,) = call(
        back_kernel,
        [((rows_all, width), bf16)],
        [grad_inner, w_hidden_near, gain, unit, inverse],
        scratch=[pltpu.VMEM((rows_all, width), f32)],
        limit=14,
        after=[first],
    )
    slots, *slots_sent = call(
        slot_kernel,
        [((peers, rows_peer, width), bf16)] + [((2 * rows_peer, width), bf16)] * (levels - 1),
        [share, grad_hidden],
        limit=6,
        after=[near_other, received_other],
    )
    slots_other = swap(slots, "member", cores, 1)
    slots_arrived = spread(slots_sent, steps)
    message_first, middle, last, message_near = call(
        functools.partial(message_kernel, variables, early, levels),
        [
            ((count, width), bf16),
            ((2 * rest + packed, width), bf16),
            ((2 * block + packed, width), bf16),
            ((half, width), f32),
        ],
        [received_keep, received_other, slots, slots_other, held_far, far_other],
        limit=10,
    )
    message_first_other = swap(message_first, "space", peers, 1)
    middle_other = swap(middle, "space", peers, 1)
    hidden_early = call(
        functools.partial(hidden_early_kernel, variables, width),
        [((block, wide), bf16)] * early,
        [held_near, near_other, first_other],
        limit=6,
    )
    hidden_parts = spread(hidden_early, steps[:early])
    (last,) = call(
        ride_kernel,
        [((2 * block + packed + levels * rows_peer, width), bf16)],
        [last, slots] + slots_arrived,
        limit=4,
        after=hidden_early[:1],
    )
    last_other = swap(last, "space", peers, 1)
    message_parts = []
    for i in range(early):
        (piece,) = call(
            functools.partial(message_early_kernel, i * block),
            [((block, width), bf16)],
            [message_near, message_first_other],
            limit=6,
            after=hidden_parts[1 : 1 + i],
        )
        message_parts.append(swap(piece, "space", peers, steps[i]))
    late = call(
        functools.partial(late_kernel, variables, early),
        [((2 * block + packed, width), bf16)] * (levels - 1 - early),
        [held_near, near_other, message_near, middle_other],
        limit=6,
    )
    late_parts = spread(late, steps[early:])
    token = ((8, lanes), f32)
    latent_grad, latent_done = call(
        owner_kernel,
        [(latents.shape, bf16), token],
        [pick, w_msg, slots, last_other] + slots_arrived,
        scratch=[pltpu.VMEM((peers, rows_peer, width), bf16)],
        limit=8,
    )
    hidden_weight_grad, out_weight_grad, loss, hidden_done = call(
        functools.partial(hidden_sum_kernel, variables, 1.0 / (points * peers * variables), early),
        [((block, width), f32), ((block, variables), f32), ((1,), f32), token],
        [held_near, near_other, last_other] + hidden_parts + late_parts,
        limit=8,
        scalar_outs=(2,),
        after=[latent_done],
    )
    (message_partial,) = call(
        functools.partial(message_partial_kernel, early - 1),
        [((block, width), f32)],
        [message_near, last_other] + message_parts[:-1] + late_parts,
        limit=6,
        after=[hidden_done],
    )
    (msg_weight_grad,) = call(
        message_sum_kernel, [((block, width), f32)], [message_partial, message_parts[-1]], limit=4
    )
    return (latent_grad, loss, msg_weight_grad, hidden_weight_grad, out_weight_grad)


def solution(mesh):
    placed = (
        P(("groups", "member"), "space", None),
        P(("groups", "space"), None),
        P(),
        P(),
        P(),
        P(),
        P(("groups", "member"), None, "space"),
        P(None, ("groups", "space")),
        P(("groups", "space")),
        P("space", None, None),
        P("space"),
        P("space"),
        P("space"),
    )
    return jax.shard_map(
        on_device,
        mesh=mesh,
        in_specs=placed,
        out_specs=(
            P(("groups", "member"), "space", None),
            P("groups"),
            P(("groups", "space", "member"), None),
            P(("groups", "space", "member"), None),
            P(("groups", "space", "member"), None),
        ),
        check_vma=False,
    )
```
